32 devices in a mesh: batch: 8 (over z, core), seq: 4 (over y, x).
Axes of the slice: x: 2, y: 2, z: 4, core: 2. Of those that a mesh axis runs over, the one named last changes fastest.
Arguments:
- frames_in: bfloat16 [8, 1024, 1024], P('batch', 'seq'), may hold values from -6 to 6
- cotangent: bfloat16 [8, 1024, 1024], P('batch', 'seq'), may hold values from -6 to 6
- levels: int32 [8], P('batch'), may hold values from 1 to 12
- lengths: int32 [8], replicated, may hold values from 256 to 1024, as said below
- token_mask: int32 [8, 1024], P('batch', 'seq'), may hold values 0 or 1
- cond_table: bfloat16 [13, 1024], replicated, may hold values from -3 to 3
- norm_gains: bfloat16 [5, 1024], replicated, may hold values from 0.25 to 1.75
- w_ffn1_up: bfloat16 [1024, 4096], replicated, may hold values from -0.1875 to 0.1875
- w_ffn1_down: bfloat16 [4096, 1024], replicated, may hold values from -0.1875 to 0.1875
- w_qkv: bfloat16 [1024, 3072], replicated, may hold values from -0.25 to 0.25
- w_out: bfloat16 [1024, 1024], replicated, may hold values from -1.5 to 1.5
- w_glu: bfloat16 [1024, 2048], replicated, may hold values from -0.1875 to 0.1875
- conv_kernel: bfloat16 [5, 1024], replicated, may hold values from -2.5 to 2.5
- bn_gain: bfloat16 [1024], replicated, may hold values from 0.25 to 1.75
- batchnorm_shift_bias: bfloat16 [1024], replicated, may hold values from -3 to 3
- w_conv_out: bfloat16 [1024, 1024], replicated, may hold values from -0.1875 to 0.1875
- w_ffn2_up: bfloat16 [1024, 4096], replicated, may hold values from -0.1875 to 0.1875
- w_ffn2_down: bfloat16 [4096, 1024], replicated, may hold values from -0.1875 to 0.1875
- running_mean: float32 [1024], replicated, may hold values from -0.24 to 0.24
- running_var: float32 [1024], replicated, may hold values from 0.02 to 0.1
Outputs:
- out: bfloat16 [8, 1024, 1024], P('batch', 'seq')
- input_grad: bfloat16 [8, 1024, 1024], P('batch', 'seq')
- cond_grad: float32 [13, 1024], P(None, 'seq')
- gains_grad: float32 [5, 1024], P(None, 'seq')
- w_ffn1_up_grad: float32 [1024, 4096], P('seq', 'batch')
- w_ffn1_down_grad: float32 [4096, 1024], P(('batch', 'seq'))
- w_qkv_grad: float32 [1024, 3072], P('seq', 'batch')
- w_out_grad: float32 [1024, 1024], P('seq', 'batch')
- w_glu_grad: float32 [1024, 2048], P('seq', 'batch')
- kernel_grad: float32 [5, 1024], P(None, 'seq')
- bn_gain_grad: float32 [1024], replicated
- bn_bias_grad: float32 [1024], replicated
- w_conv_out_grad: float32 [1024, 1024], P('seq', 'batch')
- w_ffn2_up_grad: float32 [1024, 4096], P('seq', 'batch')
- w_ffn2_down_grad: float32 [4096, 1024], P(('batch', 'seq'))
- new_running_mean: float32 [1024], replicated
- new_running_var: float32 [1024], replicated
The draws below stay inside these ranges and needn't reach their ends.
Inputs may be any that keep to these rules, and one draw needn't show every extreme that they name: `lengths`: each item has between 256 and 1024 valid frames, a prefix of the item; at least one item is valid throughout.
All inputs are finite; a program needn't handle non-finite values. No bound on the sum of `token_mask` on one device may be relied on, other than what follows from the above.
Results may differ from the reference program's by a relative error of at most 0.024.
Values may be sent and summed in bfloat16 or wider, within the bound.
A program may use at most 448 MiB of HBM per device.

```python
import math
import jax
import jax.numpy as jnp
from jax import lax

D = 1024
HEADS = 16
HD = 64
FF = 4096
KERNEL = 5
LEVELS = 12
LENGTH = 1024
ITEMS = 8


def draw_lengths(key, part):
    spread = jax.random.randint(key, (ITEMS,), LENGTH // 4, LENGTH + 1)
    longest = jax.random.randint(jax.random.fold_in(key, 7), (), 0, ITEMS)
    return jnp.where(jnp.arange(ITEMS) == longest, LENGTH, spread).astype(jnp.int32)


def set_ends(array, rng, smallest, high):
    longest = array.shape.index(max(array.shape))
    spots = []
    for shift in (0, 1):
        where = [jax.random.randint(jax.random.fold_in(rng, axis), (), 0, length) for axis, length in enumerate(array.shape)]
        where[longest] = (where[longest] + shift) % array.shape[longest]
        spots.append(tuple(where))
    return array.at[spots[0]].set(smallest).at[spots[1]].set(high)


def block_scale(stream_key, shape, shards, low, high):
    level = 1.0
    for position, blocks in shards:
        heights = jax.random.uniform(jax.random.fold_in(jax.random.fold_in(stream_key, 6), position), (blocks,), jnp.float32, low / len(shards), high / len(shards))
        level = level * jnp.repeat(jnp.exp(heights), shape[position] // blocks).reshape((-1,) + (1,) * (len(shape) - 1 - position))
    return level


def bell_draw(stream_key, dims, width, bound, cuts=(), held_as=jnp.bfloat16):
    drawn = width * jax.random.normal(stream_key, dims, jnp.float32)
    if cuts:
        drawn = drawn * block_scale(stream_key, dims, cuts, -0.22, 0.18)
    return jnp.clip(drawn, -bound, bound).astype(held_as)


def setup_inputs(seed: int = 0) -> dict:
    splits = jax.random.split(jax.random.key(seed), 21)
    return {
        "frames_in": bell_draw(splits[0], (ITEMS, LENGTH, D), 1.0, 6.0, ((0, 8), (1, 4))),
        "cotangent": bell_draw(splits[1], (ITEMS, LENGTH, D), 1.0, 6.0, ((0, 8), (1, 4))),
        "levels": set_ends(jax.random.randint(splits[2], (ITEMS,), 1, LEVELS + 1), jax.random.fold_in(splits[2], 1), 1, LEVELS).astype(jnp.int32),
        "lengths": draw_lengths(jax.random.fold_in(splits[20], 71), 0),
        "token_mask": set_ends((jax.random.randint(splits[4], (ITEMS, LENGTH), 0, 2) < 1).astype(jnp.int32), jax.random.fold_in(splits[4], 1), 0, 1),
        "cond_table": bell_draw(splits[5], (LEVELS + 1, D), 0.5, 3.0),
        "norm_gains": jnp.clip(1.0 + 0.15 * jax.random.normal(splits[6], (5, D), jnp.float32), 0.25, 1.75).astype(jnp.bfloat16),
        "w_ffn1_up": bell_draw(splits[7], (D, FF), D ** -0.5, 0.1875),
        "w_ffn1_down": bell_draw(splits[8], (FF, D), (FF // 4) ** -0.5, 0.1875),
        "w_qkv": bell_draw(splits[9], (D, 3 * D), (D // 2) ** -0.5, 0.25),
        "w_out": bell_draw(splits[10], (D, D), (D // 64) ** -0.5, 1.5),
        "w_glu": bell_draw(splits[11], (D, 2 * D), D ** -0.5, 0.1875),
        "conv_kernel": bell_draw(splits[12], (KERNEL, D), KERNEL ** -0.5, 2.5),
        "bn_gain": jnp.clip(1.0 + 0.15 * jax.random.normal(splits[13], (D,), jnp.float32), 0.25, 1.75).astype(jnp.bfloat16),
        "batchnorm_shift_bias": bell_draw(splits[14], (D,), 0.5, 3.0),
        "w_conv_out": bell_draw(splits[15], (D, D), D ** -0.5, 0.1875),
        "w_ffn2_up": bell_draw(splits[16], (D, FF), D ** -0.5, 0.1875),
        "w_ffn2_down": bell_draw(splits[17], (FF, D), (FF // 4) ** -0.5, 0.1875),
        "running_mean": bell_draw(splits[18], (D,), 0.04, 0.24, (), jnp.float32),
        "running_var": jnp.clip(jnp.exp(jax.random.uniform(splits[19], (D,), jnp.float32, math.log(0.02), math.log(0.1))), 0.02, 0.1),
    }


EPSILON = 1e-05
MASKED_SCORE = -1000000000.0
PRECISE = lax.Precision.HIGHEST

@jax.custom_vjp
def low(v):
    return lax.optimization_barrier(v.astype(jnp.bfloat16)).astype(jnp.float32)

@jax.custom_vjp
def low_back(v):
    return v

def low_keep(v):
    return (low(v), None)

def low_pass(kept, grad):
    return (grad,)

def back_keep(v):
    return (v, None)

def back_low(kept, grad):
    return (low(grad),)
low.defvjp(low_keep, low_pass)
low_back.defvjp(back_keep, back_low)

def layer_norm(values, gain_row):
    centre = values - lax.optimization_barrier(jnp.mean(values, axis=-1, keepdims=True))
    spread = lax.optimization_barrier(jnp.mean(centre * centre, axis=-1, keepdims=True))
    return centre * lax.rsqrt(spread + EPSILON) * gain_row

def rope_tables(positions, head_size):
    half_size = head_size // 2
    inv_freqs = jnp.exp(jnp.arange(half_size).astype(jnp.float32) * (-2.0 * math.log(10000.0) / head_size))
    angles = positions.astype(jnp.float32)[:, None] * inv_freqs[None, :]
    return (jnp.cos(angles), jnp.sin(angles))

def rotate(values, cosine, sine_table):
    half_size = values.shape[-1] // 2
    first_half = values[..., :half_size]
    second_half = values[..., half_size:]
    return jnp.concatenate([first_half * cosine - second_half * sine_table, second_half * cosine + first_half * sine_table], axis=-1)

def project(values, weight):
    return jnp.einsum('ild,de->ile', values, weight, precision=PRECISE, preferred_element_type=jnp.float32)

def feed_forward(values, gain_row, up_weight, down_weight):
    lowered = low(layer_norm(values, gain_row))
    hidden = low_back(project(lowered, up_weight))
    act_rows = low(hidden * jax.nn.sigmoid(hidden))
    branch = low_back(project(act_rows, down_weight))
    return values + 0.5 * branch

def attend_one(pieces):
    query_head, key_head, value_head, keep_row = pieces
    scores = low_back(jnp.dot(query_head, key_head.T, precision=PRECISE, preferred_element_type=jnp.float32))
    scores = jnp.where(keep_row[None, :] > 0.5, scores, MASKED_SCORE)
    row_peak = lax.optimization_barrier(jnp.max(scores, axis=-1, keepdims=True))
    exp_scores = jnp.exp(scores - row_peak)
    probs_row = exp_scores / lax.optimization_barrier(jnp.sum(exp_scores, axis=-1, keepdims=True))
    return jnp.dot(low(probs_row), value_head, precision=PRECISE, preferred_element_type=jnp.float32)

def forward(frames_in, cond_table, norm_gains, w_ffn1_up, w_ffn1_down, w_qkv, w_out, w_glu, conv_kernel, bn_gain, batchnorm_shift_bias, w_conv_out, w_ffn2_up, w_ffn2_down, level_hot, masked, valid):
    level_rows = jnp.einsum('il,ld->id', level_hot, cond_table[:LEVELS], precision=PRECISE)
    rows_zero = frames_in + level_rows[:, None, :] + masked[:, :, None] * cond_table[LEVELS][None, None, :]
    rows_one = feed_forward(rows_zero, norm_gains[0], w_ffn1_up, w_ffn1_down)
    attn_in = low(layer_norm(rows_one, norm_gains[1]))
    qkv_rows = low_back(project(attn_in, w_qkv)).reshape(ITEMS, LENGTH, HEADS, 3, HD)
    cosine, sine_table = rope_tables(jnp.arange(LENGTH), HD)
    query_rot = low(rotate(qkv_rows[:, :, :, 0], cosine[:, None], sine_table[:, None]) * 0.125)
    key_rot = low(rotate(qkv_rows[:, :, :, 1], cosine[:, None], sine_table[:, None]))
    value_low = low(qkv_rows[:, :, :, 2])
    query_heads = query_rot.transpose(0, 2, 1, 3).reshape(ITEMS * HEADS, LENGTH, HD)
    key_heads = key_rot.transpose(0, 2, 1, 3).reshape(ITEMS * HEADS, LENGTH, HD)
    value_heads = value_low.transpose(0, 2, 1, 3).reshape(ITEMS * HEADS, LENGTH, HD)
    keep_rows = jnp.repeat(valid, HEADS, axis=0)
    mixed_heads = lax.map(jax.checkpoint(attend_one), (query_heads, key_heads, value_heads, keep_rows))
    mixed_rows = mixed_heads.reshape(ITEMS, HEADS, LENGTH, HD).transpose(0, 2, 1, 3).reshape(ITEMS, LENGTH, D)
    attn_out = low_back(low(mixed_rows))
    rows_two = rows_one + low_back(project(attn_out, w_out))
    conv_in = low(layer_norm(rows_two, norm_gains[2]))
    glu_pre = low_back(project(conv_in, w_glu))
    glu_rows = low(glu_pre[..., :D] * jax.nn.sigmoid(glu_pre[..., D:]) * valid[..., None])
    half_size = KERNEL // 2
    padded = jnp.pad(glu_rows, ((0, 0), (half_size, half_size), (0, 0)))
    convolved_rows = jnp.zeros_like(glu_rows)
    for tap_index in range(KERNEL):
        convolved_rows = convolved_rows + conv_kernel[tap_index] * padded[:, tap_index:tap_index + LENGTH]
    convolved_rows = low_back(convolved_rows)
    weight_rows = valid[..., None]
    count_of_frames = jnp.sum(valid)
    batchnorm_frame_mean = lax.optimization_barrier(jnp.sum(convolved_rows * weight_rows, axis=(0, 1))) / count_of_frames
    bn_var = lax.optimization_barrier(jnp.sum(convolved_rows * convolved_rows * weight_rows, axis=(0, 1))) / count_of_frames - batchnorm_frame_mean * batchnorm_frame_mean
    batchnorm_input_rows = (convolved_rows - batchnorm_frame_mean) * lax.rsqrt(bn_var + EPSILON) * bn_gain + batchnorm_shift_bias
    act_rows = low(batchnorm_input_rows * jax.nn.sigmoid(batchnorm_input_rows))
    rows_three = rows_two + low_back(project(act_rows, w_conv_out))
    rows_four = feed_forward(rows_three, norm_gains[3], w_ffn2_up, w_ffn2_down)
    return (layer_norm(rows_four, norm_gains[4]), (batchnorm_frame_mean, bn_var))

def reference(frames_in, cotangent, levels, lengths, token_mask, cond_table, norm_gains, w_ffn1_up, w_ffn1_down, w_qkv, w_out, w_glu, conv_kernel, bn_gain, batchnorm_shift_bias, w_conv_out, w_ffn2_up, w_ffn2_down, running_mean, running_var):
    level_hot = (levels[:, None] - 1 == jnp.arange(LEVELS)[None, :]).astype(jnp.float32)
    valid = (jnp.arange(LENGTH)[None, :] < lengths[:, None]).astype(jnp.float32)
    masked = token_mask.astype(jnp.float32)
    params = tuple((entry.astype(jnp.float32) for entry in (frames_in, cond_table, norm_gains, w_ffn1_up, w_ffn1_down, w_qkv, w_out, w_glu, conv_kernel, bn_gain, batchnorm_shift_bias, w_conv_out, w_ffn2_up, w_ffn2_down)))

    def wrapped(*values):
        return forward(*values, level_hot, masked, valid)
    result, pullback, stats = jax.vjp(wrapped, *params, has_aux=True)
    batchnorm_frame_mean, bn_var = stats
    grads = pullback(cotangent.astype(jnp.float32))
    count_of_frames = jnp.sum(lengths).astype(jnp.float32)
    new_mean = 0.9 * running_mean + 0.1 * batchnorm_frame_mean
    new_var = 0.9 * running_var + 0.1 * bn_var * count_of_frames / (count_of_frames - 1.0)
    return (result.astype(jnp.bfloat16), grads[0].astype(jnp.bfloat16), grads[1], grads[2], grads[3], grads[4], grads[5], grads[6], grads[7], grads[8], grads[9], grads[10], grads[11], grads[12], grads[13], new_mean, new_var)
```

```python
import functools
import math

import jax
import jax.numpy as jnp
from jax import lax
from jax.experimental import pallas as pl
from jax.experimental.pallas import tpu as pltpu
from jax.sharding import PartitionSpec as P

MESH = pl.DeviceIdType.MESH

HEADS = 16
HD = 64


EPSILON = 1e-05
MASKED_SCORE = -1000000000.0


def extended(array, sides, width):
    for axis, dim in sides:
        devices, length = (lax.axis_size(axis), array.shape[dim])
        up = [(i, (i + 1) % devices) for i in range(devices - 1)]
        down = [(j, i) for i, j in up]
        last = lax.slice_in_dim(array, length - width, length, axis=dim)
        leading = lax.slice_in_dim(array, 0, width, axis=dim)
        before = lax.ppermute(last, axis, up)
        after = lax.ppermute(leading, axis, down)
        array = jnp.concatenate([before, array, after], axis=dim)
    return array


def layer_norm(values, gain_row):
    centre = values - jnp.mean(values, axis=-1, keepdims=True)
    spread = jnp.mean(centre * centre, axis=-1, keepdims=True)
    return centre * lax.rsqrt(spread + EPSILON) * gain_row


def rope_tables(positions, head_size):
    half_size = head_size // 2
    inv_freqs = jnp.exp(
        jnp.arange(half_size).astype(jnp.float32) * (-2.0 * math.log(10000.0) / head_size)
    )
    angles = positions.astype(jnp.float32)[:, None] * inv_freqs[None, :]
    return (jnp.cos(angles), jnp.sin(angles))


def rotate(values, cosine, sine_table):
    half_size = values.shape[-1] // 2
    first_half = values[..., :half_size]
    second_half = values[..., half_size:]
    return jnp.concatenate(
        [
            first_half * cosine - second_half * sine_table,
            second_half * cosine + first_half * sine_table,
        ],
        axis=-1,
    )


def unrotate(grads, cosine, sine_table):
    half_size = grads.shape[-1] // 2
    first_half = grads[..., :half_size]
    second_half = grads[..., half_size:]
    return jnp.concatenate(
        [
            first_half * cosine + second_half * sine_table,
            second_half * cosine - first_half * sine_table,
        ],
        axis=-1,
    )


def times_transposed(left_side, weight):
    return lax.dot_general(
        left_side, weight, (((1,), (1,)), ((), ())), preferred_element_type=jnp.float32
    )


def pair_frames(rows_in):
    frames, groups, group_width = rows_in.shape
    paired = rows_in.reshape(frames // 2, 2, groups, group_width).transpose(0, 2, 1, 3)
    return paired.reshape(frames // 2, groups, 2 * group_width)


def unpair_frames(rows_in):
    pairs, groups, double_width = rows_in.shape
    split_rows = rows_in.reshape(pairs, groups, 2, double_width // 2).transpose(0, 2, 1, 3)
    return split_rows.reshape(2 * pairs, groups * (double_width // 2))


def ffn_forward(values, gain_row, up_weight, down_weight):
    normed, ln_pull = jax.vjp(layer_norm, values, gain_row)
    lowered = normed.astype(jnp.bfloat16)
    hidden = jnp.dot(lowered, up_weight, preferred_element_type=jnp.float32)
    act_rows = (hidden * jax.nn.sigmoid(hidden)).astype(jnp.bfloat16)
    branch = jnp.dot(act_rows, down_weight, preferred_element_type=jnp.float32)
    return (values + 0.5 * branch, (ln_pull, lowered, hidden, act_rows))


def ffn_backward(grad_in, saved_state, up_weight, down_weight):
    ln_pull, lowered, hidden, act_rows = saved_state
    grad_branch = (0.5 * grad_in).astype(jnp.bfloat16)
    grad_act = times_transposed(grad_branch, down_weight)
    gate_sig = jax.nn.sigmoid(hidden)
    grad_hidden = (grad_act * gate_sig * (1.0 + hidden * (1.0 - gate_sig))).astype(jnp.bfloat16)
    grad_normed = times_transposed(grad_hidden, up_weight)
    grad_values, grad_gain = ln_pull(grad_normed)
    return (grad_in + grad_values, grad_gain, (lowered, grad_hidden), (act_rows, grad_branch))


def sum_kernel(groups, batches, rows_ref, total_ref, seq_slots, part, batch_slots, sends, arrivals):
    s, b = lax.axis_index("seq"), lax.axis_index("batch")
    peers = [(b, lax.rem(s + k, groups)) for k in range(1, groups)]
    peers += [(lax.rem(b + k, batches), s) for k in range(1, batches)]
    barrier = pltpu.get_barrier_semaphore()
    for peer in peers:
        pl.semaphore_signal(barrier, inc=1, device_id=peer, device_id_type=MESH)
    pl.semaphore_wait(barrier, len(peers))

    def spread(source, slots, mine, first, count):
        slots[mine] = source[...]
        copies = []
        for k in range(first, first + count):
            copies.append(
                pltpu.make_async_remote_copy(
                    src_ref=source,
                    dst_ref=slots.at[mine],
                    send_sem=sends.at[k],
                    recv_sem=arrivals.at[k],
                    device_id=peers[k],
                    device_id_type=MESH,
                )
            )
            copies[-1].start()
        for copy in copies:
            copy.wait()
        total = slots[0]
        for i in range(1, count + 1):
            total = total + slots[i]
        return total

    part[...] = spread(rows_ref, seq_slots, s, 0, groups - 1)
    total_ref[...] = spread(part, batch_slots, b, groups - 1, batches - 1)


def sum_everywhere(rows, collective_id):
    groups, batches = lax.axis_size("seq"), lax.axis_size("batch")
    copies = groups + batches - 2
    return pl.pallas_call(
        functools.partial(sum_kernel, groups, batches),
        out_shape=jax.ShapeDtypeStruct(rows.shape, jnp.float32),
        in_specs=[pl.BlockSpec(memory_space=pltpu.VMEM)],
        out_specs=pl.BlockSpec(memory_space=pltpu.VMEM),
        scratch_shapes=[
            pltpu.VMEM((groups, *rows.shape), jnp.float32),
            pltpu.VMEM(rows.shape, jnp.float32),
            pltpu.VMEM((batches, *rows.shape), jnp.float32),
            pltpu.SemaphoreType.DMA((copies,)),
            pltpu.SemaphoreType.DMA((copies,)),
        ],
        compiler_params=pltpu.CompilerParams(
            collective_id=collective_id, has_side_effects=True, vmem_limit_bytes=32 << 20
        ),
    )(rows)


def halving_steps(first_seq):
    seq_bits = [("seq", k) for k in range(lax.axis_size("seq").bit_length() - 1)]
    batch_bits = [("batch", k) for k in range(1, lax.axis_size("batch").bit_length() - 1)]
    if first_seq:
        seq_bits = seq_bits[::-1]
    return [("batch", 0)] + seq_bits + batch_bits


def relative_place(place, steps, axis):
    flips = 0
    for order, (name, bit) in enumerate(steps):
        if name == axis:
            flips = flips | (((place >> (len(steps) - 1 - order)) & 1) << bit)
    return flips


def product_kernel(steps, tall, rows, cols, group, where, left_ref, right_ref, out_ref):
    step = pl.program_id(0)
    for inner in range(group):
        place = step * group + inner
        b = where[0] ^ relative_place(place, steps, "batch")
        s = where[1] ^ relative_place(place, steps, "seq")
        if tall:
            left = left_ref[:, pl.ds(pl.multiple_of((b * lax.axis_size("seq") + s) * rows, rows), rows)]
            right = right_ref[...]
        else:
            left = left_ref[:, pl.ds(pl.multiple_of(s * rows, rows), rows)]
            right = right_ref[:, pl.ds(pl.multiple_of(b * cols, cols), cols)]
        out_ref[inner] = lax.dot_general(
            left, right, (((0,), (0,)), ((), ())), preferred_element_type=jnp.float32
        ).astype(jnp.bfloat16)


def block_products(left, right, tall, steps):
    batches, groups = lax.axis_size("batch"), lax.axis_size("seq")
    places = batches * groups
    if tall:
        rows, cols = left.shape[1] // places, right.shape[1]
    else:
        rows, cols = left.shape[1] // groups, right.shape[1] // batches
    me = jnp.stack([lax.axis_index("batch"), lax.axis_index("seq")]).astype(jnp.int32)
    if rows % 128 == 0 and cols % 128 == 0:
        group = 4
        return pl.pallas_call(
            functools.partial(product_kernel, steps, tall, rows, cols, group),
            out_shape=jax.ShapeDtypeStruct((places, rows, cols), jnp.bfloat16),
            grid_spec=pltpu.PrefetchScalarGridSpec(
                num_scalar_prefetch=1,
                grid=(places // group,),
                in_specs=[
                    pl.BlockSpec(left.shape, lambda i, where: (0, 0)),
                    pl.BlockSpec(right.shape, lambda i, where: (0, 0)),
                ],
                out_specs=pl.BlockSpec((group, rows, cols), lambda i, where: (i, 0, 0)),
            ),
            compiler_params=pltpu.CompilerParams(vmem_limit_bytes=40 << 20),
            cost_estimate=pl.CostEstimate(
                flops=2 * left.shape[0] * left.shape[1] * right.shape[1],
                bytes_accessed=2 * (left.size + right.size + left.shape[1] * right.shape[1]),
                transcendentals=0,
            ),
        )(me, left, right)
    whole = lax.dot_general(
        left, right, (((0,), (0,)), ((), ())), preferred_element_type=jnp.float32
    ).astype(jnp.bfloat16)
    if tall:
        blocks = whole.reshape(batches, groups, rows, cols)
    else:
        blocks = whole.reshape(groups, rows, batches, cols).transpose(2, 0, 1, 3)
    batch_bits, seq_bits = batches.bit_length() - 1, groups.bit_length() - 1
    blocks = blocks.reshape((2,) * (batch_bits + seq_bits) + (rows, cols))
    dims = []
    for name, bit in steps:
        dim = batch_bits - 1 - bit if name == "batch" else batch_bits + seq_bits - 1 - bit
        mine = (me[0] if name == "batch" else me[1]) >> bit & 1
        blocks = jnp.where(mine == 1, jnp.flip(blocks, dim), blocks)
        dims.append(dim)
    return blocks.transpose(*dims, len(dims), len(dims) + 1).reshape(places, rows, cols)


def owned_sum(left, right, tall, first_seq):
    steps = halving_steps(first_seq)
    blocks = block_products(left, right, tall, steps)
    for axis, bit in steps:
        half = blocks.shape[0] // 2
        pairs = [(i, i ^ (1 << bit)) for i in range(lax.axis_size(axis))]
        arrived = lax.ppermute(blocks[half:], axis, pairs)
        total = blocks[:half].astype(jnp.float32) + arrived.astype(jnp.float32)
        blocks = total.astype(jnp.bfloat16) if half > 1 else total
    return blocks[0]


def shards(
    frames_in,
    cotangent,
    levels,
    lengths,
    token_mask,
    cond_table,
    norm_gains,
    w_ffn1_up,
    w_ffn1_down,
    w_qkv,
    w_out,
    w_glu,
    conv_kernel,
    bn_gain,
    batchnorm_shift_bias,
    w_conv_out,
    w_ffn2_up,
    w_ffn2_down,
    running_mean,
    running_var,
):
    frames = frames_in.shape[1]
    model_width = frames_in.shape[2]
    ff_width = w_ffn1_up.shape[1]
    groups = lax.axis_size("seq")
    batches = lax.axis_size("batch")
    seq_index = lax.axis_index("seq")
    item_index = lax.axis_index("batch")
    seq_length = frames * groups
    local_heads = HEADS // groups
    head_width = local_heads * HD
    level_count = cond_table.shape[0] - 1
    cond_rows = cond_table.astype(jnp.float32)
    gain_rows = norm_gains.astype(jnp.float32)
    level_hot = (jnp.arange(level_count) == levels[0] - 1).astype(jnp.float32)
    level_vector = jnp.sum(level_hot[:, None] * cond_rows[:level_count], axis=0)
    mask_column = token_mask[0].astype(jnp.float32)[:, None]
    start_rows = (
        frames_in[0].astype(jnp.float32)
        + level_vector[None, :]
        + mask_column * cond_rows[level_count][None, :]
    )
    length = lax.dynamic_slice_in_dim(lengths, item_index, 1)[0]
    positions = seq_index * frames + jnp.arange(frames)
    unpadded_rows = (positions < length).astype(jnp.float32)[:, None]
    rows_one, ffn1_state = ffn_forward(start_rows, gain_rows[0], w_ffn1_up, w_ffn1_down)
    normed_attn, attn_pull = jax.vjp(layer_norm, rows_one, gain_rows[1])
    attn_in = normed_attn.astype(jnp.bfloat16)
    qkv_rows = jnp.dot(attn_in, w_qkv, preferred_element_type=jnp.float32).reshape(
        frames, HEADS, 3, HD
    )
    cosine, sine_table = rope_tables(positions, HD)
    query_rot = rotate(qkv_rows[:, :, 0], cosine[:, None], sine_table[:, None]) * 0.125
    key_rot = rotate(qkv_rows[:, :, 1], cosine[:, None], sine_table[:, None])
    packed = jnp.stack([query_rot, key_rot, qkv_rows[:, :, 2]], axis=2).astype(jnp.bfloat16)
    incoming = lax.all_to_all(
        pair_frames(packed.reshape(frames, groups, local_heads * 3 * HD)),
        "seq",
        split_axis=1,
        concat_axis=0,
        tiled=True,
    )
    whole_heads = incoming.reshape(seq_length, local_heads, 3, HD)
    query_all = whole_heads[:, :, 0]
    key_all = whole_heads[:, :, 1]
    value_all = whole_heads[:, :, 2]
    key_valid = (jnp.arange(seq_length) < length)[None, None, :]
    block_rows = min(512, seq_length)
    block_count = seq_length // block_rows
    query_blocks = query_all.reshape(block_count, block_rows, local_heads, HD)

    def attend_block(query_block):
        scores = jnp.einsum(
            "qhd,khd->hqk", query_block, key_all, preferred_element_type=jnp.float32
        )
        scores = jnp.where(key_valid, scores, MASKED_SCORE)
        row_peak = jnp.max(scores, axis=-1, keepdims=True)
        exp_scores = jnp.exp(scores - row_peak)
        row_total = jnp.sum(exp_scores, axis=-1, keepdims=True)
        probs_low = (exp_scores / row_total).astype(jnp.bfloat16)
        mixed_block = jnp.einsum(
            "hqk,khd->qhd", probs_low, value_all, preferred_element_type=jnp.float32
        )
        return (mixed_block.astype(jnp.bfloat16), (row_peak + jnp.log(row_total))[:, :, 0])

    mixed_blocks, lse_blocks = lax.map(attend_block, query_blocks)
    mixed_rows = mixed_blocks.reshape(seq_length // 2, 1, 2 * head_width)
    attn_out = unpair_frames(
        lax.all_to_all(mixed_rows, "seq", split_axis=0, concat_axis=1, tiled=True)
    )
    rows_two = rows_one + jnp.dot(attn_out, w_out, preferred_element_type=jnp.float32)
    normed_conv, conv_pull = jax.vjp(layer_norm, rows_two, gain_rows[2])
    conv_in = normed_conv.astype(jnp.bfloat16)
    glu_pre = jnp.dot(conv_in, w_glu, preferred_element_type=jnp.float32)
    up_half = glu_pre[:, :model_width]
    glu_sig = jax.nn.sigmoid(glu_pre[:, model_width:])
    glu_low = (up_half * glu_sig * unpadded_rows).astype(jnp.bfloat16)
    taps = conv_kernel.shape[0]
    half_size = taps // 2
    kernel_rows = conv_kernel.astype(jnp.float32)
    padded = extended(glu_low, (("seq", 0),), half_size)
    convolved_rows = jnp.zeros((frames, model_width), jnp.float32)
    for tap_index in range(taps):
        convolved_rows = (
            convolved_rows + kernel_rows[tap_index] * padded[tap_index : tap_index + frames]
        )
    sum_rows = jnp.sum(convolved_rows * unpadded_rows, axis=0)
    sum_squares = jnp.sum(convolved_rows * convolved_rows * unpadded_rows, axis=0)
    totals = sum_everywhere(jnp.stack([sum_rows, sum_squares]), 1)
    total_sum, total_squares = totals[0], totals[1]
    count_of_frames = jnp.sum(lengths).astype(jnp.float32)
    batchnorm_frame_mean = total_sum / count_of_frames
    bn_var = total_squares / count_of_frames - batchnorm_frame_mean * batchnorm_frame_mean
    batchnorm_inverse_deviation = lax.rsqrt(bn_var + EPSILON)
    batchnorm_scale_factor = bn_gain.astype(jnp.float32)
    normalized_rows = (convolved_rows - batchnorm_frame_mean) * batchnorm_inverse_deviation
    batchnorm_input_rows = normalized_rows * batchnorm_scale_factor + batchnorm_shift_bias.astype(
        jnp.float32
    )
    bn_sig = jax.nn.sigmoid(batchnorm_input_rows)
    conv_act = (batchnorm_input_rows * bn_sig).astype(jnp.bfloat16)
    rows_three = rows_two + jnp.dot(conv_act, w_conv_out, preferred_element_type=jnp.float32)
    rows_four, ffn2_state = ffn_forward(rows_three, gain_rows[3], w_ffn2_up, w_ffn2_down)
    normed_out, out_pull = jax.vjp(layer_norm, rows_four, gain_rows[4])
    out_rows = normed_out.astype(jnp.bfloat16)
    grad_four, grad_gain_four = out_pull(cotangent[0].astype(jnp.float32))
    grad_three, grad_gain_three, ffn2_up_pair, ffn2_down_pair = ffn_backward(
        grad_four, ffn2_state, w_ffn2_up, w_ffn2_down
    )
    grad_r2 = grad_three.astype(jnp.bfloat16)
    batchnorm_gradient = (
        times_transposed(grad_r2, w_conv_out)
        * bn_sig
        * (1.0 + batchnorm_input_rows * (1.0 - bn_sig))
    )
    gradient_totals = sum_everywhere(
        jnp.stack(
            [
                jnp.sum(batchnorm_gradient, axis=0),
                jnp.sum(batchnorm_gradient * normalized_rows, axis=0),
            ]
        ),
        2,
    )
    gradient_sum_total, gradient_normalized_sum = gradient_totals[0], gradient_totals[1]
    grad_conv = (
        batchnorm_scale_factor
        * batchnorm_inverse_deviation
        * (
            batchnorm_gradient
            - unpadded_rows
            * (gradient_sum_total + normalized_rows * gradient_normalized_sum)
            / count_of_frames
        )
    ).astype(jnp.bfloat16)
    grad_pad = extended(grad_conv, (("seq", 0),), half_size)
    grad_glu = jnp.zeros((frames, model_width), jnp.float32)
    kernel_terms = []
    for tap_index in range(taps):
        offset = 2 * half_size - tap_index
        grad_glu = grad_glu + kernel_rows[tap_index] * grad_pad[offset : offset + frames]
        kernel_terms.append(
            jnp.einsum(
                "fd,fd->d",
                padded[tap_index : tap_index + frames],
                grad_conv,
                preferred_element_type=jnp.float32,
            )
        )
    kernel_grads = jnp.stack(kernel_terms, axis=0)
    grad_glu = grad_glu * unpadded_rows
    grad_gl = jnp.concatenate(
        [grad_glu * glu_sig, grad_glu * up_half * glu_sig * (1.0 - glu_sig)], axis=1
    ).astype(jnp.bfloat16)
    grad_conv_in, grad_gain_two = conv_pull(times_transposed(grad_gl, w_glu))
    grad_two = grad_three + grad_conv_in
    grad_r = grad_two.astype(jnp.bfloat16)
    grad_attn_out = times_transposed(grad_r, w_out).astype(jnp.bfloat16)
    grad_heads = lax.all_to_all(
        pair_frames(grad_attn_out.reshape(frames, groups, head_width)),
        "seq",
        split_axis=1,
        concat_axis=0,
        tiled=True,
    )
    grad_blocks = grad_heads.reshape(block_count, block_rows, local_heads, HD)

    def attend_back(carry_pair, pieces):
        grad_key, grad_value = carry_pair
        query_block, grad_block, lse_block = pieces
        scores = jnp.einsum(
            "qhd,khd->hqk", query_block, key_all, preferred_element_type=jnp.float32
        )
        scores = jnp.where(key_valid, scores, MASKED_SCORE)
        probs_row = jnp.exp(scores - lse_block[:, :, None])
        probs_low = probs_row.astype(jnp.bfloat16)
        grad_value = grad_value + jnp.einsum(
            "hqk,qhd->khd", probs_low, grad_block, preferred_element_type=jnp.float32
        )
        grad_probs = jnp.einsum(
            "qhd,khd->hqk", grad_block, value_all, preferred_element_type=jnp.float32
        )
        grad_scores = (
            probs_row * (grad_probs - jnp.sum(probs_row * grad_probs, axis=-1, keepdims=True))
        ).astype(jnp.bfloat16)
        grad_query = jnp.einsum(
            "hqk,khd->qhd", grad_scores, key_all, preferred_element_type=jnp.float32
        )
        grad_key = grad_key + jnp.einsum(
            "hqk,qhd->khd", grad_scores, query_block, preferred_element_type=jnp.float32
        )
        return ((grad_key, grad_value), grad_query)

    zero_heads = jnp.zeros((seq_length, local_heads, HD), jnp.float32)
    key_value_grads, query_grads = lax.scan(
        attend_back, (zero_heads, zero_heads), (query_blocks, grad_blocks, lse_blocks)
    )
    cos_all, sin_all = rope_tables(jnp.arange(seq_length), HD)
    grad_query_pre = (
        unrotate(
            query_grads.reshape(seq_length, local_heads, HD), cos_all[:, None], sin_all[:, None]
        )
        * 0.125
    )
    grad_key_pre = unrotate(key_value_grads[0], cos_all[:, None], sin_all[:, None])
    stacked = jnp.stack([grad_query_pre, grad_key_pre, key_value_grads[1]], axis=2).astype(
        jnp.bfloat16
    )
    returned = lax.all_to_all(
        stacked.reshape(seq_length // 2, 1, 2 * local_heads * 3 * HD),
        "seq",
        split_axis=0,
        concat_axis=1,
        tiled=True,
    )
    grad_qkv = unpair_frames(returned)
    grad_attn_part, grad_gain_one = attn_pull(times_transposed(grad_qkv, w_qkv))
    grad_one = grad_two + grad_attn_part
    grad_zero, grad_gain_zero, ffn1_up_pair, ffn1_down_pair = ffn_backward(
        grad_one, ffn1_state, w_ffn1_up, w_ffn1_down
    )
    column_total = jnp.sum(grad_zero, axis=0)
    cond_grad_rows = jnp.concatenate(
        [
            level_hot[:, None] * column_total[None, :],
            jnp.sum(mask_column * grad_zero, axis=0)[None, :],
        ],
        axis=0,
    )
    gain_grads = jnp.stack(
        [grad_gain_zero, grad_gain_one, grad_gain_two, grad_gain_three, grad_gain_four], axis=0
    )
    small_rows = jnp.concatenate([gain_grads, cond_grad_rows, kernel_grads], axis=0)
    small_sums = sum_everywhere(small_rows, 3)
    seq_width = model_width // groups
    small_piece = lax.dynamic_slice_in_dim(small_sums, seq_index * seq_width, seq_width, axis=1)
    cond_end = 5 + level_count + 1
    new_mean = 0.9 * running_mean + 0.1 * batchnorm_frame_mean
    new_var = 0.9 * running_var + 0.1 * bn_var * count_of_frames / (count_of_frames - 1.0)
    return (
        out_rows[None],
        grad_zero.astype(jnp.bfloat16)[None],
        small_piece[5:cond_end],
        small_piece[0:5],
        owned_sum(*ffn1_up_pair, False, False),
        owned_sum(*ffn1_down_pair, True, True),
        owned_sum(attn_in, grad_qkv, False, True),
        owned_sum(attn_out, grad_r, False, False),
        owned_sum(conv_in, grad_gl, False, True),
        small_piece[cond_end : cond_end + taps],
        gradient_normalized_sum,
        gradient_sum_total,
        owned_sum(conv_act, grad_r2, False, False),
        owned_sum(*ffn2_up_pair, False, False),
        owned_sum(*ffn2_down_pair, True, True),
        new_mean,
        new_var,
    )


def solution(mesh):
    in_specs = (
        P("batch", "seq", None),
        P("batch", "seq", None),
        P("batch"),
        P(),
        P("batch", "seq"),
        P(),
        P(),
        P(),
        P(),
        P(),
        P(),
        P(),
        P(),
        P(),
        P(),
        P(),
        P(),
        P(),
        P(),
        P(),
    )
    out_specs = (
        P("batch", "seq", None),
        P("batch", "seq", None),
        P(None, "seq"),
        P(None, "seq"),
        P("seq", "batch"),
        P(("batch", "seq"), None),
        P("seq", "batch"),
        P("seq", "batch"),
        P("seq", "batch"),
        P(None, "seq"),
        P(),
        P(),
        P("seq", "batch"),
        P("seq", "batch"),
        P(("batch", "seq"), None),
        P(),
        P(),
    )
    return jax.shard_map(shards, mesh=mesh, in_specs=in_specs, out_specs=out_specs, check_vma=False)
```

```python
import functools
import math

import jax
import jax.numpy as jnp
from jax import lax
from jax.experimental import pallas as pl
from jax.experimental.pallas import tpu as pltpu
from jax.sharding import PartitionSpec as P

MESH = pl.DeviceIdType.MESH

HEADS = 16
HD = 64


EPSILON = 1e-05
MASKED_SCORE = -1000000000.0


def extended(array, sides, width):
    for axis, dim in sides:
        devices, length = (lax.axis_size(axis), array.shape[dim])
        up = [(i, (i + 1) % devices) for i in range(devices - 1)]
        down = [(j, i) for i, j in up]
        last = lax.slice_in_dim(array, length - width, length, axis=dim)
        leading = lax.slice_in_dim(array, 0, width, axis=dim)
        before = lax.ppermute(last, axis, up)
        after = lax.ppermute(leading, axis, down)
        array = jnp.concatenate([before, array, after], axis=dim)
    return array


def layer_norm(values, gain_row):
    centre = values - jnp.mean(values, axis=-1, keepdims=True)
    spread = jnp.mean(centre * centre, axis=-1, keepdims=True)
    return centre * lax.rsqrt(spread + EPSILON) * gain_row


def rope_tables(positions, head_size):
    half_size = head_size // 2
    inv_freqs = jnp.exp(
        jnp.arange(half_size).astype(jnp.float32) * (-2.0 * math.log(10000.0) / head_size)
    )
    angles = positions.astype(jnp.float32)[:, None] * inv_freqs[None, :]
    return (jnp.cos(angles), jnp.sin(angles))


def times_transposed(left_side, weight):
    return lax.dot_general(
        left_side, weight, (((1,), (1,)), ((), ())), preferred_element_type=jnp.float32
    )


def ffn_forward(values, gain_row, up_weight, down_weight):
    normed, ln_pull = jax.vjp(layer_norm, values, gain_row)
    lowered = normed.astype(jnp.bfloat16)
    hidden = jnp.dot(lowered, up_weight, preferred_element_type=jnp.float32)
    act_rows = (hidden * jax.nn.sigmoid(hidden)).astype(jnp.bfloat16)
    branch = jnp.dot(act_rows, down_weight, preferred_element_type=jnp.float32)
    return (values + 0.5 * branch, (ln_pull, lowered, hidden, act_rows))


def ffn_backward(grad_in, saved_state, up_weight, down_weight):
    ln_pull, lowered, hidden, act_rows = saved_state
    grad_branch = (0.5 * grad_in).astype(jnp.bfloat16)
    grad_act = times_transposed(grad_branch, down_weight)
    gate_sig = jax.nn.sigmoid(hidden)
    grad_hidden = (grad_act * gate_sig * (1.0 + hidden * (1.0 - gate_sig))).astype(jnp.bfloat16)
    grad_normed = times_transposed(grad_hidden, up_weight)
    grad_values, grad_gain = ln_pull(grad_normed)
    return (grad_in + grad_values, grad_gain, (lowered, grad_hidden), (act_rows, grad_branch))


def sum_kernel(groups, batches, rows_ref, total_ref, seq_slots, part, batch_slots, sends, arrivals):
    s, b = lax.axis_index("seq"), lax.axis_index("batch")
    peers = [(b, lax.rem(s + k, groups)) for k in range(1, groups)]
    peers += [(lax.rem(b + k, batches), s) for k in range(1, batches)]
    barrier = pltpu.get_barrier_semaphore()
    for peer in peers:
        pl.semaphore_signal(barrier, inc=1, device_id=peer, device_id_type=MESH)
    pl.semaphore_wait(barrier, len(peers))

    def spread(source, slots, mine, first, count):
        slots[mine] = source[...]
        copies = []
        for k in range(first, first + count):
            copies.append(
                pltpu.make_async_remote_copy(
                    src_ref=source,
                    dst_ref=slots.at[mine],
                    send_sem=sends.at[k],
                    recv_sem=arrivals.at[k],
                    device_id=peers[k],
                    device_id_type=MESH,
                )
            )
            copies[-1].start()
        for copy in copies:
            copy.wait()
        total = slots[0]
        for i in range(1, count + 1):
            total = total + slots[i]
        return total

    part[...] = spread(rows_ref, seq_slots, s, 0, groups - 1)
    total_ref[...] = spread(part, batch_slots, b, groups - 1, batches - 1)


def sum_everywhere(rows, collective_id):
    groups, batches = lax.axis_size("seq"), lax.axis_size("batch")
    copies = groups + batches - 2
    return pl.pallas_call(
        functools.partial(sum_kernel, groups, batches),
        out_shape=jax.ShapeDtypeStruct(rows.shape, jnp.float32),
        in_specs=[pl.BlockSpec(memory_space=pltpu.VMEM)],
        out_specs=pl.BlockSpec(memory_space=pltpu.VMEM),
        scratch_shapes=[
            pltpu.VMEM((groups, *rows.shape), jnp.float32),
            pltpu.VMEM(rows.shape, jnp.float32),
            pltpu.VMEM((batches, *rows.shape), jnp.float32),
            pltpu.SemaphoreType.DMA((copies,)),
            pltpu.SemaphoreType.DMA((copies,)),
        ],
        compiler_params=pltpu.CompilerParams(
            collective_id=collective_id, has_side_effects=True, vmem_limit_bytes=32 << 20
        ),
    )(rows)


def halving_steps(first_seq):
    seq_bits = [("seq", k) for k in range(lax.axis_size("seq").bit_length() - 1)]
    batch_bits = [("batch", k) for k in range(1, lax.axis_size("batch").bit_length() - 1)]
    if first_seq:
        seq_bits = seq_bits[::-1]
    return [("batch", 0)] + seq_bits + batch_bits


def relative_place(place, steps, axis):
    flips = 0
    for order, (name, bit) in enumerate(steps):
        if name == axis:
            flips = flips | (((place >> (len(steps) - 1 - order)) & 1) << bit)
    return flips


def product_kernel(steps, tall, rows, cols, group, where, left_ref, right_ref, out_ref):
    step = pl.program_id(0)
    for inner in range(group):
        place = step * group + inner
        b = where[0] ^ relative_place(place, steps, "batch")
        s = where[1] ^ relative_place(place, steps, "seq")
        if tall:
            left = left_ref[:, pl.ds(pl.multiple_of((b * lax.axis_size("seq") + s) * rows, rows), rows)]
            right = right_ref[...]
        else:
            left = left_ref[:, pl.ds(pl.multiple_of(s * rows, rows), rows)]
            right = right_ref[:, pl.ds(pl.multiple_of(b * cols, cols), cols)]
        out_ref[inner] = lax.dot_general(
            left, right, (((0,), (0,)), ((), ())), preferred_element_type=jnp.float32
        ).astype(jnp.bfloat16)


def block_products(left, right, tall, steps):
    batches, groups = lax.axis_size("batch"), lax.axis_size("seq")
    places = batches * groups
    if tall:
        rows, cols = left.shape[1] // places, right.shape[1]
    else:
        rows, cols = left.shape[1] // groups, right.shape[1] // batches
    me = jnp.stack([lax.axis_index("batch"), lax.axis_index("seq")]).astype(jnp.int32)
    if rows % 128 == 0 and cols % 128 == 0:
        group = 4
        return pl.pallas_call(
            functools.partial(product_kernel, steps, tall, rows, cols, group),
            out_shape=jax.ShapeDtypeStruct((places, rows, cols), jnp.bfloat16),
            grid_spec=pltpu.PrefetchScalarGridSpec(
                num_scalar_prefetch=1,
                grid=(places // group,),
                in_specs=[
                    pl.BlockSpec(left.shape, lambda i, where: (0, 0)),
                    pl.BlockSpec(right.shape, lambda i, where: (0, 0)),
                ],
                out_specs=pl.BlockSpec((group, rows, cols), lambda i, where: (i, 0, 0)),
            ),
            compiler_params=pltpu.CompilerParams(vmem_limit_bytes=40 << 20),
            cost_estimate=pl.CostEstimate(
                flops=2 * left.shape[0] * left.shape[1] * right.shape[1],
                bytes_accessed=2 * (left.size + right.size + left.shape[1] * right.shape[1]),
                transcendentals=0,
            ),
        )(me, left, right)
    whole = lax.dot_general(
        left, right, (((0,), (0,)), ((), ())), preferred_element_type=jnp.float32
    ).astype(jnp.bfloat16)
    if tall:
        blocks = whole.reshape(batches, groups, rows, cols)
    else:
        blocks = whole.reshape(groups, rows, batches, cols).transpose(2, 0, 1, 3)
    batch_bits, seq_bits = batches.bit_length() - 1, groups.bit_length() - 1
    blocks = blocks.reshape((2,) * (batch_bits + seq_bits) + (rows, cols))
    dims = []
    for name, bit in steps:
        dim = batch_bits - 1 - bit if name == "batch" else batch_bits + seq_bits - 1 - bit
        mine = (me[0] if name == "batch" else me[1]) >> bit & 1
        blocks = jnp.where(mine == 1, jnp.flip(blocks, dim), blocks)
        dims.append(dim)
    return blocks.transpose(*dims, len(dims), len(dims) + 1).reshape(places, rows, cols)


def owned_sum(left, right, tall, first_seq):
    steps = halving_steps(first_seq)
    blocks = block_products(left, right, tall, steps)
    for axis, bit in steps:
        half = blocks.shape[0] // 2
        pairs = [(i, i ^ (1 << bit)) for i in range(lax.axis_size(axis))]
        arrived = lax.ppermute(blocks[half:], axis, pairs)
        total = blocks[:half].astype(jnp.float32) + arrived.astype(jnp.float32)
        blocks = total.astype(jnp.bfloat16) if half > 1 else total
    return blocks[0]


def attend_kernel(
    groups, heads, length_ref, qkv_ref, cos_ref, sin_ref, whole_ref, out_ref,
    stage, result, sends, arrivals, out_sends, out_arrivals, own_sem,
):
    s, b = lax.axis_index("seq"), lax.axis_index("batch")
    frames = qkv_ref.shape[0]
    total_frames = whole_ref.shape[0]
    block = heads * 3 * HD
    width = heads * HD
    greet_seq(groups, s, b)

    def rows_of(place):
        return pl.ds(pl.multiple_of(place * frames, frames), frames)

    def heads_copy(target, sender):
        return pltpu.make_async_remote_copy(
            src_ref=stage.at[target],
            dst_ref=whole_ref.at[rows_of(sender)],
            send_sem=sends.at[target],
            recv_sem=arrivals.at[sender],
            device_id=(b, target),
            device_id_type=MESH,
        )

    for column in range(0, groups * block, 128):
        pattern = (column // 128) % 3
        values = qkv_ref[:, column : column + 128]
        turned = (values * cos_ref[pattern] + partner_lanes(values) * sin_ref[pattern]).astype(
            jnp.bfloat16
        )
        start = column
        while start < column + 128:
            place = start // block
            end = min(column + 128, (place + 1) * block)
            stage[place, :, start - place * block : end - place * block] = turned[
                :, start - column : end - column
            ]
            if end == (place + 1) * block:

                @pl.when(s != place)
                def _():
                    heads_copy(place, s).start()

                @pl.when(s == place)
                def _():
                    whole_ref[rows_of(s), :] = stage[place]

            start = end
    for k in range(1, groups):
        heads_copy(s, lax.rem(s + k, groups)).wait_recv()

    valid = lax.broadcasted_iota(jnp.int32, (1, total_frames), 1) < length_ref[0]

    def out_place(owner):
        if width % 128 == 0:
            return out_ref.at[:, pl.ds(pl.multiple_of(owner * width, width), width)]
        return out_ref.at[owner]

    def result_copy(target, sender):
        return pltpu.make_async_remote_copy(
            src_ref=result.at[target],
            dst_ref=out_place(sender),
            send_sem=out_sends.at[target],
            recv_sem=out_arrivals.at[sender],
            device_id=(b, target),
            device_id_type=MESH,
        )

    def one_block(k, carry):
        place = lax.rem(s + k, groups)
        for h in range(heads):
            base = h * 3 * HD
            query = whole_ref[rows_of(place), base : base + HD]
            key = whole_ref[:, base + HD : base + 2 * HD]
            value = whole_ref[:, base + 2 * HD : base + 3 * HD]
            scores = times_transposed(query, key)
            scores = jnp.where(valid, scores, MASKED_SCORE)
            exp_scores = jnp.exp(scores - jnp.max(scores, axis=-1, keepdims=True))
            share = 1.0 / jnp.sum(exp_scores, axis=-1, keepdims=True)
            probs = (exp_scores * share).astype(jnp.bfloat16)
            mixed = jnp.dot(probs, value, preferred_element_type=jnp.float32)
            result[place, :, h * HD : (h + 1) * HD] = mixed.astype(jnp.bfloat16)

        @pl.when(k < groups)
        def _():
            result_copy(place, s).start()

        return carry

    lax.fori_loop(1, groups + 1, one_block, 0)
    own = pltpu.make_async_copy(result.at[s], out_place(s), own_sem)
    own.start()
    for k in range(1, groups):
        other = lax.rem(s + k, groups)
        heads_copy(other, s).wait_send()
        result_copy(other, s).wait_send()
        result_copy(s, other).wait_recv()
    own.wait()


def greet_seq(groups, s, b):
    barrier = pltpu.get_barrier_semaphore()
    for k in range(1, groups):
        pl.semaphore_signal(
            barrier, inc=1, device_id=(b, lax.rem(s + k, groups)), device_id_type=MESH
        )
    pl.semaphore_wait(barrier, groups - 1)


def partner_lanes(values):
    lanes = lax.broadcasted_iota(jnp.int32, values.shape, 1)
    return jnp.where(
        lanes % HD < HD // 2,
        pltpu.roll(values, 128 - HD // 2, 1),
        pltpu.roll(values, HD // 2, 1),
    )


def attend(qkv_rows, length, cosine, sine):
    groups = lax.axis_size("seq")
    frames = qkv_rows.shape[0]
    heads = HEADS // groups
    width = heads * HD
    signs = jnp.where(jnp.arange(HD) < HD // 2, -1.0, 1.0)
    cos_head = jnp.concatenate([cosine, cosine], axis=1)
    sin_head = jnp.concatenate([sine, sine], axis=1) * signs
    ones, zeros = jnp.ones_like(cos_head), jnp.zeros_like(cos_head)
    cos_pair = jnp.concatenate([cos_head * 0.125, cos_head, ones] * 2, axis=1)
    sin_pair = jnp.concatenate([sin_head * 0.125, sin_head, zeros] * 2, axis=1)
    cos_three = jnp.stack([cos_pair[:, 128 * i : 128 * (i + 1)] for i in range(3)])
    sin_three = jnp.stack([sin_pair[:, 128 * i : 128 * (i + 1)] for i in range(3)])
    direct = width % 128 == 0
    out_shape = (frames, groups * width) if direct else (groups, frames, width)
    total = frames * groups
    vmem = pl.BlockSpec(memory_space=pltpu.VMEM)
    whole, out = pl.pallas_call(
        functools.partial(attend_kernel, groups, heads),
        out_shape=(
            jax.ShapeDtypeStruct((total, 3 * width), jnp.bfloat16),
            jax.ShapeDtypeStruct(out_shape, jnp.bfloat16),
        ),
        in_specs=[pl.BlockSpec(memory_space=pltpu.SMEM), vmem, vmem, vmem],
        out_specs=(vmem, pl.BlockSpec(memory_space=pl.ANY)),
        scratch_shapes=[
            pltpu.VMEM((groups, frames, 3 * width), jnp.bfloat16),
            pltpu.VMEM((groups, frames, width), jnp.bfloat16),
            pltpu.SemaphoreType.DMA((groups,)),
            pltpu.SemaphoreType.DMA((groups,)),
            pltpu.SemaphoreType.DMA((groups,)),
            pltpu.SemaphoreType.DMA((groups,)),
            pltpu.SemaphoreType.DMA,
        ],
        compiler_params=pltpu.CompilerParams(
            collective_id=4, has_side_effects=True, vmem_limit_bytes=48 << 20
        ),
        cost_estimate=pl.CostEstimate(
            flops=4 * heads * HD * total * total,
            bytes_accessed=4 * qkv_rows.size + 2 * total * 4 * width,
            transcendentals=heads * total * total,
        ),
    )(length.reshape(1), qkv_rows, cos_three, sin_three)
    if not direct:
        out = out.transpose(1, 0, 2).reshape(frames, groups * width)
    return whole, out


def attend_back_kernel(
    groups, heads, length_ref, whole_ref, grad_ref, cos_ref, sin_ref, out_ref,
    stage, grads, result, query_key, value_total, sends, arrivals, out_sends, out_arrivals, own_sem,
):
    s, b = lax.axis_index("seq"), lax.axis_index("batch")
    frames = grad_ref.shape[0]
    total_frames = whole_ref.shape[0]
    block = heads * 3 * HD
    width = heads * HD
    greet_seq(groups, s, b)

    def rows_of(place):
        return pl.ds(pl.multiple_of(place * frames, frames), frames)

    def grad_copy(target, sender):
        return pltpu.make_async_remote_copy(
            src_ref=stage.at[target],
            dst_ref=grads.at[rows_of(sender)],
            send_sem=sends.at[target],
            recv_sem=arrivals.at[sender],
            device_id=(b, target),
            device_id_type=MESH,
        )

    for place in range(groups):
        stage[place] = grad_ref[:, place * width : (place + 1) * width]

        @pl.when(s != place)
        def _():
            grad_copy(place, s).start()

        @pl.when(s == place)
        def _():
            grads[rows_of(s), :] = stage[place]

    part_heads = 2 if heads % 2 == 0 else heads
    parts = heads // part_heads
    span = part_heads * 3 * HD

    def out_place(owner, part):
        if block % 128 == 0:
            start = pl.multiple_of(owner * block + part * span, 128)
            return out_ref.at[:, pl.ds(start, span)]
        return out_ref.at[owner, :, pl.ds(part * span, span)]

    def result_copy(target, sender, part):
        return pltpu.make_async_remote_copy(
            src_ref=result.at[part, rows_of(target)],
            dst_ref=out_place(sender, part),
            send_sem=out_sends.at[part, target],
            recv_sem=out_arrivals.at[part, sender],
            device_id=(b, target),
            device_id_type=MESH,
        )

    valid = lax.broadcasted_iota(jnp.int32, (total_frames, 1), 0) < length_ref[0]
    for h in range(heads):
        base = h * 3 * HD
        key = whole_ref[:, base + HD : base + 2 * HD]
        key_turned = key.T
        value = whole_ref[:, base + 2 * HD : base + 3 * HD]
        query_key[...] = jnp.zeros_like(query_key)
        value_total[...] = jnp.zeros_like(value_total)

        def one_block(k, carry, h=h, base=base, key=key, key_turned=key_turned, value=value):
            place = lax.rem(s + k, groups)
            if h == 0:

                @pl.when(k > 0)
                def _():
                    grad_copy(s, place).wait_recv()

            query = whole_ref[rows_of(place), base : base + HD]
            grad = grads[rows_of(place), h * HD : (h + 1) * HD]
            scores = jnp.where(valid, times_transposed(key, query), MASKED_SCORE)
            exp_scores = jnp.exp(scores - jnp.max(scores, axis=0, keepdims=True))
            probs = exp_scores * (1.0 / jnp.sum(exp_scores, axis=0, keepdims=True))
            value_total[...] += jnp.dot(
                probs.astype(jnp.bfloat16), grad, preferred_element_type=jnp.float32
            )
            grad_probs = times_transposed(value, grad)
            mean = jnp.sum(probs * grad_probs, axis=0, keepdims=True)
            grad_scores = (probs * (grad_probs - mean)).astype(jnp.bfloat16)
            query_key[:, HD:] += jnp.dot(grad_scores, query, preferred_element_type=jnp.float32)
            query_key[rows_of(place), :HD] = jnp.dot(
                key_turned, grad_scores, preferred_element_type=jnp.float32
            ).T
            return carry

        lax.fori_loop(0, groups, one_block, 0)
        part, inside = h // part_heads, (h % part_heads) * 3 * HD
        both = query_key[...]
        turned = both * cos_ref[...] + partner_lanes(both) * sin_ref[...]
        result[part, :, inside : inside + 2 * HD] = turned.astype(jnp.bfloat16)
        result[part, :, inside + 2 * HD : inside + 3 * HD] = value_total[...].astype(jnp.bfloat16)
        if (h + 1) % part_heads == 0:
            for k in range(1, groups):
                result_copy(lax.rem(s + k, groups), s, part).start()
    owns = []
    for part in range(parts):
        owns.append(
            pltpu.make_async_copy(
                result.at[part, rows_of(s)], out_place(s, part), own_sem.at[part]
            )
        )
        owns[-1].start()
    for k in range(1, groups):
        other = lax.rem(s + k, groups)
        grad_copy(other, s).wait_send()
        for part in range(parts):
            result_copy(other, s, part).wait_send()
            result_copy(s, other, part).wait_recv()
    for own in owns:
        own.wait()


def attend_back(whole, grad_attn, length, cosine, sine):
    groups = lax.axis_size("seq")
    frames = grad_attn.shape[0]
    heads = HEADS // groups
    width = heads * HD
    block = 3 * width
    total = frames * groups
    signs = jnp.where(jnp.arange(HD) < HD // 2, 1.0, -1.0)
    cos_head = jnp.concatenate([cosine, cosine], axis=1)
    sin_head = jnp.concatenate([sine, sine], axis=1) * signs
    cos_both = jnp.concatenate([cos_head * 0.125, cos_head], axis=1)
    sin_both = jnp.concatenate([sin_head * 0.125, sin_head], axis=1)
    part_heads = 2 if heads % 2 == 0 else heads
    parts = heads // part_heads
    direct = block % 128 == 0
    out_shape = (frames, groups * block) if direct else (groups, frames, block)
    vmem = pl.BlockSpec(memory_space=pltpu.VMEM)
    out = pl.pallas_call(
        functools.partial(attend_back_kernel, groups, heads),
        out_shape=jax.ShapeDtypeStruct(out_shape, jnp.bfloat16),
        in_specs=[pl.BlockSpec(memory_space=pltpu.SMEM), vmem, vmem, vmem, vmem],
        out_specs=pl.BlockSpec(memory_space=pl.ANY),
        scratch_shapes=[
            pltpu.VMEM((groups, frames, width), jnp.bfloat16),
            pltpu.VMEM((total, width), jnp.bfloat16),
            pltpu.VMEM((parts, total, part_heads * 3 * HD), jnp.bfloat16),
            pltpu.VMEM((total, 2 * HD), jnp.float32),
            pltpu.VMEM((total, HD), jnp.float32),
            pltpu.SemaphoreType.DMA((groups,)),
            pltpu.SemaphoreType.DMA((groups,)),
            pltpu.SemaphoreType.DMA((parts, groups)),
            pltpu.SemaphoreType.DMA((parts, groups)),
            pltpu.SemaphoreType.DMA((parts,)),
        ],
        compiler_params=pltpu.CompilerParams(
            collective_id=5, has_side_effects=True, vmem_limit_bytes=48 << 20
        ),
        cost_estimate=pl.CostEstimate(
            flops=10 * heads * HD * total * total,
            bytes_accessed=2 * total * 8 * width,
            transcendentals=heads * total * total,
        ),
    )(length.reshape(1), whole, grad_attn, cos_both, sin_both)
    if not direct:
        out = out.transpose(1, 0, 2).reshape(frames, groups * block)
    return out


def shards(
    frames_in,
    cotangent,
    levels,
    lengths,
    token_mask,
    cond_table,
    norm_gains,
    w_ffn1_up,
    w_ffn1_down,
    w_qkv,
    w_out,
    w_glu,
    conv_kernel,
    bn_gain,
    batchnorm_shift_bias,
    w_conv_out,
    w_ffn2_up,
    w_ffn2_down,
    running_mean,
    running_var,
):
    frames = frames_in.shape[1]
    model_width = frames_in.shape[2]
    ff_width = w_ffn1_up.shape[1]
    groups = lax.axis_size("seq")
    batches = lax.axis_size("batch")
    seq_index = lax.axis_index("seq")
    item_index = lax.axis_index("batch")
    seq_length = frames * groups
    level_count = cond_table.shape[0] - 1
    cond_rows = cond_table.astype(jnp.float32)
    gain_rows = norm_gains.astype(jnp.float32)
    level_hot = (jnp.arange(level_count) == levels[0] - 1).astype(jnp.float32)
    level_vector = jnp.sum(level_hot[:, None] * cond_rows[:level_count], axis=0)
    mask_column = token_mask[0].astype(jnp.float32)[:, None]
    start_rows = (
        frames_in[0].astype(jnp.float32)
        + level_vector[None, :]
        + mask_column * cond_rows[level_count][None, :]
    )
    length = lax.dynamic_slice_in_dim(lengths, item_index, 1)[0]
    positions = seq_index * frames + jnp.arange(frames)
    unpadded_rows = (positions < length).astype(jnp.float32)[:, None]
    rows_one, ffn1_state = ffn_forward(start_rows, gain_rows[0], w_ffn1_up, w_ffn1_down)
    normed_attn, attn_pull = jax.vjp(layer_norm, rows_one, gain_rows[1])
    attn_in = normed_attn.astype(jnp.bfloat16)
    qkv_rows = jnp.dot(attn_in, w_qkv, preferred_element_type=jnp.float32)
    cosine, sine_table = rope_tables(positions, HD)
    whole_heads, attn_out = attend(qkv_rows, length, cosine, sine_table)
    rows_two = rows_one + jnp.dot(attn_out, w_out, preferred_element_type=jnp.float32)
    normed_conv, conv_pull = jax.vjp(layer_norm, rows_two, gain_rows[2])
    conv_in = normed_conv.astype(jnp.bfloat16)
    glu_pre = jnp.dot(conv_in, w_glu, preferred_element_type=jnp.float32)
    up_half = glu_pre[:, :model_width]
    glu_sig = jax.nn.sigmoid(glu_pre[:, model_width:])
    glu_low = (up_half * glu_sig * unpadded_rows).astype(jnp.bfloat16)
    taps = conv_kernel.shape[0]
    half_size = taps // 2
    kernel_rows = conv_kernel.astype(jnp.float32)
    padded = extended(glu_low, (("seq", 0),), half_size)
    convolved_rows = jnp.zeros((frames, model_width), jnp.float32)
    for tap_index in range(taps):
        convolved_rows = (
            convolved_rows + kernel_rows[tap_index] * padded[tap_index : tap_index + frames]
        )
    sum_rows = jnp.sum(convolved_rows * unpadded_rows, axis=0)
    sum_squares = jnp.sum(convolved_rows * convolved_rows * unpadded_rows, axis=0)
    totals = sum_everywhere(jnp.stack([sum_rows, sum_squares]), 1)
    total_sum, total_squares = totals[0], totals[1]
    count_of_frames = jnp.sum(lengths).astype(jnp.float32)
    batchnorm_frame_mean = total_sum / count_of_frames
    bn_var = total_squares / count_of_frames - batchnorm_frame_mean * batchnorm_frame_mean
    batchnorm_inverse_deviation = lax.rsqrt(bn_var + EPSILON)
    batchnorm_scale_factor = bn_gain.astype(jnp.float32)
    normalized_rows = (convolved_rows - batchnorm_frame_mean) * batchnorm_inverse_deviation
    batchnorm_input_rows = normalized_rows * batchnorm_scale_factor + batchnorm_shift_bias.astype(
        jnp.float32
    )
    bn_sig = jax.nn.sigmoid(batchnorm_input_rows)
    conv_act = (batchnorm_input_rows * bn_sig).astype(jnp.bfloat16)
    rows_three = rows_two + jnp.dot(conv_act, w_conv_out, preferred_element_type=jnp.float32)
    rows_four, ffn2_state = ffn_forward(rows_three, gain_rows[3], w_ffn2_up, w_ffn2_down)
    normed_out, out_pull = jax.vjp(layer_norm, rows_four, gain_rows[4])
    out_rows = normed_out.astype(jnp.bfloat16)
    grad_four, grad_gain_four = out_pull(cotangent[0].astype(jnp.float32))
    grad_three, grad_gain_three, ffn2_up_pair, ffn2_down_pair = ffn_backward(
        grad_four, ffn2_state, w_ffn2_up, w_ffn2_down
    )
    grad_r2 = grad_three.astype(jnp.bfloat16)
    batchnorm_gradient = (
        times_transposed(grad_r2, w_conv_out)
        * bn_sig
        * (1.0 + batchnorm_input_rows * (1.0 - bn_sig))
    )
    gradient_totals = sum_everywhere(
        jnp.stack(
            [
                jnp.sum(batchnorm_gradient, axis=0),
                jnp.sum(batchnorm_gradient * normalized_rows, axis=0),
            ]
        ),
        2,
    )
    gradient_sum_total, gradient_normalized_sum = gradient_totals[0], gradient_totals[1]
    grad_conv = (
        batchnorm_scale_factor
        * batchnorm_inverse_deviation
        * (
            batchnorm_gradient
            - unpadded_rows
            * (gradient_sum_total + normalized_rows * gradient_normalized_sum)
            / count_of_frames
        )
    ).astype(jnp.bfloat16)
    grad_pad = extended(grad_conv, (("seq", 0),), half_size)
    grad_glu = jnp.zeros((frames, model_width), jnp.float32)
    kernel_terms = []
    for tap_index in range(taps):
        offset = 2 * half_size - tap_index
        grad_glu = grad_glu + kernel_rows[tap_index] * grad_pad[offset : offset + frames]
        kernel_terms.append(
            jnp.einsum(
                "fd,fd->d",
                padded[tap_index : tap_index + frames],
                grad_conv,
                preferred_element_type=jnp.float32,
            )
        )
    kernel_grads = jnp.stack(kernel_terms, axis=0)
    grad_glu = grad_glu * unpadded_rows
    grad_gl = jnp.concatenate(
        [grad_glu * glu_sig, grad_glu * up_half * glu_sig * (1.0 - glu_sig)], axis=1
    ).astype(jnp.bfloat16)
    grad_conv_in, grad_gain_two = conv_pull(times_transposed(grad_gl, w_glu))
    grad_two = grad_three + grad_conv_in
    grad_r = grad_two.astype(jnp.bfloat16)
    grad_attn_out = times_transposed(grad_r, w_out).astype(jnp.bfloat16)
    cos_all, sin_all = rope_tables(jnp.arange(seq_length), HD)
    grad_qkv = attend_back(whole_heads, grad_attn_out, length, cos_all, sin_all)
    grad_attn_part, grad_gain_one = attn_pull(times_transposed(grad_qkv, w_qkv))
    grad_one = grad_two + grad_attn_part
    grad_zero, grad_gain_zero, ffn1_up_pair, ffn1_down_pair = ffn_backward(
        grad_one, ffn1_state, w_ffn1_up, w_ffn1_down
    )
    column_total = jnp.sum(grad_zero, axis=0)
    cond_grad_rows = jnp.concatenate(
        [
            level_hot[:, None] * column_total[None, :],
            jnp.sum(mask_column * grad_zero, axis=0)[None, :],
        ],
        axis=0,
    )
    gain_grads = jnp.stack(
        [grad_gain_zero, grad_gain_one, grad_gain_two, grad_gain_three, grad_gain_four], axis=0
    )
    small_rows = jnp.concatenate([gain_grads, cond_grad_rows, kernel_grads], axis=0)
    small_sums = sum_everywhere(small_rows, 3)
    seq_width = model_width // groups
    small_piece = lax.dynamic_slice_in_dim(small_sums, seq_index * seq_width, seq_width, axis=1)
    cond_end = 5 + level_count + 1
    new_mean = 0.9 * running_mean + 0.1 * batchnorm_frame_mean
    new_var = 0.9 * running_var + 0.1 * bn_var * count_of_frames / (count_of_frames - 1.0)
    return (
        out_rows[None],
        grad_zero.astype(jnp.bfloat16)[None],
        small_piece[5:cond_end],
        small_piece[0:5],
        owned_sum(*ffn1_up_pair, False, False),
        owned_sum(*ffn1_down_pair, True, True),
        owned_sum(attn_in, grad_qkv, False, True),
        owned_sum(attn_out, grad_r, False, False),
        owned_sum(conv_in, grad_gl, False, True),
        small_piece[cond_end : cond_end + taps],
        gradient_normalized_sum,
        gradient_sum_total,
        owned_sum(conv_act, grad_r2, False, False),
        owned_sum(*ffn2_up_pair, False, False),
        owned_sum(*ffn2_down_pair, True, True),
        new_mean,
        new_var,
    )


def solution(mesh):
    in_specs = (
        P("batch", "seq", None),
        P("batch", "seq", None),
        P("batch"),
        P(),
        P("batch", "seq"),
        P(),
        P(),
        P(),
        P(),
        P(),
        P(),
        P(),
        P(),
        P(),
        P(),
        P(),
        P(),
        P(),
        P(),
        P(),
    )
    out_specs = (
        P("batch", "seq", None),
        P("batch", "seq", None),
        P(None, "seq"),
        P(None, "seq"),
        P("seq", "batch"),
        P(("batch", "seq"), None),
        P("seq", "batch"),
        P("seq", "batch"),
        P("seq", "batch"),
        P(None, "seq"),
        P(),
        P(),
        P("seq", "batch"),
        P("seq", "batch"),
        P(("batch", "seq"), None),
        P(),
        P(),
    )
    return jax.shard_map(shards, mesh=mesh, in_specs=in_specs, out_specs=out_specs, check_vma=False)
```

```python
import functools
import math

import jax
import jax.numpy as jnp
from jax import lax
from jax.experimental import pallas as pl
from jax.experimental.pallas import tpu as pltpu
from jax.sharding import PartitionSpec as P

MESH = pl.DeviceIdType.MESH

HEADS = 16
HD = 64


EPSILON = 1e-05
MASKED_SCORE = -1000000000.0


def extended(array, sides, width):
    for axis, dim in sides:
        devices, length = (lax.axis_size(axis), array.shape[dim])
        up = [(i, (i + 1) % devices) for i in range(devices - 1)]
        down = [(j, i) for i, j in up]
        last = lax.slice_in_dim(array, length - width, length, axis=dim)
        leading = lax.slice_in_dim(array, 0, width, axis=dim)
        before = lax.ppermute(last, axis, up)
        after = lax.ppermute(leading, axis, down)
        array = jnp.concatenate([before, array, after], axis=dim)
    return array


def layer_norm(values, gain_row):
    centre = values - jnp.mean(values, axis=-1, keepdims=True)
    spread = jnp.mean(centre * centre, axis=-1, keepdims=True)
    return centre * lax.rsqrt(spread + EPSILON) * gain_row


def rope_tables(positions, head_size):
    half_size = head_size // 2
    inv_freqs = jnp.exp(
        jnp.arange(half_size).astype(jnp.float32) * (-2.0 * math.log(10000.0) / head_size)
    )
    angles = positions.astype(jnp.float32)[:, None] * inv_freqs[None, :]
    return (jnp.cos(angles), jnp.sin(angles))


def times_transposed(left_side, weight):
    return lax.dot_general(
        left_side, weight, (((1,), (1,)), ((), ())), preferred_element_type=jnp.float32
    )


def ffn_forward(values, gain_row, up_weight, down_weight):
    normed, ln_pull = jax.vjp(layer_norm, values, gain_row)
    lowered = normed.astype(jnp.bfloat16)
    hidden = jnp.dot(lowered, up_weight, preferred_element_type=jnp.float32)
    act_rows = (hidden * jax.nn.sigmoid(hidden)).astype(jnp.bfloat16)
    branch = jnp.dot(act_rows, down_weight, preferred_element_type=jnp.float32)
    return (values + 0.5 * branch, (ln_pull, lowered, hidden, act_rows))


def ffn_backward(grad_in, saved_state, up_weight, down_weight):
    ln_pull, lowered, hidden, act_rows = saved_state
    grad_branch = (0.5 * grad_in).astype(jnp.bfloat16)
    grad_act = times_transposed(grad_branch, down_weight)
    gate_sig = jax.nn.sigmoid(hidden)
    grad_hidden = (grad_act * gate_sig * (1.0 + hidden * (1.0 - gate_sig))).astype(jnp.bfloat16)
    grad_normed = times_transposed(grad_hidden, up_weight)
    grad_values, grad_gain = ln_pull(grad_normed)
    return (grad_in + grad_values, grad_gain, (lowered, grad_hidden), (act_rows, grad_branch))


def sum_kernel(groups, batches, rows_ref, total_ref, seq_slots, part, batch_slots, sends, arrivals):
    s, b = lax.axis_index("seq"), lax.axis_index("batch")
    peers = [(b, lax.rem(s + k, groups)) for k in range(1, groups)]
    peers += [(lax.rem(b + k, batches), s) for k in range(1, batches)]
    barrier = pltpu.get_barrier_semaphore()
    for peer in peers:
        pl.semaphore_signal(barrier, inc=1, device_id=peer, device_id_type=MESH)
    pl.semaphore_wait(barrier, len(peers))

    def spread(source, slots, mine, first, count):
        slots[mine] = source[...]
        copies = []
        for k in range(first, first + count):
            copies.append(
                pltpu.make_async_remote_copy(
                    src_ref=source,
                    dst_ref=slots.at[mine],
                    send_sem=sends.at[k],
                    recv_sem=arrivals.at[k],
                    device_id=peers[k],
                    device_id_type=MESH,
                )
            )
            copies[-1].start()
        for copy in copies:
            copy.wait()
        total = slots[0]
        for i in range(1, count + 1):
            total = total + slots[i]
        return total

    part[...] = spread(rows_ref, seq_slots, s, 0, groups - 1)
    total_ref[...] = spread(part, batch_slots, b, groups - 1, batches - 1)


def sum_everywhere(rows, collective_id):
    groups, batches = lax.axis_size("seq"), lax.axis_size("batch")
    copies = groups + batches - 2
    return pl.pallas_call(
        functools.partial(sum_kernel, groups, batches),
        out_shape=jax.ShapeDtypeStruct(rows.shape, jnp.float32),
        in_specs=[pl.BlockSpec(memory_space=pltpu.VMEM)],
        out_specs=pl.BlockSpec(memory_space=pltpu.VMEM),
        scratch_shapes=[
            pltpu.VMEM((groups, *rows.shape), jnp.float32),
            pltpu.VMEM(rows.shape, jnp.float32),
            pltpu.VMEM((batches, *rows.shape), jnp.float32),
            pltpu.SemaphoreType.DMA((copies,)),
            pltpu.SemaphoreType.DMA((copies,)),
        ],
        compiler_params=pltpu.CompilerParams(
            collective_id=collective_id, has_side_effects=True, vmem_limit_bytes=32 << 20
        ),
    )(rows)


def halving_steps(first_seq):
    seq_bits = [("seq", k) for k in range(lax.axis_size("seq").bit_length() - 1)]
    batch_bits = [("batch", k) for k in range(1, lax.axis_size("batch").bit_length() - 1)]
    if first_seq:
        seq_bits = seq_bits[::-1]
    return [("batch", 0)] + seq_bits + batch_bits


def relative_place(place, steps, axis):
    flips = 0
    for order, (name, bit) in enumerate(steps):
        if name == axis:
            flips = flips | (((place >> (len(steps) - 1 - order)) & 1) << bit)
    return flips


def product_kernel(steps, tall, rows, cols, group, where, left_ref, right_ref, out_ref):
    step = pl.program_id(0)
    for inner in range(group):
        place = step * group + inner
        b = where[0] ^ relative_place(place, steps, "batch")
        s = where[1] ^ relative_place(place, steps, "seq")
        if tall:
            left = left_ref[:, pl.ds(pl.multiple_of((b * lax.axis_size("seq") + s) * rows, rows), rows)]
            right = right_ref[...]
        else:
            left = left_ref[:, pl.ds(pl.multiple_of(s * rows, rows), rows)]
            right = right_ref[:, pl.ds(pl.multiple_of(b * cols, cols), cols)]
        out_ref[inner] = lax.dot_general(
            left, right, (((0,), (0,)), ((), ())), preferred_element_type=jnp.float32
        ).astype(jnp.bfloat16)


def block_products(left, right, tall, steps):
    batches, groups = lax.axis_size("batch"), lax.axis_size("seq")
    places = batches * groups
    if tall:
        rows, cols = left.shape[1] // places, right.shape[1]
    else:
        rows, cols = left.shape[1] // groups, right.shape[1] // batches
    me = jnp.stack([lax.axis_index("batch"), lax.axis_index("seq")]).astype(jnp.int32)
    if rows % 128 == 0 and cols % 128 == 0:
        group = 4
        return pl.pallas_call(
            functools.partial(product_kernel, steps, tall, rows, cols, group),
            out_shape=jax.ShapeDtypeStruct((places, rows, cols), jnp.bfloat16),
            grid_spec=pltpu.PrefetchScalarGridSpec(
                num_scalar_prefetch=1,
                grid=(places // group,),
                in_specs=[
                    pl.BlockSpec(left.shape, lambda i, where: (0, 0)),
                    pl.BlockSpec(right.shape, lambda i, where: (0, 0)),
                ],
                out_specs=pl.BlockSpec((group, rows, cols), lambda i, where: (i, 0, 0)),
            ),
            compiler_params=pltpu.CompilerParams(vmem_limit_bytes=40 << 20),
            cost_estimate=pl.CostEstimate(
                flops=2 * left.shape[0] * left.shape[1] * right.shape[1],
                bytes_accessed=2 * (left.size + right.size + left.shape[1] * right.shape[1]),
                transcendentals=0,
            ),
        )(me, left, right)
    whole = lax.dot_general(
        left, right, (((0,), (0,)), ((), ())), preferred_element_type=jnp.float32
    ).astype(jnp.bfloat16)
    if tall:
        blocks = whole.reshape(batches, groups, rows, cols)
    else:
        blocks = whole.reshape(groups, rows, batches, cols).transpose(2, 0, 1, 3)
    batch_bits, seq_bits = batches.bit_length() - 1, groups.bit_length() - 1
    blocks = blocks.reshape((2,) * (batch_bits + seq_bits) + (rows, cols))
    dims = []
    for name, bit in steps:
        dim = batch_bits - 1 - bit if name == "batch" else batch_bits + seq_bits - 1 - bit
        mine = (me[0] if name == "batch" else me[1]) >> bit & 1
        blocks = jnp.where(mine == 1, jnp.flip(blocks, dim), blocks)
        dims.append(dim)
    return blocks.transpose(*dims, len(dims), len(dims) + 1).reshape(places, rows, cols)


def owned_sum(left, right, tall, first_seq):
    steps = halving_steps(first_seq)
    blocks = block_products(left, right, tall, steps)
    for axis, bit in steps:
        half = blocks.shape[0] // 2
        pairs = [(i, i ^ (1 << bit)) for i in range(lax.axis_size(axis))]
        arrived = lax.ppermute(blocks[half:], axis, pairs)
        total = blocks[:half].astype(jnp.float32) + arrived.astype(jnp.float32)
        blocks = total.astype(jnp.bfloat16) if half > 1 else total
    return blocks[0]


def attend_kernel(
    groups, heads, length_ref, qkv_ref, cos_ref, sin_ref, whole_ref, out_ref,
    stage, result, sends, arrivals, out_sends, out_arrivals, own_sem,
):
    s, b = lax.axis_index("seq"), lax.axis_index("batch")
    frames = qkv_ref.shape[0]
    total_frames = whole_ref.shape[0]
    block = heads * 3 * HD
    width = heads * HD
    greet_seq(groups, s, b)

    def rows_of(place):
        return pl.ds(pl.multiple_of(place * frames, frames), frames)

    def heads_copy(target, sender):
        return pltpu.make_async_remote_copy(
            src_ref=stage.at[target],
            dst_ref=whole_ref.at[rows_of(sender)],
            send_sem=sends.at[target],
            recv_sem=arrivals.at[sender],
            device_id=(b, target),
            device_id_type=MESH,
        )

    for column in range(0, groups * block, 128):
        pattern = (column // 128) % 3
        values = qkv_ref[:, column : column + 128]
        turned = (values * cos_ref[pattern] + partner_lanes(values) * sin_ref[pattern]).astype(
            jnp.bfloat16
        )
        start = column
        while start < column + 128:
            place = start // block
            end = min(column + 128, (place + 1) * block)
            stage[place, :, start - place * block : end - place * block] = turned[
                :, start - column : end - column
            ]
            if end == (place + 1) * block:

                @pl.when(s != place)
                def _():
                    heads_copy(place, s).start()

                @pl.when(s == place)
                def _():
                    whole_ref[rows_of(s), :] = stage[place]

            start = end
    for k in range(1, groups):
        heads_copy(s, lax.rem(s + k, groups)).wait_recv()

    valid = lax.broadcasted_iota(jnp.int32, (1, total_frames), 1) < length_ref[0]

    def out_place(owner):
        if width % 128 == 0:
            return out_ref.at[:, pl.ds(pl.multiple_of(owner * width, width), width)]
        return out_ref.at[owner]

    def result_copy(target, sender):
        return pltpu.make_async_remote_copy(
            src_ref=result.at[target],
            dst_ref=out_place(sender),
            send_sem=out_sends.at[target],
            recv_sem=out_arrivals.at[sender],
            device_id=(b, target),
            device_id_type=MESH,
        )

    def one_block(k, carry):
        place = lax.rem(s + k, groups)
        for h in range(heads):
            base = h * 3 * HD
            query = whole_ref[rows_of(place), base : base + HD]
            key = whole_ref[:, base + HD : base + 2 * HD]
            value = whole_ref[:, base + 2 * HD : base + 3 * HD]
            scores = times_transposed(query, key)
            scores = jnp.where(valid, scores, MASKED_SCORE)
            exp_scores = jnp.exp(scores - jnp.max(scores, axis=-1, keepdims=True))
            share = 1.0 / jnp.sum(exp_scores, axis=-1, keepdims=True)
            probs = (exp_scores * share).astype(jnp.bfloat16)
            mixed = jnp.dot(probs, value, preferred_element_type=jnp.float32)
            result[place, :, h * HD : (h + 1) * HD] = mixed.astype(jnp.bfloat16)

        @pl.when(k < groups)
        def _():
            result_copy(place, s).start()

        return carry

    lax.fori_loop(1, groups + 1, one_block, 0)
    own = pltpu.make_async_copy(result.at[s], out_place(s), own_sem)
    own.start()
    for k in range(1, groups):
        other = lax.rem(s + k, groups)
        heads_copy(other, s).wait_send()
        result_copy(other, s).wait_send()
        result_copy(s, other).wait_recv()
    own.wait()


def greet_seq(groups, s, b):
    barrier = pltpu.get_barrier_semaphore()
    for k in range(1, groups):
        pl.semaphore_signal(
            barrier, inc=1, device_id=(b, lax.rem(s + k, groups)), device_id_type=MESH
        )
    pl.semaphore_wait(barrier, groups - 1)


def partner_lanes(values):
    lanes = lax.broadcasted_iota(jnp.int32, values.shape, 1)
    return jnp.where(
        lanes % HD < HD // 2,
        pltpu.roll(values, 128 - HD // 2, 1),
        pltpu.roll(values, HD // 2, 1),
    )


def attend(qkv_rows, length, cosine, sine):
    groups = lax.axis_size("seq")
    frames = qkv_rows.shape[0]
    heads = HEADS // groups
    width = heads * HD
    signs = jnp.where(jnp.arange(HD) < HD // 2, -1.0, 1.0)
    cos_head = jnp.concatenate([cosine, cosine], axis=1)
    sin_head = jnp.concatenate([sine, sine], axis=1) * signs
    ones, zeros = jnp.ones_like(cos_head), jnp.zeros_like(cos_head)
    cos_pair = jnp.concatenate([cos_head * 0.125, cos_head, ones] * 2, axis=1)
    sin_pair = jnp.concatenate([sin_head * 0.125, sin_head, zeros] * 2, axis=1)
    cos_three = jnp.stack([cos_pair[:, 128 * i : 128 * (i + 1)] for i in range(3)])
    sin_three = jnp.stack([sin_pair[:, 128 * i : 128 * (i + 1)] for i in range(3)])
    direct = width % 128 == 0
    out_shape = (frames, groups * width) if direct else (groups, frames, width)
    total = frames * groups
    vmem = pl.BlockSpec(memory_space=pltpu.VMEM)
    whole, out = pl.pallas_call(
        functools.partial(attend_kernel, groups, heads),
        out_shape=(
            jax.ShapeDtypeStruct((total, 3 * width), jnp.bfloat16),
            jax.ShapeDtypeStruct(out_shape, jnp.bfloat16),
        ),
        in_specs=[pl.BlockSpec(memory_space=pltpu.SMEM), vmem, vmem, vmem],
        out_specs=(vmem, pl.BlockSpec(memory_space=pl.ANY)),
        scratch_shapes=[
            pltpu.VMEM((groups, frames, 3 * width), jnp.bfloat16),
            pltpu.VMEM((groups, frames, width), jnp.bfloat16),
            pltpu.SemaphoreType.DMA((groups,)),
            pltpu.SemaphoreType.DMA((groups,)),
            pltpu.SemaphoreType.DMA((groups,)),
            pltpu.SemaphoreType.DMA((groups,)),
            pltpu.SemaphoreType.DMA,
        ],
        compiler_params=pltpu.CompilerParams(
            collective_id=4, has_side_effects=True, vmem_limit_bytes=48 << 20
        ),
        cost_estimate=pl.CostEstimate(
            flops=4 * heads * HD * total * total,
            bytes_accessed=4 * qkv_rows.size + 2 * total * 4 * width,
            transcendentals=heads * total * total,
        ),
    )(length.reshape(1), qkv_rows, cos_three, sin_three)
    if not direct:
        out = out.transpose(1, 0, 2).reshape(frames, groups * width)
    return whole, out


def attend_back_kernel(
    groups, heads, length_ref, whole_ref, grad_ref, cos_ref, sin_ref, out_ref,
    stage, grads, result, query_key, value_total, sends, arrivals, out_sends, out_arrivals, own_sem,
):
    s, b = lax.axis_index("seq"), lax.axis_index("batch")
    frames = grad_ref.shape[0]
    total_frames = whole_ref.shape[0]
    block = heads * 3 * HD
    width = heads * HD
    greet_seq(groups, s, b)

    def rows_of(place):
        return pl.ds(pl.multiple_of(place * frames, frames), frames)

    def grad_copy(target, sender):
        return pltpu.make_async_remote_copy(
            src_ref=stage.at[target],
            dst_ref=grads.at[rows_of(sender)],
            send_sem=sends.at[target],
            recv_sem=arrivals.at[sender],
            device_id=(b, target),
            device_id_type=MESH,
        )

    for place in range(groups):
        stage[place] = grad_ref[:, place * width : (place + 1) * width]

        @pl.when(s != place)
        def _():
            grad_copy(place, s).start()

        @pl.when(s == place)
        def _():
            grads[rows_of(s), :] = stage[place]

    part_heads = 2 if heads % 2 == 0 else heads
    parts = heads // part_heads
    span = part_heads * 3 * HD

    def out_place(owner, part):
        if block % 128 == 0:
            start = pl.multiple_of(owner * block + part * span, 128)
            return out_ref.at[:, pl.ds(start, span)]
        return out_ref.at[owner, :, pl.ds(part * span, span)]

    def result_copy(target, sender, part):
        return pltpu.make_async_remote_copy(
            src_ref=result.at[part, rows_of(target)],
            dst_ref=out_place(sender, part),
            send_sem=out_sends.at[part, target],
            recv_sem=out_arrivals.at[part, sender],
            device_id=(b, target),
            device_id_type=MESH,
        )

    valid = lax.broadcasted_iota(jnp.int32, (total_frames, 1), 0) < length_ref[0]
    for h in range(heads):
        base = h * 3 * HD
        key = whole_ref[:, base + HD : base + 2 * HD]
        key_turned = key.T
        value = whole_ref[:, base + 2 * HD : base + 3 * HD]
        query_key[...] = jnp.zeros_like(query_key)
        value_total[...] = jnp.zeros_like(value_total)

        def one_block(k, carry, h=h, base=base, key=key, key_turned=key_turned, value=value):
            place = lax.rem(s + k, groups)
            if h == 0:

                @pl.when(k > 0)
                def _():
                    grad_copy(s, place).wait_recv()

            query = whole_ref[rows_of(place), base : base + HD]
            grad = grads[rows_of(place), h * HD : (h + 1) * HD]
            scores = jnp.where(valid, times_transposed(key, query), MASKED_SCORE)
            exp_scores = jnp.exp(scores - jnp.max(scores, axis=0, keepdims=True))
            probs = exp_scores * (1.0 / jnp.sum(exp_scores, axis=0, keepdims=True))
            value_total[...] += jnp.dot(
                probs.astype(jnp.bfloat16), grad, preferred_element_type=jnp.float32
            )
            grad_probs = times_transposed(value, grad)
            mean = jnp.sum(probs * grad_probs, axis=0, keepdims=True)
            grad_scores = (probs * (grad_probs - mean)).astype(jnp.bfloat16)
            query_key[:, HD:] += jnp.dot(grad_scores, query, preferred_element_type=jnp.float32)
            query_key[rows_of(place), :HD] = jnp.dot(
                key_turned, grad_scores, preferred_element_type=jnp.float32
            ).T
            return carry

        lax.fori_loop(0, groups, one_block, 0)
        part, inside = h // part_heads, (h % part_heads) * 3 * HD
        both = query_key[...]
        turned = both * cos_ref[...] + partner_lanes(both) * sin_ref[...]
        result[part, :, inside : inside + 2 * HD] = turned.astype(jnp.bfloat16)
        result[part, :, inside + 2 * HD : inside + 3 * HD] = value_total[...].astype(jnp.bfloat16)
        if (h + 1) % part_heads == 0:
            for k in range(1, groups):
                result_copy(lax.rem(s + k, groups), s, part).start()
    owns = []
    for part in range(parts):
        owns.append(
            pltpu.make_async_copy(
                result.at[part, rows_of(s)], out_place(s, part), own_sem.at[part]
            )
        )
        owns[-1].start()
    for k in range(1, groups):
        other = lax.rem(s + k, groups)
        grad_copy(other, s).wait_send()
        for part in range(parts):
            result_copy(other, s, part).wait_send()
            result_copy(s, other, part).wait_recv()
    for own in owns:
        own.wait()


def attend_back(whole, grad_attn, length, cosine, sine):
    groups = lax.axis_size("seq")
    frames = grad_attn.shape[0]
    heads = HEADS // groups
    width = heads * HD
    block = 3 * width
    total = frames * groups
    signs = jnp.where(jnp.arange(HD) < HD // 2, 1.0, -1.0)
    cos_head = jnp.concatenate([cosine, cosine], axis=1)
    sin_head = jnp.concatenate([sine, sine], axis=1) * signs
    cos_both = jnp.concatenate([cos_head * 0.125, cos_head], axis=1)
    sin_both = jnp.concatenate([sin_head * 0.125, sin_head], axis=1)
    part_heads = 2 if heads % 2 == 0 else heads
    parts = heads // part_heads
    direct = block % 128 == 0
    out_shape = (frames, groups * block) if direct else (groups, frames, block)
    vmem = pl.BlockSpec(memory_space=pltpu.VMEM)
    out = pl.pallas_call(
        functools.partial(attend_back_kernel, groups, heads),
        out_shape=jax.ShapeDtypeStruct(out_shape, jnp.bfloat16),
        in_specs=[pl.BlockSpec(memory_space=pltpu.SMEM), vmem, vmem, vmem, vmem],
        out_specs=pl.BlockSpec(memory_space=pl.ANY),
        scratch_shapes=[
            pltpu.VMEM((groups, frames, width), jnp.bfloat16),
            pltpu.VMEM((total, width), jnp.bfloat16),
            pltpu.VMEM((parts, total, part_heads * 3 * HD), jnp.bfloat16),
            pltpu.VMEM((total, 2 * HD), jnp.float32),
            pltpu.VMEM((total, HD), jnp.float32),
            pltpu.SemaphoreType.DMA((groups,)),
            pltpu.SemaphoreType.DMA((groups,)),
            pltpu.SemaphoreType.DMA((parts, groups)),
            pltpu.SemaphoreType.DMA((parts, groups)),
            pltpu.SemaphoreType.DMA((parts,)),
        ],
        compiler_params=pltpu.CompilerParams(
            collective_id=5, has_side_effects=True, vmem_limit_bytes=48 << 20
        ),
        cost_estimate=pl.CostEstimate(
            flops=10 * heads * HD * total * total,
            bytes_accessed=2 * total * 8 * width,
            transcendentals=heads * total * total,
        ),
    )(length.reshape(1), whole, grad_attn, cos_both, sin_both)
    if not direct:
        out = out.transpose(1, 0, 2).reshape(frames, groups * block)
    return out


def flipped(index, places):
    for bit, flip in places:
        mine = lax.rem(index // (1 << bit), 2)
        index = index + flip * (1 - 2 * mine) * (1 << bit)
    return index


def place_of(place, steps, axis, index):
    flips = []
    for order, (name, bit) in enumerate(steps):
        if name == axis:
            flips.append((bit, lax.rem(place // (1 << (len(steps) - 1 - order)), 2)))
    return flipped(index, flips)


def scatter_kernel(jobs, *refs):
    count = len(jobs)
    inputs, outs, scratch = refs[: 2 * count], refs[2 * count : 3 * count], refs[3 * count :]
    s, b = lax.axis_index("seq"), lax.axis_index("batch")
    core = lax.rem(b, 2)
    sibling = (b + 1 - 2 * core, s)

    def partner(step):
        axis, bit = step
        if axis == "seq":
            return (b, flipped(s, [(bit, 1)]))
        return (flipped(b, [(bit, 1)]), s)

    peers = [sibling] + [partner(step) for step in sorted(jobs[0].steps)]
    barrier = pltpu.get_barrier_semaphore()
    for peer in peers:
        pl.semaphore_signal(barrier, inc=1, device_id=peer, device_id_type=MESH)
    pl.semaphore_wait(barrier, len(peers))

    works = []
    for i, job in enumerate(jobs):
        small_in, big_in = inputs[2 * i : 2 * i + 2]
        small, big, sending, arrived, local, moves, lands, sends, recvs = scratch[9 * i : 9 * i + 9]
        frames = small_in.shape[0]
        span = big_in.shape[1] // job.batches
        own_rows, far_rows = pl.ds(0, frames), pl.ds(frames, frames)
        pieces = [(small_in, small.at[own_rows], small_in, small.at[far_rows])]
        for z in range(job.batches // 2):
            here = pl.ds(pl.multiple_of((2 * z + core) * span, 128), span)
            there = pl.ds(pl.multiple_of((2 * z + 1 - core) * span, 128), span)
            inside = pl.ds(z * span, span)
            pieces.append(
                (
                    big_in.at[:, here],
                    big.at[own_rows, inside],
                    big_in.at[:, there],
                    big.at[far_rows, inside],
                )
            )
        near, far = [], []
        for n, (own_source, own_place, far_source, far_place) in enumerate(pieces):
            near.append(pltpu.make_async_copy(own_source, own_place, local.at[n]))
            far.append(
                pltpu.make_async_remote_copy(
                    src_ref=far_source,
                    dst_ref=far_place,
                    send_sem=moves.at[n],
                    recv_sem=lands.at[n],
                    device_id=sibling,
                    device_id_type=MESH,
                )
            )
            far[-1].start()
            near[-1].start()
        works.append((near, far))

    def copy_of(i, place, step):
        sending, arrived, sends, recvs = (scratch[9 * i + j] for j in (2, 3, 7, 8))
        return pltpu.make_async_remote_copy(
            src_ref=sending.at[place - 1],
            dst_ref=arrived.at[place - 1],
            send_sem=sends.at[place - 1],
            recv_sem=recvs.at[place - 1],
            device_id=partner(step),
            device_id_type=MESH,
        )

    def block_sum(i, place, level):
        job = jobs[i]
        small, big, arrived = (scratch[9 * i + j] for j in (0, 1, 3))
        span = big.shape[1] // (job.batches // 2)
        row = place_of(place, job.steps, "seq", s)
        col = place_of(place, job.steps, "batch", b) // 2
        if job.tall:
            left = big[:, pl.ds(pl.multiple_of(col * span + row * job.rows, 128), job.rows)]
            right = small[...]
        else:
            left = small[:, pl.ds(pl.multiple_of(row * job.rows, 128), job.rows)]
            right = big[:, pl.ds(pl.multiple_of(col * span, 128), span)]
        total = lax.dot_general(
            left, right, (((0,), (0,)), ((), ())), preferred_element_type=jnp.float32
        )
        levels = len(job.steps)
        for m in range(levels - 1, level, -1):
            copy_of(i, (1 << m) + place, job.steps[levels - 1 - m]).wait_recv()
            total = total + arrived[(1 << m) + place - 1].astype(jnp.float32)
        return total

    levels = len(jobs[0].steps)
    for level in range(levels - 1, -1, -1):

        def one_place(j, carry, level=level):
            place = (2 << level) - 1 - j
            for i, job in enumerate(jobs):
                if level == levels - 1:

                    @pl.when(j == 0)
                    def _():
                        for copy in works[i][0]:
                            copy.wait()
                        for copy in works[i][1]:
                            copy.wait_recv()

                scratch[9 * i + 2][place - 1] = block_sum(i, place, level).astype(jnp.bfloat16)
                copy_of(i, place, job.steps[levels - 1 - level]).start()
            return carry

        lax.fori_loop(0, 1 << level, one_place, 0)
    for i in range(count):
        outs[i][...] = block_sum(i, 0, -1)
    for i, (near, far) in enumerate(works):
        for copy in far:
            copy.wait_send()
        for level in range(levels - 1, -1, -1):

            def one_wait(j, carry, level=level, i=i):
                copy_of(i, (1 << level) + j, jobs[i].steps[levels - 1 - level]).wait_send()
                return carry

            lax.fori_loop(0, 1 << level, one_wait, 0)


class Job:
    def __init__(self, small, big, tall, order):
        self.small, self.big, self.tall = small, big, tall
        self.batches, groups = lax.axis_size("batch"), lax.axis_size("seq")
        seq_bits = [("seq", k) for k in range(groups.bit_length() - 1)]
        batch_bits = [("batch", k) for k in range(1, self.batches.bit_length() - 1)]
        self.order = order
        if order == "x":
            self.steps = seq_bits + batch_bits
        elif order == "y":
            self.steps = seq_bits[::-1] + batch_bits
        else:
            self.steps = batch_bits[:1] + seq_bits + batch_bits[1:]
        if tall:
            self.rows = big.shape[1] // (self.batches * groups)
            self.cols = small.shape[1]
        else:
            self.rows = small.shape[1] // groups
            self.cols = big.shape[1] // self.batches

    def fits(self):
        return self.rows % 128 == 0 and self.cols % 128 == 0


def scatter_sums(jobs, collective_id):
    if not all(job.fits() for job in jobs):
        return [
            owned_sum(
                *((job.big, job.small) if job.tall else (job.small, job.big)),
                job.tall,
                job.order == "y",
            )
            for job in jobs
        ]
    scratch, operands, flops = [], [], 0
    for job in jobs:
        frames = job.small.shape[0]
        places = 1 << len(job.steps)
        pieces = 1 + job.batches // 2
        scratch += [
            pltpu.VMEM((2 * frames, job.small.shape[1]), jnp.bfloat16),
            pltpu.VMEM((2 * frames, job.big.shape[1] // 2), jnp.bfloat16),
            pltpu.VMEM((places - 1, job.rows, job.cols), jnp.bfloat16),
            pltpu.VMEM((places - 1, job.rows, job.cols), jnp.bfloat16),
            pltpu.SemaphoreType.DMA((pieces,)),
            pltpu.SemaphoreType.DMA((pieces,)),
            pltpu.SemaphoreType.DMA((pieces,)),
            pltpu.SemaphoreType.DMA((places - 1,)),
            pltpu.SemaphoreType.DMA((places - 1,)),
        ]
        operands += [job.small, job.big]
        flops += 2 * frames * job.small.shape[1] * job.big.shape[1]
    return pl.pallas_call(
        functools.partial(scatter_kernel, jobs),
        out_shape=[jax.ShapeDtypeStruct((job.rows, job.cols), jnp.float32) for job in jobs],
        in_specs=[pl.BlockSpec(memory_space=pl.ANY)] * len(operands),
        out_specs=[pl.BlockSpec(memory_space=pltpu.VMEM)] * len(jobs),
        scratch_shapes=scratch,
        compiler_params=pltpu.CompilerParams(
            collective_id=collective_id, has_side_effects=True, vmem_limit_bytes=56 << 20
        ),
        cost_estimate=pl.CostEstimate(flops=flops, bytes_accessed=flops // 512, transcendentals=0),
    )(*operands)


def shards(
    frames_in,
    cotangent,
    levels,
    lengths,
    token_mask,
    cond_table,
    norm_gains,
    w_ffn1_up,
    w_ffn1_down,
    w_qkv,
    w_out,
    w_glu,
    conv_kernel,
    bn_gain,
    batchnorm_shift_bias,
    w_conv_out,
    w_ffn2_up,
    w_ffn2_down,
    running_mean,
    running_var,
):
    frames = frames_in.shape[1]
    model_width = frames_in.shape[2]
    ff_width = w_ffn1_up.shape[1]
    groups = lax.axis_size("seq")
    batches = lax.axis_size("batch")
    seq_index = lax.axis_index("seq")
    item_index = lax.axis_index("batch")
    seq_length = frames * groups
    level_count = cond_table.shape[0] - 1
    cond_rows = cond_table.astype(jnp.float32)
    gain_rows = norm_gains.astype(jnp.float32)
    level_hot = (jnp.arange(level_count) == levels[0] - 1).astype(jnp.float32)
    level_vector = jnp.sum(level_hot[:, None] * cond_rows[:level_count], axis=0)
    mask_column = token_mask[0].astype(jnp.float32)[:, None]
    start_rows = (
        frames_in[0].astype(jnp.float32)
        + level_vector[None, :]
        + mask_column * cond_rows[level_count][None, :]
    )
    length = lax.dynamic_slice_in_dim(lengths, item_index, 1)[0]
    positions = seq_index * frames + jnp.arange(frames)
    unpadded_rows = (positions < length).astype(jnp.float32)[:, None]
    rows_one, ffn1_state = ffn_forward(start_rows, gain_rows[0], w_ffn1_up, w_ffn1_down)
    normed_attn, attn_pull = jax.vjp(layer_norm, rows_one, gain_rows[1])
    attn_in = normed_attn.astype(jnp.bfloat16)
    qkv_rows = jnp.dot(attn_in, w_qkv, preferred_element_type=jnp.float32)
    cosine, sine_table = rope_tables(positions, HD)
    whole_heads, attn_out = attend(qkv_rows, length, cosine, sine_table)
    rows_two = rows_one + jnp.dot(attn_out, w_out, preferred_element_type=jnp.float32)
    normed_conv, conv_pull = jax.vjp(layer_norm, rows_two, gain_rows[2])
    conv_in = normed_conv.astype(jnp.bfloat16)
    glu_pre = jnp.dot(conv_in, w_glu, preferred_element_type=jnp.float32)
    up_half = glu_pre[:, :model_width]
    glu_sig = jax.nn.sigmoid(glu_pre[:, model_width:])
    glu_low = (up_half * glu_sig * unpadded_rows).astype(jnp.bfloat16)
    taps = conv_kernel.shape[0]
    half_size = taps // 2
    kernel_rows = conv_kernel.astype(jnp.float32)
    padded = extended(glu_low, (("seq", 0),), half_size)
    convolved_rows = jnp.zeros((frames, model_width), jnp.float32)
    for tap_index in range(taps):
        convolved_rows = (
            convolved_rows + kernel_rows[tap_index] * padded[tap_index : tap_index + frames]
        )
    sum_rows = jnp.sum(convolved_rows * unpadded_rows, axis=0)
    sum_squares = jnp.sum(convolved_rows * convolved_rows * unpadded_rows, axis=0)
    totals = sum_everywhere(jnp.stack([sum_rows, sum_squares]), 1)
    total_sum, total_squares = totals[0], totals[1]
    count_of_frames = jnp.sum(lengths).astype(jnp.float32)
    batchnorm_frame_mean = total_sum / count_of_frames
    bn_var = total_squares / count_of_frames - batchnorm_frame_mean * batchnorm_frame_mean
    batchnorm_inverse_deviation = lax.rsqrt(bn_var + EPSILON)
    batchnorm_scale_factor = bn_gain.astype(jnp.float32)
    normalized_rows = (convolved_rows - batchnorm_frame_mean) * batchnorm_inverse_deviation
    batchnorm_input_rows = normalized_rows * batchnorm_scale_factor + batchnorm_shift_bias.astype(
        jnp.float32
    )
    bn_sig = jax.nn.sigmoid(batchnorm_input_rows)
    conv_act = (batchnorm_input_rows * bn_sig).astype(jnp.bfloat16)
    rows_three = rows_two + jnp.dot(conv_act, w_conv_out, preferred_element_type=jnp.float32)
    rows_four, ffn2_state = ffn_forward(rows_three, gain_rows[3], w_ffn2_up, w_ffn2_down)
    normed_out, out_pull = jax.vjp(layer_norm, rows_four, gain_rows[4])
    out_rows = normed_out.astype(jnp.bfloat16)
    grad_four, grad_gain_four = out_pull(cotangent[0].astype(jnp.float32))
    grad_three, grad_gain_three, ffn2_up_pair, ffn2_down_pair = ffn_backward(
        grad_four, ffn2_state, w_ffn2_up, w_ffn2_down
    )
    grad_r2 = grad_three.astype(jnp.bfloat16)
    batchnorm_gradient = (
        times_transposed(grad_r2, w_conv_out)
        * bn_sig
        * (1.0 + batchnorm_input_rows * (1.0 - bn_sig))
    )
    gradient_totals = sum_everywhere(
        jnp.stack(
            [
                jnp.sum(batchnorm_gradient, axis=0),
                jnp.sum(batchnorm_gradient * normalized_rows, axis=0),
            ]
        ),
        2,
    )
    gradient_sum_total, gradient_normalized_sum = gradient_totals[0], gradient_totals[1]
    grad_conv = (
        batchnorm_scale_factor
        * batchnorm_inverse_deviation
        * (
            batchnorm_gradient
            - unpadded_rows
            * (gradient_sum_total + normalized_rows * gradient_normalized_sum)
            / count_of_frames
        )
    ).astype(jnp.bfloat16)
    grad_pad = extended(grad_conv, (("seq", 0),), half_size)
    grad_glu = jnp.zeros((frames, model_width), jnp.float32)
    kernel_terms = []
    for tap_index in range(taps):
        offset = 2 * half_size - tap_index
        grad_glu = grad_glu + kernel_rows[tap_index] * grad_pad[offset : offset + frames]
        kernel_terms.append(
            jnp.einsum(
                "fd,fd->d",
                padded[tap_index : tap_index + frames],
                grad_conv,
                preferred_element_type=jnp.float32,
            )
        )
    kernel_grads = jnp.stack(kernel_terms, axis=0)
    grad_glu = grad_glu * unpadded_rows
    grad_gl = jnp.concatenate(
        [grad_glu * glu_sig, grad_glu * up_half * glu_sig * (1.0 - glu_sig)], axis=1
    ).astype(jnp.bfloat16)
    grad_conv_in, grad_gain_two = conv_pull(times_transposed(grad_gl, w_glu))
    grad_two = grad_three + grad_conv_in
    grad_r = grad_two.astype(jnp.bfloat16)
    grad_attn_out = times_transposed(grad_r, w_out).astype(jnp.bfloat16)
    cos_all, sin_all = rope_tables(jnp.arange(seq_length), HD)
    grad_qkv = attend_back(whole_heads, grad_attn_out, length, cos_all, sin_all)
    grad_attn_part, grad_gain_one = attn_pull(times_transposed(grad_qkv, w_qkv))
    grad_one = grad_two + grad_attn_part
    grad_zero, grad_gain_zero, ffn1_up_pair, ffn1_down_pair = ffn_backward(
        grad_one, ffn1_state, w_ffn1_up, w_ffn1_down
    )
    column_total = jnp.sum(grad_zero, axis=0)
    cond_grad_rows = jnp.concatenate(
        [
            level_hot[:, None] * column_total[None, :],
            jnp.sum(mask_column * grad_zero, axis=0)[None, :],
        ],
        axis=0,
    )
    gain_grads = jnp.stack(
        [grad_gain_zero, grad_gain_one, grad_gain_two, grad_gain_three, grad_gain_four], axis=0
    )
    middle = scatter_sums(
        [
            Job(*ffn2_up_pair, False, "x"),
            Job(*ffn2_down_pair[::-1], True, "y"),
            Job(conv_in, grad_gl, False, "z"),
            Job(attn_out, grad_r, False, "z"),
            Job(conv_act, grad_r2, False, "z"),
        ],
        6,
    )
    last = scatter_sums(
        [
            Job(*ffn1_up_pair, False, "x"),
            Job(*ffn1_down_pair[::-1], True, "y"),
            Job(attn_in, grad_qkv, False, "z"),
        ],
        7,
    )
    small_rows = jnp.concatenate([gain_grads, cond_grad_rows, kernel_grads], axis=0)
    small_sums = sum_everywhere(small_rows, 3)
    seq_width = model_width // groups
    small_piece = lax.dynamic_slice_in_dim(small_sums, seq_index * seq_width, seq_width, axis=1)
    cond_end = 5 + level_count + 1
    new_mean = 0.9 * running_mean + 0.1 * batchnorm_frame_mean
    new_var = 0.9 * running_var + 0.1 * bn_var * count_of_frames / (count_of_frames - 1.0)
    return (
        out_rows[None],
        grad_zero.astype(jnp.bfloat16)[None],
        small_piece[5:cond_end],
        small_piece[0:5],
        last[0],
        last[1],
        last[2],
        middle[3],
        middle[2],
        small_piece[cond_end : cond_end + taps],
        gradient_normalized_sum,
        gradient_sum_total,
        middle[4],
        middle[0],
        middle[1],
        new_mean,
        new_var,
    )


def solution(mesh):
    in_specs = (
        P("batch", "seq", None),
        P("batch", "seq", None),
        P("batch"),
        P(),
        P("batch", "seq"),
        P(),
        P(),
        P(),
        P(),
        P(),
        P(),
        P(),
        P(),
        P(),
        P(),
        P(),
        P(),
        P(),
        P(),
        P(),
    )
    out_specs = (
        P("batch", "seq", None),
        P("batch", "seq", None),
        P(None, "seq"),
        P(None, "seq"),
        P("seq", "batch"),
        P(("batch", "seq"), None),
        P("seq", "batch"),
        P("seq", "batch"),
        P("seq", "batch"),
        P(None, "seq"),
        P(),
        P(),
        P("seq", "batch"),
        P("seq", "batch"),
        P(("batch", "seq"), None),
        P(),
        P(),
    )
    return jax.shard_map(shards, mesh=mesh, in_specs=in_specs, out_specs=out_specs, check_vma=False)
```

```python
import functools
import math

import jax
import jax.numpy as jnp
from jax import lax
from jax.experimental import pallas as pl
from jax.experimental.pallas import tpu as pltpu
from jax.sharding import PartitionSpec as P

MESH = pl.DeviceIdType.MESH

HEADS = 16
HD = 64


EPSILON = 1e-05
MASKED_SCORE = -1000000000.0

SEGMENTS = (
    (0, 3), (1, 3), (2, 3), (2, 2), (0, 2), (1, 2), (5, 3), (2, 1), (4, 3), (0, 1), (3, 3),
    (0, 0), (5, 2), (3, 2), (0, -1), (3, 1), (5, 1), (5, 0), (4, 2), (2, 0), (4, 1), (1, 1),
    (3, 0), (4, 0), (1, 0), (5, -1), (2, -1), (4, -1), (3, -1), (1, -1),
)


def extended(array, sides, width):
    for axis, dim in sides:
        devices, length = (lax.axis_size(axis), array.shape[dim])
        up = [(i, (i + 1) % devices) for i in range(devices - 1)]
        down = [(j, i) for i, j in up]
        last = lax.slice_in_dim(array, length - width, length, axis=dim)
        leading = lax.slice_in_dim(array, 0, width, axis=dim)
        before = lax.ppermute(last, axis, up)
        after = lax.ppermute(leading, axis, down)
        array = jnp.concatenate([before, array, after], axis=dim)
    return array


def layer_norm(values, gain_row):
    centre = values - jnp.mean(values, axis=-1, keepdims=True)
    spread = jnp.mean(centre * centre, axis=-1, keepdims=True)
    return centre * lax.rsqrt(spread + EPSILON) * gain_row


def rope_tables(positions, head_size):
    half_size = head_size // 2
    inv_freqs = jnp.exp(
        jnp.arange(half_size).astype(jnp.float32) * (-2.0 * math.log(10000.0) / head_size)
    )
    angles = positions.astype(jnp.float32)[:, None] * inv_freqs[None, :]
    return (jnp.cos(angles), jnp.sin(angles))


def times_transposed(left_side, weight):
    return lax.dot_general(
        left_side, weight, (((1,), (1,)), ((), ())), preferred_element_type=jnp.float32
    )


def ffn_forward(values, gain_row, up_weight, down_weight):
    normed, ln_pull = jax.vjp(layer_norm, values, gain_row)
    lowered = normed.astype(jnp.bfloat16)
    hidden = jnp.dot(lowered, up_weight, preferred_element_type=jnp.float32)
    act_rows = (hidden * jax.nn.sigmoid(hidden)).astype(jnp.bfloat16)
    branch = jnp.dot(act_rows, down_weight, preferred_element_type=jnp.float32)
    return (values + 0.5 * branch, (ln_pull, lowered, hidden, act_rows))


def ffn_backward(grad_in, saved_state, up_weight, down_weight):
    ln_pull, lowered, hidden, act_rows = saved_state
    grad_branch = (0.5 * grad_in).astype(jnp.bfloat16)
    grad_act = times_transposed(grad_branch, down_weight)
    gate_sig = jax.nn.sigmoid(hidden)
    grad_hidden = (grad_act * gate_sig * (1.0 + hidden * (1.0 - gate_sig))).astype(jnp.bfloat16)
    grad_normed = times_transposed(grad_hidden, up_weight)
    grad_values, grad_gain = ln_pull(grad_normed)
    return (grad_in + grad_values, grad_gain, (lowered, grad_hidden), (act_rows, grad_branch))


def sum_kernel(groups, batches, scatter, rows_ref, total_ref, seq_slots, part, batch_slots, sends, arrivals):
    s, b = lax.axis_index("seq"), lax.axis_index("batch")
    peers = [(b, lax.rem(s + k, groups)) for k in range(1, groups)]
    peers += [(lax.rem(b + k, batches), s) for k in range(1, batches)]
    greet(peers)
    width = seq_slots.shape[2]

    def spread(pick, slots, mine, first, count):
        slots[mine] = pick(s)[...]
        copies = []
        for k in range(first, first + count):
            copies.append(
                pltpu.make_async_remote_copy(
                    src_ref=pick(peers[k][1]),
                    dst_ref=slots.at[mine],
                    send_sem=sends.at[k],
                    recv_sem=arrivals.at[k],
                    device_id=peers[k],
                    device_id_type=MESH,
                )
            )
            copies[-1].start()
        for copy in copies:
            copy.wait()
        total = slots[0]
        for i in range(1, count + 1):
            total = total + slots[i]
        return total

    def columns(owner):
        if not scatter:
            return rows_ref
        return rows_ref.at[:, pl.ds(pl.multiple_of(owner * width, 128), width)]

    part[...] = spread(columns, seq_slots, s, 0, groups - 1)
    total_ref[...] = spread(lambda owner: part, batch_slots, b, groups - 1, batches - 1)


def sum_everywhere(rows, collective_id, scatter=False):
    groups, batches = lax.axis_size("seq"), lax.axis_size("batch")
    copies = groups + batches - 2
    height, width = rows.shape
    share = width // groups if scatter else width
    direct = share % 128 == 0
    if not direct:
        share = width
    total = pl.pallas_call(
        functools.partial(sum_kernel, groups, batches, scatter and direct),
        out_shape=jax.ShapeDtypeStruct((height, share), jnp.float32),
        in_specs=[pl.BlockSpec(memory_space=pltpu.VMEM)],
        out_specs=pl.BlockSpec(memory_space=pltpu.VMEM),
        scratch_shapes=[
            pltpu.VMEM((groups, height, share), jnp.float32),
            pltpu.VMEM((height, share), jnp.float32),
            pltpu.VMEM((batches, height, share), jnp.float32),
            pltpu.SemaphoreType.DMA((copies,)),
            pltpu.SemaphoreType.DMA((copies,)),
        ],
        compiler_params=pltpu.CompilerParams(
            collective_id=collective_id, has_side_effects=True, vmem_limit_bytes=32 << 20
        ),
    )(rows)
    if scatter and not direct:
        share = width // groups
        total = lax.dynamic_slice_in_dim(total, lax.axis_index("seq") * share, share, axis=1)
    return total


def halving_steps(first_seq):
    seq_bits = [("seq", k) for k in range(lax.axis_size("seq").bit_length() - 1)]
    batch_bits = [("batch", k) for k in range(1, lax.axis_size("batch").bit_length() - 1)]
    if first_seq:
        seq_bits = seq_bits[::-1]
    return [("batch", 0)] + seq_bits + batch_bits


def relative_place(place, steps, axis):
    flips = 0
    for order, (name, bit) in enumerate(steps):
        if name == axis:
            flips = flips | (((place >> (len(steps) - 1 - order)) & 1) << bit)
    return flips


def product_kernel(steps, tall, rows, cols, group, where, left_ref, right_ref, out_ref):
    step = pl.program_id(0)
    for inner in range(group):
        place = step * group + inner
        b = where[0] ^ relative_place(place, steps, "batch")
        s = where[1] ^ relative_place(place, steps, "seq")
        if tall:
            left = left_ref[:, pl.ds(pl.multiple_of((b * lax.axis_size("seq") + s) * rows, rows), rows)]
            right = right_ref[...]
        else:
            left = left_ref[:, pl.ds(pl.multiple_of(s * rows, rows), rows)]
            right = right_ref[:, pl.ds(pl.multiple_of(b * cols, cols), cols)]
        out_ref[inner] = lax.dot_general(
            left, right, (((0,), (0,)), ((), ())), preferred_element_type=jnp.float32
        ).astype(jnp.bfloat16)


def block_products(left, right, tall, steps):
    batches, groups = lax.axis_size("batch"), lax.axis_size("seq")
    places = batches * groups
    if tall:
        rows, cols = left.shape[1] // places, right.shape[1]
    else:
        rows, cols = left.shape[1] // groups, right.shape[1] // batches
    me = jnp.stack([lax.axis_index("batch"), lax.axis_index("seq")]).astype(jnp.int32)
    if rows % 128 == 0 and cols % 128 == 0:
        group = 4
        return pl.pallas_call(
            functools.partial(product_kernel, steps, tall, rows, cols, group),
            out_shape=jax.ShapeDtypeStruct((places, rows, cols), jnp.bfloat16),
            grid_spec=pltpu.PrefetchScalarGridSpec(
                num_scalar_prefetch=1,
                grid=(places // group,),
                in_specs=[
                    pl.BlockSpec(left.shape, lambda i, where: (0, 0)),
                    pl.BlockSpec(right.shape, lambda i, where: (0, 0)),
                ],
                out_specs=pl.BlockSpec((group, rows, cols), lambda i, where: (i, 0, 0)),
            ),
            compiler_params=pltpu.CompilerParams(vmem_limit_bytes=40 << 20),
            cost_estimate=pl.CostEstimate(
                flops=2 * left.shape[0] * left.shape[1] * right.shape[1],
                bytes_accessed=2 * (left.size + right.size + left.shape[1] * right.shape[1]),
                transcendentals=0,
            ),
        )(me, left, right)
    whole = lax.dot_general(
        left, right, (((0,), (0,)), ((), ())), preferred_element_type=jnp.float32
    ).astype(jnp.bfloat16)
    if tall:
        blocks = whole.reshape(batches, groups, rows, cols)
    else:
        blocks = whole.reshape(groups, rows, batches, cols).transpose(2, 0, 1, 3)
    batch_bits, seq_bits = batches.bit_length() - 1, groups.bit_length() - 1
    blocks = blocks.reshape((2,) * (batch_bits + seq_bits) + (rows, cols))
    dims = []
    for name, bit in steps:
        dim = batch_bits - 1 - bit if name == "batch" else batch_bits + seq_bits - 1 - bit
        mine = (me[0] if name == "batch" else me[1]) >> bit & 1
        blocks = jnp.where(mine == 1, jnp.flip(blocks, dim), blocks)
        dims.append(dim)
    return blocks.transpose(*dims, len(dims), len(dims) + 1).reshape(places, rows, cols)


def owned_sum(left, right, tall, first_seq):
    steps = halving_steps(first_seq)
    blocks = block_products(left, right, tall, steps)
    for axis, bit in steps:
        half = blocks.shape[0] // 2
        pairs = [(i, i ^ (1 << bit)) for i in range(lax.axis_size(axis))]
        arrived = lax.ppermute(blocks[half:], axis, pairs)
        total = blocks[:half].astype(jnp.float32) + arrived.astype(jnp.float32)
        blocks = total.astype(jnp.bfloat16) if half > 1 else total
    return blocks[0]


def attend_kernel(
    groups, heads, length_ref, qkv_ref, cos_ref, sin_ref, whole_ref, out_ref,
    stage, result, sends, arrivals, out_sends, out_arrivals, own_sem,
):
    s, b = lax.axis_index("seq"), lax.axis_index("batch")
    frames = qkv_ref.shape[0]
    total_frames = whole_ref.shape[0]
    block = heads * 3 * HD
    width = heads * HD
    greet_seq(groups, s, b)

    def rows_of(place):
        return pl.ds(pl.multiple_of(place * frames, frames), frames)

    def heads_copy(target, sender):
        return pltpu.make_async_remote_copy(
            src_ref=stage.at[target],
            dst_ref=whole_ref.at[rows_of(sender)],
            send_sem=sends.at[target],
            recv_sem=arrivals.at[sender],
            device_id=(b, target),
            device_id_type=MESH,
        )

    for column in range(0, groups * block, 128):
        pattern = (column // 128) % 3
        values = qkv_ref[:, column : column + 128]
        turned = (values * cos_ref[pattern] + partner_lanes(values) * sin_ref[pattern]).astype(
            jnp.bfloat16
        )
        start = column
        while start < column + 128:
            place = start // block
            end = min(column + 128, (place + 1) * block)
            stage[place, :, start - place * block : end - place * block] = turned[
                :, start - column : end - column
            ]
            if end == (place + 1) * block:

                @pl.when(s != place)
                def _():
                    heads_copy(place, s).start()

                @pl.when(s == place)
                def _():
                    whole_ref[rows_of(s), :] = stage[place]

            start = end
    for k in range(1, groups):
        heads_copy(s, lax.rem(s + k, groups)).wait_recv()

    valid = lax.broadcasted_iota(jnp.int32, (1, total_frames), 1) < length_ref[0]

    def out_place(owner):
        if width % 128 == 0:
            return out_ref.at[:, pl.ds(pl.multiple_of(owner * width, width), width)]
        return out_ref.at[owner]

    def result_copy(target, sender):
        return pltpu.make_async_remote_copy(
            src_ref=result.at[target],
            dst_ref=out_place(sender),
            send_sem=out_sends.at[target],
            recv_sem=out_arrivals.at[sender],
            device_id=(b, target),
            device_id_type=MESH,
        )

    def one_block(k, carry):
        place = lax.rem(s + k, groups)
        for h in range(heads):
            base = h * 3 * HD
            query = whole_ref[rows_of(place), base : base + HD]
            key = whole_ref[:, base + HD : base + 2 * HD]
            value = whole_ref[:, base + 2 * HD : base + 3 * HD]
            scores = times_transposed(query, key)
            scores = jnp.where(valid, scores, MASKED_SCORE)
            exp_scores = jnp.exp(scores - jnp.max(scores, axis=-1, keepdims=True))
            share = 1.0 / jnp.sum(exp_scores, axis=-1, keepdims=True)
            probs = (exp_scores * share).astype(jnp.bfloat16)
            mixed = jnp.dot(probs, value, preferred_element_type=jnp.float32)
            result[place, :, h * HD : (h + 1) * HD] = mixed.astype(jnp.bfloat16)

        @pl.when(k < groups)
        def _():
            result_copy(place, s).start()

        return carry

    lax.fori_loop(1, groups + 1, one_block, 0)
    own = pltpu.make_async_copy(result.at[s], out_place(s), own_sem)
    own.start()
    for k in range(1, groups):
        other = lax.rem(s + k, groups)
        heads_copy(other, s).wait_send()
        result_copy(other, s).wait_send()
        result_copy(s, other).wait_recv()
    own.wait()


def greet_seq(groups, s, b):
    greet([(b, lax.rem(s + k, groups)) for k in range(1, groups)])


def partner_lanes(values):
    lanes = lax.broadcasted_iota(jnp.int32, values.shape, 1)
    return jnp.where(
        lanes % HD < HD // 2,
        pltpu.roll(values, 128 - HD // 2, 1),
        pltpu.roll(values, HD // 2, 1),
    )


def attend(qkv_rows, length, cosine, sine):
    groups = lax.axis_size("seq")
    frames = qkv_rows.shape[0]
    heads = HEADS // groups
    width = heads * HD
    signs = jnp.where(jnp.arange(HD) < HD // 2, -1.0, 1.0)
    cos_head = jnp.concatenate([cosine, cosine], axis=1)
    sin_head = jnp.concatenate([sine, sine], axis=1) * signs
    ones, zeros = jnp.ones_like(cos_head), jnp.zeros_like(cos_head)
    cos_pair = jnp.concatenate([cos_head * 0.125, cos_head, ones] * 2, axis=1)
    sin_pair = jnp.concatenate([sin_head * 0.125, sin_head, zeros] * 2, axis=1)
    cos_three = jnp.stack([cos_pair[:, 128 * i : 128 * (i + 1)] for i in range(3)])
    sin_three = jnp.stack([sin_pair[:, 128 * i : 128 * (i + 1)] for i in range(3)])
    direct = width % 128 == 0
    out_shape = (frames, groups * width) if direct else (groups, frames, width)
    total = frames * groups
    vmem = pl.BlockSpec(memory_space=pltpu.VMEM)
    whole, out = pl.pallas_call(
        functools.partial(attend_kernel, groups, heads),
        out_shape=(
            jax.ShapeDtypeStruct((total, 3 * width), jnp.bfloat16),
            jax.ShapeDtypeStruct(out_shape, jnp.bfloat16),
        ),
        in_specs=[pl.BlockSpec(memory_space=pltpu.SMEM), vmem, vmem, vmem],
        out_specs=(vmem, pl.BlockSpec(memory_space=pl.ANY)),
        scratch_shapes=[
            pltpu.VMEM((groups, frames, 3 * width), jnp.bfloat16),
            pltpu.VMEM((groups, frames, width), jnp.bfloat16),
            pltpu.SemaphoreType.DMA((groups,)),
            pltpu.SemaphoreType.DMA((groups,)),
            pltpu.SemaphoreType.DMA((groups,)),
            pltpu.SemaphoreType.DMA((groups,)),
            pltpu.SemaphoreType.DMA,
        ],
        compiler_params=pltpu.CompilerParams(
            collective_id=4, has_side_effects=True, vmem_limit_bytes=48 << 20
        ),
        cost_estimate=pl.CostEstimate(
            flops=4 * heads * HD * total * total,
            bytes_accessed=4 * qkv_rows.size + 2 * total * 4 * width,
            transcendentals=heads * total * total,
        ),
    )(length.reshape(1), qkv_rows, cos_three, sin_three)
    if not direct:
        out = out.transpose(1, 0, 2).reshape(frames, groups * width)
    return whole, out


def attend_back_kernel(
    groups, heads, length_ref, whole_ref, grad_ref, cos_ref, sin_ref, out_ref,
    stage, grads, result, query_key, value_total, sends, arrivals, out_sends, out_arrivals, own_sem,
):
    s, b = lax.axis_index("seq"), lax.axis_index("batch")
    frames = grad_ref.shape[0]
    total_frames = whole_ref.shape[0]
    block = heads * 3 * HD
    width = heads * HD
    greet_seq(groups, s, b)

    def rows_of(place):
        return pl.ds(pl.multiple_of(place * frames, frames), frames)

    def grad_copy(target, sender):
        return pltpu.make_async_remote_copy(
            src_ref=stage.at[target],
            dst_ref=grads.at[rows_of(sender)],
            send_sem=sends.at[target],
            recv_sem=arrivals.at[sender],
            device_id=(b, target),
            device_id_type=MESH,
        )

    for place in range(groups):
        stage[place] = grad_ref[:, place * width : (place + 1) * width]

        @pl.when(s != place)
        def _():
            grad_copy(place, s).start()

        @pl.when(s == place)
        def _():
            grads[rows_of(s), :] = stage[place]

    part_heads = 2 if heads % 2 == 0 else heads
    parts = heads // part_heads
    span = part_heads * 3 * HD

    def out_place(owner, part):
        if block % 128 == 0:
            start = pl.multiple_of(owner * block + part * span, 128)
            return out_ref.at[:, pl.ds(start, span)]
        return out_ref.at[owner, :, pl.ds(part * span, span)]

    def result_copy(target, sender, part):
        return pltpu.make_async_remote_copy(
            src_ref=result.at[part, rows_of(target)],
            dst_ref=out_place(sender, part),
            send_sem=out_sends.at[part, target],
            recv_sem=out_arrivals.at[part, sender],
            device_id=(b, target),
            device_id_type=MESH,
        )

    valid = lax.broadcasted_iota(jnp.int32, (total_frames, 1), 0) < length_ref[0]
    for h in range(heads):
        base = h * 3 * HD
        key = whole_ref[:, base + HD : base + 2 * HD]
        key_turned = key.T
        value = whole_ref[:, base + 2 * HD : base + 3 * HD]
        query_key[...] = jnp.zeros_like(query_key)
        value_total[...] = jnp.zeros_like(value_total)

        def one_block(k, carry, h=h, base=base, key=key, key_turned=key_turned, value=value):
            place = lax.rem(s + k, groups)
            if h == 0:

                @pl.when(k > 0)
                def _():
                    grad_copy(s, place).wait_recv()

            query = whole_ref[rows_of(place), base : base + HD]
            grad = grads[rows_of(place), h * HD : (h + 1) * HD]
            scores = jnp.where(valid, times_transposed(key, query), MASKED_SCORE)
            exp_scores = jnp.exp(scores - jnp.max(scores, axis=0, keepdims=True))
            probs = exp_scores * (1.0 / jnp.sum(exp_scores, axis=0, keepdims=True))
            value_total[...] += jnp.dot(
                probs.astype(jnp.bfloat16), grad, preferred_element_type=jnp.float32
            )
            grad_probs = times_transposed(value, grad)
            mean = jnp.sum(probs * grad_probs, axis=0, keepdims=True)
            grad_scores = (probs * (grad_probs - mean)).astype(jnp.bfloat16)
            query_key[:, HD:] += jnp.dot(grad_scores, query, preferred_element_type=jnp.float32)
            query_key[rows_of(place), :HD] = jnp.dot(
                key_turned, grad_scores, preferred_element_type=jnp.float32
            ).T
            return carry

        lax.fori_loop(0, groups, one_block, 0)
        part, inside = h // part_heads, (h % part_heads) * 3 * HD
        both = query_key[...]
        turned = both * cos_ref[...] + partner_lanes(both) * sin_ref[...]
        result[part, :, inside : inside + 2 * HD] = turned.astype(jnp.bfloat16)
        result[part, :, inside + 2 * HD : inside + 3 * HD] = value_total[...].astype(jnp.bfloat16)
        if (h + 1) % part_heads == 0:
            for k in range(1, groups):
                result_copy(lax.rem(s + k, groups), s, part).start()
    owns = []
    for part in range(parts):
        owns.append(
            pltpu.make_async_copy(
                result.at[part, rows_of(s)], out_place(s, part), own_sem.at[part]
            )
        )
        owns[-1].start()
    for k in range(1, groups):
        other = lax.rem(s + k, groups)
        grad_copy(other, s).wait_send()
        for part in range(parts):
            result_copy(other, s, part).wait_send()
            result_copy(s, other, part).wait_recv()
    for own in owns:
        own.wait()


def attend_back(whole, grad_attn, length, cosine, sine):
    groups = lax.axis_size("seq")
    frames = grad_attn.shape[0]
    heads = HEADS // groups
    width = heads * HD
    block = 3 * width
    total = frames * groups
    signs = jnp.where(jnp.arange(HD) < HD // 2, 1.0, -1.0)
    cos_head = jnp.concatenate([cosine, cosine], axis=1)
    sin_head = jnp.concatenate([sine, sine], axis=1) * signs
    cos_both = jnp.concatenate([cos_head * 0.125, cos_head], axis=1)
    sin_both = jnp.concatenate([sin_head * 0.125, sin_head], axis=1)
    part_heads = 2 if heads % 2 == 0 else heads
    parts = heads // part_heads
    direct = block % 128 == 0
    out_shape = (frames, groups * block) if direct else (groups, frames, block)
    vmem = pl.BlockSpec(memory_space=pltpu.VMEM)
    out = pl.pallas_call(
        functools.partial(attend_back_kernel, groups, heads),
        out_shape=jax.ShapeDtypeStruct(out_shape, jnp.bfloat16),
        in_specs=[pl.BlockSpec(memory_space=pltpu.SMEM), vmem, vmem, vmem, vmem],
        out_specs=pl.BlockSpec(memory_space=pl.ANY),
        scratch_shapes=[
            pltpu.VMEM((groups, frames, width), jnp.bfloat16),
            pltpu.VMEM((total, width), jnp.bfloat16),
            pltpu.VMEM((parts, total, part_heads * 3 * HD), jnp.bfloat16),
            pltpu.VMEM((total, 2 * HD), jnp.float32),
            pltpu.VMEM((total, HD), jnp.float32),
            pltpu.SemaphoreType.DMA((groups,)),
            pltpu.SemaphoreType.DMA((groups,)),
            pltpu.SemaphoreType.DMA((parts, groups)),
            pltpu.SemaphoreType.DMA((parts, groups)),
            pltpu.SemaphoreType.DMA((parts,)),
        ],
        compiler_params=pltpu.CompilerParams(
            collective_id=5, has_side_effects=True, vmem_limit_bytes=48 << 20
        ),
        cost_estimate=pl.CostEstimate(
            flops=10 * heads * HD * total * total,
            bytes_accessed=2 * total * 8 * width,
            transcendentals=heads * total * total,
        ),
    )(length.reshape(1), whole, grad_attn, cos_both, sin_both)
    if not direct:
        out = out.transpose(1, 0, 2).reshape(frames, groups * block)
    return out


def flipped(index, places):
    for bit, flip in places:
        mine = lax.rem(index // (1 << bit), 2)
        index = index + flip * (1 - 2 * mine) * (1 << bit)
    return index


def place_of(place, steps, axis, index):
    flips = []
    for order, (name, bit) in enumerate(steps):
        if name == axis:
            flips.append((bit, lax.rem(place // (1 << (len(steps) - 1 - order)), 2)))
    return flipped(index, flips)


class Job:
    def __init__(self, parts, tall, order):
        self.parts, self.tall, self.arrived = parts, tall, None
        self.batches, self.groups = lax.axis_size("batch"), lax.axis_size("seq")
        bits = {
            "x": [("seq", 0)],
            "y": [("seq", k) for k in range(1, self.groups.bit_length() - 1)],
            "1": [("batch", 1)],
            "2": [("batch", k) for k in range(2, self.batches.bit_length() - 1)],
        }
        self.steps = [step for letter in order for step in bits[letter]]
        self.levels = len(self.steps)
        self.half = 1 << (self.levels - 1)
        if tall:
            ((small, big),) = parts
            self.rows = big.shape[1] // (self.batches * self.groups)
            self.widths = [small.shape[1]]
        else:
            self.rows = parts[0][0].shape[1] // self.groups
            self.widths = [big.shape[1] // self.batches for _, big in parts]
        self.cols = sum(self.widths)
        self.pieces = len(parts) * (1 + self.batches // 2)

    def fits(self):
        return self.rows % 128 == 0 and all(width % 128 == 0 for width in self.widths)

    def operands(self):
        return [array for part in self.parts for array in part]

    def flops(self):
        return sum(2 * small.size * big.shape[1] for small, big in self.parts)

    def operand_scratch(self):
        scratch = []
        for small, big in self.parts:
            scratch.append(pltpu.VMEM((2 * small.shape[0], small.shape[1]), jnp.bfloat16))
            scratch.append(pltpu.VMEM((2 * big.shape[0], big.shape[1] // 2), jnp.bfloat16))
        return scratch + [pltpu.SemaphoreType.DMA((self.pieces,))] * 3

    def step_of(self, level):
        return self.steps[self.levels - 1 - level]


def greet(peers):
    barrier = pltpu.get_barrier_semaphore()
    for peer in peers:
        pl.semaphore_signal(barrier, inc=1, device_id=peer, device_id_type=MESH)
    pl.semaphore_wait(barrier, len(peers))


def sibling_of(s, b):
    return (b + 1 - 2 * lax.rem(b, 2), s)


def partner_of(s, b, step):
    axis, bit = step
    if axis == "seq":
        return (b, flipped(s, [(bit, 1)]))
    return (flipped(b, [(bit, 1)]), s)


def swap_operands(job, inputs, held, s, b):
    core = lax.rem(b, 2)
    local, moves, lands = held[2 * len(job.parts) :]
    near, far = [], []

    def bring(own_source, own_place, far_source, far_place):
        n = len(near)
        near.append(pltpu.make_async_copy(own_source, own_place, local.at[n]))
        far.append(
            pltpu.make_async_remote_copy(
                src_ref=far_source,
                dst_ref=far_place,
                send_sem=moves.at[n],
                recv_sem=lands.at[n],
                device_id=sibling_of(s, b),
                device_id_type=MESH,
            )
        )
        far[-1].start()
        near[-1].start()

    for i in range(len(job.parts)):
        small_in, big_in = inputs[2 * i : 2 * i + 2]
        small, big = held[2 * i : 2 * i + 2]
        frames = small_in.shape[0]
        span = big_in.shape[1] // job.batches
        own_rows, far_rows = pl.ds(0, frames), pl.ds(frames, frames)
        bring(small_in, small.at[own_rows], small_in, small.at[far_rows])
        for z in range(job.batches // 2):
            here = pl.ds(pl.multiple_of((2 * z + core) * span, 128), span)
            there = pl.ds(pl.multiple_of((2 * z + 1 - core) * span, 128), span)
            inside = pl.ds(z * span, span)
            bring(
                big_in.at[:, here],
                big.at[own_rows, inside],
                big_in.at[:, there],
                big.at[far_rows, inside],
            )
    return near, far


def wait_operands(near, far):
    for copy in near:
        copy.wait()
    for copy in far:
        copy.wait_recv()


def block_product(job, held, part, place, s, b):
    small, big = held[2 * part : 2 * part + 2]
    span = big.shape[1] // (job.batches // 2)
    row = place_of(place, job.steps, "seq", s)
    col = place_of(place, job.steps, "batch", b) // 2
    if job.tall:
        left = big[:, pl.ds(pl.multiple_of(col * span + row * job.rows, 128), job.rows)]
        right = small[...]
    else:
        left = small[:, pl.ds(pl.multiple_of(row * job.rows, 128), job.rows)]
        right = big[:, pl.ds(pl.multiple_of(col * span, 128), span)]
    return lax.dot_general(
        left, right, (((0,), (0,)), ((), ())), preferred_element_type=jnp.float32
    )


def columns_of(job, part):
    start = sum(job.widths[:part])
    return slice(start, start + job.widths[part])


def first_kernel(job, *refs):
    count = 2 * len(job.parts)
    inputs, out, held = refs[:count], refs[count], refs[count + 1 :]
    s, b = lax.axis_index("seq"), lax.axis_index("batch")
    greet([sibling_of(s, b)])
    near, far = swap_operands(job, inputs, held, s, b)
    wait_operands(near, far)

    def one_place(j, carry):
        for part in range(len(job.parts)):
            total = block_product(job, held, part, job.half + j, s, b)
            out[j, :, columns_of(job, part)] = total.astype(jnp.bfloat16)
        return carry

    lax.fori_loop(0, job.half, one_place, 0)
    for copy in far:
        copy.wait_send()


def first_blocks(job, collective_id):
    operands = job.operands()
    return pl.pallas_call(
        functools.partial(first_kernel, job),
        out_shape=jax.ShapeDtypeStruct((job.half, job.rows, job.cols), jnp.bfloat16),
        in_specs=[pl.BlockSpec(memory_space=pl.ANY)] * len(operands),
        out_specs=pl.BlockSpec(memory_space=pltpu.VMEM),
        scratch_shapes=job.operand_scratch(),
        compiler_params=pltpu.CompilerParams(
            collective_id=collective_id, has_side_effects=True, vmem_limit_bytes=24 << 20
        ),
        cost_estimate=pl.CostEstimate(
            flops=job.flops() // 2, bytes_accessed=8 << 20, transcendentals=0
        ),
    )(*operands)


def send_first(job, collective_id):
    if job.fits():
        axis, bit = job.steps[0]
        pairs = [(i, i ^ (1 << bit)) for i in range(lax.axis_size(axis))]
        job.sent = first_blocks(job, collective_id)
        job.arrived = lax.ppermute(job.sent, axis, pairs)
    return job


def scatter_kernel(jobs, sequence, *refs):
    inputs, outs, scratch = [], [], []
    refs = list(refs)
    for job in jobs:
        take = 2 * len(job.parts) + (job.arrived is not None)
        inputs.append(refs[:take])
        refs = refs[take:]
    for job in jobs:
        outs.append(refs[: len(job.parts)])
        refs = refs[len(job.parts) :]
    for job in jobs:
        take = 2 * len(job.parts) + 3 + 5
        scratch.append((refs[: take - 5], *refs[take - 5 : take]))
        refs = refs[take:]
    s, b = lax.axis_index("seq"), lax.axis_index("batch")
    greet([sibling_of(s, b)] + [partner_of(s, b, step) for step in sorted(jobs[0].steps)])

    def slot_of(job, place):
        return lax.rem(place, job.half)

    def copy_of(i, place, level):
        job = jobs[i]
        _, sending, arrived, sends, recvs, _ = scratch[i]
        return pltpu.make_async_remote_copy(
            src_ref=sending.at[slot_of(job, place)],
            dst_ref=arrived.at[place - 1],
            send_sem=sends.at[slot_of(job, place)],
            recv_sem=recvs.at[place - 1],
            device_id=partner_of(s, b, job.step_of(level)),
            device_id_type=MESH,
        )

    def first_copy(i):
        job = jobs[i]
        return pltpu.make_async_copy(
            inputs[i][-1],
            scratch[i][2].at[pl.ds(job.half - 1, job.half)],
            scratch[i][5],
        )

    works = []
    for i, job in enumerate(jobs):
        works.append(swap_operands(job, inputs[i], scratch[i][0], s, b))
        if job.arrived is not None:
            first_copy(i).start()

    def block_sums(i, place, level):
        job = jobs[i]
        held, _, arrived = scratch[i][:3]
        for m in range(job.levels - 1, level, -1):
            if m < job.levels - 1 or job.arrived is None:
                copy_of(i, (1 << m) + place, m).wait_recv()
        totals = []
        for part in range(len(job.parts)):
            total = block_product(job, held, part, place, s, b)
            for m in range(job.levels - 1, level, -1):
                came = arrived[(1 << m) + place - 1, :, columns_of(job, part)]
                total = total + came.astype(jnp.float32)
            totals.append(total)
        return totals

    def send_block(i, place, level):
        job = jobs[i]
        sending = scratch[i][1]
        totals = block_sums(i, place, level)
        if level < job.levels - 1 and job.arrived is None:
            copy_of(i, place + job.half, job.levels - 1).wait_send()
        for part, total in enumerate(totals):
            sending[slot_of(job, place), :, columns_of(job, part)] = total.astype(jnp.bfloat16)
        copy_of(i, place, level).start()

    levels = jobs[0].levels
    ready = set()
    for i, level in sequence:
        job = jobs[i]
        if i not in ready:
            ready.add(i)
            wait_operands(*works[i])
            if job.arrived is not None:
                first_copy(i).wait()
        if level < 0:
            for part, total in enumerate(block_sums(i, 0, -1)):
                outs[i][part][...] = total
        elif level < levels - 1 or job.arrived is None:

            def one_place(j, carry, level=level, i=i):
                send_block(i, (2 << level) - 1 - j, level)
                return carry

            lax.fori_loop(0, 1 << level, one_place, 0)
    for i, job in enumerate(jobs):
        for copy in works[i][1]:
            copy.wait_send()
        if job.arrived is None:
            copy_of(i, job.half, levels - 1).wait_send()
        for level in range(levels - 1):

            def one_wait(j, carry, level=level, i=i):
                copy_of(i, (1 << level) + j, level).wait_send()
                return carry

            lax.fori_loop(0, 1 << level, one_wait, 0)


def scatter_sums(jobs, sequence, collective_id):
    if not all(job.fits() for job in jobs):
        return [
            [
                owned_sum(*((big, small) if job.tall else (small, big)), job.tall, job.tall)
                for small, big in job.parts
            ]
            for job in jobs
        ]
    scratch, operands, outs = [], [], []
    for job in jobs:
        block = (job.rows, job.cols)
        scratch += job.operand_scratch()
        scratch += [
            pltpu.VMEM((job.half, *block), jnp.bfloat16),
            pltpu.VMEM((2 * job.half - 1, *block), jnp.bfloat16),
            pltpu.SemaphoreType.DMA((job.half,)),
            pltpu.SemaphoreType.DMA((2 * job.half - 1,)),
            pltpu.SemaphoreType.DMA,
        ]
        operands += job.operands()
        if job.arrived is not None:
            operands.append(job.arrived)
        outs += [jax.ShapeDtypeStruct((job.rows, width), jnp.float32) for width in job.widths]
    results = list(
        pl.pallas_call(
            functools.partial(scatter_kernel, jobs, sequence),
            out_shape=outs,
            in_specs=[pl.BlockSpec(memory_space=pl.ANY)] * len(operands),
            out_specs=[pl.BlockSpec(memory_space=pltpu.VMEM)] * len(outs),
            scratch_shapes=scratch,
            compiler_params=pltpu.CompilerParams(
                collective_id=collective_id, has_side_effects=True, vmem_limit_bytes=60 << 20
            ),
            cost_estimate=pl.CostEstimate(
                flops=sum(job.flops() for job in jobs), bytes_accessed=400 << 20, transcendentals=0
            ),
        )(*operands)
    )
    return [[results.pop(0) for _ in job.parts] for job in jobs]


def shards(
    frames_in,
    cotangent,
    levels,
    lengths,
    token_mask,
    cond_table,
    norm_gains,
    w_ffn1_up,
    w_ffn1_down,
    w_qkv,
    w_out,
    w_glu,
    conv_kernel,
    bn_gain,
    batchnorm_shift_bias,
    w_conv_out,
    w_ffn2_up,
    w_ffn2_down,
    running_mean,
    running_var,
):
    frames = frames_in.shape[1]
    model_width = frames_in.shape[2]
    ff_width = w_ffn1_up.shape[1]
    groups = lax.axis_size("seq")
    batches = lax.axis_size("batch")
    seq_index = lax.axis_index("seq")
    item_index = lax.axis_index("batch")
    seq_length = frames * groups
    level_count = cond_table.shape[0] - 1
    cond_rows = cond_table.astype(jnp.float32)
    gain_rows = norm_gains.astype(jnp.float32)
    level_hot = (jnp.arange(level_count) == levels[0] - 1).astype(jnp.float32)
    level_vector = jnp.sum(level_hot[:, None] * cond_rows[:level_count], axis=0)
    mask_column = token_mask[0].astype(jnp.float32)[:, None]
    start_rows = (
        frames_in[0].astype(jnp.float32)
        + level_vector[None, :]
        + mask_column * cond_rows[level_count][None, :]
    )
    length = lax.dynamic_slice_in_dim(lengths, item_index, 1)[0]
    positions = seq_index * frames + jnp.arange(frames)
    unpadded_rows = (positions < length).astype(jnp.float32)[:, None]
    rows_one, ffn1_state = ffn_forward(start_rows, gain_rows[0], w_ffn1_up, w_ffn1_down)
    normed_attn, attn_pull = jax.vjp(layer_norm, rows_one, gain_rows[1])
    attn_in = normed_attn.astype(jnp.bfloat16)
    qkv_rows = jnp.dot(attn_in, w_qkv, preferred_element_type=jnp.float32)
    cosine, sine_table = rope_tables(positions, HD)
    whole_heads, attn_out = attend(qkv_rows, length, cosine, sine_table)
    rows_two = rows_one + jnp.dot(attn_out, w_out, preferred_element_type=jnp.float32)
    normed_conv, conv_pull = jax.vjp(layer_norm, rows_two, gain_rows[2])
    conv_in = normed_conv.astype(jnp.bfloat16)
    glu_pre = jnp.dot(conv_in, w_glu, preferred_element_type=jnp.float32)
    up_half = glu_pre[:, :model_width]
    glu_sig = jax.nn.sigmoid(glu_pre[:, model_width:])
    glu_low = (up_half * glu_sig * unpadded_rows).astype(jnp.bfloat16)
    taps = conv_kernel.shape[0]
    half_size = taps // 2
    kernel_rows = conv_kernel.astype(jnp.float32)
    padded = extended(glu_low, (("seq", 0),), half_size)
    convolved_rows = jnp.zeros((frames, model_width), jnp.float32)
    for tap_index in range(taps):
        convolved_rows = (
            convolved_rows + kernel_rows[tap_index] * padded[tap_index : tap_index + frames]
        )
    sum_rows = jnp.sum(convolved_rows * unpadded_rows, axis=0)
    sum_squares = jnp.sum(convolved_rows * convolved_rows * unpadded_rows, axis=0)
    totals = sum_everywhere(jnp.stack([sum_rows, sum_squares]), 1)
    total_sum, total_squares = totals[0], totals[1]
    count_of_frames = jnp.sum(lengths).astype(jnp.float32)
    batchnorm_frame_mean = total_sum / count_of_frames
    bn_var = total_squares / count_of_frames - batchnorm_frame_mean * batchnorm_frame_mean
    batchnorm_inverse_deviation = lax.rsqrt(bn_var + EPSILON)
    batchnorm_scale_factor = bn_gain.astype(jnp.float32)
    normalized_rows = (convolved_rows - batchnorm_frame_mean) * batchnorm_inverse_deviation
    batchnorm_input_rows = normalized_rows * batchnorm_scale_factor + batchnorm_shift_bias.astype(
        jnp.float32
    )
    bn_sig = jax.nn.sigmoid(batchnorm_input_rows)
    conv_act = (batchnorm_input_rows * bn_sig).astype(jnp.bfloat16)
    rows_three = rows_two + jnp.dot(conv_act, w_conv_out, preferred_element_type=jnp.float32)
    rows_four, ffn2_state = ffn_forward(rows_three, gain_rows[3], w_ffn2_up, w_ffn2_down)
    normed_out, out_pull = jax.vjp(layer_norm, rows_four, gain_rows[4])
    out_rows = normed_out.astype(jnp.bfloat16)
    grad_four, grad_gain_four = out_pull(cotangent[0].astype(jnp.float32))
    grad_three, grad_gain_three, ffn2_up_pair, ffn2_down_pair = ffn_backward(
        grad_four, ffn2_state, w_ffn2_up, w_ffn2_down
    )
    grad_r2 = grad_three.astype(jnp.bfloat16)
    batchnorm_gradient = (
        times_transposed(grad_r2, w_conv_out)
        * bn_sig
        * (1.0 + batchnorm_input_rows * (1.0 - bn_sig))
    )
    gradient_totals = sum_everywhere(
        jnp.stack(
            [
                jnp.sum(batchnorm_gradient, axis=0),
                jnp.sum(batchnorm_gradient * normalized_rows, axis=0),
            ]
        ),
        2,
    )
    gradient_sum_total, gradient_normalized_sum = gradient_totals[0], gradient_totals[1]
    grad_conv = (
        batchnorm_scale_factor
        * batchnorm_inverse_deviation
        * (
            batchnorm_gradient
            - unpadded_rows
            * (gradient_sum_total + normalized_rows * gradient_normalized_sum)
            / count_of_frames
        )
    ).astype(jnp.bfloat16)
    grad_pad = extended(grad_conv, (("seq", 0),), half_size)
    grad_glu = jnp.zeros((frames, model_width), jnp.float32)
    kernel_terms = []
    for tap_index in range(taps):
        offset = 2 * half_size - tap_index
        grad_glu = grad_glu + kernel_rows[tap_index] * grad_pad[offset : offset + frames]
        kernel_terms.append(
            jnp.einsum(
                "fd,fd->d",
                padded[tap_index : tap_index + frames],
                grad_conv,
                preferred_element_type=jnp.float32,
            )
        )
    kernel_grads = jnp.stack(kernel_terms, axis=0)
    grad_glu = grad_glu * unpadded_rows
    grad_gl = jnp.concatenate(
        [grad_glu * glu_sig, grad_glu * up_half * glu_sig * (1.0 - glu_sig)], axis=1
    ).astype(jnp.bfloat16)
    grad_conv_in, grad_gain_two = conv_pull(times_transposed(grad_gl, w_glu))
    grad_two = grad_three + grad_conv_in
    grad_r = grad_two.astype(jnp.bfloat16)
    grad_attn_out = times_transposed(grad_r, w_out).astype(jnp.bfloat16)
    cos_all, sin_all = rope_tables(jnp.arange(seq_length), HD)
    grad_qkv = attend_back(whole_heads, grad_attn_out, length, cos_all, sin_all)
    grad_attn_part, grad_gain_one = attn_pull(times_transposed(grad_qkv, w_qkv))
    grad_one = grad_two + grad_attn_part
    grad_zero, grad_gain_zero, ffn1_up_pair, ffn1_down_pair = ffn_backward(
        grad_one, ffn1_state, w_ffn1_up, w_ffn1_down
    )
    column_total = jnp.sum(grad_zero, axis=0)
    cond_grad_rows = jnp.concatenate(
        [
            level_hot[:, None] * column_total[None, :],
            jnp.sum(mask_column * grad_zero, axis=0)[None, :],
        ],
        axis=0,
    )
    gain_grads = jnp.stack(
        [grad_gain_zero, grad_gain_one, grad_gain_two, grad_gain_three, grad_gain_four], axis=0
    )
    jobs = [
        Job([ffn2_up_pair], False, "yx12"),
        Job([ffn2_down_pair[::-1]], True, "12xy"),
        Job([(conv_in, grad_gl), (attn_out, grad_r), (conv_act, grad_r2)], False, "xy12"),
        Job([(attn_in, grad_qkv)], False, "x12y"),
        Job([ffn1_down_pair[::-1]], True, "yx12"),
        Job([ffn1_up_pair], False, "yx12"),
    ]
    sums = scatter_sums(jobs, SEGMENTS, 7)
    small_rows = jnp.concatenate([gain_grads, cond_grad_rows, kernel_grads], axis=0)
    small_rows = jnp.pad(small_rows, ((0, -small_rows.shape[0] % 8), (0, 0)))
    small_piece = sum_everywhere(small_rows, 3, scatter=True)
    cond_end = 5 + level_count + 1
    new_mean = 0.9 * running_mean + 0.1 * batchnorm_frame_mean
    new_var = 0.9 * running_var + 0.1 * bn_var * count_of_frames / (count_of_frames - 1.0)
    return (
        out_rows[None],
        grad_zero.astype(jnp.bfloat16)[None],
        small_piece[5:cond_end],
        small_piece[0:5],
        sums[5][0],
        sums[4][0],
        sums[3][0],
        sums[2][1],
        sums[2][0],
        small_piece[cond_end : cond_end + taps],
        gradient_normalized_sum,
        gradient_sum_total,
        sums[2][2],
        sums[0][0],
        sums[1][0],
        new_mean,
        new_var,
    )


def solution(mesh):
    in_specs = (
        P("batch", "seq", None),
        P("batch", "seq", None),
        P("batch"),
        P(),
        P("batch", "seq"),
        P(),
        P(),
        P(),
        P(),
        P(),
        P(),
        P(),
        P(),
        P(),
        P(),
        P(),
        P(),
        P(),
        P(),
        P(),
    )
    out_specs = (
        P("batch", "seq", None),
        P("batch", "seq", None),
        P(None, "seq"),
        P(None, "seq"),
        P("seq", "batch"),
        P(("batch", "seq"), None),
        P("seq", "batch"),
        P("seq", "batch"),
        P("seq", "batch"),
        P(None, "seq"),
        P(),
        P(),
        P("seq", "batch"),
        P("seq", "batch"),
        P(("batch", "seq"), None),
        P(),
        P(),
    )
    return jax.shard_map(shards, mesh=mesh, in_specs=in_specs, out_specs=out_specs, check_vma=False)
```

```python
import functools
import math

import jax
import jax.numpy as jnp
from jax import lax
from jax.experimental import pallas as pl
from jax.experimental.pallas import tpu as pltpu
from jax.sharding import PartitionSpec as P

MESH = pl.DeviceIdType.MESH

HEADS = 16
HD = 64


EPSILON = 1e-05
MASKED_SCORE = -1000000000.0

SEGMENTS = (
    (0, 3), (1, 3), (2, 3), (2, 2), (0, 2), (1, 2), (5, 3), (2, 1), (4, 3), (0, 1), (3, 3),
    (0, 0), (5, 2), (3, 2), (0, -1), (3, 1), (5, 1), (5, 0), (4, 2), (2, 0), (4, 1), (1, 1),
    (3, 0), (4, 0), (1, 0), (5, -1), (2, -1), (4, -1), (3, -1), (1, -1),
)


def extended(array, sides, width):
    for axis, dim in sides:
        devices, length = (lax.axis_size(axis), array.shape[dim])
        up = [(i, (i + 1) % devices) for i in range(devices - 1)]
        down = [(j, i) for i, j in up]
        last = lax.slice_in_dim(array, length - width, length, axis=dim)
        leading = lax.slice_in_dim(array, 0, width, axis=dim)
        before = lax.ppermute(last, axis, up)
        after = lax.ppermute(leading, axis, down)
        array = jnp.concatenate([before, array, after], axis=dim)
    return array


def layer_norm(values, gain_row):
    centre = values - jnp.mean(values, axis=-1, keepdims=True)
    spread = jnp.mean(centre * centre, axis=-1, keepdims=True)
    return centre * lax.rsqrt(spread + EPSILON) * gain_row


def rope_tables(positions, head_size):
    half_size = head_size // 2
    inv_freqs = jnp.exp(
        jnp.arange(half_size).astype(jnp.float32) * (-2.0 * math.log(10000.0) / head_size)
    )
    angles = positions.astype(jnp.float32)[:, None] * inv_freqs[None, :]
    return (jnp.cos(angles), jnp.sin(angles))


def times_transposed(left_side, weight):
    return lax.dot_general(
        left_side, weight, (((1,), (1,)), ((), ())), preferred_element_type=jnp.float32
    )


def ffn_forward(values, gain_row, up_weight, down_weight):
    normed, ln_pull = jax.vjp(layer_norm, values, gain_row)
    lowered = normed.astype(jnp.bfloat16)
    hidden = jnp.dot(lowered, up_weight, preferred_element_type=jnp.float32)
    act_rows = (hidden * jax.nn.sigmoid(hidden)).astype(jnp.bfloat16)
    branch = jnp.dot(act_rows, down_weight, preferred_element_type=jnp.float32)
    return (values + 0.5 * branch, (ln_pull, lowered, hidden, act_rows))


def ffn_backward(grad_in, saved_state, up_weight, down_weight):
    ln_pull, lowered, hidden, act_rows = saved_state
    grad_branch = (0.5 * grad_in).astype(jnp.bfloat16)
    grad_act = times_transposed(grad_branch, down_weight)
    gate_sig = jax.nn.sigmoid(hidden)
    grad_hidden = (grad_act * gate_sig * (1.0 + hidden * (1.0 - gate_sig))).astype(jnp.bfloat16)
    grad_normed = times_transposed(grad_hidden, up_weight)
    grad_values, grad_gain = ln_pull(grad_normed)
    return (grad_in + grad_values, grad_gain, (lowered, grad_hidden), (act_rows, grad_branch))


def sum_peers(groups, batches, s, b):
    peers = [(b, lax.rem(s + k, groups)) for k in range(1, groups)]
    return peers + [(lax.rem(b + k, batches), s) for k in range(1, batches)]


def spread(pick, slots, mine, peers, span, sends, arrivals):
    slots[mine] = pick(mine)[...]
    copies = []
    for k in span:
        copies.append(
            pltpu.make_async_remote_copy(
                src_ref=pick(peers[k][1]),
                dst_ref=slots.at[mine],
                send_sem=sends.at[k],
                recv_sem=arrivals.at[k],
                device_id=peers[k],
                device_id_type=MESH,
            )
        )
        copies[-1].start()

    def finish():
        for copy in copies:
            copy.wait()
        total = slots[0]
        for i in range(1, len(copies) + 1):
            total = total + slots[i]
        return total

    return finish


def sum_kernel(groups, batches, rows_ref, total_ref, seq_slots, part, batch_slots, sends, arrivals):
    s, b = lax.axis_index("seq"), lax.axis_index("batch")
    peers = sum_peers(groups, batches, s, b)
    greet(peers)
    first = range(groups - 1)
    second = range(groups - 1, groups + batches - 2)
    part[...] = spread(lambda owner: rows_ref, seq_slots, s, peers, first, sends, arrivals)()
    total_ref[...] = spread(lambda owner: part, batch_slots, b, peers, second, sends, arrivals)()


def sum_scratch(height, width):
    groups, batches = lax.axis_size("seq"), lax.axis_size("batch")
    return [
        pltpu.VMEM((groups, height, width), jnp.float32),
        pltpu.VMEM((height, width), jnp.float32),
        pltpu.VMEM((batches, height, width), jnp.float32),
        pltpu.SemaphoreType.DMA((groups + batches - 2,)),
        pltpu.SemaphoreType.DMA((groups + batches - 2,)),
    ]


def sum_everywhere(rows, collective_id):
    groups, batches = lax.axis_size("seq"), lax.axis_size("batch")
    return pl.pallas_call(
        functools.partial(sum_kernel, groups, batches),
        out_shape=jax.ShapeDtypeStruct(rows.shape, jnp.float32),
        in_specs=[pl.BlockSpec(memory_space=pltpu.VMEM)],
        out_specs=pl.BlockSpec(memory_space=pltpu.VMEM),
        scratch_shapes=sum_scratch(*rows.shape),
        compiler_params=pltpu.CompilerParams(
            collective_id=collective_id, has_side_effects=True, vmem_limit_bytes=4 << 20
        ),
    )(rows)


def halving_steps(first_seq):
    seq_bits = [("seq", k) for k in range(lax.axis_size("seq").bit_length() - 1)]
    batch_bits = [("batch", k) for k in range(1, lax.axis_size("batch").bit_length() - 1)]
    if first_seq:
        seq_bits = seq_bits[::-1]
    return [("batch", 0)] + seq_bits + batch_bits


def relative_place(place, steps, axis):
    flips = 0
    for order, (name, bit) in enumerate(steps):
        if name == axis:
            flips = flips | (((place >> (len(steps) - 1 - order)) & 1) << bit)
    return flips


def product_kernel(steps, tall, rows, cols, group, where, left_ref, right_ref, out_ref):
    step = pl.program_id(0)
    for inner in range(group):
        place = step * group + inner
        b = where[0] ^ relative_place(place, steps, "batch")
        s = where[1] ^ relative_place(place, steps, "seq")
        if tall:
            left = left_ref[:, pl.ds(pl.multiple_of((b * lax.axis_size("seq") + s) * rows, rows), rows)]
            right = right_ref[...]
        else:
            left = left_ref[:, pl.ds(pl.multiple_of(s * rows, rows), rows)]
            right = right_ref[:, pl.ds(pl.multiple_of(b * cols, cols), cols)]
        out_ref[inner] = lax.dot_general(
            left, right, (((0,), (0,)), ((), ())), preferred_element_type=jnp.float32
        ).astype(jnp.bfloat16)


def block_products(left, right, tall, steps):
    batches, groups = lax.axis_size("batch"), lax.axis_size("seq")
    places = batches * groups
    if tall:
        rows, cols = left.shape[1] // places, right.shape[1]
    else:
        rows, cols = left.shape[1] // groups, right.shape[1] // batches
    me = jnp.stack([lax.axis_index("batch"), lax.axis_index("seq")]).astype(jnp.int32)
    if rows % 128 == 0 and cols % 128 == 0:
        group = 4
        return pl.pallas_call(
            functools.partial(product_kernel, steps, tall, rows, cols, group),
            out_shape=jax.ShapeDtypeStruct((places, rows, cols), jnp.bfloat16),
            grid_spec=pltpu.PrefetchScalarGridSpec(
                num_scalar_prefetch=1,
                grid=(places // group,),
                in_specs=[
                    pl.BlockSpec(left.shape, lambda i, where: (0, 0)),
                    pl.BlockSpec(right.shape, lambda i, where: (0, 0)),
                ],
                out_specs=pl.BlockSpec((group, rows, cols), lambda i, where: (i, 0, 0)),
            ),
            compiler_params=pltpu.CompilerParams(vmem_limit_bytes=40 << 20),
            cost_estimate=pl.CostEstimate(
                flops=2 * left.shape[0] * left.shape[1] * right.shape[1],
                bytes_accessed=2 * (left.size + right.size + left.shape[1] * right.shape[1]),
                transcendentals=0,
            ),
        )(me, left, right)
    whole = lax.dot_general(
        left, right, (((0,), (0,)), ((), ())), preferred_element_type=jnp.float32
    ).astype(jnp.bfloat16)
    if tall:
        blocks = whole.reshape(batches, groups, rows, cols)
    else:
        blocks = whole.reshape(groups, rows, batches, cols).transpose(2, 0, 1, 3)
    batch_bits, seq_bits = batches.bit_length() - 1, groups.bit_length() - 1
    blocks = blocks.reshape((2,) * (batch_bits + seq_bits) + (rows, cols))
    dims = []
    for name, bit in steps:
        dim = batch_bits - 1 - bit if name == "batch" else batch_bits + seq_bits - 1 - bit
        mine = (me[0] if name == "batch" else me[1]) >> bit & 1
        blocks = jnp.where(mine == 1, jnp.flip(blocks, dim), blocks)
        dims.append(dim)
    return blocks.transpose(*dims, len(dims), len(dims) + 1).reshape(places, rows, cols)


def owned_sum(left, right, tall, first_seq):
    steps = halving_steps(first_seq)
    blocks = block_products(left, right, tall, steps)
    for axis, bit in steps:
        half = blocks.shape[0] // 2
        pairs = [(i, i ^ (1 << bit)) for i in range(lax.axis_size(axis))]
        arrived = lax.ppermute(blocks[half:], axis, pairs)
        total = blocks[:half].astype(jnp.float32) + arrived.astype(jnp.float32)
        blocks = total.astype(jnp.bfloat16) if half > 1 else total
    return blocks[0]


def attend_kernel(
    groups, heads, length_ref, qkv_ref, cos_ref, sin_ref, whole_ref, out_ref,
    stage, result, sends, arrivals, out_sends, out_arrivals, own_sem,
):
    s, b = lax.axis_index("seq"), lax.axis_index("batch")
    frames = qkv_ref.shape[0]
    total_frames = whole_ref.shape[0]
    block = heads * 3 * HD
    width = heads * HD
    parts = stage.shape[0]
    span, narrow = block // parts, width // parts
    greet_seq(groups, s, b)

    def rows_of(place):
        return pl.ds(pl.multiple_of(place * frames, frames), frames)

    def heads_copy(target, sender, part):
        return pltpu.make_async_remote_copy(
            src_ref=stage.at[part, target],
            dst_ref=whole_ref.at[rows_of(sender), pl.ds(part * span, span)],
            send_sem=sends.at[part, target],
            recv_sem=arrivals.at[part, sender],
            device_id=(b, target),
            device_id_type=MESH,
        )

    columns = range(0, groups * block, 128)
    for column in sorted(columns, key=lambda c: (c % block // span if parts > 1 else 0, c)):
        pattern = (column // 128) % 3
        values = qkv_ref[:, column : column + 128]
        turned = (values * cos_ref[pattern] + partner_lanes(values) * sin_ref[pattern]).astype(
            jnp.bfloat16
        )
        start = column
        while start < column + 128:
            place, part = start // block, start % block // span
            first = place * block + part * span
            end = min(column + 128, first + span)
            stage[part, place, :, start - first : end - first] = turned[
                :, start - column : end - column
            ]
            if end == first + span:

                @pl.when(s != place)
                def _():
                    heads_copy(place, s, part).start()

                @pl.when(s == place)
                def _():
                    whole_ref[rows_of(s), part * span : (part + 1) * span] = stage[part, place]

            start = end

    valid = lax.broadcasted_iota(jnp.int32, (1, total_frames), 1) < length_ref[0]

    def out_place(owner, part):
        if narrow % 128 == 0:
            start = pl.multiple_of(owner * width + part * narrow, 128)
            return out_ref.at[:, pl.ds(start, narrow)]
        return out_ref.at[owner]

    def result_copy(target, sender, part):
        return pltpu.make_async_remote_copy(
            src_ref=result.at[part, target],
            dst_ref=out_place(sender, part),
            send_sem=out_sends.at[part, target],
            recv_sem=out_arrivals.at[part, sender],
            device_id=(b, target),
            device_id_type=MESH,
        )

    owns = []
    for part in range(parts):
        for k in range(1, groups):
            heads_copy(s, lax.rem(s + k, groups), part).wait_recv()

        def one_block(k, carry, part=part):
            place = lax.rem(s + k, groups)
            for h in range(heads // parts):
                base = part * span + h * 3 * HD
                query = whole_ref[rows_of(place), base : base + HD]
                key = whole_ref[:, base + HD : base + 2 * HD]
                value = whole_ref[:, base + 2 * HD : base + 3 * HD]
                scores = times_transposed(query, key)
                scores = jnp.where(valid, scores, MASKED_SCORE)
                exp_scores = jnp.exp(scores - jnp.max(scores, axis=-1, keepdims=True))
                share = 1.0 / jnp.sum(exp_scores, axis=-1, keepdims=True)
                probs = (exp_scores * share).astype(jnp.bfloat16)
                mixed = jnp.dot(probs, value, preferred_element_type=jnp.float32)
                result[part, place, :, h * HD : (h + 1) * HD] = mixed.astype(jnp.bfloat16)

            @pl.when(k < groups)
            def _():
                result_copy(place, s, part).start()

            return carry

        lax.fori_loop(1, groups + 1, one_block, 0)
        owns.append(pltpu.make_async_copy(result.at[part, s], out_place(s, part), own_sem.at[part]))
        owns[-1].start()
    for part in range(parts):
        for k in range(1, groups):
            other = lax.rem(s + k, groups)
            heads_copy(other, s, part).wait_send()
            result_copy(other, s, part).wait_send()
            result_copy(s, other, part).wait_recv()
    for own in owns:
        own.wait()


def greet_seq(groups, s, b):
    greet([(b, lax.rem(s + k, groups)) for k in range(1, groups)])


def partner_lanes(values):
    lanes = lax.broadcasted_iota(jnp.int32, values.shape, 1)
    return jnp.where(
        lanes % HD < HD // 2,
        pltpu.roll(values, 128 - HD // 2, 1),
        pltpu.roll(values, HD // 2, 1),
    )


def attend(qkv_rows, length, cosine, sine):
    groups = lax.axis_size("seq")
    frames = qkv_rows.shape[0]
    heads = HEADS // groups
    width = heads * HD
    signs = jnp.where(jnp.arange(HD) < HD // 2, -1.0, 1.0)
    cos_head = jnp.concatenate([cosine, cosine], axis=1)
    sin_head = jnp.concatenate([sine, sine], axis=1) * signs
    ones, zeros = jnp.ones_like(cos_head), jnp.zeros_like(cos_head)
    cos_pair = jnp.concatenate([cos_head * 0.125, cos_head, ones] * 2, axis=1)
    sin_pair = jnp.concatenate([sin_head * 0.125, sin_head, zeros] * 2, axis=1)
    cos_three = jnp.stack([cos_pair[:, 128 * i : 128 * (i + 1)] for i in range(3)])
    sin_three = jnp.stack([sin_pair[:, 128 * i : 128 * (i + 1)] for i in range(3)])
    parts = heads // 2 if heads % 2 == 0 else 1
    direct = width // parts % 128 == 0
    out_shape = (frames, groups * width) if direct else (groups, frames, width)
    total = frames * groups
    vmem = pl.BlockSpec(memory_space=pltpu.VMEM)
    whole, out = pl.pallas_call(
        functools.partial(attend_kernel, groups, heads),
        out_shape=(
            jax.ShapeDtypeStruct((total, 3 * width), jnp.bfloat16),
            jax.ShapeDtypeStruct(out_shape, jnp.bfloat16),
        ),
        in_specs=[pl.BlockSpec(memory_space=pltpu.SMEM), vmem, vmem, vmem],
        out_specs=(vmem, pl.BlockSpec(memory_space=pl.ANY)),
        scratch_shapes=[
            pltpu.VMEM((parts, groups, frames, 3 * width // parts), jnp.bfloat16),
            pltpu.VMEM((parts, groups, frames, width // parts), jnp.bfloat16),
            pltpu.SemaphoreType.DMA((parts, groups)),
            pltpu.SemaphoreType.DMA((parts, groups)),
            pltpu.SemaphoreType.DMA((parts, groups)),
            pltpu.SemaphoreType.DMA((parts, groups)),
            pltpu.SemaphoreType.DMA((parts,)),
        ],
        compiler_params=pltpu.CompilerParams(
            collective_id=4, has_side_effects=True, vmem_limit_bytes=20 << 20
        ),
        cost_estimate=pl.CostEstimate(
            flops=4 * heads * HD * total * total,
            bytes_accessed=4 * qkv_rows.size + 2 * total * 4 * width,
            transcendentals=heads * total * total,
        ),
    )(length.reshape(1), qkv_rows, cos_three, sin_three)
    if not direct:
        out = out.transpose(1, 0, 2).reshape(frames, groups * width)
    return whole, out


def attend_back_kernel(
    groups, heads, length_ref, whole_ref, grad_ref, cos_ref, sin_ref, out_ref,
    stage, grads, result, query_key, value_total, sends, arrivals, out_sends, out_arrivals, own_sem,
):
    s, b = lax.axis_index("seq"), lax.axis_index("batch")
    frames = grad_ref.shape[0]
    total_frames = whole_ref.shape[0]
    block = heads * 3 * HD
    width = heads * HD
    greet_seq(groups, s, b)

    def rows_of(place):
        return pl.ds(pl.multiple_of(place * frames, frames), frames)

    def grad_copy(target, sender):
        return pltpu.make_async_remote_copy(
            src_ref=stage.at[target],
            dst_ref=grads.at[rows_of(sender)],
            send_sem=sends.at[target],
            recv_sem=arrivals.at[sender],
            device_id=(b, target),
            device_id_type=MESH,
        )

    for place in range(groups):
        stage[place] = grad_ref[:, place * width : (place + 1) * width]

        @pl.when(s != place)
        def _():
            grad_copy(place, s).start()

        @pl.when(s == place)
        def _():
            grads[rows_of(s), :] = stage[place]

    part_heads = 2 if heads % 2 == 0 else heads
    parts = heads // part_heads
    span = part_heads * 3 * HD

    def out_place(owner, part):
        if block % 128 == 0:
            start = pl.multiple_of(owner * block + part * span, 128)
            return out_ref.at[:, pl.ds(start, span)]
        return out_ref.at[owner, :, pl.ds(part * span, span)]

    def result_copy(target, sender, part):
        return pltpu.make_async_remote_copy(
            src_ref=result.at[part, rows_of(target)],
            dst_ref=out_place(sender, part),
            send_sem=out_sends.at[part, target],
            recv_sem=out_arrivals.at[part, sender],
            device_id=(b, target),
            device_id_type=MESH,
        )

    valid = lax.broadcasted_iota(jnp.int32, (total_frames, 1), 0) < length_ref[0]
    for h in range(heads):
        base = h * 3 * HD
        key = whole_ref[:, base + HD : base + 2 * HD]
        key_turned = key.T
        value = whole_ref[:, base + 2 * HD : base + 3 * HD]
        query_key[...] = jnp.zeros_like(query_key)
        value_total[...] = jnp.zeros_like(value_total)

        def one_block(k, carry, h=h, base=base, key=key, key_turned=key_turned, value=value):
            place = lax.rem(s + k, groups)
            if h == 0:

                @pl.when(k > 0)
                def _():
                    grad_copy(s, place).wait_recv()

            query = whole_ref[rows_of(place), base : base + HD]
            grad = grads[rows_of(place), h * HD : (h + 1) * HD]
            scores = jnp.where(valid, times_transposed(key, query), MASKED_SCORE)
            exp_scores = jnp.exp(scores - jnp.max(scores, axis=0, keepdims=True))
            probs = exp_scores * (1.0 / jnp.sum(exp_scores, axis=0, keepdims=True))
            value_total[...] += jnp.dot(
                probs.astype(jnp.bfloat16), grad, preferred_element_type=jnp.float32
            )
            grad_probs = times_transposed(value, grad)
            mean = jnp.sum(probs * grad_probs, axis=0, keepdims=True)
            grad_scores = (probs * (grad_probs - mean)).astype(jnp.bfloat16)
            query_key[:, HD:] += jnp.dot(grad_scores, query, preferred_element_type=jnp.float32)
            query_key[rows_of(place), :HD] = jnp.dot(
                key_turned, grad_scores, preferred_element_type=jnp.float32
            ).T
            return carry

        lax.fori_loop(0, groups, one_block, 0)
        part, inside = h // part_heads, (h % part_heads) * 3 * HD
        both = query_key[...]
        turned = both * cos_ref[...] + partner_lanes(both) * sin_ref[...]
        result[part, :, inside : inside + 2 * HD] = turned.astype(jnp.bfloat16)
        result[part, :, inside + 2 * HD : inside + 3 * HD] = value_total[...].astype(jnp.bfloat16)
        if (h + 1) % part_heads == 0:
            for k in range(1, groups):
                result_copy(lax.rem(s + k, groups), s, part).start()
    owns = []
    for part in range(parts):
        owns.append(
            pltpu.make_async_copy(
                result.at[part, rows_of(s)], out_place(s, part), own_sem.at[part]
            )
        )
        owns[-1].start()
    for k in range(1, groups):
        other = lax.rem(s + k, groups)
        grad_copy(other, s).wait_send()
        for part in range(parts):
            result_copy(other, s, part).wait_send()
            result_copy(s, other, part).wait_recv()
    for own in owns:
        own.wait()


def attend_back(whole, grad_attn, length, cosine, sine):
    groups = lax.axis_size("seq")
    frames = grad_attn.shape[0]
    heads = HEADS // groups
    width = heads * HD
    block = 3 * width
    total = frames * groups
    signs = jnp.where(jnp.arange(HD) < HD // 2, 1.0, -1.0)
    cos_head = jnp.concatenate([cosine, cosine], axis=1)
    sin_head = jnp.concatenate([sine, sine], axis=1) * signs
    cos_both = jnp.concatenate([cos_head * 0.125, cos_head], axis=1)
    sin_both = jnp.concatenate([sin_head * 0.125, sin_head], axis=1)
    part_heads = 2 if heads % 2 == 0 else heads
    parts = heads // part_heads
    direct = block % 128 == 0
    out_shape = (frames, groups * block) if direct else (groups, frames, block)
    vmem = pl.BlockSpec(memory_space=pltpu.VMEM)
    out = pl.pallas_call(
        functools.partial(attend_back_kernel, groups, heads),
        out_shape=jax.ShapeDtypeStruct(out_shape, jnp.bfloat16),
        in_specs=[pl.BlockSpec(memory_space=pltpu.SMEM), vmem, vmem, vmem, vmem],
        out_specs=pl.BlockSpec(memory_space=pl.ANY),
        scratch_shapes=[
            pltpu.VMEM((groups, frames, width), jnp.bfloat16),
            pltpu.VMEM((total, width), jnp.bfloat16),
            pltpu.VMEM((parts, total, part_heads * 3 * HD), jnp.bfloat16),
            pltpu.VMEM((total, 2 * HD), jnp.float32),
            pltpu.VMEM((total, HD), jnp.float32),
            pltpu.SemaphoreType.DMA((groups,)),
            pltpu.SemaphoreType.DMA((groups,)),
            pltpu.SemaphoreType.DMA((parts, groups)),
            pltpu.SemaphoreType.DMA((parts, groups)),
            pltpu.SemaphoreType.DMA((parts,)),
        ],
        compiler_params=pltpu.CompilerParams(
            collective_id=5, has_side_effects=True, vmem_limit_bytes=24 << 20
        ),
        cost_estimate=pl.CostEstimate(
            flops=10 * heads * HD * total * total,
            bytes_accessed=2 * total * 8 * width,
            transcendentals=heads * total * total,
        ),
    )(length.reshape(1), whole, grad_attn, cos_both, sin_both)
    if not direct:
        out = out.transpose(1, 0, 2).reshape(frames, groups * block)
    return out


def flipped(index, places):
    for bit, flip in places:
        mine = lax.rem(index // (1 << bit), 2)
        index = index + flip * (1 - 2 * mine) * (1 << bit)
    return index


def place_of(place, steps, axis, index):
    flips = []
    for order, (name, bit) in enumerate(steps):
        if name == axis:
            flips.append((bit, lax.rem(place // (1 << (len(steps) - 1 - order)), 2)))
    return flipped(index, flips)


class Job:
    def __init__(self, parts, tall, order):
        self.parts, self.tall = parts, tall
        self.batches, self.groups = lax.axis_size("batch"), lax.axis_size("seq")
        bits = {
            "x": [("seq", 0)],
            "y": [("seq", k) for k in range(1, self.groups.bit_length() - 1)],
            "1": [("batch", 1)],
            "2": [("batch", k) for k in range(2, self.batches.bit_length() - 1)],
        }
        self.steps = [step for letter in order for step in bits[letter]]
        self.levels = len(self.steps)
        self.half = 1 << (self.levels - 1)
        if tall:
            ((small, big),) = parts
            self.rows = big.shape[1] // (self.batches * self.groups)
            self.widths = [small.shape[1]]
        else:
            self.rows = parts[0][0].shape[1] // self.groups
            self.widths = [big.shape[1] // self.batches for _, big in parts]
        self.cols = sum(self.widths)
        self.pieces = len(parts) * (1 + self.batches // 2)

    def fits(self):
        return self.rows % 128 == 0 and all(width % 128 == 0 for width in self.widths)

    def operands(self):
        return [array for part in self.parts for array in part]

    def flops(self):
        return sum(2 * small.size * big.shape[1] for small, big in self.parts)

    def operand_scratch(self):
        scratch = []
        for small, big in self.parts:
            scratch.append(pltpu.VMEM((2 * small.shape[0], small.shape[1]), jnp.bfloat16))
            scratch.append(pltpu.VMEM((2 * big.shape[0], big.shape[1] // 2), jnp.bfloat16))
        return scratch + [pltpu.SemaphoreType.DMA((self.pieces,))] * 3

    def step_of(self, level):
        return self.steps[self.levels - 1 - level]


def greet(peers):
    barrier = pltpu.get_barrier_semaphore()
    for peer in peers:
        pl.semaphore_signal(barrier, inc=1, device_id=peer, device_id_type=MESH)
    pl.semaphore_wait(barrier, len(peers))


def sibling_of(s, b):
    return (b + 1 - 2 * lax.rem(b, 2), s)


def partner_of(s, b, step):
    axis, bit = step
    if axis == "seq":
        return (b, flipped(s, [(bit, 1)]))
    return (flipped(b, [(bit, 1)]), s)


def swap_operands(job, inputs, held, s, b):
    core = lax.rem(b, 2)
    local, moves, lands = held[2 * len(job.parts) :]
    near, far = [], []

    def bring(own_source, own_place, far_source, far_place):
        n = len(near)
        near.append(pltpu.make_async_copy(own_source, own_place, local.at[n]))
        far.append(
            pltpu.make_async_remote_copy(
                src_ref=far_source,
                dst_ref=far_place,
                send_sem=moves.at[n],
                recv_sem=lands.at[n],
                device_id=sibling_of(s, b),
                device_id_type=MESH,
            )
        )
        far[-1].start()
        near[-1].start()

    for i in range(len(job.parts)):
        small_in, big_in = inputs[2 * i : 2 * i + 2]
        small, big = held[2 * i : 2 * i + 2]
        frames = small_in.shape[0]
        span = big_in.shape[1] // job.batches
        own_rows, far_rows = pl.ds(0, frames), pl.ds(frames, frames)
        bring(small_in, small.at[own_rows], small_in, small.at[far_rows])
        for z in range(job.batches // 2):
            here = pl.ds(pl.multiple_of((2 * z + core) * span, 128), span)
            there = pl.ds(pl.multiple_of((2 * z + 1 - core) * span, 128), span)
            inside = pl.ds(z * span, span)
            bring(
                big_in.at[:, here],
                big.at[own_rows, inside],
                big_in.at[:, there],
                big.at[far_rows, inside],
            )
    return near, far


def wait_operands(near, far):
    for copy in near:
        copy.wait()
    for copy in far:
        copy.wait_recv()


def block_product(job, held, part, place, s, b):
    small, big = held[2 * part : 2 * part + 2]
    span = big.shape[1] // (job.batches // 2)
    row = place_of(place, job.steps, "seq", s)
    col = place_of(place, job.steps, "batch", b) // 2
    if job.tall:
        left = big[:, pl.ds(pl.multiple_of(col * span + row * job.rows, 128), job.rows)]
        right = small[...]
    else:
        left = small[:, pl.ds(pl.multiple_of(row * job.rows, 128), job.rows)]
        right = big[:, pl.ds(pl.multiple_of(col * span, 128), span)]
    return lax.dot_general(
        left, right, (((0,), (0,)), ((), ())), preferred_element_type=jnp.float32
    )


def columns_of(job, part):
    start = sum(job.widths[:part])
    return slice(start, start + job.widths[part])


def scatter_kernel(jobs, sequence, *refs):
    refs = list(refs)

    def take(count):
        taken = refs[:count]
        del refs[:count]
        return taken

    inputs = [take(2 * len(job.parts)) for job in jobs]
    (rows_ref,) = take(1)
    outs = [take(len(job.parts)) for job in jobs]
    (small_total,) = take(1)
    scratch = [(take(2 * len(job.parts) + 3), *take(4)) for job in jobs]
    seq_slots, part_sum, batch_slots, small_sends, small_arrivals = take(5)
    batches, groups = jobs[0].batches, jobs[0].groups
    s, b = lax.axis_index("seq"), lax.axis_index("batch")
    peers = sum_peers(groups, batches, s, b)
    greet(peers)

    def slot_of(job, place):
        return lax.rem(place, job.half)

    def copy_of(i, place, level):
        job = jobs[i]
        _, sending, arrived, sends, recvs = scratch[i]
        return pltpu.make_async_remote_copy(
            src_ref=sending.at[slot_of(job, place)],
            dst_ref=arrived.at[place - 1],
            send_sem=sends.at[slot_of(job, place)],
            recv_sem=recvs.at[place - 1],
            device_id=partner_of(s, b, job.step_of(level)),
            device_id_type=MESH,
        )

    works = [swap_operands(job, inputs[i], scratch[i][0], s, b) for i, job in enumerate(jobs)]

    def columns(owner):
        width = part_sum.shape[1]
        return rows_ref.at[:, pl.ds(pl.multiple_of(owner * width, 128), width)]

    over_seq = spread(
        columns, seq_slots, s, peers, range(groups - 1), small_sends, small_arrivals
    )

    def block_sums(i, place, level):
        job = jobs[i]
        held, _, arrived = scratch[i][:3]
        for m in range(job.levels - 1, level, -1):
            copy_of(i, (1 << m) + place, m).wait_recv()
        totals = []
        for part in range(len(job.parts)):
            total = block_product(job, held, part, place, s, b)
            for m in range(job.levels - 1, level, -1):
                came = arrived[(1 << m) + place - 1, :, columns_of(job, part)]
                total = total + came.astype(jnp.float32)
            totals.append(total)
        return totals

    def send_block(i, place, level):
        job = jobs[i]
        totals = block_sums(i, place, level)
        if level < job.levels - 1:
            copy_of(i, place + job.half, job.levels - 1).wait_send()
        for part, total in enumerate(totals):
            scratch[i][1][slot_of(job, place), :, columns_of(job, part)] = total.astype(jnp.bfloat16)
        copy_of(i, place, level).start()

    levels = jobs[0].levels
    ready = set()
    over_batch = None
    for i, level in sequence:
        job = jobs[i]
        if i not in ready:
            ready.add(i)
            wait_operands(*works[i])
        if level < 0:
            for part, total in enumerate(block_sums(i, 0, -1)):
                outs[i][part][...] = total
            continue

        def one_place(j, carry, level=level, i=i):
            send_block(i, (2 << level) - 1 - j, level)
            return carry

        lax.fori_loop(0, 1 << level, one_place, 0)
        if over_batch is None:
            part_sum[...] = over_seq()
            over_batch = spread(
                lambda owner: part_sum,
                batch_slots,
                b,
                peers,
                range(groups - 1, groups + batches - 2),
                small_sends,
                small_arrivals,
            )
    small_total[...] = over_batch()
    for i, job in enumerate(jobs):
        for copy in works[i][1]:
            copy.wait_send()
        copy_of(i, job.half, levels - 1).wait_send()
        for level in range(levels - 1):

            def one_wait(j, carry, level=level, i=i):
                copy_of(i, (1 << level) + j, level).wait_send()
                return carry

            lax.fori_loop(0, 1 << level, one_wait, 0)


def pass_kernel(count, *refs):
    for source, target in zip(refs[:count], refs[count:]):
        target[...] = source[...]


def scatter_sums(jobs, sequence, rows, collective_id):
    height, width = rows.shape
    width = width // jobs[0].groups
    if width % 128 or not all(job.fits() for job in jobs):
        total = sum_everywhere(rows, collective_id)
        share = lax.dynamic_slice_in_dim(total, lax.axis_index("seq") * width, width, axis=1)
        sums = [
            [
                owned_sum(*((big, small) if job.tall else (small, big)), job.tall, job.tall)
                for small, big in job.parts
            ]
            for job in jobs
        ]
        return sums, share
    scratch, operands, outs = [], [], []
    for job in jobs:
        block = (job.rows, job.cols)
        scratch += job.operand_scratch()
        scratch += [
            pltpu.VMEM((job.half, *block), jnp.bfloat16),
            pltpu.VMEM((2 * job.half - 1, *block), jnp.bfloat16),
            pltpu.SemaphoreType.DMA((job.half,)),
            pltpu.SemaphoreType.DMA((2 * job.half - 1,)),
        ]
        operands += job.operands()
        outs += [jax.ShapeDtypeStruct((job.rows, width), jnp.float32) for width in job.widths]
    vmem = pl.BlockSpec(memory_space=pltpu.VMEM)
    *results, share = pl.pallas_call(
        functools.partial(scatter_kernel, jobs, sequence),
        out_shape=[*outs, jax.ShapeDtypeStruct((height, width), jnp.float32)],
        in_specs=[pl.BlockSpec(memory_space=pl.ANY)] * len(operands) + [vmem],
        out_specs=[vmem] * (len(outs) + 1),
        scratch_shapes=scratch + sum_scratch(height, width),
        compiler_params=pltpu.CompilerParams(
            collective_id=collective_id, has_side_effects=True, vmem_limit_bytes=60 << 20
        ),
        cost_estimate=pl.CostEstimate(
            flops=sum(job.flops() for job in jobs), bytes_accessed=400 << 20, transcendentals=0
        ),
    )(*operands, rows)
    passes = 4
    specs = [pl.BlockSpec((out.shape[0] // passes, out.shape[1]), lambda i: (i, 0)) for out in outs]
    results = list(
        pl.pallas_call(
            functools.partial(pass_kernel, len(outs)),
            out_shape=outs,
            grid=(passes,),
            in_specs=specs,
            out_specs=specs,
            compiler_params=pltpu.CompilerParams(vmem_limit_bytes=60 << 20),
        )(*results)
    )
    return [[results.pop(0) for _ in job.parts] for job in jobs], share


def shards(
    frames_in,
    cotangent,
    levels,
    lengths,
    token_mask,
    cond_table,
    norm_gains,
    w_ffn1_up,
    w_ffn1_down,
    w_qkv,
    w_out,
    w_glu,
    conv_kernel,
    bn_gain,
    batchnorm_shift_bias,
    w_conv_out,
    w_ffn2_up,
    w_ffn2_down,
    running_mean,
    running_var,
):
    frames = frames_in.shape[1]
    model_width = frames_in.shape[2]
    ff_width = w_ffn1_up.shape[1]
    groups = lax.axis_size("seq")
    batches = lax.axis_size("batch")
    seq_index = lax.axis_index("seq")
    item_index = lax.axis_index("batch")
    seq_length = frames * groups
    level_count = cond_table.shape[0] - 1
    cond_rows = cond_table.astype(jnp.float32)
    gain_rows = norm_gains.astype(jnp.float32)
    level_hot = (jnp.arange(level_count) == levels[0] - 1).astype(jnp.float32)
    level_vector = jnp.sum(level_hot[:, None] * cond_rows[:level_count], axis=0)
    mask_column = token_mask[0].astype(jnp.float32)[:, None]
    start_rows = (
        frames_in[0].astype(jnp.float32)
        + level_vector[None, :]
        + mask_column * cond_rows[level_count][None, :]
    )
    length = lax.dynamic_slice_in_dim(lengths, item_index, 1)[0]
    positions = seq_index * frames + jnp.arange(frames)
    unpadded_rows = (positions < length).astype(jnp.float32)[:, None]
    rows_one, ffn1_state = ffn_forward(start_rows, gain_rows[0], w_ffn1_up, w_ffn1_down)
    normed_attn, attn_pull = jax.vjp(layer_norm, rows_one, gain_rows[1])
    attn_in = normed_attn.astype(jnp.bfloat16)
    qkv_rows = jnp.dot(attn_in, w_qkv, preferred_element_type=jnp.float32)
    cosine, sine_table = rope_tables(positions, HD)
    whole_heads, attn_out = attend(qkv_rows, length, cosine, sine_table)
    rows_two = rows_one + jnp.dot(attn_out, w_out, preferred_element_type=jnp.float32)
    normed_conv, conv_pull = jax.vjp(layer_norm, rows_two, gain_rows[2])
    conv_in = normed_conv.astype(jnp.bfloat16)
    glu_pre = jnp.dot(conv_in, w_glu, preferred_element_type=jnp.float32)
    up_half = glu_pre[:, :model_width]
    glu_sig = jax.nn.sigmoid(glu_pre[:, model_width:])
    glu_low = (up_half * glu_sig * unpadded_rows).astype(jnp.bfloat16)
    taps = conv_kernel.shape[0]
    half_size = taps // 2
    kernel_rows = conv_kernel.astype(jnp.float32)
    padded = extended(glu_low, (("seq", 0),), half_size)
    convolved_rows = jnp.zeros((frames, model_width), jnp.float32)
    for tap_index in range(taps):
        convolved_rows = (
            convolved_rows + kernel_rows[tap_index] * padded[tap_index : tap_index + frames]
        )
    sum_rows = jnp.sum(convolved_rows * unpadded_rows, axis=0)
    sum_squares = jnp.sum(convolved_rows * convolved_rows * unpadded_rows, axis=0)
    totals = sum_everywhere(jnp.stack([sum_rows, sum_squares]), 1)
    total_sum, total_squares = totals[0], totals[1]
    count_of_frames = jnp.sum(lengths).astype(jnp.float32)
    batchnorm_frame_mean = total_sum / count_of_frames
    bn_var = total_squares / count_of_frames - batchnorm_frame_mean * batchnorm_frame_mean
    batchnorm_inverse_deviation = lax.rsqrt(bn_var + EPSILON)
    batchnorm_scale_factor = bn_gain.astype(jnp.float32)
    normalized_rows = (convolved_rows - batchnorm_frame_mean) * batchnorm_inverse_deviation
    batchnorm_input_rows = normalized_rows * batchnorm_scale_factor + batchnorm_shift_bias.astype(
        jnp.float32
    )
    bn_sig = jax.nn.sigmoid(batchnorm_input_rows)
    conv_act = (batchnorm_input_rows * bn_sig).astype(jnp.bfloat16)
    rows_three = rows_two + jnp.dot(conv_act, w_conv_out, preferred_element_type=jnp.float32)
    rows_four, ffn2_state = ffn_forward(rows_three, gain_rows[3], w_ffn2_up, w_ffn2_down)
    normed_out, out_pull = jax.vjp(layer_norm, rows_four, gain_rows[4])
    out_rows = normed_out.astype(jnp.bfloat16)
    grad_four, grad_gain_four = out_pull(cotangent[0].astype(jnp.float32))
    grad_three, grad_gain_three, ffn2_up_pair, ffn2_down_pair = ffn_backward(
        grad_four, ffn2_state, w_ffn2_up, w_ffn2_down
    )
    grad_r2 = grad_three.astype(jnp.bfloat16)
    batchnorm_gradient = (
        times_transposed(grad_r2, w_conv_out)
        * bn_sig
        * (1.0 + batchnorm_input_rows * (1.0 - bn_sig))
    )
    gradient_totals = sum_everywhere(
        jnp.stack(
            [
                jnp.sum(batchnorm_gradient, axis=0),
                jnp.sum(batchnorm_gradient * normalized_rows, axis=0),
            ]
        ),
        2,
    )
    gradient_sum_total, gradient_normalized_sum = gradient_totals[0], gradient_totals[1]
    grad_conv = (
        batchnorm_scale_factor
        * batchnorm_inverse_deviation
        * (
            batchnorm_gradient
            - unpadded_rows
            * (gradient_sum_total + normalized_rows * gradient_normalized_sum)
            / count_of_frames
        )
    ).astype(jnp.bfloat16)
    grad_pad = extended(grad_conv, (("seq", 0),), half_size)
    grad_glu = jnp.zeros((frames, model_width), jnp.float32)
    kernel_terms = []
    for tap_index in range(taps):
        offset = 2 * half_size - tap_index
        grad_glu = grad_glu + kernel_rows[tap_index] * grad_pad[offset : offset + frames]
        kernel_terms.append(
            jnp.einsum(
                "fd,fd->d",
                padded[tap_index : tap_index + frames],
                grad_conv,
                preferred_element_type=jnp.float32,
            )
        )
    kernel_grads = jnp.stack(kernel_terms, axis=0)
    grad_glu = grad_glu * unpadded_rows
    grad_gl = jnp.concatenate(
        [grad_glu * glu_sig, grad_glu * up_half * glu_sig * (1.0 - glu_sig)], axis=1
    ).astype(jnp.bfloat16)
    grad_conv_in, grad_gain_two = conv_pull(times_transposed(grad_gl, w_glu))
    grad_two = grad_three + grad_conv_in
    grad_r = grad_two.astype(jnp.bfloat16)
    grad_attn_out = times_transposed(grad_r, w_out).astype(jnp.bfloat16)
    cos_all, sin_all = rope_tables(jnp.arange(seq_length), HD)
    grad_qkv = attend_back(whole_heads, grad_attn_out, length, cos_all, sin_all)
    grad_attn_part, grad_gain_one = attn_pull(times_transposed(grad_qkv, w_qkv))
    grad_one = grad_two + grad_attn_part
    grad_zero, grad_gain_zero, ffn1_up_pair, ffn1_down_pair = ffn_backward(
        grad_one, ffn1_state, w_ffn1_up, w_ffn1_down
    )
    column_total = jnp.sum(grad_zero, axis=0)
    cond_grad_rows = jnp.concatenate(
        [
            level_hot[:, None] * column_total[None, :],
            jnp.sum(mask_column * grad_zero, axis=0)[None, :],
        ],
        axis=0,
    )
    gain_grads = jnp.stack(
        [grad_gain_zero, grad_gain_one, grad_gain_two, grad_gain_three, grad_gain_four], axis=0
    )
    small_rows = jnp.concatenate([gain_grads, cond_grad_rows, kernel_grads], axis=0)
    small_rows = jnp.pad(small_rows, ((0, -small_rows.shape[0] % 8), (0, 0)))
    jobs = [
        Job([ffn2_up_pair], False, "yx12"),
        Job([ffn2_down_pair[::-1]], True, "12xy"),
        Job([(conv_in, grad_gl), (attn_out, grad_r), (conv_act, grad_r2)], False, "xy12"),
        Job([(attn_in, grad_qkv)], False, "x12y"),
        Job([ffn1_down_pair[::-1]], True, "yx12"),
        Job([ffn1_up_pair], False, "yx12"),
    ]
    sums, small_piece = scatter_sums(jobs, SEGMENTS, small_rows, 7)
    cond_end = 5 + level_count + 1
    new_mean = 0.9 * running_mean + 0.1 * batchnorm_frame_mean
    new_var = 0.9 * running_var + 0.1 * bn_var * count_of_frames / (count_of_frames - 1.0)
    return (
        out_rows[None],
        grad_zero.astype(jnp.bfloat16)[None],
        small_piece[5:cond_end],
        small_piece[0:5],
        sums[5][0],
        sums[4][0],
        sums[3][0],
        sums[2][1],
        sums[2][0],
        small_piece[cond_end : cond_end + taps],
        gradient_normalized_sum,
        gradient_sum_total,
        sums[2][2],
        sums[0][0],
        sums[1][0],
        new_mean,
        new_var,
    )


def solution(mesh):
    in_specs = (
        P("batch", "seq", None),
        P("batch", "seq", None),
        P("batch"),
        P(),
        P("batch", "seq"),
        P(),
        P(),
        P(),
        P(),
        P(),
        P(),
        P(),
        P(),
        P(),
        P(),
        P(),
        P(),
        P(),
        P(),
        P(),
    )
    out_specs = (
        P("batch", "seq", None),
        P("batch", "seq", None),
        P(None, "seq"),
        P(None, "seq"),
        P("seq", "batch"),
        P(("batch", "seq"), None),
        P("seq", "batch"),
        P("seq", "batch"),
        P("seq", "batch"),
        P(None, "seq"),
        P(),
        P(),
        P("seq", "batch"),
        P("seq", "batch"),
        P(("batch", "seq"), None),
        P(),
        P(),
    )
    return jax.shard_map(shards, mesh=mesh, in_specs=in_specs, out_specs=out_specs, check_vma=False)
```

```python
import functools
import math

import jax
import jax.numpy as jnp
from jax import lax
from jax.experimental import pallas as pl
from jax.experimental.pallas import tpu as pltpu
from jax.sharding import PartitionSpec as P

MESH = pl.DeviceIdType.MESH

HEADS = 16
HD = 64


EPSILON = 1e-05
MASKED_SCORE = -1000000000.0

SEGMENTS = (
    (2, 3), (0, 2), (1, 3), (0, 1), (5, 2), (1, 2), (3, 2), (4, 3), (2, 2), (1, 1), (5, 1),
    (0, 0), (1, 0), (2, 1), (3, 1), (3, 0), (4, 2), (2, 0), (0, -1), (4, 1), (3, -1), (4, 0),
    (2, -1), (5, 0), (1, -1), (5, -1), (4, -1),
)
SWAPS = (2, 0, 4, 5, 1, 3)


def extended(array, sides, width):
    for axis, dim in sides:
        devices, length = (lax.axis_size(axis), array.shape[dim])
        up = [(i, (i + 1) % devices) for i in range(devices - 1)]
        down = [(j, i) for i, j in up]
        last = lax.slice_in_dim(array, length - width, length, axis=dim)
        leading = lax.slice_in_dim(array, 0, width, axis=dim)
        before = lax.ppermute(last, axis, up)
        after = lax.ppermute(leading, axis, down)
        array = jnp.concatenate([before, array, after], axis=dim)
    return array


def layer_norm(values, gain_row):
    centre = values - jnp.mean(values, axis=-1, keepdims=True)
    spread = jnp.mean(centre * centre, axis=-1, keepdims=True)
    return centre * lax.rsqrt(spread + EPSILON) * gain_row


def rope_tables(positions, head_size):
    half_size = head_size // 2
    inv_freqs = jnp.exp(
        jnp.arange(half_size).astype(jnp.float32) * (-2.0 * math.log(10000.0) / head_size)
    )
    angles = positions.astype(jnp.float32)[:, None] * inv_freqs[None, :]
    return (jnp.cos(angles), jnp.sin(angles))


def times_transposed(left_side, weight):
    return lax.dot_general(
        left_side, weight, (((1,), (1,)), ((), ())), preferred_element_type=jnp.float32
    )


def ffn_forward(values, gain_row, up_weight, down_weight):
    normed, ln_pull = jax.vjp(layer_norm, values, gain_row)
    lowered = normed.astype(jnp.bfloat16)
    hidden = jnp.dot(lowered, up_weight, preferred_element_type=jnp.float32)
    act_rows = (hidden * jax.nn.sigmoid(hidden)).astype(jnp.bfloat16)
    branch = jnp.dot(act_rows, down_weight, preferred_element_type=jnp.float32)
    return (values + 0.5 * branch, (ln_pull, lowered, hidden, act_rows))


def ffn_backward(grad_in, saved_state, up_weight, down_weight):
    ln_pull, lowered, hidden, act_rows = saved_state
    grad_branch = (0.5 * grad_in).astype(jnp.bfloat16)
    grad_act = times_transposed(grad_branch, down_weight)
    gate_sig = jax.nn.sigmoid(hidden)
    grad_hidden = (grad_act * gate_sig * (1.0 + hidden * (1.0 - gate_sig))).astype(jnp.bfloat16)
    grad_normed = times_transposed(grad_hidden, up_weight)
    grad_values, grad_gain = ln_pull(grad_normed)
    return (grad_in + grad_values, grad_gain, (lowered, grad_hidden), (act_rows, grad_branch))


def sum_peers(groups, batches, s, b):
    peers = [(b, lax.rem(s + k, groups)) for k in range(1, groups)]
    return peers + [(lax.rem(b + k, batches), s) for k in range(1, batches)]


def spread(pick, slots, mine, peers, span, sends, arrivals):
    slots[mine] = pick(mine)[...]
    copies = []
    for k in span:
        copies.append(
            pltpu.make_async_remote_copy(
                src_ref=pick(peers[k][1]),
                dst_ref=slots.at[mine],
                send_sem=sends.at[k],
                recv_sem=arrivals.at[k],
                device_id=peers[k],
                device_id_type=MESH,
            )
        )
        copies[-1].start()

    def finish():
        for copy in copies:
            copy.wait()
        total = slots[0]
        for i in range(1, len(copies) + 1):
            total = total + slots[i]
        return total

    return finish


def sum_kernel(groups, batches, rows_ref, total_ref, seq_slots, part, batch_slots, sends, arrivals):
    s, b = lax.axis_index("seq"), lax.axis_index("batch")
    peers = sum_peers(groups, batches, s, b)
    greet(peers)
    first = range(groups - 1)
    second = range(groups - 1, groups + batches - 2)
    part[...] = spread(lambda owner: rows_ref, seq_slots, s, peers, first, sends, arrivals)()
    total_ref[...] = spread(lambda owner: part, batch_slots, b, peers, second, sends, arrivals)()


def sum_scratch(height, width):
    groups, batches = lax.axis_size("seq"), lax.axis_size("batch")
    return [
        pltpu.VMEM((groups, height, width), jnp.float32),
        pltpu.VMEM((height, width), jnp.float32),
        pltpu.VMEM((batches, height, width), jnp.float32),
        pltpu.SemaphoreType.DMA((groups + batches - 2,)),
        pltpu.SemaphoreType.DMA((groups + batches - 2,)),
    ]


def sum_everywhere(rows, collective_id):
    groups, batches = lax.axis_size("seq"), lax.axis_size("batch")
    return pl.pallas_call(
        functools.partial(sum_kernel, groups, batches),
        out_shape=jax.ShapeDtypeStruct(rows.shape, jnp.float32),
        in_specs=[pl.BlockSpec(memory_space=pltpu.VMEM)],
        out_specs=pl.BlockSpec(memory_space=pltpu.VMEM),
        scratch_shapes=sum_scratch(*rows.shape),
        compiler_params=pltpu.CompilerParams(
            collective_id=collective_id, has_side_effects=True, vmem_limit_bytes=4 << 20
        ),
    )(rows)


def halving_steps(first_seq):
    seq_bits = [("seq", k) for k in range(lax.axis_size("seq").bit_length() - 1)]
    batch_bits = [("batch", k) for k in range(1, lax.axis_size("batch").bit_length() - 1)]
    if first_seq:
        seq_bits = seq_bits[::-1]
    return [("batch", 0)] + seq_bits + batch_bits


def relative_place(place, steps, axis):
    flips = 0
    for order, (name, bit) in enumerate(steps):
        if name == axis:
            flips = flips | (((place >> (len(steps) - 1 - order)) & 1) << bit)
    return flips


def product_kernel(steps, tall, rows, cols, group, where, left_ref, right_ref, out_ref):
    step = pl.program_id(0)
    for inner in range(group):
        place = step * group + inner
        b = where[0] ^ relative_place(place, steps, "batch")
        s = where[1] ^ relative_place(place, steps, "seq")
        if tall:
            left = left_ref[:, pl.ds(pl.multiple_of((b * lax.axis_size("seq") + s) * rows, rows), rows)]
            right = right_ref[...]
        else:
            left = left_ref[:, pl.ds(pl.multiple_of(s * rows, rows), rows)]
            right = right_ref[:, pl.ds(pl.multiple_of(b * cols, cols), cols)]
        out_ref[inner] = lax.dot_general(
            left, right, (((0,), (0,)), ((), ())), preferred_element_type=jnp.float32
        ).astype(jnp.bfloat16)


def block_products(left, right, tall, steps):
    batches, groups = lax.axis_size("batch"), lax.axis_size("seq")
    places = batches * groups
    if tall:
        rows, cols = left.shape[1] // places, right.shape[1]
    else:
        rows, cols = left.shape[1] // groups, right.shape[1] // batches
    me = jnp.stack([lax.axis_index("batch"), lax.axis_index("seq")]).astype(jnp.int32)
    if rows % 128 == 0 and cols % 128 == 0:
        group = 4
        return pl.pallas_call(
            functools.partial(product_kernel, steps, tall, rows, cols, group),
            out_shape=jax.ShapeDtypeStruct((places, rows, cols), jnp.bfloat16),
            grid_spec=pltpu.PrefetchScalarGridSpec(
                num_scalar_prefetch=1,
                grid=(places // group,),
                in_specs=[
                    pl.BlockSpec(left.shape, lambda i, where: (0, 0)),
                    pl.BlockSpec(right.shape, lambda i, where: (0, 0)),
                ],
                out_specs=pl.BlockSpec((group, rows, cols), lambda i, where: (i, 0, 0)),
            ),
            compiler_params=pltpu.CompilerParams(vmem_limit_bytes=40 << 20),
            cost_estimate=pl.CostEstimate(
                flops=2 * left.shape[0] * left.shape[1] * right.shape[1],
                bytes_accessed=2 * (left.size + right.size + left.shape[1] * right.shape[1]),
                transcendentals=0,
            ),
        )(me, left, right)
    whole = lax.dot_general(
        left, right, (((0,), (0,)), ((), ())), preferred_element_type=jnp.float32
    ).astype(jnp.bfloat16)
    if tall:
        blocks = whole.reshape(batches, groups, rows, cols)
    else:
        blocks = whole.reshape(groups, rows, batches, cols).transpose(2, 0, 1, 3)
    batch_bits, seq_bits = batches.bit_length() - 1, groups.bit_length() - 1
    blocks = blocks.reshape((2,) * (batch_bits + seq_bits) + (rows, cols))
    dims = []
    for name, bit in steps:
        dim = batch_bits - 1 - bit if name == "batch" else batch_bits + seq_bits - 1 - bit
        mine = (me[0] if name == "batch" else me[1]) >> bit & 1
        blocks = jnp.where(mine == 1, jnp.flip(blocks, dim), blocks)
        dims.append(dim)
    return blocks.transpose(*dims, len(dims), len(dims) + 1).reshape(places, rows, cols)


def owned_sum(left, right, tall, first_seq):
    steps = halving_steps(first_seq)
    blocks = block_products(left, right, tall, steps)
    for axis, bit in steps:
        half = blocks.shape[0] // 2
        pairs = [(i, i ^ (1 << bit)) for i in range(lax.axis_size(axis))]
        arrived = lax.ppermute(blocks[half:], axis, pairs)
        total = blocks[:half].astype(jnp.float32) + arrived.astype(jnp.float32)
        blocks = total.astype(jnp.bfloat16) if half > 1 else total
    return blocks[0]


def attend_kernel(groups, heads, side, *refs):
    refs = list(refs)

    def take(count):
        taken = refs[:count]
        del refs[:count]
        return taken

    length_ref, qkv_ref, cos_ref, sin_ref = take(4)
    side_in = take(len(side.inputs))
    whole_ref, out_ref = take(2)
    side_out = take(len(side.outs))
    stage, result, sends, arrivals, out_sends, out_arrivals, own_sem = take(7)
    s, b = lax.axis_index("seq"), lax.axis_index("batch")
    frames = qkv_ref.shape[0]
    total_frames = whole_ref.shape[0]
    block = heads * 3 * HD
    width = heads * HD
    parts = stage.shape[0]
    span, narrow = block // parts, width // parts
    greet_seq(groups, s, b, side)
    side.start(side_in, side_out, refs, s, b)

    def rows_of(place):
        return pl.ds(pl.multiple_of(place * frames, frames), frames)

    def heads_copy(target, sender, part):
        return pltpu.make_async_remote_copy(
            src_ref=stage.at[part, target],
            dst_ref=whole_ref.at[rows_of(sender), pl.ds(part * span, span)],
            send_sem=sends.at[part, target],
            recv_sem=arrivals.at[part, sender],
            device_id=(b, target),
            device_id_type=MESH,
        )

    columns = range(0, groups * block, 128)
    for column in sorted(columns, key=lambda c: (c % block // span if parts > 1 else 0, c)):
        pattern = (column // 128) % 3
        values = qkv_ref[:, column : column + 128]
        turned = (values * cos_ref[pattern] + partner_lanes(values) * sin_ref[pattern]).astype(
            jnp.bfloat16
        )
        start = column
        while start < column + 128:
            place, part = start // block, start % block // span
            first = place * block + part * span
            end = min(column + 128, first + span)
            stage[part, place, :, start - first : end - first] = turned[
                :, start - column : end - column
            ]
            if end == first + span:

                @pl.when(s != place)
                def _():
                    heads_copy(place, s, part).start()

                @pl.when(s == place)
                def _():
                    whole_ref[rows_of(s), part * span : (part + 1) * span] = stage[part, place]

            start = end

    valid = lax.broadcasted_iota(jnp.int32, (1, total_frames), 1) < length_ref[0]

    def out_place(owner, part):
        if narrow % 128 == 0:
            start = pl.multiple_of(owner * width + part * narrow, 128)
            return out_ref.at[:, pl.ds(start, narrow)]
        return out_ref.at[owner]

    def result_copy(target, sender, part):
        return pltpu.make_async_remote_copy(
            src_ref=result.at[part, target],
            dst_ref=out_place(sender, part),
            send_sem=out_sends.at[part, target],
            recv_sem=out_arrivals.at[part, sender],
            device_id=(b, target),
            device_id_type=MESH,
        )

    owns = []
    for part in range(parts):
        for k in range(1, groups):
            heads_copy(s, lax.rem(s + k, groups), part).wait_recv()

        def one_block(k, carry, part=part):
            place = lax.rem(s + k, groups)
            for h in range(heads // parts):
                base = part * span + h * 3 * HD
                query = whole_ref[rows_of(place), base : base + HD]
                key = whole_ref[:, base + HD : base + 2 * HD]
                value = whole_ref[:, base + 2 * HD : base + 3 * HD]
                scores = times_transposed(query, key)
                scores = jnp.where(valid, scores, MASKED_SCORE)
                exp_scores = jnp.exp(scores - jnp.max(scores, axis=-1, keepdims=True))
                share = 1.0 / jnp.sum(exp_scores, axis=-1, keepdims=True)
                probs = (exp_scores * share).astype(jnp.bfloat16)
                mixed = jnp.dot(probs, value, preferred_element_type=jnp.float32)
                result[part, place, :, h * HD : (h + 1) * HD] = mixed.astype(jnp.bfloat16)

            @pl.when(k < groups)
            def _():
                result_copy(place, s, part).start()

            return carry

        lax.fori_loop(1, groups + 1, one_block, 0)
        owns.append(pltpu.make_async_copy(result.at[part, s], out_place(s, part), own_sem.at[part]))
        owns[-1].start()
    for part in range(parts):
        for k in range(1, groups):
            other = lax.rem(s + k, groups)
            heads_copy(other, s, part).wait_send()
            result_copy(other, s, part).wait_send()
            result_copy(s, other, part).wait_recv()
    for own in owns:
        own.wait()
    side.wait()


def greet_seq(groups, s, b, side):
    greet([(b, lax.rem(s + k, groups)) for k in range(1, groups)] + side.peers(s, b))


def partner_lanes(values):
    lanes = lax.broadcasted_iota(jnp.int32, values.shape, 1)
    return jnp.where(
        lanes % HD < HD // 2,
        pltpu.roll(values, 128 - HD // 2, 1),
        pltpu.roll(values, HD // 2, 1),
    )


def attend(qkv_rows, length, cosine, sine, side):
    groups = lax.axis_size("seq")
    frames = qkv_rows.shape[0]
    heads = HEADS // groups
    width = heads * HD
    signs = jnp.where(jnp.arange(HD) < HD // 2, -1.0, 1.0)
    cos_head = jnp.concatenate([cosine, cosine], axis=1)
    sin_head = jnp.concatenate([sine, sine], axis=1) * signs
    ones, zeros = jnp.ones_like(cos_head), jnp.zeros_like(cos_head)
    cos_pair = jnp.concatenate([cos_head * 0.125, cos_head, ones] * 2, axis=1)
    sin_pair = jnp.concatenate([sin_head * 0.125, sin_head, zeros] * 2, axis=1)
    cos_three = jnp.stack([cos_pair[:, 128 * i : 128 * (i + 1)] for i in range(3)])
    sin_three = jnp.stack([sin_pair[:, 128 * i : 128 * (i + 1)] for i in range(3)])
    parts = heads // 2 if heads % 2 == 0 else 1
    direct = width // parts % 128 == 0
    out_shape = (frames, groups * width) if direct else (groups, frames, width)
    total = frames * groups
    vmem = pl.BlockSpec(memory_space=pltpu.VMEM)
    whole, out, *brought = pl.pallas_call(
        functools.partial(attend_kernel, groups, heads, side),
        out_shape=(
            jax.ShapeDtypeStruct((total, 3 * width), jnp.bfloat16),
            jax.ShapeDtypeStruct(out_shape, jnp.bfloat16),
            *side.outs,
        ),
        in_specs=[pl.BlockSpec(memory_space=pltpu.SMEM), vmem, vmem, vmem]
        + [pl.BlockSpec(memory_space=pl.ANY)] * len(side.inputs),
        out_specs=(vmem, *[pl.BlockSpec(memory_space=pl.ANY)] * (1 + len(side.outs))),
        scratch_shapes=[
            pltpu.VMEM((parts, groups, frames, 3 * width // parts), jnp.bfloat16),
            pltpu.VMEM((parts, groups, frames, width // parts), jnp.bfloat16),
            pltpu.SemaphoreType.DMA((parts, groups)),
            pltpu.SemaphoreType.DMA((parts, groups)),
            pltpu.SemaphoreType.DMA((parts, groups)),
            pltpu.SemaphoreType.DMA((parts, groups)),
            pltpu.SemaphoreType.DMA((parts,)),
            *side.scratch,
        ],
        compiler_params=pltpu.CompilerParams(
            collective_id=4, has_side_effects=True, vmem_limit_bytes=20 << 20
        ),
        cost_estimate=pl.CostEstimate(
            flops=4 * heads * HD * total * total,
            bytes_accessed=4 * qkv_rows.size + 2 * total * 4 * width,
            transcendentals=heads * total * total,
        ),
    )(length.reshape(1), qkv_rows, cos_three, sin_three, *side.inputs)
    if not direct:
        out = out.transpose(1, 0, 2).reshape(frames, groups * width)
    return whole, out, brought


def attend_back_kernel(groups, heads, side, *refs):
    refs = list(refs)

    def take(count):
        taken = refs[:count]
        del refs[:count]
        return taken

    length_ref, whole_ref, grad_ref, cos_ref, sin_ref = take(5)
    side_in = take(len(side.inputs))
    (out_ref,) = take(1)
    side_out = take(len(side.outs))
    stage, grads, result, query_key, value_total = take(5)
    sends, arrivals, out_sends, out_arrivals, own_sem = take(5)
    s, b = lax.axis_index("seq"), lax.axis_index("batch")
    frames = grad_ref.shape[0]
    total_frames = whole_ref.shape[0]
    block = heads * 3 * HD
    width = heads * HD
    greet_seq(groups, s, b, side)
    side.start(side_in, side_out, refs, s, b)

    def rows_of(place):
        return pl.ds(pl.multiple_of(place * frames, frames), frames)

    def grad_copy(target, sender):
        return pltpu.make_async_remote_copy(
            src_ref=stage.at[target],
            dst_ref=grads.at[rows_of(sender)],
            send_sem=sends.at[target],
            recv_sem=arrivals.at[sender],
            device_id=(b, target),
            device_id_type=MESH,
        )

    for place in range(groups):
        stage[place] = grad_ref[:, place * width : (place + 1) * width]

        @pl.when(s != place)
        def _():
            grad_copy(place, s).start()

        @pl.when(s == place)
        def _():
            grads[rows_of(s), :] = stage[place]

    part_heads = 2 if heads % 2 == 0 else heads
    parts = heads // part_heads
    span = part_heads * 3 * HD

    def out_place(owner, part):
        if block % 128 == 0:
            start = pl.multiple_of(owner * block + part * span, 128)
            return out_ref.at[:, pl.ds(start, span)]
        return out_ref.at[owner, :, pl.ds(part * span, span)]

    def result_copy(target, sender, part):
        return pltpu.make_async_remote_copy(
            src_ref=result.at[part, rows_of(target)],
            dst_ref=out_place(sender, part),
            send_sem=out_sends.at[part, target],
            recv_sem=out_arrivals.at[part, sender],
            device_id=(b, target),
            device_id_type=MESH,
        )

    valid = lax.broadcasted_iota(jnp.int32, (total_frames, 1), 0) < length_ref[0]
    for h in range(heads):
        base = h * 3 * HD
        key = whole_ref[:, base + HD : base + 2 * HD]
        key_turned = key.T
        value = whole_ref[:, base + 2 * HD : base + 3 * HD]
        query_key[...] = jnp.zeros_like(query_key)
        value_total[...] = jnp.zeros_like(value_total)

        def one_block(k, carry, h=h, base=base, key=key, key_turned=key_turned, value=value):
            place = lax.rem(s + k, groups)
            if h == 0:

                @pl.when(k > 0)
                def _():
                    grad_copy(s, place).wait_recv()

            query = whole_ref[rows_of(place), base : base + HD]
            grad = grads[rows_of(place), h * HD : (h + 1) * HD]
            scores = jnp.where(valid, times_transposed(key, query), MASKED_SCORE)
            exp_scores = jnp.exp(scores - jnp.max(scores, axis=0, keepdims=True))
            probs = exp_scores * (1.0 / jnp.sum(exp_scores, axis=0, keepdims=True))
            value_total[...] += jnp.dot(
                probs.astype(jnp.bfloat16), grad, preferred_element_type=jnp.float32
            )
            grad_probs = times_transposed(value, grad)
            mean = jnp.sum(probs * grad_probs, axis=0, keepdims=True)
            grad_scores = (probs * (grad_probs - mean)).astype(jnp.bfloat16)
            query_key[:, HD:] += jnp.dot(grad_scores, query, preferred_element_type=jnp.float32)
            query_key[rows_of(place), :HD] = jnp.dot(
                key_turned, grad_scores, preferred_element_type=jnp.float32
            ).T
            return carry

        lax.fori_loop(0, groups, one_block, 0)
        part, inside = h // part_heads, (h % part_heads) * 3 * HD
        both = query_key[...]
        turned = both * cos_ref[...] + partner_lanes(both) * sin_ref[...]
        result[part, :, inside : inside + 2 * HD] = turned.astype(jnp.bfloat16)
        result[part, :, inside + 2 * HD : inside + 3 * HD] = value_total[...].astype(jnp.bfloat16)
        if (h + 1) % part_heads == 0:
            for k in range(1, groups):
                result_copy(lax.rem(s + k, groups), s, part).start()
    owns = []
    for part in range(parts):
        owns.append(
            pltpu.make_async_copy(
                result.at[part, rows_of(s)], out_place(s, part), own_sem.at[part]
            )
        )
        owns[-1].start()
    for k in range(1, groups):
        other = lax.rem(s + k, groups)
        grad_copy(other, s).wait_send()
        for part in range(parts):
            result_copy(other, s, part).wait_send()
            result_copy(s, other, part).wait_recv()
    for own in owns:
        own.wait()
    side.wait()


def attend_back(whole, grad_attn, length, cosine, sine, side):
    groups = lax.axis_size("seq")
    frames = grad_attn.shape[0]
    heads = HEADS // groups
    width = heads * HD
    block = 3 * width
    total = frames * groups
    signs = jnp.where(jnp.arange(HD) < HD // 2, 1.0, -1.0)
    cos_head = jnp.concatenate([cosine, cosine], axis=1)
    sin_head = jnp.concatenate([sine, sine], axis=1) * signs
    cos_both = jnp.concatenate([cos_head * 0.125, cos_head], axis=1)
    sin_both = jnp.concatenate([sin_head * 0.125, sin_head], axis=1)
    part_heads = 2 if heads % 2 == 0 else heads
    parts = heads // part_heads
    direct = block % 128 == 0
    out_shape = (frames, groups * block) if direct else (groups, frames, block)
    vmem = pl.BlockSpec(memory_space=pltpu.VMEM)
    out, *brought = pl.pallas_call(
        functools.partial(attend_back_kernel, groups, heads, side),
        out_shape=[jax.ShapeDtypeStruct(out_shape, jnp.bfloat16), *side.outs],
        in_specs=[pl.BlockSpec(memory_space=pltpu.SMEM), vmem, vmem, vmem, vmem]
        + [pl.BlockSpec(memory_space=pl.ANY)] * len(side.inputs),
        out_specs=[pl.BlockSpec(memory_space=pl.ANY)] * (1 + len(side.outs)),
        scratch_shapes=[
            pltpu.VMEM((groups, frames, width), jnp.bfloat16),
            pltpu.VMEM((total, width), jnp.bfloat16),
            pltpu.VMEM((parts, total, part_heads * 3 * HD), jnp.bfloat16),
            pltpu.VMEM((total, 2 * HD), jnp.float32),
            pltpu.VMEM((total, HD), jnp.float32),
            pltpu.SemaphoreType.DMA((groups,)),
            pltpu.SemaphoreType.DMA((groups,)),
            pltpu.SemaphoreType.DMA((parts, groups)),
            pltpu.SemaphoreType.DMA((parts, groups)),
            pltpu.SemaphoreType.DMA((parts,)),
            *side.scratch,
        ],
        compiler_params=pltpu.CompilerParams(
            collective_id=5, has_side_effects=True, vmem_limit_bytes=24 << 20
        ),
        cost_estimate=pl.CostEstimate(
            flops=10 * heads * HD * total * total,
            bytes_accessed=2 * total * 8 * width,
            transcendentals=heads * total * total,
        ),
    )(length.reshape(1), whole, grad_attn, cos_both, sin_both, *side.inputs)
    if not direct:
        out = out.transpose(1, 0, 2).reshape(frames, groups * block)
    return out, brought


def flipped(index, places):
    for bit, flip in places:
        mine = lax.rem(index // (1 << bit), 2)
        index = index + flip * (1 - 2 * mine) * (1 << bit)
    return index


def place_of(place, steps, axis, index):
    flips = []
    for order, (name, bit) in enumerate(steps):
        if name == axis:
            flips.append((bit, lax.rem(place // (1 << (len(steps) - 1 - order)), 2)))
    return flipped(index, flips)


class Job:
    def __init__(self, parts, tall, order, far=None, gathered=None):
        self.parts, self.tall, self.far, self.gathered = parts, tall, far, gathered
        self.batches, self.groups = lax.axis_size("batch"), lax.axis_size("seq")
        bits = {
            "x": [("seq", 0)],
            "y": [("seq", k) for k in range(1, self.groups.bit_length() - 1)],
            "1": [("batch", 1)],
            "2": [("batch", k) for k in range(2, self.batches.bit_length() - 1)],
        }
        letters = order if far is None else order.replace("1", "")
        self.steps = [step for letter in letters for step in bits[letter]]
        self.sharing = 2 if far is None else 4
        self.spans = self.batches // self.sharing
        self.levels = len(self.steps)
        self.half = 1 << (self.levels - 1)
        if tall:
            ((small, big),) = parts
            self.rows = big.shape[1] // (self.batches * self.groups)
            self.widths = [small.shape[1]]
        else:
            self.rows = parts[0][0].shape[1] // self.groups
            self.widths = [big.shape[1] // self.batches for _, big in parts]
        self.cols = sum(self.widths)
        self.near_pieces = len(parts) * (self.sharing // 2 + self.spans)
        self.far_pieces = len(parts) * (self.sharing // 2 + (self.sharing - 1) * self.spans)
        if gathered is not None:
            self.near_pieces += 3
            self.far_pieces -= 3 * self.spans

    def fits(self):
        return self.rows % 128 == 0 and all(width % 128 == 0 for width in self.widths)

    def operands(self):
        extra = [array for array in (self.far, self.gathered) if array is not None]
        return [array for part in self.parts for array in part] + extra

    def flops(self):
        return sum(2 * small.size * big.shape[1] for small, big in self.parts)

    def operand_scratch(self):
        scratch, sharing = [], self.sharing
        for small, big in self.parts:
            frames = sharing * small.shape[0]
            scratch.append(pltpu.VMEM((frames, small.shape[1]), jnp.bfloat16))
            scratch.append(pltpu.VMEM((frames, big.shape[1] // sharing), jnp.bfloat16))
        return scratch + [
            pltpu.SemaphoreType.DMA((self.near_pieces,)),
            pltpu.SemaphoreType.DMA((self.far_pieces,)),
            pltpu.SemaphoreType.DMA((self.far_pieces,)),
        ]

    def step_of(self, level):
        return self.steps[self.levels - 1 - level]


def greet(peers):
    barrier = pltpu.get_barrier_semaphore()
    for peer in peers:
        pl.semaphore_signal(barrier, inc=1, device_id=peer, device_id_type=MESH)
    pl.semaphore_wait(barrier, len(peers))


def sibling_of(s, b):
    return (b + 1 - 2 * lax.rem(b, 2), s)


def partner_of(s, b, step):
    axis, bit = step
    if axis == "seq":
        return (b, flipped(s, [(bit, 1)]))
    return (flipped(b, [(bit, 1)]), s)


def quarters(s, b, n):
    core, z = lax.rem(b, 2), lax.rem(b // 2, 2)
    mine, other = 2 * (2 * n + z), 2 * (2 * n + 1 - z)
    return [
        (sibling_of(s, b), mine + 1 - core),
        ((flipped(b, [(1, 1)]), s), other + core),
        ((flipped(b, [(0, 1), (1, 1)]), s), other + 1 - core),
    ]


class Side:
    def __init__(self, rows, wide):
        self.rows, self.wide = rows, wide
        batches = lax.axis_size("batch")
        self.inputs = [*rows, *wide]
        self.outs = [jax.ShapeDtypeStruct(array.shape, array.dtype) for array in rows]
        self.outs += [
            jax.ShapeDtypeStruct((3, array.shape[0], array.shape[1] // 4), array.dtype)
            for array in wide
        ]
        self.count = len(rows) + len(wide) * 3 * (batches // 4)
        self.scratch = [pltpu.SemaphoreType.DMA((self.count,))] * 2 if self.count else []

    def peers(self, s, b):
        return [peer for peer, _ in quarters(s, b, 0)] if self.count else []

    def start(self, inputs, outs, sems, s, b):
        self.copies = []

        def send(source, place, peer):
            n = len(self.copies)
            self.copies.append(
                pltpu.make_async_remote_copy(
                    src_ref=source,
                    dst_ref=place,
                    send_sem=sems[0].at[n],
                    recv_sem=sems[1].at[n],
                    device_id=peer,
                    device_id_type=MESH,
                )
            )
            self.copies[-1].start()

        for i, array in enumerate(self.rows):
            send(inputs[i], outs[i], (flipped(b, [(1, 1)]), s))
        for i, array in enumerate(self.wide, len(self.rows)):
            batches = lax.axis_size("batch")
            span = array.shape[1] // batches
            for n in range(batches // 4):
                for k, (peer, owner) in enumerate(quarters(s, b, n)):
                    columns = pl.ds(pl.multiple_of(owner * span, 128), span)
                    send(inputs[i].at[:, columns], outs[i].at[k, :, pl.ds(n * span, span)], peer)

    def wait(self):
        for copy in self.copies:
            copy.wait()


def swap_operands(job, inputs, held, s, b):
    local, moves, lands = held[2 * len(job.parts) :]
    near, far = [], []

    def bring(source, place, peer=None):
        if peer is None:
            near.append(pltpu.make_async_copy(source, place, local.at[len(near)]))
            near[-1].start()
            return
        n = len(far)
        far.append(
            pltpu.make_async_remote_copy(
                src_ref=source,
                dst_ref=place,
                send_sem=moves.at[n],
                recv_sem=lands.at[n],
                device_id=peer,
                device_id_type=MESH,
            )
        )
        far[-1].start()

    core, z = lax.rem(b, 2), lax.rem(b // 2, 2)
    sibling = sibling_of(s, b)
    for i in range(len(job.parts)):
        small_in, big_in = inputs[2 * i : 2 * i + 2]
        small, big = held[2 * i : 2 * i + 2]
        frames = small_in.shape[0]
        span = big_in.shape[1] // job.batches

        def rows(k):
            return pl.ds(k * frames, frames)

        def columns(owner):
            return pl.ds(pl.multiple_of(owner * span, 128), span)

        bring(small_in, small.at[rows(1)], sibling)
        bring(small_in, small.at[rows(0)])
        if job.far is not None:
            bring(inputs[2], small.at[rows(3)], sibling)
            bring(inputs[2], small.at[rows(2)])
        if job.gathered is not None:
            for k in range(3):
                bring(inputs[3].at[k], big.at[rows(k + 1)])
        for n in range(job.spans):
            inside = pl.ds(n * span, span)
            if job.far is None:
                bring(big_in.at[:, columns(2 * n + 1 - core)], big.at[rows(1), inside], sibling)
                bring(big_in.at[:, columns(2 * n + core)], big.at[rows(0), inside])
                continue
            if job.gathered is None:
                for k, (peer, owner) in enumerate(quarters(s, b, n)):
                    bring(big_in.at[:, columns(owner)], big.at[rows(k + 1), inside], peer)
            bring(big_in.at[:, columns(2 * (2 * n + z) + core)], big.at[rows(0), inside])
    return near, far


def wait_operands(near, far):
    for copy in near:
        copy.wait()
    for copy in far:
        copy.wait_recv()


def block_product(job, held, part, place, s, b):
    small, big = held[2 * part : 2 * part + 2]
    span = big.shape[1] // job.spans
    row = place_of(place, job.steps, "seq", s)
    col = place_of(place, job.steps, "batch", b) // job.sharing
    if job.tall:
        left = big[:, pl.ds(pl.multiple_of(col * span + row * job.rows, 128), job.rows)]
        right = small[...]
    else:
        left = small[:, pl.ds(pl.multiple_of(row * job.rows, 128), job.rows)]
        right = big[:, pl.ds(pl.multiple_of(col * span, 128), span)]
    return lax.dot_general(
        left, right, (((0,), (0,)), ((), ())), preferred_element_type=jnp.float32
    )


def columns_of(job, part):
    start = sum(job.widths[:part])
    return slice(start, start + job.widths[part])


def scatter_kernel(jobs, sequence, *refs):
    refs = list(refs)

    def take(count):
        taken = refs[:count]
        del refs[:count]
        return taken

    inputs = [take(len(job.operands())) for job in jobs]
    (rows_ref,) = take(1)
    outs = [take(len(job.parts)) for job in jobs]
    (small_total,) = take(1)
    scratch = [(take(2 * len(job.parts) + 3), *take(4)) for job in jobs]
    seq_slots, part_sum, batch_slots, small_sends, small_arrivals = take(5)
    batches, groups = jobs[0].batches, jobs[0].groups
    s, b = lax.axis_index("seq"), lax.axis_index("batch")
    peers = sum_peers(groups, batches, s, b)
    greet(peers)

    def slot_of(job, place):
        return lax.rem(place, job.half)

    def copy_of(i, place, level):
        job = jobs[i]
        _, sending, arrived, sends, recvs = scratch[i]
        return pltpu.make_async_remote_copy(
            src_ref=sending.at[slot_of(job, place)],
            dst_ref=arrived.at[place - 1],
            send_sem=sends.at[slot_of(job, place)],
            recv_sem=recvs.at[place - 1],
            device_id=partner_of(s, b, job.step_of(level)),
            device_id_type=MESH,
        )

    works = {i: swap_operands(jobs[i], inputs[i], scratch[i][0], s, b) for i in SWAPS}

    def columns(owner):
        width = part_sum.shape[1]
        return rows_ref.at[:, pl.ds(pl.multiple_of(owner * width, 128), width)]

    over_seq = spread(
        columns, seq_slots, s, peers, range(groups - 1), small_sends, small_arrivals
    )

    def block_sums(i, place, level):
        job = jobs[i]
        held, _, arrived = scratch[i][:3]
        for m in range(job.levels - 1, level, -1):
            copy_of(i, (1 << m) + place, m).wait_recv()
        totals = []
        for part in range(len(job.parts)):
            total = block_product(job, held, part, place, s, b)
            for m in range(job.levels - 1, level, -1):
                came = arrived[(1 << m) + place - 1, :, columns_of(job, part)]
                total = total + came.astype(jnp.float32)
            totals.append(total)
        return totals

    def send_block(i, place, level):
        job = jobs[i]
        totals = block_sums(i, place, level)
        if level < job.levels - 1:
            copy_of(i, place + job.half, job.levels - 1).wait_send()
        for part, total in enumerate(totals):
            scratch[i][1][slot_of(job, place), :, columns_of(job, part)] = total.astype(jnp.bfloat16)
        copy_of(i, place, level).start()

    ready = set()
    over_batch = None
    for i, level in sequence:
        job = jobs[i]
        if i not in ready:
            ready.add(i)
            wait_operands(*works[i])
        if level < 0:
            for part, total in enumerate(block_sums(i, 0, -1)):
                outs[i][part][...] = total
            continue

        def one_place(j, carry, level=level, i=i):
            send_block(i, (2 << level) - 1 - j, level)
            return carry

        lax.fori_loop(0, 1 << level, one_place, 0)
        if over_batch is None:
            part_sum[...] = over_seq()
            over_batch = spread(
                lambda owner: part_sum,
                batch_slots,
                b,
                peers,
                range(groups - 1, groups + batches - 2),
                small_sends,
                small_arrivals,
            )
    small_total[...] = over_batch()
    for i, job in enumerate(jobs):
        for copy in works[i][1]:
            copy.wait_send()
        copy_of(i, job.half, job.levels - 1).wait_send()
        for level in range(job.levels - 1):

            def one_wait(j, carry, level=level, i=i):
                copy_of(i, (1 << level) + j, level).wait_send()
                return carry

            lax.fori_loop(0, 1 << level, one_wait, 0)


def pass_kernel(count, *refs):
    for source, target in zip(refs[:count], refs[count:]):
        target[...] = source[...]


def scatter_sums(jobs, sequence, rows, collective_id):
    height, width = rows.shape
    width = width // jobs[0].groups
    if width % 128 or not all(job.fits() for job in jobs):
        total = sum_everywhere(rows, collective_id)
        share = lax.dynamic_slice_in_dim(total, lax.axis_index("seq") * width, width, axis=1)
        sums = [
            [
                owned_sum(*((big, small) if job.tall else (small, big)), job.tall, job.tall)
                for small, big in job.parts
            ]
            for job in jobs
        ]
        return sums, share
    scratch, operands, outs = [], [], []
    for job in jobs:
        block = (job.rows, job.cols)
        scratch += job.operand_scratch()
        scratch += [
            pltpu.VMEM((job.half, *block), jnp.bfloat16),
            pltpu.VMEM((2 * job.half - 1, *block), jnp.bfloat16),
            pltpu.SemaphoreType.DMA((job.half,)),
            pltpu.SemaphoreType.DMA((2 * job.half - 1,)),
        ]
        operands += job.operands()
        outs += [jax.ShapeDtypeStruct((job.rows, width), jnp.float32) for width in job.widths]
    vmem = pl.BlockSpec(memory_space=pltpu.VMEM)
    *results, share = pl.pallas_call(
        functools.partial(scatter_kernel, jobs, sequence),
        out_shape=[*outs, jax.ShapeDtypeStruct((height, width), jnp.float32)],
        in_specs=[pl.BlockSpec(memory_space=pl.ANY)] * len(operands) + [vmem],
        out_specs=[vmem] * (len(outs) + 1),
        scratch_shapes=scratch + sum_scratch(height, width),
        compiler_params=pltpu.CompilerParams(
            collective_id=collective_id, has_side_effects=True, vmem_limit_bytes=60 << 20
        ),
        cost_estimate=pl.CostEstimate(
            flops=sum(job.flops() for job in jobs), bytes_accessed=400 << 20, transcendentals=0
        ),
    )(*operands, rows)
    passes = 4
    specs = [pl.BlockSpec((out.shape[0] // passes, out.shape[1]), lambda i: (i, 0)) for out in outs]
    results = list(
        pl.pallas_call(
            functools.partial(pass_kernel, len(outs)),
            out_shape=outs,
            grid=(passes,),
            in_specs=specs,
            out_specs=specs,
            compiler_params=pltpu.CompilerParams(vmem_limit_bytes=60 << 20),
        )(*results)
    )
    return [[results.pop(0) for _ in job.parts] for job in jobs], share


def shards(
    frames_in,
    cotangent,
    levels,
    lengths,
    token_mask,
    cond_table,
    norm_gains,
    w_ffn1_up,
    w_ffn1_down,
    w_qkv,
    w_out,
    w_glu,
    conv_kernel,
    bn_gain,
    batchnorm_shift_bias,
    w_conv_out,
    w_ffn2_up,
    w_ffn2_down,
    running_mean,
    running_var,
):
    frames = frames_in.shape[1]
    model_width = frames_in.shape[2]
    ff_width = w_ffn1_up.shape[1]
    groups = lax.axis_size("seq")
    batches = lax.axis_size("batch")
    seq_index = lax.axis_index("seq")
    item_index = lax.axis_index("batch")
    seq_length = frames * groups
    level_count = cond_table.shape[0] - 1
    cond_rows = cond_table.astype(jnp.float32)
    gain_rows = norm_gains.astype(jnp.float32)
    level_hot = (jnp.arange(level_count) == levels[0] - 1).astype(jnp.float32)
    level_vector = jnp.sum(level_hot[:, None] * cond_rows[:level_count], axis=0)
    mask_column = token_mask[0].astype(jnp.float32)[:, None]
    start_rows = (
        frames_in[0].astype(jnp.float32)
        + level_vector[None, :]
        + mask_column * cond_rows[level_count][None, :]
    )
    length = lax.dynamic_slice_in_dim(lengths, item_index, 1)[0]
    positions = seq_index * frames + jnp.arange(frames)
    unpadded_rows = (positions < length).astype(jnp.float32)[:, None]
    rows_one, ffn1_state = ffn_forward(start_rows, gain_rows[0], w_ffn1_up, w_ffn1_down)
    normed_attn, attn_pull = jax.vjp(layer_norm, rows_one, gain_rows[1])
    attn_in = normed_attn.astype(jnp.bfloat16)
    qkv_rows = jnp.dot(attn_in, w_qkv, preferred_element_type=jnp.float32)
    cosine, sine_table = rope_tables(positions, HD)
    fit = (
        model_width // groups % 128 == 0
        and model_width // batches % 128 == 0
        and ff_width // (groups * batches) % 128 == 0
    )
    side = Side([ffn1_state[1], attn_in] if fit else [], [])
    whole_heads, attn_out, brought = attend(qkv_rows, length, cosine, sine_table, side)
    far_ffn1, far_attn = brought if fit else (None, None)
    rows_two = rows_one + jnp.dot(attn_out, w_out, preferred_element_type=jnp.float32)
    normed_conv, conv_pull = jax.vjp(layer_norm, rows_two, gain_rows[2])
    conv_in = normed_conv.astype(jnp.bfloat16)
    glu_pre = jnp.dot(conv_in, w_glu, preferred_element_type=jnp.float32)
    up_half = glu_pre[:, :model_width]
    glu_sig = jax.nn.sigmoid(glu_pre[:, model_width:])
    glu_low = (up_half * glu_sig * unpadded_rows).astype(jnp.bfloat16)
    taps = conv_kernel.shape[0]
    half_size = taps // 2
    kernel_rows = conv_kernel.astype(jnp.float32)
    padded = extended(glu_low, (("seq", 0),), half_size)
    convolved_rows = jnp.zeros((frames, model_width), jnp.float32)
    for tap_index in range(taps):
        convolved_rows = (
            convolved_rows + kernel_rows[tap_index] * padded[tap_index : tap_index + frames]
        )
    sum_rows = jnp.sum(convolved_rows * unpadded_rows, axis=0)
    sum_squares = jnp.sum(convolved_rows * convolved_rows * unpadded_rows, axis=0)
    totals = sum_everywhere(jnp.stack([sum_rows, sum_squares]), 1)
    total_sum, total_squares = totals[0], totals[1]
    count_of_frames = jnp.sum(lengths).astype(jnp.float32)
    batchnorm_frame_mean = total_sum / count_of_frames
    bn_var = total_squares / count_of_frames - batchnorm_frame_mean * batchnorm_frame_mean
    batchnorm_inverse_deviation = lax.rsqrt(bn_var + EPSILON)
    batchnorm_scale_factor = bn_gain.astype(jnp.float32)
    normalized_rows = (convolved_rows - batchnorm_frame_mean) * batchnorm_inverse_deviation
    batchnorm_input_rows = normalized_rows * batchnorm_scale_factor + batchnorm_shift_bias.astype(
        jnp.float32
    )
    bn_sig = jax.nn.sigmoid(batchnorm_input_rows)
    conv_act = (batchnorm_input_rows * bn_sig).astype(jnp.bfloat16)
    rows_three = rows_two + jnp.dot(conv_act, w_conv_out, preferred_element_type=jnp.float32)
    rows_four, ffn2_state = ffn_forward(rows_three, gain_rows[3], w_ffn2_up, w_ffn2_down)
    normed_out, out_pull = jax.vjp(layer_norm, rows_four, gain_rows[4])
    out_rows = normed_out.astype(jnp.bfloat16)
    grad_four, grad_gain_four = out_pull(cotangent[0].astype(jnp.float32))
    grad_three, grad_gain_three, ffn2_up_pair, ffn2_down_pair = ffn_backward(
        grad_four, ffn2_state, w_ffn2_up, w_ffn2_down
    )
    grad_r2 = grad_three.astype(jnp.bfloat16)
    batchnorm_gradient = (
        times_transposed(grad_r2, w_conv_out)
        * bn_sig
        * (1.0 + batchnorm_input_rows * (1.0 - bn_sig))
    )
    gradient_totals = sum_everywhere(
        jnp.stack(
            [
                jnp.sum(batchnorm_gradient, axis=0),
                jnp.sum(batchnorm_gradient * normalized_rows, axis=0),
            ]
        ),
        2,
    )
    gradient_sum_total, gradient_normalized_sum = gradient_totals[0], gradient_totals[1]
    grad_conv = (
        batchnorm_scale_factor
        * batchnorm_inverse_deviation
        * (
            batchnorm_gradient
            - unpadded_rows
            * (gradient_sum_total + normalized_rows * gradient_normalized_sum)
            / count_of_frames
        )
    ).astype(jnp.bfloat16)
    grad_pad = extended(grad_conv, (("seq", 0),), half_size)
    grad_glu = jnp.zeros((frames, model_width), jnp.float32)
    kernel_terms = []
    for tap_index in range(taps):
        offset = 2 * half_size - tap_index
        grad_glu = grad_glu + kernel_rows[tap_index] * grad_pad[offset : offset + frames]
        kernel_terms.append(
            jnp.einsum(
                "fd,fd->d",
                padded[tap_index : tap_index + frames],
                grad_conv,
                preferred_element_type=jnp.float32,
            )
        )
    kernel_grads = jnp.stack(kernel_terms, axis=0)
    grad_glu = grad_glu * unpadded_rows
    grad_gl = jnp.concatenate(
        [grad_glu * glu_sig, grad_glu * up_half * glu_sig * (1.0 - glu_sig)], axis=1
    ).astype(jnp.bfloat16)
    grad_conv_in, grad_gain_two = conv_pull(times_transposed(grad_gl, w_glu))
    grad_two = grad_three + grad_conv_in
    grad_r = grad_two.astype(jnp.bfloat16)
    grad_attn_out = times_transposed(grad_r, w_out).astype(jnp.bfloat16)
    cos_all, sin_all = rope_tables(jnp.arange(seq_length), HD)
    side = Side([ffn2_up_pair[0]] if fit else [], [ffn2_up_pair[1]] if fit else [])
    grad_qkv, brought = attend_back(whole_heads, grad_attn_out, length, cos_all, sin_all, side)
    far_ffn2, gathered = brought if fit else (None, None)
    grad_attn_part, grad_gain_one = attn_pull(times_transposed(grad_qkv, w_qkv))
    grad_one = grad_two + grad_attn_part
    grad_zero, grad_gain_zero, ffn1_up_pair, ffn1_down_pair = ffn_backward(
        grad_one, ffn1_state, w_ffn1_up, w_ffn1_down
    )
    column_total = jnp.sum(grad_zero, axis=0)
    cond_grad_rows = jnp.concatenate(
        [
            level_hot[:, None] * column_total[None, :],
            jnp.sum(mask_column * grad_zero, axis=0)[None, :],
        ],
        axis=0,
    )
    gain_grads = jnp.stack(
        [grad_gain_zero, grad_gain_one, grad_gain_two, grad_gain_three, grad_gain_four], axis=0
    )
    small_rows = jnp.concatenate([gain_grads, cond_grad_rows, kernel_grads], axis=0)
    small_rows = jnp.pad(small_rows, ((0, -small_rows.shape[0] % 8), (0, 0)))
    jobs = [
        Job([ffn2_up_pair], False, "1yx2", far_ffn2, gathered),
        Job([ffn2_down_pair[::-1]], True, "y12x"),
        Job([(conv_in, grad_gl), (attn_out, grad_r), (conv_act, grad_r2)], False, "xy12"),
        Job([(attn_in, grad_qkv)], False, "1xy2", far_attn),
        Job([ffn1_down_pair[::-1]], True, "xy12"),
        Job([ffn1_up_pair], False, "12xy", far_ffn1),
    ]
    sums, small_piece = scatter_sums(jobs, SEGMENTS, small_rows, 7)
    cond_end = 5 + level_count + 1
    new_mean = 0.9 * running_mean + 0.1 * batchnorm_frame_mean
    new_var = 0.9 * running_var + 0.1 * bn_var * count_of_frames / (count_of_frames - 1.0)
    return (
        out_rows[None],
        grad_zero.astype(jnp.bfloat16)[None],
        small_piece[5:cond_end],
        small_piece[0:5],
        sums[5][0],
        sums[4][0],
        sums[3][0],
        sums[2][1],
        sums[2][0],
        small_piece[cond_end : cond_end + taps],
        gradient_normalized_sum,
        gradient_sum_total,
        sums[2][2],
        sums[0][0],
        sums[1][0],
        new_mean,
        new_var,
    )


def solution(mesh):
    in_specs = (
        P("batch", "seq", None),
        P("batch", "seq", None),
        P("batch"),
        P(),
        P("batch", "seq"),
        P(),
        P(),
        P(),
        P(),
        P(),
        P(),
        P(),
        P(),
        P(),
        P(),
        P(),
        P(),
        P(),
        P(),
        P(),
    )
    out_specs = (
        P("batch", "seq", None),
        P("batch", "seq", None),
        P(None, "seq"),
        P(None, "seq"),
        P("seq", "batch"),
        P(("batch", "seq"), None),
        P("seq", "batch"),
        P("seq", "batch"),
        P("seq", "batch"),
        P(None, "seq"),
        P(),
        P(),
        P("seq", "batch"),
        P("seq", "batch"),
        P(("batch", "seq"), None),
        P(),
        P(),
    )
    return jax.shard_map(shards, mesh=mesh, in_specs=in_specs, out_specs=out_specs, check_vma=False)
```

```python
import functools
import math

import jax
import jax.numpy as jnp
from jax import lax
from jax.experimental import pallas as pl
from jax.experimental.pallas import tpu as pltpu
from jax.sharding import PartitionSpec as P

MESH = pl.DeviceIdType.MESH

HEADS = 16
HD = 64


EPSILON = 1e-05
MASKED_SCORE = -1000000000.0

SEGMENTS = (
    (2, 3), (0, 2), (1, 3), (0, 1), (5, 2), (1, 2), (3, 2), (4, 3), (2, 2), (1, 1), (5, 1),
    (0, 0), (1, 0), (2, 1), (3, 1), (3, 0), (4, 2), (2, 0), (0, -1), (4, 1), (3, -1), (4, 0),
    (2, -1), (5, 0), (1, -1), (5, -1), (4, -1),
)
SWAPS = (2, 0, 4, 5, 1, 3)


def layer_norm(values, gain_row):
    centre = values - jnp.mean(values, axis=-1, keepdims=True)
    spread = jnp.mean(centre * centre, axis=-1, keepdims=True)
    return centre * lax.rsqrt(spread + EPSILON) * gain_row


def rope_tables(positions, head_size):
    half_size = head_size // 2
    inv_freqs = jnp.exp(
        jnp.arange(half_size).astype(jnp.float32) * (-2.0 * math.log(10000.0) / head_size)
    )
    angles = positions.astype(jnp.float32)[:, None] * inv_freqs[None, :]
    return (jnp.cos(angles), jnp.sin(angles))


def times_transposed(left_side, weight):
    return lax.dot_general(
        left_side, weight, (((1,), (1,)), ((), ())), preferred_element_type=jnp.float32
    )


def ffn_forward(values, gain_row, up_weight, down_weight):
    normed, ln_pull = jax.vjp(layer_norm, values, gain_row)
    lowered = normed.astype(jnp.bfloat16)
    hidden = jnp.dot(lowered, up_weight, preferred_element_type=jnp.float32)
    act_rows = (hidden * jax.nn.sigmoid(hidden)).astype(jnp.bfloat16)
    branch = jnp.dot(act_rows, down_weight, preferred_element_type=jnp.float32)
    return (values + 0.5 * branch, (ln_pull, lowered, hidden, act_rows))


def ffn_backward(grad_in, saved_state, up_weight, down_weight):
    ln_pull, lowered, hidden, act_rows = saved_state
    grad_branch = (0.5 * grad_in).astype(jnp.bfloat16)
    grad_act = times_transposed(grad_branch, down_weight)
    gate_sig = jax.nn.sigmoid(hidden)
    grad_hidden = (grad_act * gate_sig * (1.0 + hidden * (1.0 - gate_sig))).astype(jnp.bfloat16)
    grad_normed = times_transposed(grad_hidden, up_weight)
    grad_values, grad_gain = ln_pull(grad_normed)
    return (grad_in + grad_values, grad_gain, (lowered, grad_hidden), (act_rows, grad_branch))


def sum_peers(groups, batches, s, b):
    peers = [(b, lax.rem(s + k, groups)) for k in range(1, groups)]
    return peers + [(lax.rem(b + k, batches), s) for k in range(1, batches)]


def spread(pick, slots, mine, peers, span, sends, arrivals):
    slots[mine] = pick(mine)[...]
    copies = []
    for k in span:
        copies.append(
            pltpu.make_async_remote_copy(
                src_ref=pick(peers[k][1]),
                dst_ref=slots.at[mine],
                send_sem=sends.at[k],
                recv_sem=arrivals.at[k],
                device_id=peers[k],
                device_id_type=MESH,
            )
        )
        copies[-1].start()

    def finish():
        for copy in copies:
            copy.wait()
        total = slots[0]
        for i in range(1, len(copies) + 1):
            total = total + slots[i]
        return total

    return finish


def sum_kernel(groups, batches, rows_ref, total_ref, seq_slots, part, batch_slots, sends, arrivals):
    s, b = lax.axis_index("seq"), lax.axis_index("batch")
    peers = sum_peers(groups, batches, s, b)
    greet(peers)
    first = range(groups - 1)
    second = range(groups - 1, groups + batches - 2)
    part[...] = spread(lambda owner: rows_ref, seq_slots, s, peers, first, sends, arrivals)()
    total_ref[...] = spread(lambda owner: part, batch_slots, b, peers, second, sends, arrivals)()


def sum_scratch(height, width):
    groups, batches = lax.axis_size("seq"), lax.axis_size("batch")
    return [
        pltpu.VMEM((groups, height, width), jnp.float32),
        pltpu.VMEM((height, width), jnp.float32),
        pltpu.VMEM((batches, height, width), jnp.float32),
        pltpu.SemaphoreType.DMA((groups + batches - 2,)),
        pltpu.SemaphoreType.DMA((groups + batches - 2,)),
    ]


def sum_everywhere(rows, collective_id):
    groups, batches = lax.axis_size("seq"), lax.axis_size("batch")
    return pl.pallas_call(
        functools.partial(sum_kernel, groups, batches),
        out_shape=jax.ShapeDtypeStruct(rows.shape, jnp.float32),
        in_specs=[pl.BlockSpec(memory_space=pltpu.VMEM)],
        out_specs=pl.BlockSpec(memory_space=pltpu.VMEM),
        scratch_shapes=sum_scratch(*rows.shape),
        compiler_params=pltpu.CompilerParams(
            collective_id=collective_id, has_side_effects=True, vmem_limit_bytes=4 << 20
        ),
    )(rows)


def edge_copies(groups, s, b, rows_ref, before, after, tile, sends, arrivals, first):
    up = pltpu.make_async_remote_copy(
        src_ref=rows_ref.at[pl.ds(rows_ref.shape[0] - tile, tile)],
        dst_ref=before,
        send_sem=sends.at[first],
        recv_sem=arrivals.at[first],
        device_id=(b, lax.rem(s + 1, groups)),
        device_id_type=MESH,
    )
    down = pltpu.make_async_remote_copy(
        src_ref=rows_ref.at[pl.ds(0, tile)],
        dst_ref=after,
        send_sem=sends.at[first + 1],
        recv_sem=arrivals.at[first + 1],
        device_id=(b, lax.rem(s + groups - 1, groups)),
        device_id_type=MESH,
    )
    return up, down


def start_edges(groups, s, copies):
    @pl.when(s < groups - 1)
    def _():
        for up, _ in copies:
            up.start()

    @pl.when(s > 0)
    def _():
        for _, down in copies:
            down.start()


def wait_edges_sent(groups, s, copies):
    @pl.when(s < groups - 1)
    def _():
        for up, _ in copies:
            up.wait_send()

    @pl.when(s > 0)
    def _():
        for _, down in copies:
            down.wait_send()


def valid_rows(first, count, length):
    positions = first + lax.broadcasted_iota(jnp.int32, (count, 1), 0)
    return (positions < length).astype(jnp.float32)


def convolve_kernel(
    groups, batches, taps, length_ref, glu_ref, kernel_ref, out_ref, padded_ref, total_ref,
    before, after, local, edge_sends, edge_arrivals, seq_slots, part, batch_slots, sends, arrivals,
):
    s, b = lax.axis_index("seq"), lax.axis_index("batch")
    peers = sum_peers(groups, batches, s, b)
    signal(peers)
    frames, width = glu_ref.shape
    padded_ref[8 : 8 + frames, :] = glu_ref[...].astype(jnp.float32)
    wait_signals(peers)
    edges = [edge_copies(groups, s, b, glu_ref, before, after, 16, edge_sends, edge_arrivals, 0)]
    start_edges(groups, s, edges)

    @pl.when(s > 0)
    def _():
        edges[0][0].wait_recv()
        padded_ref[0:8, :] = before[8:16, :].astype(jnp.float32)

    @pl.when(s == 0)
    def _():
        padded_ref[0:8, :] = jnp.zeros((8, width), jnp.float32)

    @pl.when(s < groups - 1)
    def _():
        edges[0][1].wait_recv()
        padded_ref[8 + frames :, :] = after[0:8, :].astype(jnp.float32)

    @pl.when(s == groups - 1)
    def _():
        padded_ref[8 + frames :, :] = jnp.zeros((8, width), jnp.float32)

    valid = valid_rows(s * frames, frames, length_ref[0])
    for column in range(0, width, 128):
        lanes = slice(column, column + 128)
        total = jnp.zeros((frames, 128), jnp.float32)
        for k in range(taps):
            start = 8 - taps // 2 + k
            total = total + kernel_ref[k : k + 1, lanes] * padded_ref[start : start + frames, lanes]
        out_ref[:, lanes] = total
        kept = total * valid
        local[0:1, lanes] = jnp.sum(kept, axis=0, keepdims=True)
        local[1:2, lanes] = jnp.sum(kept * total, axis=0, keepdims=True)
    first, second = range(groups - 1), range(groups - 1, groups + batches - 2)
    part[...] = spread(lambda owner: local, seq_slots, s, peers, first, sends, arrivals)()
    total_ref[...] = spread(lambda owner: part, batch_slots, b, peers, second, sends, arrivals)()
    wait_edges_sent(groups, s, edges)


def convolve(glu_low, kernel_rows, length):
    groups, batches = lax.axis_size("seq"), lax.axis_size("batch")
    frames, width = glu_low.shape
    taps = kernel_rows.shape[0]
    vmem = pl.BlockSpec(memory_space=pltpu.VMEM)
    return pl.pallas_call(
        functools.partial(convolve_kernel, groups, batches, taps),
        out_shape=[
            jax.ShapeDtypeStruct((frames, width), jnp.float32),
            jax.ShapeDtypeStruct((frames + 16, width), jnp.float32),
            jax.ShapeDtypeStruct((2, width), jnp.float32),
        ],
        in_specs=[pl.BlockSpec(memory_space=pltpu.SMEM), vmem, vmem],
        out_specs=[vmem] * 3,
        scratch_shapes=[
            pltpu.VMEM((16, width), jnp.bfloat16),
            pltpu.VMEM((16, width), jnp.bfloat16),
            pltpu.VMEM((2, width), jnp.float32),
            pltpu.SemaphoreType.DMA((2,)),
            pltpu.SemaphoreType.DMA((2,)),
            *sum_scratch(2, width),
        ],
        compiler_params=pltpu.CompilerParams(
            collective_id=1, has_side_effects=True, vmem_limit_bytes=8 << 20
        ),
    )(length.reshape(1), glu_low, kernel_rows)


def convolve_back_kernel(
    groups, batches, taps, length_ref, count_ref, grad_ref, conv_ref, padded_ref, kernel_ref, norm_ref,
    out_ref, taps_ref, total_ref, edge_rows, spread_rows, local, edge_sends, edge_arrivals,
    seq_slots, part, batch_slots, sends, arrivals,
):
    s, b = lax.axis_index("seq"), lax.axis_index("batch")
    peers = sum_peers(groups, batches, s, b)
    signal(peers)
    frames, width = grad_ref.shape

    def normalized(values, lanes):
        return (values - norm_ref[0:1, lanes]) * norm_ref[1:2, lanes]

    for column in range(0, width, 128):
        lanes = slice(column, column + 128)
        grads = grad_ref[:, lanes]
        local[0:1, lanes] = jnp.sum(grads, axis=0, keepdims=True)
        local[1:2, lanes] = jnp.sum(
            grads * normalized(conv_ref[:, lanes], lanes), axis=0, keepdims=True
        )
    wait_signals(peers)
    edges = [
        edge_copies(
            groups, s, b, ref, edge_rows.at[2 * i], edge_rows.at[2 * i + 1], 8,
            edge_sends, edge_arrivals, 2 * i,
        )
        for i, ref in enumerate((grad_ref, conv_ref))
    ]
    start_edges(groups, s, edges)
    first, second = range(groups - 1), range(groups - 1, groups + batches - 2)
    part[...] = spread(lambda owner: local, seq_slots, s, peers, first, sends, arrivals)()
    total_ref[...] = spread(lambda owner: part, batch_slots, b, peers, second, sends, arrivals)()

    length = length_ref[0]
    share = 1.0 / count_ref[0]

    def conv_grad(grads, values, valid, lanes):
        sums = total_ref[0:1, lanes] + normalized(values, lanes) * total_ref[1:2, lanes]
        rows = norm_ref[2:3, lanes] * norm_ref[1:2, lanes] * (grads - valid * sums * share)
        return rows.astype(jnp.bfloat16).astype(jnp.float32)

    @pl.when(s > 0)
    def _():
        for up, _ in edges:
            up.wait_recv()
        spread_rows[0:8, :] = conv_grad(
            edge_rows[0], edge_rows[2], valid_rows(s * frames - 8, 8, length), slice(None)
        )

    @pl.when(s == 0)
    def _():
        spread_rows[0:8, :] = jnp.zeros((8, width), jnp.float32)

    @pl.when(s < groups - 1)
    def _():
        for _, down in edges:
            down.wait_recv()
        spread_rows[8 + frames :, :] = conv_grad(
            edge_rows[1], edge_rows[3], valid_rows((s + 1) * frames, 8, length), slice(None)
        )

    @pl.when(s == groups - 1)
    def _():
        spread_rows[8 + frames :, :] = jnp.zeros((8, width), jnp.float32)

    valid = valid_rows(s * frames, frames, length)
    taps_ref[...] = jnp.zeros_like(taps_ref)
    for column in range(0, width, 128):
        lanes = slice(column, column + 128)
        own = conv_grad(grad_ref[:, lanes], conv_ref[:, lanes], valid, lanes)
        spread_rows[8 : 8 + frames, lanes] = own
        total = jnp.zeros((frames, 128), jnp.float32)
        for k in range(taps):
            start = 8 + taps // 2 - k
            total = total + kernel_ref[k : k + 1, lanes] * spread_rows[start : start + frames, lanes]
            start = 8 - taps // 2 + k
            taps_ref[k : k + 1, lanes] = jnp.sum(
                padded_ref[start : start + frames, lanes] * own, axis=0, keepdims=True
            )
        out_ref[:, lanes] = total * valid
    wait_edges_sent(groups, s, edges)


def convolve_back(grads, convolved, padded, kernel_rows, norm_rows, length, count):
    groups, batches = lax.axis_size("seq"), lax.axis_size("batch")
    frames, width = grads.shape
    taps = kernel_rows.shape[0]
    vmem, smem = pl.BlockSpec(memory_space=pltpu.VMEM), pl.BlockSpec(memory_space=pltpu.SMEM)
    return pl.pallas_call(
        functools.partial(convolve_back_kernel, groups, batches, taps),
        out_shape=[
            jax.ShapeDtypeStruct((frames, width), jnp.float32),
            jax.ShapeDtypeStruct((8, width), jnp.float32),
            jax.ShapeDtypeStruct((2, width), jnp.float32),
        ],
        in_specs=[smem, smem, vmem, vmem, vmem, vmem, vmem],
        out_specs=[vmem] * 3,
        scratch_shapes=[
            pltpu.VMEM((4, 8, width), jnp.float32),
            pltpu.VMEM((frames + 16, width), jnp.float32),
            pltpu.VMEM((2, width), jnp.float32),
            pltpu.SemaphoreType.DMA((4,)),
            pltpu.SemaphoreType.DMA((4,)),
            *sum_scratch(2, width),
        ],
        compiler_params=pltpu.CompilerParams(
            collective_id=2, has_side_effects=True, vmem_limit_bytes=12 << 20
        ),
    )(length.reshape(1), count.reshape(1), grads, convolved, padded, kernel_rows, norm_rows)


def halving_steps(first_seq):
    seq_bits = [("seq", k) for k in range(lax.axis_size("seq").bit_length() - 1)]
    batch_bits = [("batch", k) for k in range(1, lax.axis_size("batch").bit_length() - 1)]
    if first_seq:
        seq_bits = seq_bits[::-1]
    return [("batch", 0)] + seq_bits + batch_bits


def relative_place(place, steps, axis):
    flips = 0
    for order, (name, bit) in enumerate(steps):
        if name == axis:
            flips = flips | (((place >> (len(steps) - 1 - order)) & 1) << bit)
    return flips


def product_kernel(steps, tall, rows, cols, group, where, left_ref, right_ref, out_ref):
    step = pl.program_id(0)
    for inner in range(group):
        place = step * group + inner
        b = where[0] ^ relative_place(place, steps, "batch")
        s = where[1] ^ relative_place(place, steps, "seq")
        if tall:
            left = left_ref[:, pl.ds(pl.multiple_of((b * lax.axis_size("seq") + s) * rows, rows), rows)]
            right = right_ref[...]
        else:
            left = left_ref[:, pl.ds(pl.multiple_of(s * rows, rows), rows)]
            right = right_ref[:, pl.ds(pl.multiple_of(b * cols, cols), cols)]
        out_ref[inner] = lax.dot_general(
            left, right, (((0,), (0,)), ((), ())), preferred_element_type=jnp.float32
        ).astype(jnp.bfloat16)


def block_products(left, right, tall, steps):
    batches, groups = lax.axis_size("batch"), lax.axis_size("seq")
    places = batches * groups
    if tall:
        rows, cols = left.shape[1] // places, right.shape[1]
    else:
        rows, cols = left.shape[1] // groups, right.shape[1] // batches
    me = jnp.stack([lax.axis_index("batch"), lax.axis_index("seq")]).astype(jnp.int32)
    if rows % 128 == 0 and cols % 128 == 0:
        group = 4
        return pl.pallas_call(
            functools.partial(product_kernel, steps, tall, rows, cols, group),
            out_shape=jax.ShapeDtypeStruct((places, rows, cols), jnp.bfloat16),
            grid_spec=pltpu.PrefetchScalarGridSpec(
                num_scalar_prefetch=1,
                grid=(places // group,),
                in_specs=[
                    pl.BlockSpec(left.shape, lambda i, where: (0, 0)),
                    pl.BlockSpec(right.shape, lambda i, where: (0, 0)),
                ],
                out_specs=pl.BlockSpec((group, rows, cols), lambda i, where: (i, 0, 0)),
            ),
            compiler_params=pltpu.CompilerParams(vmem_limit_bytes=40 << 20),
            cost_estimate=pl.CostEstimate(
                flops=2 * left.shape[0] * left.shape[1] * right.shape[1],
                bytes_accessed=2 * (left.size + right.size + left.shape[1] * right.shape[1]),
                transcendentals=0,
            ),
        )(me, left, right)
    whole = lax.dot_general(
        left, right, (((0,), (0,)), ((), ())), preferred_element_type=jnp.float32
    ).astype(jnp.bfloat16)
    if tall:
        blocks = whole.reshape(batches, groups, rows, cols)
    else:
        blocks = whole.reshape(groups, rows, batches, cols).transpose(2, 0, 1, 3)
    batch_bits, seq_bits = batches.bit_length() - 1, groups.bit_length() - 1
    blocks = blocks.reshape((2,) * (batch_bits + seq_bits) + (rows, cols))
    dims = []
    for name, bit in steps:
        dim = batch_bits - 1 - bit if name == "batch" else batch_bits + seq_bits - 1 - bit
        mine = (me[0] if name == "batch" else me[1]) >> bit & 1
        blocks = jnp.where(mine == 1, jnp.flip(blocks, dim), blocks)
        dims.append(dim)
    return blocks.transpose(*dims, len(dims), len(dims) + 1).reshape(places, rows, cols)


def owned_sum(left, right, tall, first_seq):
    steps = halving_steps(first_seq)
    blocks = block_products(left, right, tall, steps)
    for axis, bit in steps:
        half = blocks.shape[0] // 2
        pairs = [(i, i ^ (1 << bit)) for i in range(lax.axis_size(axis))]
        arrived = lax.ppermute(blocks[half:], axis, pairs)
        total = blocks[:half].astype(jnp.float32) + arrived.astype(jnp.float32)
        blocks = total.astype(jnp.bfloat16) if half > 1 else total
    return blocks[0]


def attend_kernel(groups, heads, side, *refs):
    refs = list(refs)

    def take(count):
        taken = refs[:count]
        del refs[:count]
        return taken

    length_ref, qkv_ref, cos_ref, sin_ref = take(4)
    side_in = take(len(side.inputs))
    whole_ref, out_ref = take(2)
    side_out = take(len(side.outs))
    stage, result, sends, arrivals, out_sends, out_arrivals, own_sem = take(7)
    s, b = lax.axis_index("seq"), lax.axis_index("batch")
    frames = qkv_ref.shape[0]
    total_frames = whole_ref.shape[0]
    block = heads * 3 * HD
    width = heads * HD
    parts = stage.shape[0]
    span, narrow = block // parts, width // parts
    greet_seq(groups, s, b, side)
    side.start(side_in, side_out, refs, s, b)

    def rows_of(place):
        return pl.ds(pl.multiple_of(place * frames, frames), frames)

    def heads_copy(target, sender, part):
        return pltpu.make_async_remote_copy(
            src_ref=stage.at[part, target],
            dst_ref=whole_ref.at[rows_of(sender), pl.ds(part * span, span)],
            send_sem=sends.at[part, target],
            recv_sem=arrivals.at[part, sender],
            device_id=(b, target),
            device_id_type=MESH,
        )

    columns = range(0, groups * block, 128)
    for column in sorted(columns, key=lambda c: (c % block // span if parts > 1 else 0, c)):
        pattern = (column // 128) % 3
        values = qkv_ref[:, column : column + 128]
        turned = (values * cos_ref[pattern] + partner_lanes(values) * sin_ref[pattern]).astype(
            jnp.bfloat16
        )
        start = column
        while start < column + 128:
            place, part = start // block, start % block // span
            first = place * block + part * span
            end = min(column + 128, first + span)
            stage[part, place, :, start - first : end - first] = turned[
                :, start - column : end - column
            ]
            if end == first + span:

                @pl.when(s != place)
                def _():
                    heads_copy(place, s, part).start()

                @pl.when(s == place)
                def _():
                    whole_ref[rows_of(s), part * span : (part + 1) * span] = stage[part, place]

            start = end

    valid = lax.broadcasted_iota(jnp.int32, (1, total_frames), 1) < length_ref[0]

    def out_place(owner, part):
        if narrow % 128 == 0:
            start = pl.multiple_of(owner * width + part * narrow, 128)
            return out_ref.at[:, pl.ds(start, narrow)]
        return out_ref.at[owner]

    def result_copy(target, sender, part):
        return pltpu.make_async_remote_copy(
            src_ref=result.at[part, target],
            dst_ref=out_place(sender, part),
            send_sem=out_sends.at[part, target],
            recv_sem=out_arrivals.at[part, sender],
            device_id=(b, target),
            device_id_type=MESH,
        )

    owns = []
    for part in range(parts):
        for k in range(1, groups):
            heads_copy(s, lax.rem(s + k, groups), part).wait_recv()

        def one_block(k, carry, part=part):
            place = lax.rem(s + k, groups)
            for h in range(heads // parts):
                base = part * span + h * 3 * HD
                query = whole_ref[rows_of(place), base : base + HD]
                key = whole_ref[:, base + HD : base + 2 * HD]
                value = whole_ref[:, base + 2 * HD : base + 3 * HD]
                scores = times_transposed(query, key)
                scores = jnp.where(valid, scores, MASKED_SCORE)
                exp_scores = jnp.exp(scores - jnp.max(scores, axis=-1, keepdims=True))
                share = 1.0 / jnp.sum(exp_scores, axis=-1, keepdims=True)
                probs = (exp_scores * share).astype(jnp.bfloat16)
                mixed = jnp.dot(probs, value, preferred_element_type=jnp.float32)
                result[part, place, :, h * HD : (h + 1) * HD] = mixed.astype(jnp.bfloat16)

            @pl.when(k < groups)
            def _():
                result_copy(place, s, part).start()

            return carry

        lax.fori_loop(1, groups + 1, one_block, 0)
        owns.append(pltpu.make_async_copy(result.at[part, s], out_place(s, part), own_sem.at[part]))
        owns[-1].start()
    for part in range(parts):
        for k in range(1, groups):
            other = lax.rem(s + k, groups)
            heads_copy(other, s, part).wait_send()
            result_copy(other, s, part).wait_send()
            result_copy(s, other, part).wait_recv()
    for own in owns:
        own.wait()
    side.wait()


def greet_seq(groups, s, b, side):
    greet([(b, lax.rem(s + k, groups)) for k in range(1, groups)] + side.peers(s, b))


def partner_lanes(values):
    lanes = lax.broadcasted_iota(jnp.int32, values.shape, 1)
    return jnp.where(
        lanes % HD < HD // 2,
        pltpu.roll(values, 128 - HD // 2, 1),
        pltpu.roll(values, HD // 2, 1),
    )


def attend(qkv_rows, length, cosine, sine, side):
    groups = lax.axis_size("seq")
    frames = qkv_rows.shape[0]
    heads = HEADS // groups
    width = heads * HD
    signs = jnp.where(jnp.arange(HD) < HD // 2, -1.0, 1.0)
    cos_head = jnp.concatenate([cosine, cosine], axis=1)
    sin_head = jnp.concatenate([sine, sine], axis=1) * signs
    ones, zeros = jnp.ones_like(cos_head), jnp.zeros_like(cos_head)
    cos_pair = jnp.concatenate([cos_head * 0.125, cos_head, ones] * 2, axis=1)
    sin_pair = jnp.concatenate([sin_head * 0.125, sin_head, zeros] * 2, axis=1)
    cos_three = jnp.stack([cos_pair[:, 128 * i : 128 * (i + 1)] for i in range(3)])
    sin_three = jnp.stack([sin_pair[:, 128 * i : 128 * (i + 1)] for i in range(3)])
    parts = heads // 2 if heads % 2 == 0 else 1
    direct = width // parts % 128 == 0
    out_shape = (frames, groups * width) if direct else (groups, frames, width)
    total = frames * groups
    vmem = pl.BlockSpec(memory_space=pltpu.VMEM)
    whole, out, *brought = pl.pallas_call(
        functools.partial(attend_kernel, groups, heads, side),
        out_shape=(
            jax.ShapeDtypeStruct((total, 3 * width), jnp.bfloat16),
            jax.ShapeDtypeStruct(out_shape, jnp.bfloat16),
            *side.outs,
        ),
        in_specs=[pl.BlockSpec(memory_space=pltpu.SMEM), vmem, vmem, vmem]
        + [pl.BlockSpec(memory_space=pl.ANY)] * len(side.inputs),
        out_specs=(vmem, *[pl.BlockSpec(memory_space=pl.ANY)] * (1 + len(side.outs))),
        scratch_shapes=[
            pltpu.VMEM((parts, groups, frames, 3 * width // parts), jnp.bfloat16),
            pltpu.VMEM((parts, groups, frames, width // parts), jnp.bfloat16),
            pltpu.SemaphoreType.DMA((parts, groups)),
            pltpu.SemaphoreType.DMA((parts, groups)),
            pltpu.SemaphoreType.DMA((parts, groups)),
            pltpu.SemaphoreType.DMA((parts, groups)),
            pltpu.SemaphoreType.DMA((parts,)),
            *side.scratch,
        ],
        compiler_params=pltpu.CompilerParams(
            collective_id=4, has_side_effects=True, vmem_limit_bytes=20 << 20
        ),
        cost_estimate=pl.CostEstimate(
            flops=4 * heads * HD * total * total,
            bytes_accessed=4 * qkv_rows.size + 2 * total * 4 * width,
            transcendentals=heads * total * total,
        ),
    )(length.reshape(1), qkv_rows, cos_three, sin_three, *side.inputs)
    if not direct:
        out = out.transpose(1, 0, 2).reshape(frames, groups * width)
    return whole, out, brought


def attend_back_kernel(groups, heads, side, *refs):
    refs = list(refs)

    def take(count):
        taken = refs[:count]
        del refs[:count]
        return taken

    length_ref, whole_ref, grad_ref, cos_ref, sin_ref = take(5)
    side_in = take(len(side.inputs))
    (out_ref,) = take(1)
    side_out = take(len(side.outs))
    stage, grads, result, query_key, value_total = take(5)
    sends, arrivals, out_sends, out_arrivals, own_sem = take(5)
    s, b = lax.axis_index("seq"), lax.axis_index("batch")
    frames = grad_ref.shape[0]
    total_frames = whole_ref.shape[0]
    block = heads * 3 * HD
    width = heads * HD
    greet_seq(groups, s, b, side)
    side.start(side_in, side_out, refs, s, b)

    def rows_of(place):
        return pl.ds(pl.multiple_of(place * frames, frames), frames)

    def grad_copy(target, sender):
        return pltpu.make_async_remote_copy(
            src_ref=stage.at[target],
            dst_ref=grads.at[rows_of(sender)],
            send_sem=sends.at[target],
            recv_sem=arrivals.at[sender],
            device_id=(b, target),
            device_id_type=MESH,
        )

    for place in range(groups):
        stage[place] = grad_ref[:, place * width : (place + 1) * width]

        @pl.when(s != place)
        def _():
            grad_copy(place, s).start()

        @pl.when(s == place)
        def _():
            grads[rows_of(s), :] = stage[place]

    part_heads = 2 if heads % 2 == 0 else heads
    parts = heads // part_heads
    span = part_heads * 3 * HD

    def out_place(owner, part):
        if block % 128 == 0:
            start = pl.multiple_of(owner * block + part * span, 128)
            return out_ref.at[:, pl.ds(start, span)]
        return out_ref.at[owner, :, pl.ds(part * span, span)]

    def result_copy(target, sender, part):
        return pltpu.make_async_remote_copy(
            src_ref=result.at[part, rows_of(target)],
            dst_ref=out_place(sender, part),
            send_sem=out_sends.at[part, target],
            recv_sem=out_arrivals.at[part, sender],
            device_id=(b, target),
            device_id_type=MESH,
        )

    valid = lax.broadcasted_iota(jnp.int32, (total_frames, 1), 0) < length_ref[0]
    for h in range(heads):
        base = h * 3 * HD
        key = whole_ref[:, base + HD : base + 2 * HD]
        key_turned = key.T
        value = whole_ref[:, base + 2 * HD : base + 3 * HD]
        query_key[...] = jnp.zeros_like(query_key)
        value_total[...] = jnp.zeros_like(value_total)

        def one_block(k, carry, h=h, base=base, key=key, key_turned=key_turned, value=value):
            place = lax.rem(s + k, groups)
            if h == 0:

                @pl.when(k > 0)
                def _():
                    grad_copy(s, place).wait_recv()

            query = whole_ref[rows_of(place), base : base + HD]
            grad = grads[rows_of(place), h * HD : (h + 1) * HD]
            scores = jnp.where(valid, times_transposed(key, query), MASKED_SCORE)
            exp_scores = jnp.exp(scores - jnp.max(scores, axis=0, keepdims=True))
            probs = exp_scores * (1.0 / jnp.sum(exp_scores, axis=0, keepdims=True))
            value_total[...] += jnp.dot(
                probs.astype(jnp.bfloat16), grad, preferred_element_type=jnp.float32
            )
            grad_probs = times_transposed(value, grad)
            mean = jnp.sum(probs * grad_probs, axis=0, keepdims=True)
            grad_scores = (probs * (grad_probs - mean)).astype(jnp.bfloat16)
            query_key[:, HD:] += jnp.dot(grad_scores, query, preferred_element_type=jnp.float32)
            query_key[rows_of(place), :HD] = jnp.dot(
                key_turned, grad_scores, preferred_element_type=jnp.float32
            ).T
            return carry

        lax.fori_loop(0, groups, one_block, 0)
        part, inside = h // part_heads, (h % part_heads) * 3 * HD
        both = query_key[...]
        turned = both * cos_ref[...] + partner_lanes(both) * sin_ref[...]
        result[part, :, inside : inside + 2 * HD] = turned.astype(jnp.bfloat16)
        result[part, :, inside + 2 * HD : inside + 3 * HD] = value_total[...].astype(jnp.bfloat16)
        if (h + 1) % part_heads == 0:
            for k in range(1, groups):
                result_copy(lax.rem(s + k, groups), s, part).start()
    owns = []
    for part in range(parts):
        owns.append(
            pltpu.make_async_copy(
                result.at[part, rows_of(s)], out_place(s, part), own_sem.at[part]
            )
        )
        owns[-1].start()
    for k in range(1, groups):
        other = lax.rem(s + k, groups)
        grad_copy(other, s).wait_send()
        for part in range(parts):
            result_copy(other, s, part).wait_send()
            result_copy(s, other, part).wait_recv()
    for own in owns:
        own.wait()
    side.wait()


def attend_back(whole, grad_attn, length, cosine, sine, side):
    groups = lax.axis_size("seq")
    frames = grad_attn.shape[0]
    heads = HEADS // groups
    width = heads * HD
    block = 3 * width
    total = frames * groups
    signs = jnp.where(jnp.arange(HD) < HD // 2, 1.0, -1.0)
    cos_head = jnp.concatenate([cosine, cosine], axis=1)
    sin_head = jnp.concatenate([sine, sine], axis=1) * signs
    cos_both = jnp.concatenate([cos_head * 0.125, cos_head], axis=1)
    sin_both = jnp.concatenate([sin_head * 0.125, sin_head], axis=1)
    part_heads = 2 if heads % 2 == 0 else heads
    parts = heads // part_heads
    direct = block % 128 == 0
    out_shape = (frames, groups * block) if direct else (groups, frames, block)
    vmem = pl.BlockSpec(memory_space=pltpu.VMEM)
    out, *brought = pl.pallas_call(
        functools.partial(attend_back_kernel, groups, heads, side),
        out_shape=[jax.ShapeDtypeStruct(out_shape, jnp.bfloat16), *side.outs],
        in_specs=[pl.BlockSpec(memory_space=pltpu.SMEM), vmem, vmem, vmem, vmem]
        + [pl.BlockSpec(memory_space=pl.ANY)] * len(side.inputs),
        out_specs=[pl.BlockSpec(memory_space=pl.ANY)] * (1 + len(side.outs)),
        scratch_shapes=[
            pltpu.VMEM((groups, frames, width), jnp.bfloat16),
            pltpu.VMEM((total, width), jnp.bfloat16),
            pltpu.VMEM((parts, total, part_heads * 3 * HD), jnp.bfloat16),
            pltpu.VMEM((total, 2 * HD), jnp.float32),
            pltpu.VMEM((total, HD), jnp.float32),
            pltpu.SemaphoreType.DMA((groups,)),
            pltpu.SemaphoreType.DMA((groups,)),
            pltpu.SemaphoreType.DMA((parts, groups)),
            pltpu.SemaphoreType.DMA((parts, groups)),
            pltpu.SemaphoreType.DMA((parts,)),
            *side.scratch,
        ],
        compiler_params=pltpu.CompilerParams(
            collective_id=5, has_side_effects=True, vmem_limit_bytes=24 << 20
        ),
        cost_estimate=pl.CostEstimate(
            flops=10 * heads * HD * total * total,
            bytes_accessed=2 * total * 8 * width,
            transcendentals=heads * total * total,
        ),
    )(length.reshape(1), whole, grad_attn, cos_both, sin_both, *side.inputs)
    if not direct:
        out = out.transpose(1, 0, 2).reshape(frames, groups * block)
    return out, brought


def flipped(index, places):
    for bit, flip in places:
        mine = lax.rem(index // (1 << bit), 2)
        index = index + flip * (1 - 2 * mine) * (1 << bit)
    return index


def place_of(place, steps, axis, index):
    flips = []
    for order, (name, bit) in enumerate(steps):
        if name == axis:
            flips.append((bit, lax.rem(place // (1 << (len(steps) - 1 - order)), 2)))
    return flipped(index, flips)


class Job:
    def __init__(self, parts, tall, order, far=None, gathered=None):
        self.parts, self.tall, self.far, self.gathered = parts, tall, far, gathered
        self.batches, self.groups = lax.axis_size("batch"), lax.axis_size("seq")
        bits = {
            "x": [("seq", 0)],
            "y": [("seq", k) for k in range(1, self.groups.bit_length() - 1)],
            "1": [("batch", 1)],
            "2": [("batch", k) for k in range(2, self.batches.bit_length() - 1)],
        }
        letters = order if far is None else order.replace("1", "")
        self.steps = [step for letter in letters for step in bits[letter]]
        self.sharing = 2 if far is None else 4
        self.spans = self.batches // self.sharing
        self.levels = len(self.steps)
        self.half = 1 << (self.levels - 1)
        if tall:
            ((small, big),) = parts
            self.rows = big.shape[1] // (self.batches * self.groups)
            self.widths = [small.shape[1]]
        else:
            self.rows = parts[0][0].shape[1] // self.groups
            self.widths = [big.shape[1] // self.batches for _, big in parts]
        self.cols = sum(self.widths)
        self.near_pieces = len(parts) * (self.sharing // 2 + self.spans)
        self.far_pieces = len(parts) * (self.sharing // 2 + (self.sharing - 1) * self.spans)
        if gathered is not None:
            self.near_pieces += 3
            self.far_pieces -= 3 * self.spans

    def fits(self):
        return self.rows % 128 == 0 and all(width % 128 == 0 for width in self.widths)

    def operands(self):
        extra = [array for array in (self.far, self.gathered) if array is not None]
        return [array for part in self.parts for array in part] + extra

    def flops(self):
        return sum(2 * small.size * big.shape[1] for small, big in self.parts)

    def operand_scratch(self):
        scratch, sharing = [], self.sharing
        for small, big in self.parts:
            frames = sharing * small.shape[0]
            scratch.append(pltpu.VMEM((frames, small.shape[1]), jnp.bfloat16))
            scratch.append(pltpu.VMEM((frames, big.shape[1] // sharing), jnp.bfloat16))
        return scratch + [
            pltpu.SemaphoreType.DMA((self.near_pieces,)),
            pltpu.SemaphoreType.DMA((self.far_pieces,)),
            pltpu.SemaphoreType.DMA((self.far_pieces,)),
        ]

    def step_of(self, level):
        return self.steps[self.levels - 1 - level]


def signal(peers):
    barrier = pltpu.get_barrier_semaphore()
    for peer in peers:
        pl.semaphore_signal(barrier, inc=1, device_id=peer, device_id_type=MESH)


def wait_signals(peers):
    pl.semaphore_wait(pltpu.get_barrier_semaphore(), len(peers))


def greet(peers):
    signal(peers)
    wait_signals(peers)


def sibling_of(s, b):
    return (b + 1 - 2 * lax.rem(b, 2), s)


def partner_of(s, b, step):
    axis, bit = step
    if axis == "seq":
        return (b, flipped(s, [(bit, 1)]))
    return (flipped(b, [(bit, 1)]), s)


def quarters(s, b, n):
    core, z = lax.rem(b, 2), lax.rem(b // 2, 2)
    mine, other = 2 * (2 * n + z), 2 * (2 * n + 1 - z)
    return [
        (sibling_of(s, b), mine + 1 - core),
        ((flipped(b, [(1, 1)]), s), other + core),
        ((flipped(b, [(0, 1), (1, 1)]), s), other + 1 - core),
    ]


class Side:
    def __init__(self, rows, wide):
        self.rows, self.wide = rows, wide
        batches = lax.axis_size("batch")
        self.inputs = [*rows, *wide]
        self.outs = [jax.ShapeDtypeStruct(array.shape, array.dtype) for array in rows]
        self.outs += [
            jax.ShapeDtypeStruct((3, array.shape[0], array.shape[1] // 4), array.dtype)
            for array in wide
        ]
        self.count = len(rows) + len(wide) * 3 * (batches // 4)
        self.scratch = [pltpu.SemaphoreType.DMA((self.count,))] * 2 if self.count else []

    def peers(self, s, b):
        return [peer for peer, _ in quarters(s, b, 0)] if self.count else []

    def start(self, inputs, outs, sems, s, b):
        self.copies = []

        def send(source, place, peer):
            n = len(self.copies)
            self.copies.append(
                pltpu.make_async_remote_copy(
                    src_ref=source,
                    dst_ref=place,
                    send_sem=sems[0].at[n],
                    recv_sem=sems[1].at[n],
                    device_id=peer,
                    device_id_type=MESH,
                )
            )
            self.copies[-1].start()

        for i, array in enumerate(self.rows):
            send(inputs[i], outs[i], (flipped(b, [(1, 1)]), s))
        for i, array in enumerate(self.wide, len(self.rows)):
            batches = lax.axis_size("batch")
            span = array.shape[1] // batches
            for n in range(batches // 4):
                for k, (peer, owner) in enumerate(quarters(s, b, n)):
                    columns = pl.ds(pl.multiple_of(owner * span, 128), span)
                    send(inputs[i].at[:, columns], outs[i].at[k, :, pl.ds(n * span, span)], peer)

    def wait(self):
        for copy in self.copies:
            copy.wait()


def swap_operands(job, inputs, held, s, b):
    local, moves, lands = held[2 * len(job.parts) :]
    near, far = [], []

    def bring(source, place, peer=None):
        if peer is None:
            near.append(pltpu.make_async_copy(source, place, local.at[len(near)]))
            near[-1].start()
            return
        n = len(far)
        far.append(
            pltpu.make_async_remote_copy(
                src_ref=source,
                dst_ref=place,
                send_sem=moves.at[n],
                recv_sem=lands.at[n],
                device_id=peer,
                device_id_type=MESH,
            )
        )
        far[-1].start()

    core, z = lax.rem(b, 2), lax.rem(b // 2, 2)
    sibling = sibling_of(s, b)
    for i in range(len(job.parts)):
        small_in, big_in = inputs[2 * i : 2 * i + 2]
        small, big = held[2 * i : 2 * i + 2]
        frames = small_in.shape[0]
        span = big_in.shape[1] // job.batches

        def rows(k):
            return pl.ds(k * frames, frames)

        def columns(owner):
            return pl.ds(pl.multiple_of(owner * span, 128), span)

        bring(small_in, small.at[rows(1)], sibling)
        bring(small_in, small.at[rows(0)])
        if job.far is not None:
            bring(inputs[2], small.at[rows(3)], sibling)
            bring(inputs[2], small.at[rows(2)])
        if job.gathered is not None:
            for k in range(3):
                bring(inputs[3].at[k], big.at[rows(k + 1)])
        for n in range(job.spans):
            inside = pl.ds(n * span, span)
            if job.far is None:
                bring(big_in.at[:, columns(2 * n + 1 - core)], big.at[rows(1), inside], sibling)
                bring(big_in.at[:, columns(2 * n + core)], big.at[rows(0), inside])
                continue
            if job.gathered is None:
                for k, (peer, owner) in enumerate(quarters(s, b, n)):
                    bring(big_in.at[:, columns(owner)], big.at[rows(k + 1), inside], peer)
            bring(big_in.at[:, columns(2 * (2 * n + z) + core)], big.at[rows(0), inside])
    return near, far


def wait_operands(near, far):
    for copy in near:
        copy.wait()
    for copy in far:
        copy.wait_recv()


def block_product(job, held, part, place, s, b):
    small, big = held[2 * part : 2 * part + 2]
    span = big.shape[1] // job.spans
    row = place_of(place, job.steps, "seq", s)
    col = place_of(place, job.steps, "batch", b) // job.sharing
    if job.tall:
        left = big[:, pl.ds(pl.multiple_of(col * span + row * job.rows, 128), job.rows)]
        right = small[...]
    else:
        left = small[:, pl.ds(pl.multiple_of(row * job.rows, 128), job.rows)]
        right = big[:, pl.ds(pl.multiple_of(col * span, 128), span)]
    return lax.dot_general(
        left, right, (((0,), (0,)), ((), ())), preferred_element_type=jnp.float32
    )


def columns_of(job, part):
    start = sum(job.widths[:part])
    return slice(start, start + job.widths[part])


def scatter_kernel(jobs, sequence, *refs):
    refs = list(refs)

    def take(count):
        taken = refs[:count]
        del refs[:count]
        return taken

    inputs = [take(len(job.operands())) for job in jobs]
    (rows_ref,) = take(1)
    outs = [take(len(job.parts)) for job in jobs]
    (small_total,) = take(1)
    scratch = [(take(2 * len(job.parts) + 3), *take(4)) for job in jobs]
    seq_slots, part_sum, batch_slots, small_sends, small_arrivals = take(5)
    batches, groups = jobs[0].batches, jobs[0].groups
    s, b = lax.axis_index("seq"), lax.axis_index("batch")
    peers = sum_peers(groups, batches, s, b)
    greet(peers)

    def slot_of(job, place):
        return lax.rem(place, job.half)

    def copy_of(i, place, level):
        job = jobs[i]
        _, sending, arrived, sends, recvs = scratch[i]
        return pltpu.make_async_remote_copy(
            src_ref=sending.at[slot_of(job, place)],
            dst_ref=arrived.at[place - 1],
            send_sem=sends.at[slot_of(job, place)],
            recv_sem=recvs.at[place - 1],
            device_id=partner_of(s, b, job.step_of(level)),
            device_id_type=MESH,
        )

    works = {i: swap_operands(jobs[i], inputs[i], scratch[i][0], s, b) for i in SWAPS}

    def columns(owner):
        width = part_sum.shape[1]
        return rows_ref.at[:, pl.ds(pl.multiple_of(owner * width, 128), width)]

    over_seq = spread(
        columns, seq_slots, s, peers, range(groups - 1), small_sends, small_arrivals
    )

    def block_sums(i, place, level):
        job = jobs[i]
        held, _, arrived = scratch[i][:3]
        for m in range(job.levels - 1, level, -1):
            copy_of(i, (1 << m) + place, m).wait_recv()
        totals = []
        for part in range(len(job.parts)):
            total = block_product(job, held, part, place, s, b)
            for m in range(job.levels - 1, level, -1):
                came = arrived[(1 << m) + place - 1, :, columns_of(job, part)]
                total = total + came.astype(jnp.float32)
            totals.append(total)
        return totals

    def send_block(i, place, level):
        job = jobs[i]
        totals = block_sums(i, place, level)
        if level < job.levels - 1:
            copy_of(i, place + job.half, job.levels - 1).wait_send()
        for part, total in enumerate(totals):
            scratch[i][1][slot_of(job, place), :, columns_of(job, part)] = total.astype(jnp.bfloat16)
        copy_of(i, place, level).start()

    ready = set()
    over_batch = None
    for i, level in sequence:
        job = jobs[i]
        if i not in ready:
            ready.add(i)
            wait_operands(*works[i])
        if level < 0:
            for part, total in enumerate(block_sums(i, 0, -1)):
                outs[i][part][...] = total
            continue

        def one_place(j, carry, level=level, i=i):
            send_block(i, (2 << level) - 1 - j, level)
            return carry

        lax.fori_loop(0, 1 << level, one_place, 0)
        if over_batch is None:
            part_sum[...] = over_seq()
            over_batch = spread(
                lambda owner: part_sum,
                batch_slots,
                b,
                peers,
                range(groups - 1, groups + batches - 2),
                small_sends,
                small_arrivals,
            )
    small_total[...] = over_batch()
    for i, job in enumerate(jobs):
        for copy in works[i][1]:
            copy.wait_send()
        copy_of(i, job.half, job.levels - 1).wait_send()
        for level in range(job.levels - 1):

            def one_wait(j, carry, level=level, i=i):
                copy_of(i, (1 << level) + j, level).wait_send()
                return carry

            lax.fori_loop(0, 1 << level, one_wait, 0)


def pass_kernel(count, *refs):
    for source, target in zip(refs[:count], refs[count:]):
        target[...] = source[...]


def scatter_sums(jobs, sequence, rows, collective_id):
    height, width = rows.shape
    width = width // jobs[0].groups
    if width % 128 or not all(job.fits() for job in jobs):
        total = sum_everywhere(rows, collective_id)
        share = lax.dynamic_slice_in_dim(total, lax.axis_index("seq") * width, width, axis=1)
        sums = [
            [
                owned_sum(*((big, small) if job.tall else (small, big)), job.tall, job.tall)
                for small, big in job.parts
            ]
            for job in jobs
        ]
        return sums, share
    scratch, operands, outs = [], [], []
    for job in jobs:
        block = (job.rows, job.cols)
        scratch += job.operand_scratch()
        scratch += [
            pltpu.VMEM((job.half, *block), jnp.bfloat16),
            pltpu.VMEM((2 * job.half - 1, *block), jnp.bfloat16),
            pltpu.SemaphoreType.DMA((job.half,)),
            pltpu.SemaphoreType.DMA((2 * job.half - 1,)),
        ]
        operands += job.operands()
        outs += [jax.ShapeDtypeStruct((job.rows, width), jnp.float32) for width in job.widths]
    vmem = pl.BlockSpec(memory_space=pltpu.VMEM)
    *results, share = pl.pallas_call(
        functools.partial(scatter_kernel, jobs, sequence),
        out_shape=[*outs, jax.ShapeDtypeStruct((height, width), jnp.float32)],
        in_specs=[pl.BlockSpec(memory_space=pl.ANY)] * len(operands) + [vmem],
        out_specs=[vmem] * (len(outs) + 1),
        scratch_shapes=scratch + sum_scratch(height, width),
        compiler_params=pltpu.CompilerParams(
            collective_id=collective_id, has_side_effects=True, vmem_limit_bytes=60 << 20
        ),
        cost_estimate=pl.CostEstimate(
            flops=sum(job.flops() for job in jobs), bytes_accessed=400 << 20, transcendentals=0
        ),
    )(*operands, rows)
    passes = 4
    specs = [pl.BlockSpec((out.shape[0] // passes, out.shape[1]), lambda i: (i, 0)) for out in outs]
    results = list(
        pl.pallas_call(
            functools.partial(pass_kernel, len(outs)),
            out_shape=outs,
            grid=(passes,),
            in_specs=specs,
            out_specs=specs,
            compiler_params=pltpu.CompilerParams(vmem_limit_bytes=60 << 20),
        )(*results)
    )
    return [[results.pop(0) for _ in job.parts] for job in jobs], share


def shards(
    frames_in,
    cotangent,
    levels,
    lengths,
    token_mask,
    cond_table,
    norm_gains,
    w_ffn1_up,
    w_ffn1_down,
    w_qkv,
    w_out,
    w_glu,
    conv_kernel,
    bn_gain,
    batchnorm_shift_bias,
    w_conv_out,
    w_ffn2_up,
    w_ffn2_down,
    running_mean,
    running_var,
):
    frames = frames_in.shape[1]
    model_width = frames_in.shape[2]
    ff_width = w_ffn1_up.shape[1]
    groups = lax.axis_size("seq")
    batches = lax.axis_size("batch")
    seq_index = lax.axis_index("seq")
    item_index = lax.axis_index("batch")
    seq_length = frames * groups
    level_count = cond_table.shape[0] - 1
    cond_rows = cond_table.astype(jnp.float32)
    gain_rows = norm_gains.astype(jnp.float32)
    level_hot = (jnp.arange(level_count) == levels[0] - 1).astype(jnp.float32)
    level_vector = jnp.sum(level_hot[:, None] * cond_rows[:level_count], axis=0)
    mask_column = token_mask[0].astype(jnp.float32)[:, None]
    start_rows = (
        frames_in[0].astype(jnp.float32)
        + level_vector[None, :]
        + mask_column * cond_rows[level_count][None, :]
    )
    length = lax.dynamic_slice_in_dim(lengths, item_index, 1)[0]
    positions = seq_index * frames + jnp.arange(frames)
    unpadded_rows = (positions < length).astype(jnp.float32)[:, None]
    rows_one, ffn1_state = ffn_forward(start_rows, gain_rows[0], w_ffn1_up, w_ffn1_down)
    normed_attn, attn_pull = jax.vjp(layer_norm, rows_one, gain_rows[1])
    attn_in = normed_attn.astype(jnp.bfloat16)
    qkv_rows = jnp.dot(attn_in, w_qkv, preferred_element_type=jnp.float32)
    cosine, sine_table = rope_tables(positions, HD)
    fit = (
        model_width // groups % 128 == 0
        and model_width // batches % 128 == 0
        and ff_width // (groups * batches) % 128 == 0
    )
    side = Side([ffn1_state[1], attn_in] if fit else [], [])
    whole_heads, attn_out, brought = attend(qkv_rows, length, cosine, sine_table, side)
    far_ffn1, far_attn = brought if fit else (None, None)
    rows_two = rows_one + jnp.dot(attn_out, w_out, preferred_element_type=jnp.float32)
    normed_conv, conv_pull = jax.vjp(layer_norm, rows_two, gain_rows[2])
    conv_in = normed_conv.astype(jnp.bfloat16)
    glu_pre = jnp.dot(conv_in, w_glu, preferred_element_type=jnp.float32)
    up_half = glu_pre[:, :model_width]
    glu_sig = jax.nn.sigmoid(glu_pre[:, model_width:])
    glu_low = (up_half * glu_sig * unpadded_rows).astype(jnp.bfloat16)
    taps = conv_kernel.shape[0]
    kernel_rows = conv_kernel.astype(jnp.float32)
    convolved_rows, padded, totals = convolve(glu_low, kernel_rows, length)
    total_sum, total_squares = totals[0], totals[1]
    count_of_frames = jnp.sum(lengths).astype(jnp.float32)
    batchnorm_frame_mean = total_sum / count_of_frames
    bn_var = total_squares / count_of_frames - batchnorm_frame_mean * batchnorm_frame_mean
    batchnorm_inverse_deviation = lax.rsqrt(bn_var + EPSILON)
    batchnorm_scale_factor = bn_gain.astype(jnp.float32)
    normalized_rows = (convolved_rows - batchnorm_frame_mean) * batchnorm_inverse_deviation
    batchnorm_input_rows = normalized_rows * batchnorm_scale_factor + batchnorm_shift_bias.astype(
        jnp.float32
    )
    bn_sig = jax.nn.sigmoid(batchnorm_input_rows)
    conv_act = (batchnorm_input_rows * bn_sig).astype(jnp.bfloat16)
    rows_three = rows_two + jnp.dot(conv_act, w_conv_out, preferred_element_type=jnp.float32)
    rows_four, ffn2_state = ffn_forward(rows_three, gain_rows[3], w_ffn2_up, w_ffn2_down)
    normed_out, out_pull = jax.vjp(layer_norm, rows_four, gain_rows[4])
    out_rows = normed_out.astype(jnp.bfloat16)
    grad_four, grad_gain_four = out_pull(cotangent[0].astype(jnp.float32))
    grad_three, grad_gain_three, ffn2_up_pair, ffn2_down_pair = ffn_backward(
        grad_four, ffn2_state, w_ffn2_up, w_ffn2_down
    )
    grad_r2 = grad_three.astype(jnp.bfloat16)
    batchnorm_gradient = (
        times_transposed(grad_r2, w_conv_out)
        * bn_sig
        * (1.0 + batchnorm_input_rows * (1.0 - bn_sig))
    )
    norm_rows = jnp.stack(
        [batchnorm_frame_mean, batchnorm_inverse_deviation, batchnorm_scale_factor], axis=0
    )
    grad_glu, kernel_grads, gradient_totals = convolve_back(
        batchnorm_gradient, convolved_rows, padded, kernel_rows, norm_rows, length, count_of_frames
    )
    kernel_grads = kernel_grads[:taps]
    gradient_sum_total, gradient_normalized_sum = gradient_totals[0], gradient_totals[1]
    grad_gl = jnp.concatenate(
        [grad_glu * glu_sig, grad_glu * up_half * glu_sig * (1.0 - glu_sig)], axis=1
    ).astype(jnp.bfloat16)
    grad_conv_in, grad_gain_two = conv_pull(times_transposed(grad_gl, w_glu))
    grad_two = grad_three + grad_conv_in
    grad_r = grad_two.astype(jnp.bfloat16)
    grad_attn_out = times_transposed(grad_r, w_out).astype(jnp.bfloat16)
    cos_all, sin_all = rope_tables(jnp.arange(seq_length), HD)
    side = Side([ffn2_up_pair[0]] if fit else [], [ffn2_up_pair[1]] if fit else [])
    grad_qkv, brought = attend_back(whole_heads, grad_attn_out, length, cos_all, sin_all, side)
    far_ffn2, gathered = brought if fit else (None, None)
    grad_attn_part, grad_gain_one = attn_pull(times_transposed(grad_qkv, w_qkv))
    grad_one = grad_two + grad_attn_part
    grad_zero, grad_gain_zero, ffn1_up_pair, ffn1_down_pair = ffn_backward(
        grad_one, ffn1_state, w_ffn1_up, w_ffn1_down
    )
    column_total = jnp.sum(grad_zero, axis=0)
    cond_grad_rows = jnp.concatenate(
        [
            level_hot[:, None] * column_total[None, :],
            jnp.sum(mask_column * grad_zero, axis=0)[None, :],
        ],
        axis=0,
    )
    gain_grads = jnp.stack(
        [grad_gain_zero, grad_gain_one, grad_gain_two, grad_gain_three, grad_gain_four], axis=0
    )
    small_rows = jnp.concatenate([gain_grads, cond_grad_rows, kernel_grads], axis=0)
    small_rows = jnp.pad(small_rows, ((0, -small_rows.shape[0] % 8), (0, 0)))
    jobs = [
        Job([ffn2_up_pair], False, "1yx2", far_ffn2, gathered),
        Job([ffn2_down_pair[::-1]], True, "y12x"),
        Job([(conv_in, grad_gl), (attn_out, grad_r), (conv_act, grad_r2)], False, "xy12"),
        Job([(attn_in, grad_qkv)], False, "1xy2", far_attn),
        Job([ffn1_down_pair[::-1]], True, "xy12"),
        Job([ffn1_up_pair], False, "12xy", far_ffn1),
    ]
    sums, small_piece = scatter_sums(jobs, SEGMENTS, small_rows, 7)
    cond_end = 5 + level_count + 1
    new_mean = 0.9 * running_mean + 0.1 * batchnorm_frame_mean
    new_var = 0.9 * running_var + 0.1 * bn_var * count_of_frames / (count_of_frames - 1.0)
    return (
        out_rows[None],
        grad_zero.astype(jnp.bfloat16)[None],
        small_piece[5:cond_end],
        small_piece[0:5],
        sums[5][0],
        sums[4][0],
        sums[3][0],
        sums[2][1],
        sums[2][0],
        small_piece[cond_end : cond_end + taps],
        gradient_normalized_sum,
        gradient_sum_total,
        sums[2][2],
        sums[0][0],
        sums[1][0],
        new_mean,
        new_var,
    )


def solution(mesh):
    in_specs = (
        P("batch", "seq", None),
        P("batch", "seq", None),
        P("batch"),
        P(),
        P("batch", "seq"),
        P(),
        P(),
        P(),
        P(),
        P(),
        P(),
        P(),
        P(),
        P(),
        P(),
        P(),
        P(),
        P(),
        P(),
        P(),
    )
    out_specs = (
        P("batch", "seq", None),
        P("batch", "seq", None),
        P(None, "seq"),
        P(None, "seq"),
        P("seq", "batch"),
        P(("batch", "seq"), None),
        P("seq", "batch"),
        P("seq", "batch"),
        P("seq", "batch"),
        P(None, "seq"),
        P(),
        P(),
        P("seq", "batch"),
        P("seq", "batch"),
        P(("batch", "seq"), None),
        P(),
        P(),
    )
    return jax.shard_map(shards, mesh=mesh, in_specs=in_specs, out_specs=out_specs, check_vma=False)
```

```python
import functools
import math

import jax
import jax.numpy as jnp
from jax import lax
from jax.experimental import pallas as pl
from jax.experimental.pallas import tpu as pltpu
from jax.sharding import PartitionSpec as P

MESH = pl.DeviceIdType.MESH

HEADS = 16
HD = 64


EPSILON = 1e-05
MASKED_SCORE = -1000000000.0

SEGMENTS = (
    (2, 3), (0, 2), (1, 3), (0, 1), (5, 2), (1, 2), (3, 2), (4, 3), (2, 2), (1, 1), (5, 1),
    (0, 0), (1, 0), (2, 1), (3, 1), (3, 0), (4, 2), (2, 0), (0, -1), (4, 1), (3, -1), (4, 0),
    (2, -1), (5, 0), (1, -1), (5, -1), (4, -1),
)
SWAPS = (2, 0, 4, 5, 1, 3)


def layer_norm(values, gain_row):
    centre = values - jnp.mean(values, axis=-1, keepdims=True)
    spread = jnp.mean(centre * centre, axis=-1, keepdims=True)
    return centre * lax.rsqrt(spread + EPSILON) * gain_row


def rope_tables(positions, head_size):
    half_size = head_size // 2
    inv_freqs = jnp.exp(
        jnp.arange(half_size).astype(jnp.float32) * (-2.0 * math.log(10000.0) / head_size)
    )
    angles = positions.astype(jnp.float32)[:, None] * inv_freqs[None, :]
    return (jnp.cos(angles), jnp.sin(angles))


def times_transposed(left_side, weight):
    return lax.dot_general(
        left_side, weight, (((1,), (1,)), ((), ())), preferred_element_type=jnp.float32
    )


def ffn_forward(values, gain_row, up_weight, down_weight):
    normed, ln_pull = jax.vjp(layer_norm, values, gain_row)
    lowered = normed.astype(jnp.bfloat16)
    hidden = jnp.dot(lowered, up_weight, preferred_element_type=jnp.float32)
    act_rows = (hidden * jax.nn.sigmoid(hidden)).astype(jnp.bfloat16)
    branch = jnp.dot(act_rows, down_weight, preferred_element_type=jnp.float32)
    return (values + 0.5 * branch, (ln_pull, lowered, hidden, act_rows))


def ffn_backward(grad_in, saved_state, up_weight, down_weight):
    ln_pull, lowered, hidden, act_rows = saved_state
    grad_branch = (0.5 * grad_in).astype(jnp.bfloat16)
    grad_act = times_transposed(grad_branch, down_weight)
    gate_sig = jax.nn.sigmoid(hidden)
    grad_hidden = (grad_act * gate_sig * (1.0 + hidden * (1.0 - gate_sig))).astype(jnp.bfloat16)
    grad_normed = times_transposed(grad_hidden, up_weight)
    grad_values, grad_gain = ln_pull(grad_normed)
    return (grad_in + grad_values, grad_gain, (lowered, grad_hidden), (act_rows, grad_branch))


def sum_peers(groups, batches, s, b):
    peers = [(b, lax.rem(s + k, groups)) for k in range(1, groups)]
    return peers + [(lax.rem(b + k, batches), s) for k in range(1, batches)]


def spread(pick, slots, mine, peers, span, sends, arrivals):
    slots[mine] = pick(mine)[...]
    copies = []
    for k in span:
        copies.append(
            pltpu.make_async_remote_copy(
                src_ref=pick(peers[k][1]),
                dst_ref=slots.at[mine],
                send_sem=sends.at[k],
                recv_sem=arrivals.at[k],
                device_id=peers[k],
                device_id_type=MESH,
            )
        )
        copies[-1].start()

    def finish():
        for copy in copies:
            copy.wait()
        total = slots[0]
        for i in range(1, len(copies) + 1):
            total = total + slots[i]
        return total

    return finish


def sum_kernel(groups, batches, rows_ref, total_ref, seq_slots, part, batch_slots, sends, arrivals):
    s, b = lax.axis_index("seq"), lax.axis_index("batch")
    peers = sum_peers(groups, batches, s, b)
    greet(peers)
    first = range(groups - 1)
    second = range(groups - 1, groups + batches - 2)
    part[...] = spread(lambda owner: rows_ref, seq_slots, s, peers, first, sends, arrivals)()
    total_ref[...] = spread(lambda owner: part, batch_slots, b, peers, second, sends, arrivals)()


def sum_scratch(height, width):
    groups, batches = lax.axis_size("seq"), lax.axis_size("batch")
    return [
        pltpu.VMEM((groups, height, width), jnp.float32),
        pltpu.VMEM((height, width), jnp.float32),
        pltpu.VMEM((batches, height, width), jnp.float32),
        pltpu.SemaphoreType.DMA((groups + batches - 2,)),
        pltpu.SemaphoreType.DMA((groups + batches - 2,)),
    ]


def sum_everywhere(rows, collective_id):
    groups, batches = lax.axis_size("seq"), lax.axis_size("batch")
    return pl.pallas_call(
        functools.partial(sum_kernel, groups, batches),
        out_shape=jax.ShapeDtypeStruct(rows.shape, jnp.float32),
        in_specs=[pl.BlockSpec(memory_space=pltpu.VMEM)],
        out_specs=pl.BlockSpec(memory_space=pltpu.VMEM),
        scratch_shapes=sum_scratch(*rows.shape),
        compiler_params=pltpu.CompilerParams(
            collective_id=collective_id, has_side_effects=True, vmem_limit_bytes=4 << 20
        ),
    )(rows)


def edge_copies(groups, s, b, rows_ref, before, after, tile, sends, arrivals, first):
    up = pltpu.make_async_remote_copy(
        src_ref=rows_ref.at[pl.ds(rows_ref.shape[0] - tile, tile)],
        dst_ref=before,
        send_sem=sends.at[first],
        recv_sem=arrivals.at[first],
        device_id=(b, lax.rem(s + 1, groups)),
        device_id_type=MESH,
    )
    down = pltpu.make_async_remote_copy(
        src_ref=rows_ref.at[pl.ds(0, tile)],
        dst_ref=after,
        send_sem=sends.at[first + 1],
        recv_sem=arrivals.at[first + 1],
        device_id=(b, lax.rem(s + groups - 1, groups)),
        device_id_type=MESH,
    )
    return up, down


def start_edges(groups, s, copies):
    @pl.when(s < groups - 1)
    def _():
        for up, _ in copies:
            up.start()

    @pl.when(s > 0)
    def _():
        for _, down in copies:
            down.start()


def wait_edges_sent(groups, s, copies):
    @pl.when(s < groups - 1)
    def _():
        for up, _ in copies:
            up.wait_send()

    @pl.when(s > 0)
    def _():
        for _, down in copies:
            down.wait_send()


def valid_rows(first, count, length):
    positions = first + lax.broadcasted_iota(jnp.int32, (count, 1), 0)
    return (positions < length).astype(jnp.float32)


def convolve_kernel(
    groups, batches, taps, length_ref, glu_ref, kernel_ref, out_ref, padded_ref, total_ref,
    before, after, local, edge_sends, edge_arrivals, seq_slots, part, batch_slots, sends, arrivals,
):
    s, b = lax.axis_index("seq"), lax.axis_index("batch")
    peers = sum_peers(groups, batches, s, b)
    signal(peers)
    frames, width = glu_ref.shape
    padded_ref[8 : 8 + frames, :] = glu_ref[...].astype(jnp.float32)
    wait_signals(peers)
    edges = [edge_copies(groups, s, b, glu_ref, before, after, 16, edge_sends, edge_arrivals, 0)]
    start_edges(groups, s, edges)

    @pl.when(s > 0)
    def _():
        edges[0][0].wait_recv()
        padded_ref[0:8, :] = before[8:16, :].astype(jnp.float32)

    @pl.when(s == 0)
    def _():
        padded_ref[0:8, :] = jnp.zeros((8, width), jnp.float32)

    @pl.when(s < groups - 1)
    def _():
        edges[0][1].wait_recv()
        padded_ref[8 + frames :, :] = after[0:8, :].astype(jnp.float32)

    @pl.when(s == groups - 1)
    def _():
        padded_ref[8 + frames :, :] = jnp.zeros((8, width), jnp.float32)

    valid = valid_rows(s * frames, frames, length_ref[0])
    for column in range(0, width, 128):
        lanes = slice(column, column + 128)
        total = jnp.zeros((frames, 128), jnp.float32)
        for k in range(taps):
            start = 8 - taps // 2 + k
            total = total + kernel_ref[k : k + 1, lanes] * padded_ref[start : start + frames, lanes]
        out_ref[:, lanes] = total
        kept = total * valid
        local[0:1, lanes] = jnp.sum(kept, axis=0, keepdims=True)
        local[1:2, lanes] = jnp.sum(kept * total, axis=0, keepdims=True)
    first, second = range(groups - 1), range(groups - 1, groups + batches - 2)
    part[...] = spread(lambda owner: local, seq_slots, s, peers, first, sends, arrivals)()
    total_ref[...] = spread(lambda owner: part, batch_slots, b, peers, second, sends, arrivals)()
    wait_edges_sent(groups, s, edges)


def convolve(glu_low, kernel_rows, length):
    groups, batches = lax.axis_size("seq"), lax.axis_size("batch")
    frames, width = glu_low.shape
    taps = kernel_rows.shape[0]
    vmem = pl.BlockSpec(memory_space=pltpu.VMEM)
    return pl.pallas_call(
        functools.partial(convolve_kernel, groups, batches, taps),
        out_shape=[
            jax.ShapeDtypeStruct((frames, width), jnp.float32),
            jax.ShapeDtypeStruct((frames + 16, width), jnp.float32),
            jax.ShapeDtypeStruct((2, width), jnp.float32),
        ],
        in_specs=[pl.BlockSpec(memory_space=pltpu.SMEM), vmem, vmem],
        out_specs=[vmem] * 3,
        scratch_shapes=[
            pltpu.VMEM((16, width), jnp.bfloat16),
            pltpu.VMEM((16, width), jnp.bfloat16),
            pltpu.VMEM((2, width), jnp.float32),
            pltpu.SemaphoreType.DMA((2,)),
            pltpu.SemaphoreType.DMA((2,)),
            *sum_scratch(2, width),
        ],
        compiler_params=pltpu.CompilerParams(
            collective_id=1, has_side_effects=True, vmem_limit_bytes=8 << 20
        ),
    )(length.reshape(1), glu_low, kernel_rows)


def convolve_back_kernel(
    groups, batches, taps, length_ref, count_ref, grad_ref, conv_ref, padded_ref, kernel_ref, norm_ref,
    out_ref, taps_ref, total_ref, edge_rows, spread_rows, local, edge_sends, edge_arrivals,
    seq_slots, part, batch_slots, sends, arrivals,
):
    s, b = lax.axis_index("seq"), lax.axis_index("batch")
    peers = sum_peers(groups, batches, s, b)
    signal(peers)
    frames, width = grad_ref.shape

    def normalized(values, lanes):
        return (values - norm_ref[0:1, lanes]) * norm_ref[1:2, lanes]

    for column in range(0, width, 128):
        lanes = slice(column, column + 128)
        grads = grad_ref[:, lanes]
        local[0:1, lanes] = jnp.sum(grads, axis=0, keepdims=True)
        local[1:2, lanes] = jnp.sum(
            grads * normalized(conv_ref[:, lanes], lanes), axis=0, keepdims=True
        )
    wait_signals(peers)
    edges = [
        edge_copies(
            groups, s, b, ref, edge_rows.at[2 * i], edge_rows.at[2 * i + 1], 8,
            edge_sends, edge_arrivals, 2 * i,
        )
        for i, ref in enumerate((grad_ref, conv_ref))
    ]
    start_edges(groups, s, edges)
    first, second = range(groups - 1), range(groups - 1, groups + batches - 2)
    part[...] = spread(lambda owner: local, seq_slots, s, peers, first, sends, arrivals)()
    total_ref[...] = spread(lambda owner: part, batch_slots, b, peers, second, sends, arrivals)()

    length = length_ref[0]
    share = 1.0 / count_ref[0]

    def conv_grad(grads, values, valid, lanes):
        sums = total_ref[0:1, lanes] + normalized(values, lanes) * total_ref[1:2, lanes]
        rows = norm_ref[2:3, lanes] * norm_ref[1:2, lanes] * (grads - valid * sums * share)
        return rows.astype(jnp.bfloat16).astype(jnp.float32)

    @pl.when(s > 0)
    def _():
        for up, _ in edges:
            up.wait_recv()
        spread_rows[0:8, :] = conv_grad(
            edge_rows[0], edge_rows[2], valid_rows(s * frames - 8, 8, length), slice(None)
        )

    @pl.when(s == 0)
    def _():
        spread_rows[0:8, :] = jnp.zeros((8, width), jnp.float32)

    @pl.when(s < groups - 1)
    def _():
        for _, down in edges:
            down.wait_recv()
        spread_rows[8 + frames :, :] = conv_grad(
            edge_rows[1], edge_rows[3], valid_rows((s + 1) * frames, 8, length), slice(None)
        )

    @pl.when(s == groups - 1)
    def _():
        spread_rows[8 + frames :, :] = jnp.zeros((8, width), jnp.float32)

    valid = valid_rows(s * frames, frames, length)
    taps_ref[...] = jnp.zeros_like(taps_ref)
    for column in range(0, width, 128):
        lanes = slice(column, column + 128)
        own = conv_grad(grad_ref[:, lanes], conv_ref[:, lanes], valid, lanes)
        spread_rows[8 : 8 + frames, lanes] = own
        total = jnp.zeros((frames, 128), jnp.float32)
        for k in range(taps):
            start = 8 + taps // 2 - k
            total = total + kernel_ref[k : k + 1, lanes] * spread_rows[start : start + frames, lanes]
            start = 8 - taps // 2 + k
            taps_ref[k : k + 1, lanes] = jnp.sum(
                padded_ref[start : start + frames, lanes] * own, axis=0, keepdims=True
            )
        out_ref[:, lanes] = total * valid
    wait_edges_sent(groups, s, edges)


def convolve_back(grads, convolved, padded, kernel_rows, norm_rows, length, count):
    groups, batches = lax.axis_size("seq"), lax.axis_size("batch")
    frames, width = grads.shape
    taps = kernel_rows.shape[0]
    vmem, smem = pl.BlockSpec(memory_space=pltpu.VMEM), pl.BlockSpec(memory_space=pltpu.SMEM)
    return pl.pallas_call(
        functools.partial(convolve_back_kernel, groups, batches, taps),
        out_shape=[
            jax.ShapeDtypeStruct((frames, width), jnp.float32),
            jax.ShapeDtypeStruct((8, width), jnp.float32),
            jax.ShapeDtypeStruct((2, width), jnp.float32),
        ],
        in_specs=[smem, smem, vmem, vmem, vmem, vmem, vmem],
        out_specs=[vmem] * 3,
        scratch_shapes=[
            pltpu.VMEM((4, 8, width), jnp.float32),
            pltpu.VMEM((frames + 16, width), jnp.float32),
            pltpu.VMEM((2, width), jnp.float32),
            pltpu.SemaphoreType.DMA((4,)),
            pltpu.SemaphoreType.DMA((4,)),
            *sum_scratch(2, width),
        ],
        compiler_params=pltpu.CompilerParams(
            collective_id=2, has_side_effects=True, vmem_limit_bytes=12 << 20
        ),
    )(length.reshape(1), count.reshape(1), grads, convolved, padded, kernel_rows, norm_rows)


def halving_steps(first_seq):
    seq_bits = [("seq", k) for k in range(lax.axis_size("seq").bit_length() - 1)]
    batch_bits = [("batch", k) for k in range(1, lax.axis_size("batch").bit_length() - 1)]
    if first_seq:
        seq_bits = seq_bits[::-1]
    return [("batch", 0)] + seq_bits + batch_bits


def relative_place(place, steps, axis):
    flips = 0
    for order, (name, bit) in enumerate(steps):
        if name == axis:
            flips = flips | (((place >> (len(steps) - 1 - order)) & 1) << bit)
    return flips


def product_kernel(steps, tall, rows, cols, group, where, left_ref, right_ref, out_ref):
    step = pl.program_id(0)
    for inner in range(group):
        place = step * group + inner
        b = where[0] ^ relative_place(place, steps, "batch")
        s = where[1] ^ relative_place(place, steps, "seq")
        if tall:
            left = left_ref[:, pl.ds(pl.multiple_of((b * lax.axis_size("seq") + s) * rows, rows), rows)]
            right = right_ref[...]
        else:
            left = left_ref[:, pl.ds(pl.multiple_of(s * rows, rows), rows)]
            right = right_ref[:, pl.ds(pl.multiple_of(b * cols, cols), cols)]
        out_ref[inner] = lax.dot_general(
            left, right, (((0,), (0,)), ((), ())), preferred_element_type=jnp.float32
        ).astype(jnp.bfloat16)


def block_products(left, right, tall, steps):
    batches, groups = lax.axis_size("batch"), lax.axis_size("seq")
    places = batches * groups
    if tall:
        rows, cols = left.shape[1] // places, right.shape[1]
    else:
        rows, cols = left.shape[1] // groups, right.shape[1] // batches
    me = jnp.stack([lax.axis_index("batch"), lax.axis_index("seq")]).astype(jnp.int32)
    if rows % 128 == 0 and cols % 128 == 0:
        group = 4
        return pl.pallas_call(
            functools.partial(product_kernel, steps, tall, rows, cols, group),
            out_shape=jax.ShapeDtypeStruct((places, rows, cols), jnp.bfloat16),
            grid_spec=pltpu.PrefetchScalarGridSpec(
                num_scalar_prefetch=1,
                grid=(places // group,),
                in_specs=[
                    pl.BlockSpec(left.shape, lambda i, where: (0, 0)),
                    pl.BlockSpec(right.shape, lambda i, where: (0, 0)),
                ],
                out_specs=pl.BlockSpec((group, rows, cols), lambda i, where: (i, 0, 0)),
            ),
            compiler_params=pltpu.CompilerParams(vmem_limit_bytes=40 << 20),
            cost_estimate=pl.CostEstimate(
                flops=2 * left.shape[0] * left.shape[1] * right.shape[1],
                bytes_accessed=2 * (left.size + right.size + left.shape[1] * right.shape[1]),
                transcendentals=0,
            ),
        )(me, left, right)
    whole = lax.dot_general(
        left, right, (((0,), (0,)), ((), ())), preferred_element_type=jnp.float32
    ).astype(jnp.bfloat16)
    if tall:
        blocks = whole.reshape(batches, groups, rows, cols)
    else:
        blocks = whole.reshape(groups, rows, batches, cols).transpose(2, 0, 1, 3)
    batch_bits, seq_bits = batches.bit_length() - 1, groups.bit_length() - 1
    blocks = blocks.reshape((2,) * (batch_bits + seq_bits) + (rows, cols))
    dims = []
    for name, bit in steps:
        dim = batch_bits - 1 - bit if name == "batch" else batch_bits + seq_bits - 1 - bit
        mine = (me[0] if name == "batch" else me[1]) >> bit & 1
        blocks = jnp.where(mine == 1, jnp.flip(blocks, dim), blocks)
        dims.append(dim)
    return blocks.transpose(*dims, len(dims), len(dims) + 1).reshape(places, rows, cols)


def owned_sum(left, right, tall, first_seq):
    steps = halving_steps(first_seq)
    blocks = block_products(left, right, tall, steps)
    for axis, bit in steps:
        half = blocks.shape[0] // 2
        pairs = [(i, i ^ (1 << bit)) for i in range(lax.axis_size(axis))]
        arrived = lax.ppermute(blocks[half:], axis, pairs)
        total = blocks[:half].astype(jnp.float32) + arrived.astype(jnp.float32)
        blocks = total.astype(jnp.bfloat16) if half > 1 else total
    return blocks[0]


def attend_kernel(groups, heads, side, *refs):
    refs = list(refs)

    def take(count):
        taken = refs[:count]
        del refs[:count]
        return taken

    length_ref, qkv_ref, cos_ref, sin_ref = take(4)
    side_in = take(len(side.inputs))
    whole_ref, out_ref = take(2)
    side_out = take(len(side.outs))
    stage, result, sends, arrivals, out_sends, out_arrivals, own_sem = take(7)
    s, b = lax.axis_index("seq"), lax.axis_index("batch")
    frames = qkv_ref.shape[0]
    total_frames = whole_ref.shape[0]
    block = heads * 3 * HD
    width = heads * HD
    parts = stage.shape[0]
    span, narrow = block // parts, width // parts
    greet_seq(groups, s, b, side)
    side.start(side_in, side_out, refs, s, b)

    def rows_of(place):
        return pl.ds(pl.multiple_of(place * frames, frames), frames)

    def heads_copy(target, sender, part):
        return pltpu.make_async_remote_copy(
            src_ref=stage.at[part, target],
            dst_ref=whole_ref.at[rows_of(sender), pl.ds(part * span, span)],
            send_sem=sends.at[part, target],
            recv_sem=arrivals.at[part, sender],
            device_id=(b, target),
            device_id_type=MESH,
        )

    columns = range(0, groups * block, 128)
    for column in sorted(columns, key=lambda c: (c % block // span if parts > 1 else 0, c)):
        pattern = (column // 128) % 3
        values = qkv_ref[:, column : column + 128]
        turned = (values * cos_ref[pattern] + partner_lanes(values) * sin_ref[pattern]).astype(
            jnp.bfloat16
        )
        start = column
        while start < column + 128:
            place, part = start // block, start % block // span
            first = place * block + part * span
            end = min(column + 128, first + span)
            stage[part, place, :, start - first : end - first] = turned[
                :, start - column : end - column
            ]
            if end == first + span:

                @pl.when(s != place)
                def _():
                    heads_copy(place, s, part).start()

                @pl.when(s == place)
                def _():
                    whole_ref[rows_of(s), part * span : (part + 1) * span] = stage[part, place]

            start = end

    valid = lax.broadcasted_iota(jnp.int32, (1, total_frames), 1) < length_ref[0]

    def out_place(owner, part):
        if narrow % 128 == 0:
            start = pl.multiple_of(owner * width + part * narrow, 128)
            return out_ref.at[:, pl.ds(start, narrow)]
        return out_ref.at[owner]

    def result_copy(target, sender, part):
        return pltpu.make_async_remote_copy(
            src_ref=result.at[part, target],
            dst_ref=out_place(sender, part),
            send_sem=out_sends.at[part, target],
            recv_sem=out_arrivals.at[part, sender],
            device_id=(b, target),
            device_id_type=MESH,
        )

    owns = []
    for part in range(parts):
        for k in range(1, groups):
            heads_copy(s, lax.rem(s + k, groups), part).wait_recv()

        def one_block(k, carry, part=part):
            place = lax.rem(s + k, groups)
            for h in range(heads // parts):
                base = part * span + h * 3 * HD
                query = whole_ref[rows_of(place), base : base + HD]
                key = whole_ref[:, base + HD : base + 2 * HD]
                value = whole_ref[:, base + 2 * HD : base + 3 * HD]
                scores = times_transposed(query, key)
                scores = jnp.where(valid, scores, MASKED_SCORE)
                exp_scores = jnp.exp(scores - jnp.max(scores, axis=-1, keepdims=True))
                share = 1.0 / jnp.sum(exp_scores, axis=-1, keepdims=True)
                probs = (exp_scores * share).astype(jnp.bfloat16)
                mixed = jnp.dot(probs, value, preferred_element_type=jnp.float32)
                result[part, place, :, h * HD : (h + 1) * HD] = mixed.astype(jnp.bfloat16)

            @pl.when(k < groups)
            def _():
                result_copy(place, s, part).start()

            return carry

        lax.fori_loop(1, groups + 1, one_block, 0)
        owns.append(pltpu.make_async_copy(result.at[part, s], out_place(s, part), own_sem.at[part]))
        owns[-1].start()
    for part in range(parts):
        for k in range(1, groups):
            other = lax.rem(s + k, groups)
            heads_copy(other, s, part).wait_send()
            result_copy(other, s, part).wait_send()
            result_copy(s, other, part).wait_recv()
    for own in owns:
        own.wait()
    side.wait()


def greet_seq(groups, s, b, side):
    greet([(b, lax.rem(s + k, groups)) for k in range(1, groups)] + side.peers(s, b))


def partner_lanes(values):
    lanes = lax.broadcasted_iota(jnp.int32, values.shape, 1)
    return jnp.where(
        lanes % HD < HD // 2,
        pltpu.roll(values, 128 - HD // 2, 1),
        pltpu.roll(values, HD // 2, 1),
    )


def attend(qkv_rows, length, cosine, sine, side):
    groups = lax.axis_size("seq")
    frames = qkv_rows.shape[0]
    heads = HEADS // groups
    width = heads * HD
    signs = jnp.where(jnp.arange(HD) < HD // 2, -1.0, 1.0)
    cos_head = jnp.concatenate([cosine, cosine], axis=1)
    sin_head = jnp.concatenate([sine, sine], axis=1) * signs
    ones, zeros = jnp.ones_like(cos_head), jnp.zeros_like(cos_head)
    cos_pair = jnp.concatenate([cos_head * 0.125, cos_head, ones] * 2, axis=1)
    sin_pair = jnp.concatenate([sin_head * 0.125, sin_head, zeros] * 2, axis=1)
    cos_three = jnp.stack([cos_pair[:, 128 * i : 128 * (i + 1)] for i in range(3)])
    sin_three = jnp.stack([sin_pair[:, 128 * i : 128 * (i + 1)] for i in range(3)])
    parts = heads // 2 if heads % 2 == 0 else 1
    direct = width // parts % 128 == 0
    out_shape = (frames, groups * width) if direct else (groups, frames, width)
    total = frames * groups
    vmem = pl.BlockSpec(memory_space=pltpu.VMEM)
    whole, out, *brought = pl.pallas_call(
        functools.partial(attend_kernel, groups, heads, side),
        out_shape=(
            jax.ShapeDtypeStruct((total, 3 * width), jnp.bfloat16),
            jax.ShapeDtypeStruct(out_shape, jnp.bfloat16),
            *side.outs,
        ),
        in_specs=[pl.BlockSpec(memory_space=pltpu.SMEM), vmem, vmem, vmem]
        + [pl.BlockSpec(memory_space=pl.ANY)] * len(side.inputs),
        out_specs=(vmem, *[pl.BlockSpec(memory_space=pl.ANY)] * (1 + len(side.outs))),
        scratch_shapes=[
            pltpu.VMEM((parts, groups, frames, 3 * width // parts), jnp.bfloat16),
            pltpu.VMEM((parts, groups, frames, width // parts), jnp.bfloat16),
            pltpu.SemaphoreType.DMA((parts, groups)),
            pltpu.SemaphoreType.DMA((parts, groups)),
            pltpu.SemaphoreType.DMA((parts, groups)),
            pltpu.SemaphoreType.DMA((parts, groups)),
            pltpu.SemaphoreType.DMA((parts,)),
            *side.scratch,
        ],
        compiler_params=pltpu.CompilerParams(
            collective_id=4, has_side_effects=True, vmem_limit_bytes=20 << 20
        ),
        cost_estimate=pl.CostEstimate(
            flops=4 * heads * HD * total * total,
            bytes_accessed=4 * qkv_rows.size + 2 * total * 4 * width,
            transcendentals=heads * total * total,
        ),
    )(length.reshape(1), qkv_rows, cos_three, sin_three, *side.inputs)
    if not direct:
        out = out.transpose(1, 0, 2).reshape(frames, groups * width)
    return whole, out, brought


def attend_back_kernel(groups, heads, side, *refs):
    refs = list(refs)

    def take(count):
        taken = refs[:count]
        del refs[:count]
        return taken

    length_ref, whole_ref, grad_ref, cos_ref, sin_ref = take(5)
    side_in = take(len(side.inputs))
    (out_ref,) = take(1)
    side_out = take(len(side.outs))
    stage, grads, result, query_key, value_total = take(5)
    sends, arrivals, out_sends, out_arrivals, own_sem = take(5)
    s, b = lax.axis_index("seq"), lax.axis_index("batch")
    frames = grad_ref.shape[0]
    total_frames = whole_ref.shape[0]
    block = heads * 3 * HD
    width = heads * HD
    greet_seq(groups, s, b, side)
    side.start(side_in, side_out, refs, s, b)

    def rows_of(place):
        return pl.ds(pl.multiple_of(place * frames, frames), frames)

    def grad_copy(target, sender):
        return pltpu.make_async_remote_copy(
            src_ref=stage.at[target],
            dst_ref=grads.at[rows_of(sender)],
            send_sem=sends.at[target],
            recv_sem=arrivals.at[sender],
            device_id=(b, target),
            device_id_type=MESH,
        )

    for place in range(groups):
        stage[place] = grad_ref[:, place * width : (place + 1) * width]

        @pl.when(s != place)
        def _():
            grad_copy(place, s).start()

        @pl.when(s == place)
        def _():
            grads[rows_of(s), :] = stage[place]

    part_heads = 2 if heads % 2 == 0 else heads
    parts = heads // part_heads
    span = part_heads * 3 * HD

    def out_place(owner, part):
        if block % 128 == 0:
            start = pl.multiple_of(owner * block + part * span, 128)
            return out_ref.at[:, pl.ds(start, span)]
        return out_ref.at[owner, :, pl.ds(part * span, span)]

    def result_copy(target, sender, part):
        return pltpu.make_async_remote_copy(
            src_ref=result.at[part, rows_of(target)],
            dst_ref=out_place(sender, part),
            send_sem=out_sends.at[part, target],
            recv_sem=out_arrivals.at[part, sender],
            device_id=(b, target),
            device_id_type=MESH,
        )

    valid = lax.broadcasted_iota(jnp.int32, (total_frames, 1), 0) < length_ref[0]
    for h in range(heads):
        base = h * 3 * HD
        key = whole_ref[:, base + HD : base + 2 * HD]
        key_turned = key.T
        value = whole_ref[:, base + 2 * HD : base + 3 * HD]
        query_key[...] = jnp.zeros_like(query_key)
        value_total[...] = jnp.zeros_like(value_total)

        def one_block(k, carry, h=h, base=base, key=key, key_turned=key_turned, value=value):
            place = lax.rem(s + k, groups)
            if h == 0:

                @pl.when(k > 0)
                def _():
                    grad_copy(s, place).wait_recv()

            query = whole_ref[rows_of(place), base : base + HD]
            grad = grads[rows_of(place), h * HD : (h + 1) * HD]
            scores = jnp.where(valid, times_transposed(key, query), MASKED_SCORE)
            exp_scores = jnp.exp(scores - jnp.max(scores, axis=0, keepdims=True))
            probs = exp_scores * (1.0 / jnp.sum(exp_scores, axis=0, keepdims=True))
            value_total[...] += jnp.dot(
                probs.astype(jnp.bfloat16), grad, preferred_element_type=jnp.float32
            )
            grad_probs = times_transposed(value, grad)
            mean = jnp.sum(probs * grad_probs, axis=0, keepdims=True)
            grad_scores = (probs * (grad_probs - mean)).astype(jnp.bfloat16)
            query_key[:, HD:] += jnp.dot(grad_scores, query, preferred_element_type=jnp.float32)
            query_key[rows_of(place), :HD] = jnp.dot(
                key_turned, grad_scores, preferred_element_type=jnp.float32
            ).T
            return carry

        lax.fori_loop(0, groups, one_block, 0)
        part, inside = h // part_heads, (h % part_heads) * 3 * HD
        both = query_key[...]
        turned = both * cos_ref[...] + partner_lanes(both) * sin_ref[...]
        result[part, :, inside : inside + 2 * HD] = turned.astype(jnp.bfloat16)
        result[part, :, inside + 2 * HD : inside + 3 * HD] = value_total[...].astype(jnp.bfloat16)
        if (h + 1) % part_heads == 0:
            for k in range(1, groups):
                result_copy(lax.rem(s + k, groups), s, part).start()
    owns = []
    for part in range(parts):
        owns.append(
            pltpu.make_async_copy(
                result.at[part, rows_of(s)], out_place(s, part), own_sem.at[part]
            )
        )
        owns[-1].start()
    for k in range(1, groups):
        other = lax.rem(s + k, groups)
        grad_copy(other, s).wait_send()
        for part in range(parts):
            result_copy(other, s, part).wait_send()
            result_copy(s, other, part).wait_recv()
    for own in owns:
        own.wait()
    side.wait()


def attend_back(whole, grad_attn, length, cosine, sine, side):
    groups = lax.axis_size("seq")
    frames = grad_attn.shape[0]
    heads = HEADS // groups
    width = heads * HD
    block = 3 * width
    total = frames * groups
    signs = jnp.where(jnp.arange(HD) < HD // 2, 1.0, -1.0)
    cos_head = jnp.concatenate([cosine, cosine], axis=1)
    sin_head = jnp.concatenate([sine, sine], axis=1) * signs
    cos_both = jnp.concatenate([cos_head * 0.125, cos_head], axis=1)
    sin_both = jnp.concatenate([sin_head * 0.125, sin_head], axis=1)
    part_heads = 2 if heads % 2 == 0 else heads
    parts = heads // part_heads
    direct = block % 128 == 0
    out_shape = (frames, groups * block) if direct else (groups, frames, block)
    vmem = pl.BlockSpec(memory_space=pltpu.VMEM)
    out, *brought = pl.pallas_call(
        functools.partial(attend_back_kernel, groups, heads, side),
        out_shape=[jax.ShapeDtypeStruct(out_shape, jnp.bfloat16), *side.outs],
        in_specs=[pl.BlockSpec(memory_space=pltpu.SMEM), vmem, vmem, vmem, vmem]
        + [pl.BlockSpec(memory_space=pl.ANY)] * len(side.inputs),
        out_specs=[pl.BlockSpec(memory_space=pl.ANY)] * (1 + len(side.outs)),
        scratch_shapes=[
            pltpu.VMEM((groups, frames, width), jnp.bfloat16),
            pltpu.VMEM((total, width), jnp.bfloat16),
            pltpu.VMEM((parts, total, part_heads * 3 * HD), jnp.bfloat16),
            pltpu.VMEM((total, 2 * HD), jnp.float32),
            pltpu.VMEM((total, HD), jnp.float32),
            pltpu.SemaphoreType.DMA((groups,)),
            pltpu.SemaphoreType.DMA((groups,)),
            pltpu.SemaphoreType.DMA((parts, groups)),
            pltpu.SemaphoreType.DMA((parts, groups)),
            pltpu.SemaphoreType.DMA((parts,)),
            *side.scratch,
        ],
        compiler_params=pltpu.CompilerParams(
            collective_id=5, has_side_effects=True, vmem_limit_bytes=24 << 20
        ),
        cost_estimate=pl.CostEstimate(
            flops=10 * heads * HD * total * total,
            bytes_accessed=2 * total * 8 * width,
            transcendentals=heads * total * total,
        ),
    )(length.reshape(1), whole, grad_attn, cos_both, sin_both, *side.inputs)
    if not direct:
        out = out.transpose(1, 0, 2).reshape(frames, groups * block)
    return out, brought


def flipped(index, places):
    for bit, flip in places:
        mine = lax.rem(index // (1 << bit), 2)
        index = index + flip * (1 - 2 * mine) * (1 << bit)
    return index


def place_of(place, steps, axis, index):
    flips = []
    for order, (name, bit) in enumerate(steps):
        if name == axis:
            flips.append((bit, lax.rem(place // (1 << (len(steps) - 1 - order)), 2)))
    return flipped(index, flips)


class Job:
    def __init__(self, parts, tall, order, far=None, gathered=None):
        self.parts, self.tall, self.far, self.gathered = parts, tall, far, gathered
        self.batches, self.groups = lax.axis_size("batch"), lax.axis_size("seq")
        bits = {
            "x": [("seq", 0)],
            "y": [("seq", k) for k in range(1, self.groups.bit_length() - 1)],
            "1": [("batch", 1)],
            "2": [("batch", k) for k in range(2, self.batches.bit_length() - 1)],
        }
        letters = order if far is None else order.replace("1", "")
        self.steps = [step for letter in letters for step in bits[letter]]
        self.sharing = 2 if far is None else 4
        self.spans = self.batches // self.sharing
        self.levels = len(self.steps)
        self.half = 1 << (self.levels - 1)
        if tall:
            ((small, big),) = parts
            self.rows = big.shape[1] // (self.batches * self.groups)
            self.widths = [small.shape[1]]
        else:
            self.rows = parts[0][0].shape[1] // self.groups
            self.widths = [big.shape[1] // self.batches for _, big in parts]
        self.cols = sum(self.widths)
        self.near_pieces = len(parts) * (self.sharing // 2 + self.spans)
        self.far_pieces = len(parts) * (self.sharing // 2 + (self.sharing - 1) * self.spans)
        if gathered is not None:
            self.near_pieces += 3
            self.far_pieces -= 3 * self.spans

    def fits(self):
        return self.rows % 128 == 0 and all(width % 128 == 0 for width in self.widths)

    def operands(self):
        extra = [array for array in (self.far, self.gathered) if array is not None]
        return [array for part in self.parts for array in part] + extra

    def flops(self):
        return sum(2 * small.size * big.shape[1] for small, big in self.parts)

    def operand_scratch(self):
        scratch, sharing = [], self.sharing
        for small, big in self.parts:
            frames = sharing * small.shape[0]
            scratch.append(pltpu.VMEM((frames, small.shape[1]), jnp.bfloat16))
            scratch.append(pltpu.VMEM((frames, big.shape[1] // sharing), jnp.bfloat16))
        return scratch + [
            pltpu.SemaphoreType.DMA((self.near_pieces,)),
            pltpu.SemaphoreType.DMA((self.far_pieces,)),
            pltpu.SemaphoreType.DMA((self.far_pieces,)),
        ]

    def step_of(self, level):
        return self.steps[self.levels - 1 - level]


def signal(peers):
    barrier = pltpu.get_barrier_semaphore()
    for peer in peers:
        pl.semaphore_signal(barrier, inc=1, device_id=peer, device_id_type=MESH)


def wait_signals(peers):
    pl.semaphore_wait(pltpu.get_barrier_semaphore(), len(peers))


def greet(peers):
    signal(peers)
    wait_signals(peers)


def sibling_of(s, b):
    return (b + 1 - 2 * lax.rem(b, 2), s)


def partner_of(s, b, step):
    axis, bit = step
    if axis == "seq":
        return (b, flipped(s, [(bit, 1)]))
    return (flipped(b, [(bit, 1)]), s)


def quarters(s, b, n):
    core, z = lax.rem(b, 2), lax.rem(b // 2, 2)
    mine, other = 2 * (2 * n + z), 2 * (2 * n + 1 - z)
    return [
        (sibling_of(s, b), mine + 1 - core),
        ((flipped(b, [(1, 1)]), s), other + core),
        ((flipped(b, [(0, 1), (1, 1)]), s), other + 1 - core),
    ]


class Side:
    def __init__(self, rows, wide):
        self.rows, self.wide = rows, wide
        batches = lax.axis_size("batch")
        self.inputs = [*rows, *wide]
        self.outs = [jax.ShapeDtypeStruct(array.shape, array.dtype) for array in rows]
        self.outs += [
            jax.ShapeDtypeStruct((3, array.shape[0], array.shape[1] // 4), array.dtype)
            for array in wide
        ]
        self.count = len(rows) + len(wide) * 3 * (batches // 4)
        self.scratch = [pltpu.SemaphoreType.DMA((self.count,))] * 2 if self.count else []

    def peers(self, s, b):
        return [peer for peer, _ in quarters(s, b, 0)] if self.count else []

    def start(self, inputs, outs, sems, s, b):
        self.copies = []

        def send(source, place, peer):
            n = len(self.copies)
            self.copies.append(
                pltpu.make_async_remote_copy(
                    src_ref=source,
                    dst_ref=place,
                    send_sem=sems[0].at[n],
                    recv_sem=sems[1].at[n],
                    device_id=peer,
                    device_id_type=MESH,
                )
            )
            self.copies[-1].start()

        for i, array in enumerate(self.rows):
            send(inputs[i], outs[i], (flipped(b, [(1, 1)]), s))
        for i, array in enumerate(self.wide, len(self.rows)):
            batches = lax.axis_size("batch")
            span = array.shape[1] // batches
            for n in range(batches // 4):
                for k, (peer, owner) in enumerate(quarters(s, b, n)):
                    columns = pl.ds(pl.multiple_of(owner * span, 128), span)
                    send(inputs[i].at[:, columns], outs[i].at[k, :, pl.ds(n * span, span)], peer)

    def wait(self):
        for copy in self.copies:
            copy.wait()


def swap_operands(job, inputs, held, s, b):
    local, moves, lands = held[2 * len(job.parts) :]
    near, far = [], []

    def bring(source, place, peer=None):
        if peer is None:
            near.append(pltpu.make_async_copy(source, place, local.at[len(near)]))
            near[-1].start()
            return
        n = len(far)
        far.append(
            pltpu.make_async_remote_copy(
                src_ref=source,
                dst_ref=place,
                send_sem=moves.at[n],
                recv_sem=lands.at[n],
                device_id=peer,
                device_id_type=MESH,
            )
        )
        far[-1].start()

    core, z = lax.rem(b, 2), lax.rem(b // 2, 2)
    sibling = sibling_of(s, b)
    for i in range(len(job.parts)):
        small_in, big_in = inputs[2 * i : 2 * i + 2]
        small, big = held[2 * i : 2 * i + 2]
        frames = small_in.shape[0]
        span = big_in.shape[1] // job.batches

        def rows(k):
            return pl.ds(k * frames, frames)

        def columns(owner):
            return pl.ds(pl.multiple_of(owner * span, 128), span)

        bring(small_in, small.at[rows(1)], sibling)
        bring(small_in, small.at[rows(0)])
        if job.far is not None:
            bring(inputs[2], small.at[rows(3)], sibling)
            bring(inputs[2], small.at[rows(2)])
        if job.gathered is not None:
            for k in range(3):
                bring(inputs[3].at[k], big.at[rows(k + 1)])
        for n in range(job.spans):
            inside = pl.ds(n * span, span)
            if job.far is None:
                bring(big_in.at[:, columns(2 * n + 1 - core)], big.at[rows(1), inside], sibling)
                bring(big_in.at[:, columns(2 * n + core)], big.at[rows(0), inside])
                continue
            if job.gathered is None:
                for k, (peer, owner) in enumerate(quarters(s, b, n)):
                    bring(big_in.at[:, columns(owner)], big.at[rows(k + 1), inside], peer)
            bring(big_in.at[:, columns(2 * (2 * n + z) + core)], big.at[rows(0), inside])
    return near, far


def wait_operands(near, far):
    for copy in near:
        copy.wait()
    for copy in far:
        copy.wait_recv()


def block_product(job, held, part, place, s, b):
    small, big = held[2 * part : 2 * part + 2]
    span = big.shape[1] // job.spans
    row = place_of(place, job.steps, "seq", s)
    col = place_of(place, job.steps, "batch", b) // job.sharing
    if job.tall:
        left = big[:, pl.ds(pl.multiple_of(col * span + row * job.rows, 128), job.rows)]
        right = small[...]
    else:
        left = small[:, pl.ds(pl.multiple_of(row * job.rows, 128), job.rows)]
        right = big[:, pl.ds(pl.multiple_of(col * span, 128), span)]
    return lax.dot_general(
        left, right, (((0,), (0,)), ((), ())), preferred_element_type=jnp.float32
    )


def columns_of(job, part):
    start = sum(job.widths[:part])
    return slice(start, start + job.widths[part])


def scatter_kernel(jobs, sequence, *refs):
    refs = list(refs)

    def take(count):
        taken = refs[:count]
        del refs[:count]
        return taken

    inputs = [take(len(job.operands())) for job in jobs]
    (rows_ref,) = take(1)
    outs = [take(len(job.parts)) for job in jobs]
    (small_total,) = take(1)
    scratch = [(take(2 * len(job.parts) + 3), *take(4)) for job in jobs]
    seq_slots, part_sum, batch_slots, small_sends, small_arrivals = take(5)
    batches, groups = jobs[0].batches, jobs[0].groups
    s, b = lax.axis_index("seq"), lax.axis_index("batch")
    peers = sum_peers(groups, batches, s, b)
    greet(peers)

    def slot_of(job, place):
        return lax.rem(place, job.half)

    def copy_of(i, place, level):
        job = jobs[i]
        _, sending, arrived, sends, recvs = scratch[i]
        return pltpu.make_async_remote_copy(
            src_ref=sending.at[slot_of(job, place)],
            dst_ref=arrived.at[place - 1],
            send_sem=sends.at[slot_of(job, place)],
            recv_sem=recvs.at[place - 1],
            device_id=partner_of(s, b, job.step_of(level)),
            device_id_type=MESH,
        )

    works = {i: swap_operands(jobs[i], inputs[i], scratch[i][0], s, b) for i in SWAPS}

    def columns(owner):
        width = part_sum.shape[1]
        return rows_ref.at[:, pl.ds(pl.multiple_of(owner * width, 128), width)]

    over_seq = spread(
        columns, seq_slots, s, peers, range(groups - 1), small_sends, small_arrivals
    )

    def block_sums(i, place, level):
        job = jobs[i]
        held, _, arrived = scratch[i][:3]
        for m in range(job.levels - 1, level, -1):
            copy_of(i, (1 << m) + place, m).wait_recv()
        totals = []
        for part in range(len(job.parts)):
            total = block_product(job, held, part, place, s, b)
            for m in range(job.levels - 1, level, -1):
                came = arrived[(1 << m) + place - 1, :, columns_of(job, part)]
                total = total + came.astype(jnp.float32)
            totals.append(total)
        return totals

    def send_block(i, place, level):
        job = jobs[i]
        totals = block_sums(i, place, level)
        if level < job.levels - 1:
            copy_of(i, place + job.half, job.levels - 1).wait_send()
        for part, total in enumerate(totals):
            scratch[i][1][slot_of(job, place), :, columns_of(job, part)] = total.astype(jnp.bfloat16)
        copy_of(i, place, level).start()

    ready = set()
    over_batch = None
    for i, level in sequence:
        job = jobs[i]
        if i not in ready:
            ready.add(i)
            wait_operands(*works[i])
        if level < 0:
            for part, total in enumerate(block_sums(i, 0, -1)):
                outs[i][part][...] = total
            continue

        def one_place(j, carry, level=level, i=i):
            send_block(i, (2 << level) - 1 - j, level)
            return carry

        lax.fori_loop(0, 1 << level, one_place, 0)
        if over_batch is None:
            part_sum[...] = over_seq()
            over_batch = spread(
                lambda owner: part_sum,
                batch_slots,
                b,
                peers,
                range(groups - 1, groups + batches - 2),
                small_sends,
                small_arrivals,
            )
    small_total[...] = over_batch()
    for i, job in enumerate(jobs):
        for copy in works[i][1]:
            copy.wait_send()
        copy_of(i, job.half, job.levels - 1).wait_send()
        for level in range(job.levels - 1):

            def one_wait(j, carry, level=level, i=i):
                copy_of(i, (1 << level) + j, level).wait_send()
                return carry

            lax.fori_loop(0, 1 << level, one_wait, 0)


def pass_kernel(count, cuts, *refs):
    sources, share, targets, pieces = refs[:count], refs[count], refs[count + 1 : -len(cuts)], refs[-len(cuts) :]
    for source, target in zip(sources, targets):
        target[...] = source[...]
    start = 0
    for cut, piece in zip(cuts, pieces):
        piece[...] = share[start : start + cut, :]
        start += cut


def scatter_sums(jobs, sequence, rows, cuts, collective_id):
    height, width = rows.shape
    width = width // jobs[0].groups
    if width % 128 or not all(job.fits() for job in jobs):
        total = sum_everywhere(rows, collective_id)
        share = lax.dynamic_slice_in_dim(total, lax.axis_index("seq") * width, width, axis=1)
        sums = [
            [
                owned_sum(*((big, small) if job.tall else (small, big)), job.tall, job.tall)
                for small, big in job.parts
            ]
            for job in jobs
        ]
        starts = [sum(cuts[:i]) for i in range(len(cuts))]
        return sums, [share[start : start + cut] for start, cut in zip(starts, cuts)]
    scratch, operands, outs = [], [], []
    for job in jobs:
        block = (job.rows, job.cols)
        scratch += job.operand_scratch()
        scratch += [
            pltpu.VMEM((job.half, *block), jnp.bfloat16),
            pltpu.VMEM((2 * job.half - 1, *block), jnp.bfloat16),
            pltpu.SemaphoreType.DMA((job.half,)),
            pltpu.SemaphoreType.DMA((2 * job.half - 1,)),
        ]
        operands += job.operands()
        outs += [jax.ShapeDtypeStruct((job.rows, width), jnp.float32) for width in job.widths]
    vmem = pl.BlockSpec(memory_space=pltpu.VMEM)
    *results, share = pl.pallas_call(
        functools.partial(scatter_kernel, jobs, sequence),
        out_shape=[*outs, jax.ShapeDtypeStruct((height, width), jnp.float32)],
        in_specs=[pl.BlockSpec(memory_space=pl.ANY)] * len(operands) + [vmem],
        out_specs=[vmem] * (len(outs) + 1),
        scratch_shapes=scratch + sum_scratch(height, width),
        compiler_params=pltpu.CompilerParams(
            collective_id=collective_id, has_side_effects=True, vmem_limit_bytes=60 << 20
        ),
        cost_estimate=pl.CostEstimate(
            flops=sum(job.flops() for job in jobs), bytes_accessed=400 << 20, transcendentals=0
        ),
    )(*operands, rows)
    passes = 2
    specs = [pl.BlockSpec((out.shape[0] // passes, out.shape[1]), lambda i: (i, 0)) for out in outs]
    whole_specs = [pl.BlockSpec((rows, width), lambda i: (0, 0)) for rows in (height, *cuts)]
    pieces = [jax.ShapeDtypeStruct((cut, width), jnp.float32) for cut in cuts]
    results = list(
        pl.pallas_call(
            functools.partial(pass_kernel, len(outs), cuts),
            out_shape=[*outs, *pieces],
            grid=(passes,),
            in_specs=[*specs, whole_specs[0]],
            out_specs=[*specs, *whole_specs[1:]],
            compiler_params=pltpu.CompilerParams(vmem_limit_bytes=60 << 20),
        )(*results, share)
    )
    sums = [[results.pop(0) for _ in job.parts] for job in jobs]
    return sums, results


def shards(
    frames_in,
    cotangent,
    levels,
    lengths,
    token_mask,
    cond_table,
    norm_gains,
    w_ffn1_up,
    w_ffn1_down,
    w_qkv,
    w_out,
    w_glu,
    conv_kernel,
    bn_gain,
    batchnorm_shift_bias,
    w_conv_out,
    w_ffn2_up,
    w_ffn2_down,
    running_mean,
    running_var,
):
    frames = frames_in.shape[1]
    model_width = frames_in.shape[2]
    ff_width = w_ffn1_up.shape[1]
    groups = lax.axis_size("seq")
    batches = lax.axis_size("batch")
    seq_index = lax.axis_index("seq")
    item_index = lax.axis_index("batch")
    seq_length = frames * groups
    level_count = cond_table.shape[0] - 1
    gain_rows = [norm_gains[row].astype(jnp.float32) for row in range(norm_gains.shape[0])]
    level_hot = (jnp.arange(level_count) == levels[0] - 1).astype(jnp.float32)
    level_vector = lax.dynamic_slice_in_dim(cond_table, levels[0] - 1, 1)[0].astype(jnp.float32)
    mask_column = token_mask[0].astype(jnp.float32)[:, None]
    start_rows = (
        frames_in[0].astype(jnp.float32)
        + level_vector[None, :]
        + mask_column * cond_table[level_count].astype(jnp.float32)[None, :]
    )
    length = lax.dynamic_slice_in_dim(lengths, item_index, 1)[0]
    positions = seq_index * frames + jnp.arange(frames)
    unpadded_rows = (positions < length).astype(jnp.float32)[:, None]
    rows_one, ffn1_state = ffn_forward(start_rows, gain_rows[0], w_ffn1_up, w_ffn1_down)
    normed_attn, attn_pull = jax.vjp(layer_norm, rows_one, gain_rows[1])
    attn_in = normed_attn.astype(jnp.bfloat16)
    qkv_rows = jnp.dot(attn_in, w_qkv, preferred_element_type=jnp.float32)
    cosine, sine_table = rope_tables(positions, HD)
    fit = (
        model_width // groups % 128 == 0
        and model_width // batches % 128 == 0
        and ff_width // (groups * batches) % 128 == 0
    )
    side = Side([ffn1_state[1], attn_in] if fit else [], [])
    whole_heads, attn_out, brought = attend(qkv_rows, length, cosine, sine_table, side)
    far_ffn1, far_attn = brought if fit else (None, None)
    rows_two = rows_one + jnp.dot(attn_out, w_out, preferred_element_type=jnp.float32)
    normed_conv, conv_pull = jax.vjp(layer_norm, rows_two, gain_rows[2])
    conv_in = normed_conv.astype(jnp.bfloat16)
    glu_pre = jnp.dot(conv_in, w_glu, preferred_element_type=jnp.float32)
    up_half = glu_pre[:, :model_width]
    glu_sig = jax.nn.sigmoid(glu_pre[:, model_width:])
    glu_low = (up_half * glu_sig * unpadded_rows).astype(jnp.bfloat16)
    taps = conv_kernel.shape[0]
    kernel_rows = conv_kernel.astype(jnp.float32)
    convolved_rows, padded, totals = convolve(glu_low, kernel_rows, length)
    total_sum, total_squares = totals[0], totals[1]
    count_of_frames = jnp.sum(lengths).astype(jnp.float32)
    batchnorm_frame_mean = total_sum / count_of_frames
    bn_var = total_squares / count_of_frames - batchnorm_frame_mean * batchnorm_frame_mean
    batchnorm_inverse_deviation = lax.rsqrt(bn_var + EPSILON)
    batchnorm_scale_factor = bn_gain.astype(jnp.float32)
    normalized_rows = (convolved_rows - batchnorm_frame_mean) * batchnorm_inverse_deviation
    batchnorm_input_rows = normalized_rows * batchnorm_scale_factor + batchnorm_shift_bias.astype(
        jnp.float32
    )
    bn_sig = jax.nn.sigmoid(batchnorm_input_rows)
    conv_act = (batchnorm_input_rows * bn_sig).astype(jnp.bfloat16)
    rows_three = rows_two + jnp.dot(conv_act, w_conv_out, preferred_element_type=jnp.float32)
    rows_four, ffn2_state = ffn_forward(rows_three, gain_rows[3], w_ffn2_up, w_ffn2_down)
    normed_out, out_pull = jax.vjp(layer_norm, rows_four, gain_rows[4])
    out_rows = normed_out.astype(jnp.bfloat16)
    grad_four, grad_gain_four = out_pull(cotangent[0].astype(jnp.float32))
    grad_three, grad_gain_three, ffn2_up_pair, ffn2_down_pair = ffn_backward(
        grad_four, ffn2_state, w_ffn2_up, w_ffn2_down
    )
    grad_r2 = grad_three.astype(jnp.bfloat16)
    batchnorm_gradient = (
        times_transposed(grad_r2, w_conv_out)
        * bn_sig
        * (1.0 + batchnorm_input_rows * (1.0 - bn_sig))
    )
    norm_rows = jnp.stack(
        [batchnorm_frame_mean, batchnorm_inverse_deviation, batchnorm_scale_factor], axis=0
    )
    grad_glu, kernel_grads, gradient_totals = convolve_back(
        batchnorm_gradient, convolved_rows, padded, kernel_rows, norm_rows, length, count_of_frames
    )
    kernel_grads = kernel_grads[:taps]
    gradient_sum_total, gradient_normalized_sum = gradient_totals[0], gradient_totals[1]
    grad_gl = jnp.concatenate(
        [grad_glu * glu_sig, grad_glu * up_half * glu_sig * (1.0 - glu_sig)], axis=1
    ).astype(jnp.bfloat16)
    grad_conv_in, grad_gain_two = conv_pull(times_transposed(grad_gl, w_glu))
    grad_two = grad_three + grad_conv_in
    grad_r = grad_two.astype(jnp.bfloat16)
    grad_attn_out = times_transposed(grad_r, w_out).astype(jnp.bfloat16)
    cos_all, sin_all = rope_tables(jnp.arange(seq_length), HD)
    side = Side([ffn2_up_pair[0]] if fit else [], [ffn2_up_pair[1]] if fit else [])
    grad_qkv, brought = attend_back(whole_heads, grad_attn_out, length, cos_all, sin_all, side)
    far_ffn2, gathered = brought if fit else (None, None)
    grad_attn_part, grad_gain_one = attn_pull(times_transposed(grad_qkv, w_qkv))
    grad_one = grad_two + grad_attn_part
    grad_zero, grad_gain_zero, ffn1_up_pair, ffn1_down_pair = ffn_backward(
        grad_one, ffn1_state, w_ffn1_up, w_ffn1_down
    )
    column_total = jnp.sum(grad_zero, axis=0)
    cond_grad_rows = jnp.concatenate(
        [
            level_hot[:, None] * column_total[None, :],
            jnp.sum(mask_column * grad_zero, axis=0)[None, :],
        ],
        axis=0,
    )
    gain_grads = jnp.stack(
        [grad_gain_zero, grad_gain_one, grad_gain_two, grad_gain_three, grad_gain_four], axis=0
    )
    small_rows = jnp.concatenate([gain_grads, cond_grad_rows, kernel_grads], axis=0)
    small_rows = jnp.pad(small_rows, ((0, -small_rows.shape[0] % 8), (0, 0)))
    jobs = [
        Job([ffn2_up_pair], False, "1yx2", far_ffn2, gathered),
        Job([ffn2_down_pair[::-1]], True, "y12x"),
        Job([(conv_in, grad_gl), (attn_out, grad_r), (conv_act, grad_r2)], False, "xy12"),
        Job([(attn_in, grad_qkv)], False, "1xy2", far_attn),
        Job([ffn1_down_pair[::-1]], True, "xy12"),
        Job([ffn1_up_pair], False, "12xy", far_ffn1),
    ]
    cuts = (5, level_count + 1, taps)
    sums, (gain_sums, cond_sums, tap_sums) = scatter_sums(jobs, SEGMENTS, small_rows, cuts, 7)
    new_mean = 0.9 * running_mean + 0.1 * batchnorm_frame_mean
    new_var = 0.9 * running_var + 0.1 * bn_var * count_of_frames / (count_of_frames - 1.0)
    return (
        out_rows[None],
        grad_zero.astype(jnp.bfloat16)[None],
        cond_sums,
        gain_sums,
        sums[5][0],
        sums[4][0],
        sums[3][0],
        sums[2][1],
        sums[2][0],
        tap_sums,
        gradient_normalized_sum,
        gradient_sum_total,
        sums[2][2],
        sums[0][0],
        sums[1][0],
        new_mean,
        new_var,
    )


def solution(mesh):
    in_specs = (
        P("batch", "seq", None),
        P("batch", "seq", None),
        P("batch"),
        P(),
        P("batch", "seq"),
        P(),
        P(),
        P(),
        P(),
        P(),
        P(),
        P(),
        P(),
        P(),
        P(),
        P(),
        P(),
        P(),
        P(),
        P(),
    )
    out_specs = (
        P("batch", "seq", None),
        P("batch", "seq", None),
        P(None, "seq"),
        P(None, "seq"),
        P("seq", "batch"),
        P(("batch", "seq"), None),
        P("seq", "batch"),
        P("seq", "batch"),
        P("seq", "batch"),
        P(None, "seq"),
        P(),
        P(),
        P("seq", "batch"),
        P("seq", "batch"),
        P(("batch", "seq"), None),
        P(),
        P(),
    )
    return jax.shard_map(shards, mesh=mesh, in_specs=in_specs, out_specs=out_specs, check_vma=False)
```

```python
import functools
import math

import jax
import jax.numpy as jnp
from jax import lax
from jax.experimental import pallas as pl
from jax.experimental.pallas import tpu as pltpu
from jax.sharding import PartitionSpec as P

MESH = pl.DeviceIdType.MESH

HEADS = 16
HD = 64


EPSILON = 1e-05
MASKED_SCORE = -1000000000.0

SEGMENTS = (
    (2, 3), (0, 2), (1, 3), (0, 1), (5, 2), (1, 2), (3, 2), (4, 3), (2, 2), (1, 1), (5, 1),
    (0, 0), (1, 0), (2, 1), (3, 1), (3, 0), (4, 2), (2, 0), (0, -1), (4, 1), (3, -1), (4, 0),
    (2, -1), (5, 0), (1, -1), (5, -1), (4, -1),
)
SWAPS = (2, 0, 4, 5, 1, 3)


def layer_norm(values, gain_row):
    centre = values - jnp.mean(values, axis=-1, keepdims=True)
    spread = jnp.mean(centre * centre, axis=-1, keepdims=True)
    return centre * lax.rsqrt(spread + EPSILON) * gain_row


def rope_tables(positions, head_size):
    half_size = head_size // 2
    inv_freqs = jnp.exp(
        jnp.arange(half_size).astype(jnp.float32) * (-2.0 * math.log(10000.0) / head_size)
    )
    angles = positions.astype(jnp.float32)[:, None] * inv_freqs[None, :]
    return (jnp.cos(angles), jnp.sin(angles))


def times_transposed(left_side, weight):
    return lax.dot_general(
        left_side, weight, (((1,), (1,)), ((), ())), preferred_element_type=jnp.float32
    )


def ffn_forward(values, gain_row, up_weight, down_weight):
    normed, ln_pull = jax.vjp(layer_norm, values, gain_row)
    lowered = normed.astype(jnp.bfloat16)
    hidden = jnp.dot(lowered, up_weight, preferred_element_type=jnp.float32)
    act_rows = (hidden * jax.nn.sigmoid(hidden)).astype(jnp.bfloat16)
    branch = jnp.dot(act_rows, down_weight, preferred_element_type=jnp.float32)
    return (values + 0.5 * branch, (ln_pull, lowered, hidden, act_rows))


def ffn_backward(grad_in, saved_state, up_weight, down_weight):
    ln_pull, lowered, hidden, act_rows = saved_state
    grad_branch = (0.5 * grad_in).astype(jnp.bfloat16)
    grad_act = times_transposed(grad_branch, down_weight)
    gate_sig = jax.nn.sigmoid(hidden)
    grad_hidden = (grad_act * gate_sig * (1.0 + hidden * (1.0 - gate_sig))).astype(jnp.bfloat16)
    grad_normed = times_transposed(grad_hidden, up_weight)
    grad_values, grad_gain = ln_pull(grad_normed)
    return (grad_in + grad_values, grad_gain, (lowered, grad_hidden), (act_rows, grad_branch))


def sum_peers(groups, batches, s, b):
    peers = [(b, lax.rem(s + k, groups)) for k in range(1, groups)]
    return peers + [(lax.rem(b + k, batches), s) for k in range(1, batches)]


def spread(pick, slots, mine, peers, span, sends, arrivals):
    slots[mine] = pick(mine)[...]
    copies = []
    for k in span:
        copies.append(
            pltpu.make_async_remote_copy(
                src_ref=pick(peers[k][1]),
                dst_ref=slots.at[mine],
                send_sem=sends.at[k],
                recv_sem=arrivals.at[k],
                device_id=peers[k],
                device_id_type=MESH,
            )
        )
        copies[-1].start()

    def finish():
        for copy in copies:
            copy.wait()
        total = slots[0]
        for i in range(1, len(copies) + 1):
            total = total + slots[i]
        return total

    return finish


def sum_kernel(groups, batches, rows_ref, total_ref, seq_slots, part, batch_slots, sends, arrivals):
    s, b = lax.axis_index("seq"), lax.axis_index("batch")
    peers = sum_peers(groups, batches, s, b)
    greet(peers)
    first = range(groups - 1)
    second = range(groups - 1, groups + batches - 2)
    part[...] = spread(lambda owner: rows_ref, seq_slots, s, peers, first, sends, arrivals)()
    total_ref[...] = spread(lambda owner: part, batch_slots, b, peers, second, sends, arrivals)()


def sum_scratch(height, width):
    groups, batches = lax.axis_size("seq"), lax.axis_size("batch")
    return [
        pltpu.VMEM((groups, height, width), jnp.float32),
        pltpu.VMEM((height, width), jnp.float32),
        pltpu.VMEM((batches, height, width), jnp.float32),
        pltpu.SemaphoreType.DMA((groups + batches - 2,)),
        pltpu.SemaphoreType.DMA((groups + batches - 2,)),
    ]


def sum_everywhere(rows, collective_id):
    groups, batches = lax.axis_size("seq"), lax.axis_size("batch")
    return pl.pallas_call(
        functools.partial(sum_kernel, groups, batches),
        out_shape=jax.ShapeDtypeStruct(rows.shape, jnp.float32),
        in_specs=[pl.BlockSpec(memory_space=pltpu.VMEM)],
        out_specs=pl.BlockSpec(memory_space=pltpu.VMEM),
        scratch_shapes=sum_scratch(*rows.shape),
        compiler_params=pltpu.CompilerParams(
            collective_id=collective_id, has_side_effects=True, vmem_limit_bytes=4 << 20
        ),
    )(rows)


def edge_copies(groups, s, b, rows_ref, before, after, tile, sends, arrivals, first):
    up = pltpu.make_async_remote_copy(
        src_ref=rows_ref.at[pl.ds(rows_ref.shape[0] - tile, tile)],
        dst_ref=before,
        send_sem=sends.at[first],
        recv_sem=arrivals.at[first],
        device_id=(b, lax.rem(s + 1, groups)),
        device_id_type=MESH,
    )
    down = pltpu.make_async_remote_copy(
        src_ref=rows_ref.at[pl.ds(0, tile)],
        dst_ref=after,
        send_sem=sends.at[first + 1],
        recv_sem=arrivals.at[first + 1],
        device_id=(b, lax.rem(s + groups - 1, groups)),
        device_id_type=MESH,
    )
    return up, down


def start_edges(groups, s, copies):
    @pl.when(s < groups - 1)
    def _():
        for up, _ in copies:
            up.start()

    @pl.when(s > 0)
    def _():
        for _, down in copies:
            down.start()


def wait_edges_sent(groups, s, copies):
    @pl.when(s < groups - 1)
    def _():
        for up, _ in copies:
            up.wait_send()

    @pl.when(s > 0)
    def _():
        for _, down in copies:
            down.wait_send()


def valid_rows(first, count, length):
    positions = first + lax.broadcasted_iota(jnp.int32, (count, 1), 0)
    return (positions < length).astype(jnp.float32)


def convolve_kernel(
    groups, batches, taps, length_ref, glu_ref, kernel_ref, out_ref, padded_ref, total_ref,
    before, after, local, edge_sends, edge_arrivals, seq_slots, part, batch_slots, sends, arrivals,
):
    s, b = lax.axis_index("seq"), lax.axis_index("batch")
    peers = sum_peers(groups, batches, s, b)
    signal(peers)
    frames, width = glu_ref.shape
    padded_ref[8 : 8 + frames, :] = glu_ref[...].astype(jnp.float32)
    wait_signals(peers)
    edges = [edge_copies(groups, s, b, glu_ref, before, after, 16, edge_sends, edge_arrivals, 0)]
    start_edges(groups, s, edges)

    @pl.when(s > 0)
    def _():
        edges[0][0].wait_recv()
        padded_ref[0:8, :] = before[8:16, :].astype(jnp.float32)

    @pl.when(s == 0)
    def _():
        padded_ref[0:8, :] = jnp.zeros((8, width), jnp.float32)

    @pl.when(s < groups - 1)
    def _():
        edges[0][1].wait_recv()
        padded_ref[8 + frames :, :] = after[0:8, :].astype(jnp.float32)

    @pl.when(s == groups - 1)
    def _():
        padded_ref[8 + frames :, :] = jnp.zeros((8, width), jnp.float32)

    valid = valid_rows(s * frames, frames, length_ref[0])
    for column in range(0, width, 128):
        lanes = slice(column, column + 128)
        total = jnp.zeros((frames, 128), jnp.float32)
        for k in range(taps):
            start = 8 - taps // 2 + k
            total = total + kernel_ref[k : k + 1, lanes] * padded_ref[start : start + frames, lanes]
        out_ref[:, lanes] = total
        kept = total * valid
        local[0:1, lanes] = jnp.sum(kept, axis=0, keepdims=True)
        local[1:2, lanes] = jnp.sum(kept * total, axis=0, keepdims=True)
    first, second = range(groups - 1), range(groups - 1, groups + batches - 2)
    part[...] = spread(lambda owner: local, seq_slots, s, peers, first, sends, arrivals)()
    total_ref[...] = spread(lambda owner: part, batch_slots, b, peers, second, sends, arrivals)()
    wait_edges_sent(groups, s, edges)


def convolve(glu_low, kernel_rows, length):
    groups, batches = lax.axis_size("seq"), lax.axis_size("batch")
    frames, width = glu_low.shape
    taps = kernel_rows.shape[0]
    vmem = pl.BlockSpec(memory_space=pltpu.VMEM)
    return pl.pallas_call(
        functools.partial(convolve_kernel, groups, batches, taps),
        out_shape=[
            jax.ShapeDtypeStruct((frames, width), jnp.float32),
            jax.ShapeDtypeStruct((frames + 16, width), jnp.float32),
            jax.ShapeDtypeStruct((2, width), jnp.float32),
        ],
        in_specs=[pl.BlockSpec(memory_space=pltpu.SMEM), vmem, vmem],
        out_specs=[vmem] * 3,
        scratch_shapes=[
            pltpu.VMEM((16, width), jnp.bfloat16),
            pltpu.VMEM((16, width), jnp.bfloat16),
            pltpu.VMEM((2, width), jnp.float32),
            pltpu.SemaphoreType.DMA((2,)),
            pltpu.SemaphoreType.DMA((2,)),
            *sum_scratch(2, width),
        ],
        compiler_params=pltpu.CompilerParams(
            collective_id=1, has_side_effects=True, vmem_limit_bytes=8 << 20
        ),
    )(length.reshape(1), glu_low, kernel_rows)


def convolve_back_kernel(
    groups, batches, taps, length_ref, count_ref, grad_ref, conv_ref, padded_ref, kernel_ref, norm_ref,
    out_ref, taps_ref, total_ref, edge_rows, spread_rows, local, edge_sends, edge_arrivals,
    seq_slots, part, batch_slots, sends, arrivals,
):
    s, b = lax.axis_index("seq"), lax.axis_index("batch")
    peers = sum_peers(groups, batches, s, b)
    signal(peers)
    frames, width = grad_ref.shape

    def normalized(values, lanes):
        return (values - norm_ref[0:1, lanes]) * norm_ref[1:2, lanes]

    for column in range(0, width, 128):
        lanes = slice(column, column + 128)
        grads = grad_ref[:, lanes]
        local[0:1, lanes] = jnp.sum(grads, axis=0, keepdims=True)
        local[1:2, lanes] = jnp.sum(
            grads * normalized(conv_ref[:, lanes], lanes), axis=0, keepdims=True
        )
    wait_signals(peers)
    edges = [
        edge_copies(
            groups, s, b, ref, edge_rows.at[2 * i], edge_rows.at[2 * i + 1], 8,
            edge_sends, edge_arrivals, 2 * i,
        )
        for i, ref in enumerate((grad_ref, conv_ref))
    ]
    start_edges(groups, s, edges)
    first, second = range(groups - 1), range(groups - 1, groups + batches - 2)
    part[...] = spread(lambda owner: local, seq_slots, s, peers, first, sends, arrivals)()
    total_ref[...] = spread(lambda owner: part, batch_slots, b, peers, second, sends, arrivals)()

    length = length_ref[0]
    share = 1.0 / count_ref[0]

    def conv_grad(grads, values, valid, lanes):
        sums = total_ref[0:1, lanes] + normalized(values, lanes) * total_ref[1:2, lanes]
        rows = norm_ref[2:3, lanes] * norm_ref[1:2, lanes] * (grads - valid * sums * share)
        return rows.astype(jnp.bfloat16).astype(jnp.float32)

    @pl.when(s > 0)
    def _():
        for up, _ in edges:
            up.wait_recv()
        spread_rows[0:8, :] = conv_grad(
            edge_rows[0], edge_rows[2], valid_rows(s * frames - 8, 8, length), slice(None)
        )

    @pl.when(s == 0)
    def _():
        spread_rows[0:8, :] = jnp.zeros((8, width), jnp.float32)

    @pl.when(s < groups - 1)
    def _():
        for _, down in edges:
            down.wait_recv()
        spread_rows[8 + frames :, :] = conv_grad(
            edge_rows[1], edge_rows[3], valid_rows((s + 1) * frames, 8, length), slice(None)
        )

    @pl.when(s == groups - 1)
    def _():
        spread_rows[8 + frames :, :] = jnp.zeros((8, width), jnp.float32)

    valid = valid_rows(s * frames, frames, length)
    taps_ref[...] = jnp.zeros_like(taps_ref)
    for column in range(0, width, 128):
        lanes = slice(column, column + 128)
        own = conv_grad(grad_ref[:, lanes], conv_ref[:, lanes], valid, lanes)
        spread_rows[8 : 8 + frames, lanes] = own
        total = jnp.zeros((frames, 128), jnp.float32)
        for k in range(taps):
            start = 8 + taps // 2 - k
            total = total + kernel_ref[k : k + 1, lanes] * spread_rows[start : start + frames, lanes]
            start = 8 - taps // 2 + k
            taps_ref[k : k + 1, lanes] = jnp.sum(
                padded_ref[start : start + frames, lanes] * own, axis=0, keepdims=True
            )
        out_ref[:, lanes] = total * valid
    wait_edges_sent(groups, s, edges)


def convolve_back(grads, convolved, padded, kernel_rows, norm_rows, length, count):
    groups, batches = lax.axis_size("seq"), lax.axis_size("batch")
    frames, width = grads.shape
    taps = kernel_rows.shape[0]
    vmem, smem = pl.BlockSpec(memory_space=pltpu.VMEM), pl.BlockSpec(memory_space=pltpu.SMEM)
    return pl.pallas_call(
        functools.partial(convolve_back_kernel, groups, batches, taps),
        out_shape=[
            jax.ShapeDtypeStruct((frames, width), jnp.float32),
            jax.ShapeDtypeStruct((8, width), jnp.float32),
            jax.ShapeDtypeStruct((2, width), jnp.float32),
        ],
        in_specs=[smem, smem, vmem, vmem, vmem, vmem, vmem],
        out_specs=[vmem] * 3,
        scratch_shapes=[
            pltpu.VMEM((4, 8, width), jnp.float32),
            pltpu.VMEM((frames + 16, width), jnp.float32),
            pltpu.VMEM((2, width), jnp.float32),
            pltpu.SemaphoreType.DMA((4,)),
            pltpu.SemaphoreType.DMA((4,)),
            *sum_scratch(2, width),
        ],
        compiler_params=pltpu.CompilerParams(
            collective_id=2, has_side_effects=True, vmem_limit_bytes=12 << 20
        ),
    )(length.reshape(1), count.reshape(1), grads, convolved, padded, kernel_rows, norm_rows)


def halving_steps(first_seq):
    seq_bits = [("seq", k) for k in range(lax.axis_size("seq").bit_length() - 1)]
    batch_bits = [("batch", k) for k in range(1, lax.axis_size("batch").bit_length() - 1)]
    if first_seq:
        seq_bits = seq_bits[::-1]
    return [("batch", 0)] + seq_bits + batch_bits


def relative_place(place, steps, axis):
    flips = 0
    for order, (name, bit) in enumerate(steps):
        if name == axis:
            flips = flips | (((place >> (len(steps) - 1 - order)) & 1) << bit)
    return flips


def product_kernel(steps, tall, rows, cols, group, where, left_ref, right_ref, out_ref):
    step = pl.program_id(0)
    for inner in range(group):
        place = step * group + inner
        b = where[0] ^ relative_place(place, steps, "batch")
        s = where[1] ^ relative_place(place, steps, "seq")
        if tall:
            left = left_ref[:, pl.ds(pl.multiple_of((b * lax.axis_size("seq") + s) * rows, rows), rows)]
            right = right_ref[...]
        else:
            left = left_ref[:, pl.ds(pl.multiple_of(s * rows, rows), rows)]
            right = right_ref[:, pl.ds(pl.multiple_of(b * cols, cols), cols)]
        out_ref[inner] = lax.dot_general(
            left, right, (((0,), (0,)), ((), ())), preferred_element_type=jnp.float32
        ).astype(jnp.bfloat16)


def block_products(left, right, tall, steps):
    batches, groups = lax.axis_size("batch"), lax.axis_size("seq")
    places = batches * groups
    if tall:
        rows, cols = left.shape[1] // places, right.shape[1]
    else:
        rows, cols = left.shape[1] // groups, right.shape[1] // batches
    me = jnp.stack([lax.axis_index("batch"), lax.axis_index("seq")]).astype(jnp.int32)
    if rows % 128 == 0 and cols % 128 == 0:
        group = 4
        return pl.pallas_call(
            functools.partial(product_kernel, steps, tall, rows, cols, group),
            out_shape=jax.ShapeDtypeStruct((places, rows, cols), jnp.bfloat16),
            grid_spec=pltpu.PrefetchScalarGridSpec(
                num_scalar_prefetch=1,
                grid=(places // group,),
                in_specs=[
                    pl.BlockSpec(left.shape, lambda i, where: (0, 0)),
                    pl.BlockSpec(right.shape, lambda i, where: (0, 0)),
                ],
                out_specs=pl.BlockSpec((group, rows, cols), lambda i, where: (i, 0, 0)),
            ),
            compiler_params=pltpu.CompilerParams(vmem_limit_bytes=40 << 20),
            cost_estimate=pl.CostEstimate(
                flops=2 * left.shape[0] * left.shape[1] * right.shape[1],
                bytes_accessed=2 * (left.size + right.size + left.shape[1] * right.shape[1]),
                transcendentals=0,
            ),
        )(me, left, right)
    whole = lax.dot_general(
        left, right, (((0,), (0,)), ((), ())), preferred_element_type=jnp.float32
    ).astype(jnp.bfloat16)
    if tall:
        blocks = whole.reshape(batches, groups, rows, cols)
    else:
        blocks = whole.reshape(groups, rows, batches, cols).transpose(2, 0, 1, 3)
    batch_bits, seq_bits = batches.bit_length() - 1, groups.bit_length() - 1
    blocks = blocks.reshape((2,) * (batch_bits + seq_bits) + (rows, cols))
    dims = []
    for name, bit in steps:
        dim = batch_bits - 1 - bit if name == "batch" else batch_bits + seq_bits - 1 - bit
        mine = (me[0] if name == "batch" else me[1]) >> bit & 1
        blocks = jnp.where(mine == 1, jnp.flip(blocks, dim), blocks)
        dims.append(dim)
    return blocks.transpose(*dims, len(dims), len(dims) + 1).reshape(places, rows, cols)


def owned_sum(left, right, tall, first_seq):
    steps = halving_steps(first_seq)
    blocks = block_products(left, right, tall, steps)
    for axis, bit in steps:
        half = blocks.shape[0] // 2
        pairs = [(i, i ^ (1 << bit)) for i in range(lax.axis_size(axis))]
        arrived = lax.ppermute(blocks[half:], axis, pairs)
        total = blocks[:half].astype(jnp.float32) + arrived.astype(jnp.float32)
        blocks = total.astype(jnp.bfloat16) if half > 1 else total
    return blocks[0]


def attend_kernel(groups, heads, side, *refs):
    refs = list(refs)

    def take(count):
        taken = refs[:count]
        del refs[:count]
        return taken

    length_ref, qkv_ref, cos_ref, sin_ref = take(4)
    side_in = take(len(side.inputs))
    whole_ref, out_ref = take(2)
    side_out = take(len(side.outs))
    stage, result, sends, arrivals, out_sends, out_arrivals, own_sem = take(7)
    s, b = lax.axis_index("seq"), lax.axis_index("batch")
    frames = qkv_ref.shape[0]
    total_frames = whole_ref.shape[0]
    block = heads * 3 * HD
    width = heads * HD
    parts = stage.shape[0]
    span, narrow = block // parts, width // parts
    greet_seq(groups, s, b, side)
    side.start(side_in, side_out, refs, s, b)

    def rows_of(place):
        return pl.ds(pl.multiple_of(place * frames, frames), frames)

    def heads_copy(target, sender, part):
        return pltpu.make_async_remote_copy(
            src_ref=stage.at[part, target],
            dst_ref=whole_ref.at[rows_of(sender), pl.ds(part * span, span)],
            send_sem=sends.at[part, target],
            recv_sem=arrivals.at[part, sender],
            device_id=(b, target),
            device_id_type=MESH,
        )

    columns = range(0, groups * block, 128)
    for column in sorted(columns, key=lambda c: (c % block // span if parts > 1 else 0, c)):
        pattern = (column // 128) % 3
        values = qkv_ref[:, column : column + 128]
        turned = (values * cos_ref[pattern] + partner_lanes(values) * sin_ref[pattern]).astype(
            jnp.bfloat16
        )
        start = column
        while start < column + 128:
            place, part = start // block, start % block // span
            first = place * block + part * span
            end = min(column + 128, first + span)
            stage[part, place, :, start - first : end - first] = turned[
                :, start - column : end - column
            ]
            if end == first + span:

                @pl.when(s != place)
                def _():
                    heads_copy(place, s, part).start()

                @pl.when(s == place)
                def _():
                    whole_ref[rows_of(s), part * span : (part + 1) * span] = stage[part, place]

            start = end

    valid = lax.broadcasted_iota(jnp.int32, (1, total_frames), 1) < length_ref[0]

    def out_place(owner, part):
        if narrow % 128 == 0:
            start = pl.multiple_of(owner * width + part * narrow, 128)
            return out_ref.at[:, pl.ds(start, narrow)]
        return out_ref.at[owner]

    def result_copy(target, sender, part):
        return pltpu.make_async_remote_copy(
            src_ref=result.at[part, target],
            dst_ref=out_place(sender, part),
            send_sem=out_sends.at[part, target],
            recv_sem=out_arrivals.at[part, sender],
            device_id=(b, target),
            device_id_type=MESH,
        )

    owns = []
    for part in range(parts):
        for k in range(1, groups):
            heads_copy(s, lax.rem(s + k, groups), part).wait_recv()

        def one_block(k, carry, part=part):
            place = lax.rem(s + k, groups)
            for h in range(heads // parts):
                base = part * span + h * 3 * HD
                query = whole_ref[rows_of(place), base : base + HD]
                key = whole_ref[:, base + HD : base + 2 * HD]
                value = whole_ref[:, base + 2 * HD : base + 3 * HD]
                scores = times_transposed(query, key)
                scores = jnp.where(valid, scores, MASKED_SCORE)
                exp_scores = jnp.exp(scores - jnp.max(scores, axis=-1, keepdims=True))
                share = 1.0 / jnp.sum(exp_scores, axis=-1, keepdims=True)
                probs = (exp_scores * share).astype(jnp.bfloat16)
                mixed = jnp.dot(probs, value, preferred_element_type=jnp.float32)
                result[part, place, :, h * HD : (h + 1) * HD] = mixed.astype(jnp.bfloat16)

            @pl.when(k < groups)
            def _():
                result_copy(place, s, part).start()

            return carry

        lax.fori_loop(1, groups + 1, one_block, 0)
        owns.append(pltpu.make_async_copy(result.at[part, s], out_place(s, part), own_sem.at[part]))
        owns[-1].start()
    for part in range(parts):
        for k in range(1, groups):
            other = lax.rem(s + k, groups)
            heads_copy(other, s, part).wait_send()
            result_copy(other, s, part).wait_send()
            result_copy(s, other, part).wait_recv()
    for own in owns:
        own.wait()
    side.wait()


def greet_seq(groups, s, b, side):
    greet([(b, lax.rem(s + k, groups)) for k in range(1, groups)] + side.peers(s, b))


def partner_lanes(values):
    lanes = lax.broadcasted_iota(jnp.int32, values.shape, 1)
    return jnp.where(
        lanes % HD < HD // 2,
        pltpu.roll(values, 128 - HD // 2, 1),
        pltpu.roll(values, HD // 2, 1),
    )


def attend(qkv_rows, length, cosine, sine, side):
    groups = lax.axis_size("seq")
    frames = qkv_rows.shape[0]
    heads = HEADS // groups
    width = heads * HD
    signs = jnp.where(jnp.arange(HD) < HD // 2, -1.0, 1.0)
    cos_head = jnp.concatenate([cosine, cosine], axis=1)
    sin_head = jnp.concatenate([sine, sine], axis=1) * signs
    ones, zeros = jnp.ones_like(cos_head), jnp.zeros_like(cos_head)
    cos_pair = jnp.concatenate([cos_head * 0.125, cos_head, ones] * 2, axis=1)
    sin_pair = jnp.concatenate([sin_head * 0.125, sin_head, zeros] * 2, axis=1)
    cos_three = jnp.stack([cos_pair[:, 128 * i : 128 * (i + 1)] for i in range(3)])
    sin_three = jnp.stack([sin_pair[:, 128 * i : 128 * (i + 1)] for i in range(3)])
    parts = heads // 2 if heads % 2 == 0 else 1
    direct = width // parts % 128 == 0
    out_shape = (frames, groups * width) if direct else (groups, frames, width)
    total = frames * groups
    vmem = pl.BlockSpec(memory_space=pltpu.VMEM)
    whole, out, *brought = pl.pallas_call(
        functools.partial(attend_kernel, groups, heads, side),
        out_shape=(
            jax.ShapeDtypeStruct((total, 3 * width), jnp.bfloat16),
            jax.ShapeDtypeStruct(out_shape, jnp.bfloat16),
            *side.outs,
        ),
        in_specs=[pl.BlockSpec(memory_space=pltpu.SMEM), vmem, vmem, vmem]
        + [pl.BlockSpec(memory_space=pl.ANY)] * len(side.inputs),
        out_specs=(vmem, *[pl.BlockSpec(memory_space=pl.ANY)] * (1 + len(side.outs))),
        scratch_shapes=[
            pltpu.VMEM((parts, groups, frames, 3 * width // parts), jnp.bfloat16),
            pltpu.VMEM((parts, groups, frames, width // parts), jnp.bfloat16),
            pltpu.SemaphoreType.DMA((parts, groups)),
            pltpu.SemaphoreType.DMA((parts, groups)),
            pltpu.SemaphoreType.DMA((parts, groups)),
            pltpu.SemaphoreType.DMA((parts, groups)),
            pltpu.SemaphoreType.DMA((parts,)),
            *side.scratch,
        ],
        compiler_params=pltpu.CompilerParams(
            collective_id=4, has_side_effects=True, vmem_limit_bytes=20 << 20
        ),
        cost_estimate=pl.CostEstimate(
            flops=4 * heads * HD * total * total,
            bytes_accessed=4 * qkv_rows.size + 2 * total * 4 * width,
            transcendentals=heads * total * total,
        ),
    )(length.reshape(1), qkv_rows, cos_three, sin_three, *side.inputs)
    if not direct:
        out = out.transpose(1, 0, 2).reshape(frames, groups * width)
    return whole, out, brought


def attend_back_kernel(groups, heads, side, *refs):
    refs = list(refs)

    def take(count):
        taken = refs[:count]
        del refs[:count]
        return taken

    length_ref, whole_ref, grad_ref, cos_ref, sin_ref = take(5)
    side_in = take(len(side.inputs))
    (out_ref,) = take(1)
    side_out = take(len(side.outs))
    stage, grads, result, query_key, value_total = take(5)
    sends, arrivals, out_sends, out_arrivals, own_sem = take(5)
    s, b = lax.axis_index("seq"), lax.axis_index("batch")
    frames = grad_ref.shape[0]
    total_frames = whole_ref.shape[0]
    block = heads * 3 * HD
    width = heads * HD
    greet_seq(groups, s, b, side)
    side.start(side_in, side_out, refs, s, b)

    def rows_of(place):
        return pl.ds(pl.multiple_of(place * frames, frames), frames)

    def grad_copy(target, sender):
        return pltpu.make_async_remote_copy(
            src_ref=stage.at[target],
            dst_ref=grads.at[rows_of(sender)],
            send_sem=sends.at[target],
            recv_sem=arrivals.at[sender],
            device_id=(b, target),
            device_id_type=MESH,
        )

    for place in range(groups):
        stage[place] = grad_ref[:, place * width : (place + 1) * width]

        @pl.when(s != place)
        def _():
            grad_copy(place, s).start()

        @pl.when(s == place)
        def _():
            grads[rows_of(s), :] = stage[place]

    part_heads = 2 if heads % 2 == 0 else heads
    parts = heads // part_heads
    span = part_heads * 3 * HD

    def out_place(owner, part):
        if block % 128 == 0:
            start = pl.multiple_of(owner * block + part * span, 128)
            return out_ref.at[:, pl.ds(start, span)]
        return out_ref.at[owner, :, pl.ds(part * span, span)]

    def result_copy(target, sender, part):
        return pltpu.make_async_remote_copy(
            src_ref=result.at[part, rows_of(target)],
            dst_ref=out_place(sender, part),
            send_sem=out_sends.at[part, target],
            recv_sem=out_arrivals.at[part, sender],
            device_id=(b, target),
            device_id_type=MESH,
        )

    valid = lax.broadcasted_iota(jnp.int32, (total_frames, 1), 0) < length_ref[0]
    for h in range(heads):
        base = h * 3 * HD
        key = whole_ref[:, base + HD : base + 2 * HD]
        key_turned = key.T
        value = whole_ref[:, base + 2 * HD : base + 3 * HD]
        query_key[...] = jnp.zeros_like(query_key)
        value_total[...] = jnp.zeros_like(value_total)

        def one_block(k, carry, h=h, base=base, key=key, key_turned=key_turned, value=value):
            place = lax.rem(s + k, groups)
            if h == 0:

                @pl.when(k > 0)
                def _():
                    grad_copy(s, place).wait_recv()

            query = whole_ref[rows_of(place), base : base + HD]
            grad = grads[rows_of(place), h * HD : (h + 1) * HD]
            scores = jnp.where(valid, times_transposed(key, query), MASKED_SCORE)
            exp_scores = jnp.exp(scores - jnp.max(scores, axis=0, keepdims=True))
            probs = exp_scores * (1.0 / jnp.sum(exp_scores, axis=0, keepdims=True))
            value_total[...] += jnp.dot(
                probs.astype(jnp.bfloat16), grad, preferred_element_type=jnp.float32
            )
            grad_probs = times_transposed(value, grad)
            mean = jnp.sum(probs * grad_probs, axis=0, keepdims=True)
            grad_scores = (probs * (grad_probs - mean)).astype(jnp.bfloat16)
            query_key[:, HD:] += jnp.dot(grad_scores, query, preferred_element_type=jnp.float32)
            query_key[rows_of(place), :HD] = jnp.dot(
                key_turned, grad_scores, preferred_element_type=jnp.float32
            ).T
            return carry

        lax.fori_loop(0, groups, one_block, 0)
        part, inside = h // part_heads, (h % part_heads) * 3 * HD
        both = query_key[...]
        turned = both * cos_ref[...] + partner_lanes(both) * sin_ref[...]
        result[part, :, inside : inside + 2 * HD] = turned.astype(jnp.bfloat16)
        result[part, :, inside + 2 * HD : inside + 3 * HD] = value_total[...].astype(jnp.bfloat16)
        if (h + 1) % part_heads == 0:
            for k in range(1, groups):
                result_copy(lax.rem(s + k, groups), s, part).start()
    owns = []
    for part in range(parts):
        owns.append(
            pltpu.make_async_copy(
                result.at[part, rows_of(s)], out_place(s, part), own_sem.at[part]
            )
        )
        owns[-1].start()
    for k in range(1, groups):
        other = lax.rem(s + k, groups)
        grad_copy(other, s).wait_send()
        for part in range(parts):
            result_copy(other, s, part).wait_send()
            result_copy(s, other, part).wait_recv()
    for own in owns:
        own.wait()
    side.wait()


def attend_back(whole, grad_attn, length, cosine, sine, side):
    groups = lax.axis_size("seq")
    frames = grad_attn.shape[0]
    heads = HEADS // groups
    width = heads * HD
    block = 3 * width
    total = frames * groups
    signs = jnp.where(jnp.arange(HD) < HD // 2, 1.0, -1.0)
    cos_head = jnp.concatenate([cosine, cosine], axis=1)
    sin_head = jnp.concatenate([sine, sine], axis=1) * signs
    cos_both = jnp.concatenate([cos_head * 0.125, cos_head], axis=1)
    sin_both = jnp.concatenate([sin_head * 0.125, sin_head], axis=1)
    part_heads = 2 if heads % 2 == 0 else heads
    parts = heads // part_heads
    direct = block % 128 == 0
    out_shape = (frames, groups * block) if direct else (groups, frames, block)
    vmem = pl.BlockSpec(memory_space=pltpu.VMEM)
    out, *brought = pl.pallas_call(
        functools.partial(attend_back_kernel, groups, heads, side),
        out_shape=[jax.ShapeDtypeStruct(out_shape, jnp.bfloat16), *side.outs],
        in_specs=[pl.BlockSpec(memory_space=pltpu.SMEM), vmem, vmem, vmem, vmem]
        + [pl.BlockSpec(memory_space=pl.ANY)] * len(side.inputs),
        out_specs=[pl.BlockSpec(memory_space=pl.ANY)] * (1 + len(side.outs)),
        scratch_shapes=[
            pltpu.VMEM((groups, frames, width), jnp.bfloat16),
            pltpu.VMEM((total, width), jnp.bfloat16),
            pltpu.VMEM((parts, total, part_heads * 3 * HD), jnp.bfloat16),
            pltpu.VMEM((total, 2 * HD), jnp.float32),
            pltpu.VMEM((total, HD), jnp.float32),
            pltpu.SemaphoreType.DMA((groups,)),
            pltpu.SemaphoreType.DMA((groups,)),
            pltpu.SemaphoreType.DMA((parts, groups)),
            pltpu.SemaphoreType.DMA((parts, groups)),
            pltpu.SemaphoreType.DMA((parts,)),
            *side.scratch,
        ],
        compiler_params=pltpu.CompilerParams(
            collective_id=5, has_side_effects=True, vmem_limit_bytes=24 << 20
        ),
        cost_estimate=pl.CostEstimate(
            flops=10 * heads * HD * total * total,
            bytes_accessed=2 * total * 8 * width,
            transcendentals=heads * total * total,
        ),
    )(length.reshape(1), whole, grad_attn, cos_both, sin_both, *side.inputs)
    if not direct:
        out = out.transpose(1, 0, 2).reshape(frames, groups * block)
    return out, brought


def flipped(index, places):
    for bit, flip in places:
        mine = lax.rem(index // (1 << bit), 2)
        index = index + flip * (1 - 2 * mine) * (1 << bit)
    return index


def place_of(place, steps, axis, index):
    flips = []
    for order, (name, bit) in enumerate(steps):
        if name == axis:
            flips.append((bit, lax.rem(place // (1 << (len(steps) - 1 - order)), 2)))
    return flipped(index, flips)


class Job:
    def __init__(self, parts, tall, order, far=None, gathered=None):
        self.parts, self.tall, self.far, self.gathered = parts, tall, far, gathered
        self.batches, self.groups = lax.axis_size("batch"), lax.axis_size("seq")
        bits = {
            "x": [("seq", 0)],
            "y": [("seq", k) for k in range(1, self.groups.bit_length() - 1)],
            "1": [("batch", 1)],
            "2": [("batch", k) for k in range(2, self.batches.bit_length() - 1)],
        }
        letters = order if far is None else order.replace("1", "")
        self.steps = [step for letter in letters for step in bits[letter]]
        self.sharing = 2 if far is None else 4
        self.spans = self.batches // self.sharing
        self.levels = len(self.steps)
        self.half = 1 << (self.levels - 1)
        if tall:
            ((small, big),) = parts
            self.rows = big.shape[1] // (self.batches * self.groups)
            self.widths = [small.shape[1]]
        else:
            self.rows = parts[0][0].shape[1] // self.groups
            self.widths = [big.shape[1] // self.batches for _, big in parts]
        self.cols = sum(self.widths)
        self.near_pieces = len(parts) * (self.sharing // 2 + self.spans)
        self.far_pieces = len(parts) * (self.sharing // 2 + (self.sharing - 1) * self.spans)
        if gathered is not None:
            self.near_pieces += 3
            self.far_pieces -= 3 * self.spans

    def fits(self):
        return self.rows % 128 == 0 and all(width % 128 == 0 for width in self.widths)

    def operands(self):
        extra = [array for array in (self.far, self.gathered) if array is not None]
        return [array for part in self.parts for array in part] + extra

    def flops(self):
        return sum(2 * small.size * big.shape[1] for small, big in self.parts)

    def operand_scratch(self):
        scratch, sharing = [], self.sharing
        for small, big in self.parts:
            frames = sharing * small.shape[0]
            scratch.append(pltpu.VMEM((frames, small.shape[1]), jnp.bfloat16))
            scratch.append(pltpu.VMEM((frames, big.shape[1] // sharing), jnp.bfloat16))
        return scratch + [
            pltpu.SemaphoreType.DMA((self.near_pieces,)),
            pltpu.SemaphoreType.DMA((self.far_pieces,)),
            pltpu.SemaphoreType.DMA((self.far_pieces,)),
        ]

    def step_of(self, level):
        return self.steps[self.levels - 1 - level]


def signal(peers):
    barrier = pltpu.get_barrier_semaphore()
    for peer in peers:
        pl.semaphore_signal(barrier, inc=1, device_id=peer, device_id_type=MESH)


def wait_signals(peers):
    pl.semaphore_wait(pltpu.get_barrier_semaphore(), len(peers))


def greet(peers):
    signal(peers)
    wait_signals(peers)


def sibling_of(s, b):
    return (b + 1 - 2 * lax.rem(b, 2), s)


def partner_of(s, b, step):
    axis, bit = step
    if axis == "seq":
        return (b, flipped(s, [(bit, 1)]))
    return (flipped(b, [(bit, 1)]), s)


def quarters(s, b, n):
    core, z = lax.rem(b, 2), lax.rem(b // 2, 2)
    mine, other = 2 * (2 * n + z), 2 * (2 * n + 1 - z)
    return [
        (sibling_of(s, b), mine + 1 - core),
        ((flipped(b, [(1, 1)]), s), other + core),
        ((flipped(b, [(0, 1), (1, 1)]), s), other + 1 - core),
    ]


class Side:
    def __init__(self, rows, wide):
        self.rows, self.wide = rows, wide
        batches = lax.axis_size("batch")
        self.inputs = [*rows, *wide]
        self.outs = [jax.ShapeDtypeStruct(array.shape, array.dtype) for array in rows]
        self.outs += [
            jax.ShapeDtypeStruct((3, array.shape[0], array.shape[1] // 4), array.dtype)
            for array in wide
        ]
        self.count = len(rows) + len(wide) * 3 * (batches // 4)
        self.scratch = [pltpu.SemaphoreType.DMA((self.count,))] * 2 if self.count else []

    def peers(self, s, b):
        return [peer for peer, _ in quarters(s, b, 0)] if self.count else []

    def start(self, inputs, outs, sems, s, b):
        self.copies = []

        def send(source, place, peer):
            n = len(self.copies)
            self.copies.append(
                pltpu.make_async_remote_copy(
                    src_ref=source,
                    dst_ref=place,
                    send_sem=sems[0].at[n],
                    recv_sem=sems[1].at[n],
                    device_id=peer,
                    device_id_type=MESH,
                )
            )
            self.copies[-1].start()

        for i, array in enumerate(self.rows):
            send(inputs[i], outs[i], (flipped(b, [(1, 1)]), s))
        for i, array in enumerate(self.wide, len(self.rows)):
            batches = lax.axis_size("batch")
            span = array.shape[1] // batches
            for n in range(batches // 4):
                for k, (peer, owner) in enumerate(quarters(s, b, n)):
                    columns = pl.ds(pl.multiple_of(owner * span, 128), span)
                    send(inputs[i].at[:, columns], outs[i].at[k, :, pl.ds(n * span, span)], peer)

    def wait(self):
        for copy in self.copies:
            copy.wait()


def swap_operands(job, inputs, held, s, b):
    local, moves, lands = held[2 * len(job.parts) :]
    near, far = [], []

    def bring(source, place, peer=None):
        if peer is None:
            near.append(pltpu.make_async_copy(source, place, local.at[len(near)]))
            near[-1].start()
            return
        n = len(far)
        far.append(
            pltpu.make_async_remote_copy(
                src_ref=source,
                dst_ref=place,
                send_sem=moves.at[n],
                recv_sem=lands.at[n],
                device_id=peer,
                device_id_type=MESH,
            )
        )
        far[-1].start()

    core, z = lax.rem(b, 2), lax.rem(b // 2, 2)
    sibling = sibling_of(s, b)
    for i in range(len(job.parts)):
        small_in, big_in = inputs[2 * i : 2 * i + 2]
        small, big = held[2 * i : 2 * i + 2]
        frames = small_in.shape[0]
        span = big_in.shape[1] // job.batches

        def rows(k):
            return pl.ds(k * frames, frames)

        def columns(owner):
            return pl.ds(pl.multiple_of(owner * span, 128), span)

        bring(small_in, small.at[rows(1)], sibling)
        bring(small_in, small.at[rows(0)])
        if job.far is not None:
            bring(inputs[2], small.at[rows(3)], sibling)
            bring(inputs[2], small.at[rows(2)])
        if job.gathered is not None:
            for k in range(3):
                bring(inputs[3].at[k], big.at[rows(k + 1)])
        for n in range(job.spans):
            inside = pl.ds(n * span, span)
            if job.far is None:
                bring(big_in.at[:, columns(2 * n + 1 - core)], big.at[rows(1), inside], sibling)
                bring(big_in.at[:, columns(2 * n + core)], big.at[rows(0), inside])
                continue
            if job.gathered is None:
                for k, (peer, owner) in enumerate(quarters(s, b, n)):
                    bring(big_in.at[:, columns(owner)], big.at[rows(k + 1), inside], peer)
            bring(big_in.at[:, columns(2 * (2 * n + z) + core)], big.at[rows(0), inside])
    return near, far


def wait_operands(near, far):
    for copy in near:
        copy.wait()
    for copy in far:
        copy.wait_recv()


def block_product(job, held, part, place, s, b):
    small, big = held[2 * part : 2 * part + 2]
    span = big.shape[1] // job.spans
    row = place_of(place, job.steps, "seq", s)
    col = place_of(place, job.steps, "batch", b) // job.sharing
    if job.tall:
        left = big[:, pl.ds(pl.multiple_of(col * span + row * job.rows, 128), job.rows)]
        right = small[...]
    else:
        left = small[:, pl.ds(pl.multiple_of(row * job.rows, 128), job.rows)]
        right = big[:, pl.ds(pl.multiple_of(col * span, 128), span)]
    return lax.dot_general(
        left, right, (((0,), (0,)), ((), ())), preferred_element_type=jnp.float32
    )


def columns_of(job, part):
    start = sum(job.widths[:part])
    return slice(start, start + job.widths[part])


def scatter_kernel(jobs, sequence, *refs):
    refs = list(refs)

    def take(count):
        taken = refs[:count]
        del refs[:count]
        return taken

    inputs = [take(len(job.operands())) for job in jobs]
    (rows_ref,) = take(1)
    outs = [take(len(job.parts)) for job in jobs]
    (small_total,) = take(1)
    scratch = [(take(2 * len(job.parts) + 3), *take(4)) for job in jobs]
    seq_slots, part_sum, batch_slots, small_sends, small_arrivals = take(5)
    batches, groups = jobs[0].batches, jobs[0].groups
    s, b = lax.axis_index("seq"), lax.axis_index("batch")
    peers = sum_peers(groups, batches, s, b)
    greet(peers)

    def slot_of(job, place):
        return lax.rem(place, job.half)

    def copy_of(i, place, level):
        job = jobs[i]
        _, sending, arrived, sends, recvs = scratch[i]
        return pltpu.make_async_remote_copy(
            src_ref=sending.at[slot_of(job, place)],
            dst_ref=arrived.at[place - 1],
            send_sem=sends.at[slot_of(job, place)],
            recv_sem=recvs.at[place - 1],
            device_id=partner_of(s, b, job.step_of(level)),
            device_id_type=MESH,
        )

    works = {i: swap_operands(jobs[i], inputs[i], scratch[i][0], s, b) for i in SWAPS}

    def columns(owner):
        width = part_sum.shape[1]
        return rows_ref.at[:, pl.ds(pl.multiple_of(owner * width, 128), width)]

    over_seq = spread(
        columns, seq_slots, s, peers, range(groups - 1), small_sends, small_arrivals
    )

    def block_sums(i, place, level):
        job = jobs[i]
        held, _, arrived = scratch[i][:3]
        for m in range(job.levels - 1, level, -1):
            copy_of(i, (1 << m) + place, m).wait_recv()
        totals = []
        for part in range(len(job.parts)):
            total = block_product(job, held, part, place, s, b)
            for m in range(job.levels - 1, level, -1):
                came = arrived[(1 << m) + place - 1, :, columns_of(job, part)]
                total = total + came.astype(jnp.float32)
            totals.append(total)
        return totals

    def send_block(i, place, level):
        job = jobs[i]
        totals = block_sums(i, place, level)
        if level < job.levels - 1:
            copy_of(i, place + job.half, job.levels - 1).wait_send()
        for part, total in enumerate(totals):
            scratch[i][1][slot_of(job, place), :, columns_of(job, part)] = total.astype(jnp.bfloat16)
        copy_of(i, place, level).start()

    ready = set()
    over_batch = None
    for i, level in sequence:
        job = jobs[i]
        if i not in ready:
            ready.add(i)
            wait_operands(*works[i])
        if level < 0:
            for part, total in enumerate(block_sums(i, 0, -1)):
                outs[i][part][...] = total
            continue

        def one_place(j, carry, level=level, i=i):
            send_block(i, (2 << level) - 1 - j, level)
            return carry

        lax.fori_loop(0, 1 << level, one_place, 0)
        if over_batch is None:
            part_sum[...] = over_seq()
            over_batch = spread(
                lambda owner: part_sum,
                batch_slots,
                b,
                peers,
                range(groups - 1, groups + batches - 2),
                small_sends,
                small_arrivals,
            )
    small_total[...] = over_batch()
    for i, job in enumerate(jobs):
        for copy in works[i][1]:
            copy.wait_send()
        copy_of(i, job.half, job.levels - 1).wait_send()
        for level in range(job.levels - 1):

            def one_wait(j, carry, level=level, i=i):
                copy_of(i, (1 << level) + j, level).wait_send()
                return carry

            lax.fori_loop(0, 1 << level, one_wait, 0)


def pass_kernel(count, cuts, *refs):
    sources, share, targets, pieces = refs[:count], refs[count], refs[count + 1 : -len(cuts)], refs[-len(cuts) :]
    for source, target in zip(sources, targets):
        target[...] = source[...]
    start = 0
    for cut, piece in zip(cuts, pieces):
        piece[...] = share[start : start + cut, :]
        start += cut


def scatter_sums(jobs, sequence, rows, cuts, collective_id):
    height, width = rows.shape
    width = width // jobs[0].groups
    if width % 128 or not all(job.fits() for job in jobs):
        total = sum_everywhere(rows, collective_id)
        share = lax.dynamic_slice_in_dim(total, lax.axis_index("seq") * width, width, axis=1)
        sums = [
            [
                owned_sum(*((big, small) if job.tall else (small, big)), job.tall, job.tall)
                for small, big in job.parts
            ]
            for job in jobs
        ]
        starts = [sum(cuts[:i]) for i in range(len(cuts))]
        return sums, [share[start : start + cut] for start, cut in zip(starts, cuts)]
    scratch, operands, outs = [], [], []
    for job in jobs:
        block = (job.rows, job.cols)
        scratch += job.operand_scratch()
        scratch += [
            pltpu.VMEM((job.half, *block), jnp.bfloat16),
            pltpu.VMEM((2 * job.half - 1, *block), jnp.bfloat16),
            pltpu.SemaphoreType.DMA((job.half,)),
            pltpu.SemaphoreType.DMA((2 * job.half - 1,)),
        ]
        operands += job.operands()
        outs += [jax.ShapeDtypeStruct((job.rows, width), jnp.float32) for width in job.widths]
    vmem = pl.BlockSpec(memory_space=pltpu.VMEM)
    *results, share = pl.pallas_call(
        functools.partial(scatter_kernel, jobs, sequence),
        out_shape=[*outs, jax.ShapeDtypeStruct((height, width), jnp.float32)],
        in_specs=[pl.BlockSpec(memory_space=pl.ANY)] * len(operands) + [vmem],
        out_specs=[vmem] * (len(outs) + 1),
        scratch_shapes=scratch + sum_scratch(height, width),
        compiler_params=pltpu.CompilerParams(
            collective_id=collective_id, has_side_effects=True, vmem_limit_bytes=60 << 20
        ),
        cost_estimate=pl.CostEstimate(
            flops=sum(job.flops() for job in jobs), bytes_accessed=400 << 20, transcendentals=0
        ),
    )(*operands, rows)
    passes = 1
    specs = [pl.BlockSpec((out.shape[0] // passes, out.shape[1]), lambda i: (i, 0)) for out in outs]
    whole_specs = [pl.BlockSpec((rows, width), lambda i: (0, 0)) for rows in (height, *cuts)]
    pieces = [jax.ShapeDtypeStruct((cut, width), jnp.float32) for cut in cuts]
    results = list(
        pl.pallas_call(
            functools.partial(pass_kernel, len(outs), cuts),
            out_shape=[*outs, *pieces],
            grid=(passes,),
            in_specs=[*specs, whole_specs[0]],
            out_specs=[*specs, *whole_specs[1:]],
            compiler_params=pltpu.CompilerParams(vmem_limit_bytes=60 << 20),
        )(*results, share)
    )
    sums = [[results.pop(0) for _ in job.parts] for job in jobs]
    return sums, results


def shards(
    frames_in,
    cotangent,
    levels,
    lengths,
    token_mask,
    cond_table,
    norm_gains,
    w_ffn1_up,
    w_ffn1_down,
    w_qkv,
    w_out,
    w_glu,
    conv_kernel,
    bn_gain,
    batchnorm_shift_bias,
    w_conv_out,
    w_ffn2_up,
    w_ffn2_down,
    running_mean,
    running_var,
):
    frames = frames_in.shape[1]
    model_width = frames_in.shape[2]
    ff_width = w_ffn1_up.shape[1]
    groups = lax.axis_size("seq")
    batches = lax.axis_size("batch")
    seq_index = lax.axis_index("seq")
    item_index = lax.axis_index("batch")
    seq_length = frames * groups
    level_count = cond_table.shape[0] - 1
    gain_rows = [norm_gains[row].astype(jnp.float32) for row in range(norm_gains.shape[0])]
    level_hot = (jnp.arange(level_count) == levels[0] - 1).astype(jnp.float32)
    level_vector = lax.dynamic_slice_in_dim(cond_table, levels[0] - 1, 1)[0].astype(jnp.float32)
    mask_column = token_mask[0].astype(jnp.float32)[:, None]
    start_rows = (
        frames_in[0].astype(jnp.float32)
        + level_vector[None, :]
        + mask_column * cond_table[level_count].astype(jnp.float32)[None, :]
    )
    length = lax.dynamic_slice_in_dim(lengths, item_index, 1)[0]
    positions = seq_index * frames + jnp.arange(frames)
    unpadded_rows = (positions < length).astype(jnp.float32)[:, None]
    rows_one, ffn1_state = ffn_forward(start_rows, gain_rows[0], w_ffn1_up, w_ffn1_down)
    normed_attn, attn_pull = jax.vjp(layer_norm, rows_one, gain_rows[1])
    attn_in = normed_attn.astype(jnp.bfloat16)
    qkv_rows = jnp.dot(attn_in, w_qkv, preferred_element_type=jnp.float32)
    cosine, sine_table = rope_tables(positions, HD)
    fit = (
        model_width // groups % 128 == 0
        and model_width // batches % 128 == 0
        and ff_width // (groups * batches) % 128 == 0
    )
    side = Side([ffn1_state[1], attn_in] if fit else [], [])
    whole_heads, attn_out, brought = attend(qkv_rows, length, cosine, sine_table, side)
    far_ffn1, far_attn = brought if fit else (None, None)
    rows_two = rows_one + jnp.dot(attn_out, w_out, preferred_element_type=jnp.float32)
    normed_conv, conv_pull = jax.vjp(layer_norm, rows_two, gain_rows[2])
    conv_in = normed_conv.astype(jnp.bfloat16)
    glu_pre = jnp.dot(conv_in, w_glu, preferred_element_type=jnp.float32)
    up_half = glu_pre[:, :model_width]
    glu_sig = jax.nn.sigmoid(glu_pre[:, model_width:])
    glu_low = (up_half * glu_sig * unpadded_rows).astype(jnp.bfloat16)
    taps = conv_kernel.shape[0]
    kernel_rows = conv_kernel.astype(jnp.float32)
    convolved_rows, padded, totals = convolve(glu_low, kernel_rows, length)
    total_sum, total_squares = totals[0], totals[1]
    count_of_frames = jnp.sum(lengths).astype(jnp.float32)
    batchnorm_frame_mean = total_sum / count_of_frames
    bn_var = total_squares / count_of_frames - batchnorm_frame_mean * batchnorm_frame_mean
    batchnorm_inverse_deviation = lax.rsqrt(bn_var + EPSILON)
    batchnorm_scale_factor = bn_gain.astype(jnp.float32)
    normalized_rows = (convolved_rows - batchnorm_frame_mean) * batchnorm_inverse_deviation
    batchnorm_input_rows = normalized_rows * batchnorm_scale_factor + batchnorm_shift_bias.astype(
        jnp.float32
    )
    bn_sig = jax.nn.sigmoid(batchnorm_input_rows)
    conv_act = (batchnorm_input_rows * bn_sig).astype(jnp.bfloat16)
    rows_three = rows_two + jnp.dot(conv_act, w_conv_out, preferred_element_type=jnp.float32)
    rows_four, ffn2_state = ffn_forward(rows_three, gain_rows[3], w_ffn2_up, w_ffn2_down)
    normed_out, out_pull = jax.vjp(layer_norm, rows_four, gain_rows[4])
    out_rows = normed_out.astype(jnp.bfloat16)
    grad_four, grad_gain_four = out_pull(cotangent[0].astype(jnp.float32))
    grad_three, grad_gain_three, ffn2_up_pair, ffn2_down_pair = ffn_backward(
        grad_four, ffn2_state, w_ffn2_up, w_ffn2_down
    )
    grad_r2 = grad_three.astype(jnp.bfloat16)
    batchnorm_gradient = (
        times_transposed(grad_r2, w_conv_out)
        * bn_sig
        * (1.0 + batchnorm_input_rows * (1.0 - bn_sig))
    )
    norm_rows = jnp.stack(
        [batchnorm_frame_mean, batchnorm_inverse_deviation, batchnorm_scale_factor], axis=0
    )
    grad_glu, kernel_grads, gradient_totals = convolve_back(
        batchnorm_gradient, convolved_rows, padded, kernel_rows, norm_rows, length, count_of_frames
    )
    kernel_grads = kernel_grads[:taps]
    gradient_sum_total, gradient_normalized_sum = gradient_totals[0], gradient_totals[1]
    grad_gl = jnp.concatenate(
        [grad_glu * glu_sig, grad_glu * up_half * glu_sig * (1.0 - glu_sig)], axis=1
    ).astype(jnp.bfloat16)
    grad_conv_in, grad_gain_two = conv_pull(times_transposed(grad_gl, w_glu))
    grad_two = grad_three + grad_conv_in
    grad_r = grad_two.astype(jnp.bfloat16)
    grad_attn_out = times_transposed(grad_r, w_out).astype(jnp.bfloat16)
    cos_all, sin_all = rope_tables(jnp.arange(seq_length), HD)
    side = Side([ffn2_up_pair[0]] if fit else [], [ffn2_up_pair[1]] if fit else [])
    grad_qkv, brought = attend_back(whole_heads, grad_attn_out, length, cos_all, sin_all, side)
    far_ffn2, gathered = brought if fit else (None, None)
    grad_attn_part, grad_gain_one = attn_pull(times_transposed(grad_qkv, w_qkv))
    grad_one = grad_two + grad_attn_part
    grad_zero, grad_gain_zero, ffn1_up_pair, ffn1_down_pair = ffn_backward(
        grad_one, ffn1_state, w_ffn1_up, w_ffn1_down
    )
    column_total = jnp.sum(grad_zero, axis=0)
    cond_grad_rows = jnp.concatenate(
        [
            level_hot[:, None] * column_total[None, :],
            jnp.sum(mask_column * grad_zero, axis=0)[None, :],
        ],
        axis=0,
    )
    gain_grads = jnp.stack(
        [grad_gain_zero, grad_gain_one, grad_gain_two, grad_gain_three, grad_gain_four], axis=0
    )
    small_rows = jnp.concatenate([gain_grads, cond_grad_rows, kernel_grads], axis=0)
    small_rows = jnp.pad(small_rows, ((0, -small_rows.shape[0] % 8), (0, 0)))
    jobs = [
        Job([ffn2_up_pair], False, "1yx2", far_ffn2, gathered),
        Job([ffn2_down_pair[::-1]], True, "y12x"),
        Job([(conv_in, grad_gl), (attn_out, grad_r), (conv_act, grad_r2)], False, "xy12"),
        Job([(attn_in, grad_qkv)], False, "1xy2", far_attn),
        Job([ffn1_down_pair[::-1]], True, "xy12"),
        Job([ffn1_up_pair], False, "12xy", far_ffn1),
    ]
    cuts = (5, level_count + 1, taps)
    sums, (gain_sums, cond_sums, tap_sums) = scatter_sums(jobs, SEGMENTS, small_rows, cuts, 7)
    new_mean = 0.9 * running_mean + 0.1 * batchnorm_frame_mean
    new_var = 0.9 * running_var + 0.1 * bn_var * count_of_frames / (count_of_frames - 1.0)
    return (
        out_rows[None],
        grad_zero.astype(jnp.bfloat16)[None],
        cond_sums,
        gain_sums,
        sums[5][0],
        sums[4][0],
        sums[3][0],
        sums[2][1],
        sums[2][0],
        tap_sums,
        gradient_normalized_sum,
        gradient_sum_total,
        sums[2][2],
        sums[0][0],
        sums[1][0],
        new_mean,
        new_var,
    )


def solution(mesh):
    in_specs = (
        P("batch", "seq", None),
        P("batch", "seq", None),
        P("batch"),
        P(),
        P("batch", "seq"),
        P(),
        P(),
        P(),
        P(),
        P(),
        P(),
        P(),
        P(),
        P(),
        P(),
        P(),
        P(),
        P(),
        P(),
        P(),
    )
    out_specs = (
        P("batch", "seq", None),
        P("batch", "seq", None),
        P(None, "seq"),
        P(None, "seq"),
        P("seq", "batch"),
        P(("batch", "seq"), None),
        P("seq", "batch"),
        P("seq", "batch"),
        P("seq", "batch"),
        P(None, "seq"),
        P(),
        P(),
        P("seq", "batch"),
        P("seq", "batch"),
        P(("batch", "seq"), None),
        P(),
        P(),
    )
    return jax.shard_map(shards, mesh=mesh, in_specs=in_specs, out_specs=out_specs, check_vma=False)
```
